32 devices in a mesh: section: 2 (over x), mp: 2 (over y), dp: 8 (over z, core).
Axes of the slice: x: 2, y: 2, z: 4, core: 2. Of those that a mesh axis runs over, the one named last changes fastest.
Arguments:
- atoms_in: bfloat16 [64, 1280, 128], P('dp', 'mp'), may hold values from -6 to 6
- atom_token: int32 [1280], replicated, may hold values from 0 to 159, never falling along the last dimension, each value on 1 to 24 neighbouring positions
- window_start: int32 [40], P('mp'), may hold values from 0 to 1152, as said below
- noise_level: int32 [64], P('dp'), may hold values from 0 to 15
- level_table: bfloat16 [16, 384], replicated, may hold values from -6 to 6
- single_trunk: bfloat16 [160, 384], replicated, may hold values from -6 to 6
- pair: bfloat16 [160, 160, 128], replicated, may hold values from -6 to 6
- atom_gain: bfloat16 [128], replicated, may hold values from 0.5 to 1.5
- atom_qkv: bfloat16 [128, 3, 128], replicated, may hold values from -0.5 to 0.5
- atom_out: bfloat16 [128, 128], replicated, may hold values from -1 to 1
- atom_agg: bfloat16 [128, 768], replicated, may hold values from -0.5 to 0.5
- cond_weight: bfloat16 [2, 384, 3, 768], replicated, may hold values from -0.3125 to 0.3125
- cond_bias: bfloat16 [2, 3, 768], replicated, may hold values from -3 to 3
- pair_weight: bfloat16 [128, 16], P(None, 'mp'), may hold values from -0.5 to 0.5
- attn_in: bfloat16 [768, 4, 768], P(None, None, 'mp'), may hold values from -0.21875 to 0.21875
- attn_out: bfloat16 [768, 768], P('mp'), may hold values from -0.875 to 0.875
- mlp_up: bfloat16 [768, 2, 1536], P(None, None, 'mp'), may hold values from -0.21875 to 0.21875
- mlp_down: bfloat16 [1536, 768], P('mp'), may hold values from -0.15625 to 0.15625
- cotangent: bfloat16 [64, 160, 768], P('dp'), may hold values from -6 to 6
Outputs:
- token_out: bfloat16 [8, 2, 4, 160, 768], P('dp', 'section')
- atoms_grad: float32 [8, 2, 4, 1280, 128], P('dp', 'section', None, 'mp')
- atom_gain_grad: float32 [128], P('section')
- atom_qkv_grad: float32 [128, 3, 128], P('section')
- atom_out_grad: float32 [128, 128], P('section')
- atom_agg_grad: float32 [128, 768], P('section')
- cond_weight_grad: float32 [2, 384, 3, 768], P('section')
- cond_bias_grad: float32 [2, 3, 768], P('section')
- pair_weight_grad: float32 [128, 16], P('section', 'mp')
- attn_in_grad: float32 [768, 4, 768], P('section', None, 'mp')
- attn_out_grad: float32 [768, 768], P('mp', 'section')
- mlp_up_grad: float32 [768, 2, 1536], P('section', None, 'mp')
- mlp_down_grad: float32 [1536, 768], P('mp', 'section')
The draws below stay inside these ranges and needn't reach their ends.
Inputs may be any that keep to these rules, and one draw needn't show every extreme that they name: `atom_token`: the atoms of one token are consecutive; each token has 1 to 24 atoms, some token exactly that many. `window_start`: window w starts between 32 * w - 64 and 32 * w + 32 - 128 // 2, limited to the atoms.
All inputs are finite; a program needn't handle non-finite values.
Results may differ from the reference program's by a relative error of at most 0.025.
Values may be sent and summed in bfloat16 or wider, within the bound.
A program may use at most 384 MiB of HBM per device.

```python
import math
import jax
import jax.numpy as jnp
import numpy as np
from jax import lax

CA = 128
ATOM_HEADS = 4
D = 768
HEADS = 16
DHEAD = 48
CS = 384
CZ = 128
FF = 1536
QBLOCK = 32
KWIN = 128
NTOK = 160
ATOM_TOK = 8
LEVELS = 16
MICRO = 2
SAMP_MB = 4
ATOMS = 1280
WINDOWS = 40
SAMPLES = 64
N_DP = 8


def draw_window_start(key, part):
    key = jax.random.fold_in(key, 7)
    jitter = jax.random.randint(key, (WINDOWS,), 0, QBLOCK + 1)
    base = jnp.arange(WINDOWS, dtype=jnp.int32) * QBLOCK - KWIN // 2
    return jnp.clip(base + jitter, 0, ATOMS - KWIN).astype(jnp.int32)


def touch_ends(values, own_key, least, largest):
    dims = values.shape
    place = [jax.random.randint(jax.random.fold_in(own_key, axis), (), 0, dims[axis]) for axis in range(len(dims))]
    values = values.at[tuple(place)].set(least)
    longest = dims.index(max(dims))
    place[longest] = (place[longest] + 1) % dims[longest]
    return values.at[tuple(place)].set(largest)


def shard_levels(own_key, extent, cuts, least, top_value):
    loudness = 1.0
    for axis_at, parts in cuts:
        draws = jax.random.uniform(jax.random.fold_in(jax.random.fold_in(own_key, 6), axis_at), (parts,), jnp.float32, least / len(cuts), top_value / len(cuts))
        loudness = loudness * jnp.repeat(jnp.exp(draws), extent[axis_at] // parts).reshape((-1,) + (1,) * (len(extent) - 1 - axis_at))
    return loudness


def length_profile(amount, total, most, slope):
    loads = [(1 << 20) // math.isqrt(grade ** slope) + 1 for grade in range(2, amount + 1)]
    surplus, holding = total - most - (amount - 1), [1] * (amount - 1)
    while surplus > 0:
        free = [i for i in range(amount - 1) if holding[i] < most]
        whole, budget = sum([loads[i] for i in free]), surplus
        for i in free:
            addition = min(most - holding[i], max(1, budget * loads[i] // whole), surplus)
            holding[i] = holding[i] + addition
            surplus = surplus - addition
    return np.array([most] + holding)


def uneven(key, number_of, total, most, skew):
    if number_of == 2:
        one = jax.random.randint(key, (), max(1, total - most), min(most, total - 1) + 1)
        return jnp.stack([one, total - one])
    lengths = jnp.asarray(length_profile(number_of, total, most, skew), jnp.int32)
    couples = (number_of - 1) // 2
    giver, sink = lengths[1:1 + 2 * couples:2], lengths[2:2 + 2 * couples:2]
    room = jnp.minimum(giver - 1, most - sink)
    moved = jax.random.randint(jax.random.fold_in(key, 1), (couples,), 0, 1 << 20) % (room + 1)
    lengths = lengths.at[1:1 + 2 * couples:2].set(giver - moved).at[2:2 + 2 * couples:2].set(sink + moved)
    return lengths[jax.random.permutation(jax.random.fold_in(key, 2), number_of)]


def noise(own_key, dims, spread, most, cuts=(), kind=jnp.bfloat16):
    drawn = jax.random.normal(own_key, dims, jnp.float32) * spread
    if len(cuts) > 0:
        drawn = shard_levels(own_key, dims, cuts, -0.22, 0.18) * drawn
    return jnp.clip(drawn, min=-most, max=most).astype(kind)


def setup_inputs(seed: int = 0) -> dict:
    key_list = jax.random.split(jax.random.key(seed), 20)
    return {
        "atoms_in": noise(key_list[0], (SAMPLES, ATOMS, CA), 1.0, 6.0, ((0, 8), (1, 2))),
        "atom_token": jnp.searchsorted(jnp.cumsum(uneven(key_list[1], NTOK, ATOMS, 3 * ATOM_TOK, 0)), jnp.arange(ATOMS), side="right").astype(jnp.int32),
        "window_start": draw_window_start(jax.random.fold_in(key_list[19], 71), 0),
        "noise_level": touch_ends(jax.random.randint(key_list[3], (SAMPLES,), 0, LEVELS), jax.random.fold_in(key_list[3], 1), 0, LEVELS - 1).astype(jnp.int32),
        "level_table": noise(key_list[4], (LEVELS, CS), 1.0, 6.0),
        "single_trunk": noise(key_list[5], (NTOK, CS), 1.0, 6.0),
        "pair": noise(key_list[6], (NTOK, NTOK, CZ), 1.0, 6.0),
        "atom_gain": jnp.clip(1.0 + 0.1 * jax.random.normal(key_list[7], (CA,), jnp.float32), 0.5, 1.5).astype(jnp.bfloat16),
        "atom_qkv": noise(key_list[8], (CA, 3, CA), CA ** -0.5, 0.5),
        "atom_out": noise(key_list[9], (CA, CA), (CA // 4) ** -0.5, 1.0),
        "atom_agg": noise(key_list[10], (CA, D), CA ** -0.5, 0.5),
        "cond_weight": noise(key_list[11], (2, CS, 3, D), CS ** -0.5, 0.3125),
        "cond_bias": noise(key_list[12], (2, 3, D), 0.5, 3.0),
        "pair_weight": noise(key_list[13], (CZ, HEADS), CZ ** -0.5, 0.5, ((1, 2),)),
        "attn_in": noise(key_list[14], (D, 4, D), D ** -0.5, 0.21875, ((2, 2),)),
        "attn_out": noise(key_list[15], (D, D), (D // HEADS) ** -0.5, 0.875, ((0, 2),)),
        "mlp_up": noise(key_list[16], (D, 2, FF), D ** -0.5, 0.21875, ((2, 2),)),
        "mlp_down": noise(key_list[17], (FF, D), FF ** -0.5, 0.15625, ((0, 2),)),
        "cotangent": noise(key_list[18], (SAMPLES, NTOK, D), 1.0, 6.0, ((0, 8),)),
    }


@jax.custom_vjp
def low(v):
    return lax.optimization_barrier(v.astype(jnp.bfloat16)).astype(jnp.float32)

@jax.custom_vjp
def low_back(v):
    return v

def low_keep(v):
    return (low(v), None)

def low_pass(kept, grad):
    return (grad,)

def back_keep(v):
    return (v, None)

def back_low(kept, grad):
    return (low(grad),)
low.defvjp(low_keep, low_pass)
low_back.defvjp(back_keep, back_low)
HIGH = lax.Precision.HIGHEST
EPS = 1e-05

def product(form, left, right):
    return jnp.einsum(form, left, right, precision=HIGH)

def layer_norm(values):
    center = values - lax.optimization_barrier(jnp.mean(values, -1, keepdims=True))
    return center * lax.rsqrt(lax.optimization_barrier(jnp.mean(center * center, -1, keepdims=True)) + EPS)

def round_both(values):
    return low(low_back(values))

def to_wide(values):
    return values.astype(jnp.float32)

def atom_block(inputs, gain, w_qkv, w_aout, w_agg, rows, member, counts):
    group = inputs.shape[0]
    atom_size = CA // ATOM_HEADS
    hidden = low(layer_norm(inputs) * gain)
    projected = product('gac,ckd->gakd', hidden, w_qkv)
    queries = round_both(projected[:, :, 0])
    keys = round_both(projected[:, :, 1])
    values = round_both(projected[:, :, 2])
    blocks = queries.reshape(group, WINDOWS, QBLOCK, ATOM_HEADS, atom_size)
    window_keys = keys[:, rows].reshape(group, WINDOWS, KWIN, ATOM_HEADS, atom_size)
    window_values = values[:, rows].reshape(group, WINDOWS, KWIN, ATOM_HEADS, atom_size)
    scores = low_back(product('gwqhe,gwkhe->gwhqk', blocks, window_keys) * atom_size ** (-0.5))
    attend = jax.nn.softmax(scores, axis=-1)
    mixed = round_both(product('gwhqk,gwkhe->gwqhe', low(attend), window_values)).reshape(group, ATOMS, CA)
    after = inputs + low_back(product('gac,cd->gad', mixed, w_aout))
    gate_pre = low_back(product('gac,cd->gad', low(after), w_agg))
    summed = product('gad,at->gtd', jax.nn.silu(gate_pre), member)
    return round_both(summed / counts[None, :, None])

def token_block(tokens, cond_low, bias, w_cond, b_cond, w_in, w_out, w_up, w_down):
    group = tokens.shape[0]
    cond = low_back(product('gnc,jckd->gnjkd', cond_low, w_cond) + b_cond)
    scale = jax.nn.sigmoid(cond[:, :, :, 0])
    shift = cond[:, :, :, 1]
    gate = jax.nn.sigmoid(cond[:, :, :, 2])
    inner = low(layer_norm(tokens) * scale[:, :, 0] + shift[:, :, 0])
    proj = product('gnd,dke->gnke', inner, w_in)
    queries = round_both(proj[:, :, 0]).reshape(group, NTOK, HEADS, DHEAD)
    keys = round_both(proj[:, :, 1]).reshape(group, NTOK, HEADS, DHEAD)
    values = round_both(proj[:, :, 2]).reshape(group, NTOK, HEADS, DHEAD)
    gate_sig = jax.nn.sigmoid(low_back(proj[:, :, 3]))
    scores = low_back(product('gqhe,gkhe->ghqk', queries, keys) * DHEAD ** (-0.5) + bias[None])
    attend = jax.nn.softmax(scores, axis=-1)
    heads_out = low_back(product('ghqk,gkhe->gqhe', low(attend), values)).reshape(group, NTOK, D)
    gated = low(heads_out * gate_sig)
    attn = low_back(product('gne,ed->gnd', gated, w_out))
    middle = tokens + gate[:, :, 0] * attn
    inner2 = low(layer_norm(middle) * scale[:, :, 1] + shift[:, :, 1])
    upward = low_back(product('gnd,dkf->gnkf', inner2, w_up))
    hidden2 = low(jax.nn.silu(upward[:, :, 0]) * upward[:, :, 1])
    mlp = low_back(product('gnf,fd->gnd', hidden2, w_down))
    return middle + gate[:, :, 1] * mlp

def reference(atoms_in, atom_token, window_start, noise_level, level_table, single_trunk, pair, atom_gain, atom_qkv, atom_out, atom_agg, cond_weight, cond_bias, pair_weight, attn_in, attn_out, mlp_up, mlp_down, cotangent):
    token_ids = jnp.arange(NTOK, dtype=jnp.int32)
    member = (atom_token[:, None] == token_ids[None, :]).astype(jnp.float32)
    counts = lax.optimization_barrier(jnp.sum(member, 0))
    rows = window_start[:, None].astype(jnp.int32) + jnp.arange(KWIN, dtype=jnp.int32)[None, :]
    level_pick = (noise_level[:, None] == jnp.arange(LEVELS, dtype=jnp.int32)[None, :]).astype(jnp.float32)
    single = to_wide(single_trunk)[None] + product('sl,lc->sc', level_pick, to_wide(level_table))[:, None, :]
    cond_low = low(layer_norm(single))
    group = math.gcd(SAMPLES, 16)
    count_groups = SAMPLES // group
    pair_wide = to_wide(pair)

    def forward(inputs, weights):
        gain, w_qkv, w_aout, w_agg, w_cond, b_cond, w_pair, w_in, w_out, w_up, w_down = weights
        bias = product('ijc,ch->hij', low(layer_norm(pair_wide)), w_pair)

        def one_group(pieces):
            group_in, group_cond = pieces
            tokens = atom_block(group_in, gain, w_qkv, w_aout, w_agg, rows, member, counts)
            return token_block(tokens, group_cond, bias, w_cond, b_cond, w_in, w_out, w_up, w_down)
        outputs = lax.map(jax.checkpoint(one_group), (inputs.reshape(count_groups, group, ATOMS, CA), cond_low.reshape(count_groups, group, NTOK, CS)))
        return outputs.reshape(SAMPLES, NTOK, D)
    weights = (to_wide(atom_gain), to_wide(atom_qkv), to_wide(atom_out), to_wide(atom_agg), to_wide(cond_weight), to_wide(cond_bias), to_wide(pair_weight), to_wide(attn_in), to_wide(attn_out), to_wide(mlp_up), to_wide(mlp_down))
    result, pull = jax.vjp(forward, to_wide(atoms_in), weights)
    grad_in, grads = pull(to_wide(cotangent))
    token_out = result.astype(jnp.bfloat16).reshape(N_DP, MICRO, SAMP_MB, NTOK, D)
    atoms_grad = grad_in.reshape(N_DP, MICRO, SAMP_MB, ATOMS, CA)
    return (token_out, atoms_grad, grads[0], grads[1], grads[2], grads[3], grads[4], grads[5], grads[6], grads[7], grads[8], grads[9], grads[10])
```

```python
import functools

import jax
import jax.numpy as jnp
from jax import lax
from jax.experimental import pallas as pl
from jax.experimental.pallas import tpu as pltpu
from jax.sharding import PartitionSpec as P

QBLOCK = 32
KWIN = 128
MICRO = 2
ATOM_HEADS = 4
SPAN = 2
EPS = 1e-05
LOW = jnp.bfloat16
WIDE = jnp.float32
MIB = 1 << 20


def mul(left, right):
    return lax.dot_general(left, right, (((1,), (0,)), ((), ())), preferred_element_type=WIDE)


def mul_nt(left, right):
    return lax.dot_general(left, right, (((1,), (1,)), ((), ())), preferred_element_type=WIDE)


def mul_tn(left, right):
    return lax.dot_general(left, right, (((0,), (0,)), ((), ())), preferred_element_type=WIDE)


def layer_norm(values):
    center = values - jnp.mean(values, -1, keepdims=True)
    inverse = lax.rsqrt(jnp.mean(center * center, -1, keepdims=True) + EPS)
    return center * inverse, inverse


def norm_back(normed, inverse, grad):
    return inverse * (
        grad
        - jnp.mean(grad, -1, keepdims=True)
        - normed * jnp.mean(grad * normed, -1, keepdims=True)
    )


def sigmoid(values):
    return 1.0 / (1.0 + jnp.exp(-values))


def params(mib, semantics=None):
    return pltpu.CompilerParams(vmem_limit_bytes=mib * MIB, dimension_semantics=semantics)


def cost(flops, moved, exps=0):
    return pl.CostEstimate(flops=int(flops), bytes_accessed=int(moved), transcendentals=int(exps))


def sds(shape, dtype):
    return jax.ShapeDtypeStruct(shape, dtype)


def pair_kernel(pair_ref, weight_ref, low_ref, bias_ref):
    normed, _ = layer_norm(pair_ref[...].astype(WIDE))
    low = normed.astype(LOW)
    low_ref[...] = low
    for i in range(low.shape[0]):
        bias_ref[:, i, :] = mul_nt(weight_ref[...], low[i])


def pair_bias(pair, weight):
    tokens, width = pair.shape[1], pair.shape[2]
    heads, block = weight.shape[0], 8
    return pl.pallas_call(
        pair_kernel,
        grid=(tokens // block,),
        in_specs=[
            pl.BlockSpec((block, tokens, width), lambda i: (i, 0, 0)),
            pl.BlockSpec((heads, width), lambda i: (0, 0)),
        ],
        out_specs=[
            pl.BlockSpec((block, tokens, width), lambda i: (i, 0, 0)),
            pl.BlockSpec((heads, block, tokens), lambda i: (0, i, 0)),
        ],
        out_shape=[sds(pair.shape, LOW), sds((heads, tokens, tokens), WIDE)],
        compiler_params=params(24),
        cost_estimate=cost(20e9, 16e6),
        name="pair_bias",
    )(pair, weight)


def pair_back_kernel(low_ref, grad_ref, out_ref):
    @pl.when(pl.program_id(0) == 0)
    def _():
        out_ref[...] = jnp.zeros_like(out_ref)

    total = out_ref[...]
    heads = grad_ref.shape[0]
    for i in range(low_ref.shape[0]):
        grad = grad_ref[:, i, :]
        high = grad.astype(LOW)
        rest = (grad - high.astype(WIDE)).astype(LOW)
        both = mul(jnp.concatenate([high, rest], 0), low_ref[i])
        total += both[:heads] + both[heads:]
    out_ref[...] = total


def pair_back(low, grad):
    tokens, width = low.shape[1], low.shape[2]
    heads, block = grad.shape[0], 8
    return pl.pallas_call(
        pair_back_kernel,
        grid=(tokens // block,),
        in_specs=[
            pl.BlockSpec((block, tokens, width), lambda i: (i, 0, 0)),
            pl.BlockSpec((heads, block, tokens), lambda i: (0, i, 0)),
        ],
        out_specs=pl.BlockSpec((heads, width), lambda i: (0, 0)),
        out_shape=sds((heads, width), WIDE),
        compiler_params=params(24),
        cost_estimate=cost(10e9, 9e6),
        name="pair_back",
    )(low, grad)


def cond_kernel(trunk_ref, level_ref, weight_ref, bias_ref, low_ref, cond_ref):
    step = pl.program_id(0)
    samples, tokens = level_ref.shape[0], trunk_ref.shape[0]

    @pl.when(step == 0)
    def _():
        trunk = trunk_ref[...].astype(WIDE)
        for s in range(samples):
            normed, _ = layer_norm(trunk + level_ref[s])
            low_ref[s * tokens : (s + 1) * tokens, :] = normed.astype(LOW)

    value = mul(low_ref[...], weight_ref[0]) + bias_ref[0]
    cond_ref[0] = jnp.where(step % 3 == 1, value, sigmoid(value))


def conditioning(trunk, levels, weight, bias):
    tokens, width = trunk.shape
    samples, parts, wide = levels.shape[0], weight.shape[0], weight.shape[2]
    rows = samples * tokens
    return pl.pallas_call(
        cond_kernel,
        grid=(parts,),
        in_specs=[
            pl.BlockSpec((tokens, width), lambda i: (0, 0)),
            pl.BlockSpec((samples, 1, width), lambda i: (0, 0, 0)),
            pl.BlockSpec((1, width, wide), lambda i: (i, 0, 0)),
            pl.BlockSpec((1, 1, wide), lambda i: (i, 0, 0)),
        ],
        out_specs=[
            pl.BlockSpec((rows, width), lambda i: (0, 0)),
            pl.BlockSpec((1, rows, wide), lambda i: (i, 0, 0)),
        ],
        out_shape=[sds((rows, width), LOW), sds((parts, rows, wide), WIDE)],
        compiler_params=params(24),
        cost_estimate=cost(4e9, 10e6),
        name="conditioning",
    )(trunk, levels, weight, bias)


def lane_heads(rows, width, size):
    return lax.broadcasted_iota(jnp.int32, (rows, width), 1) // size


def spread(values, heads):
    head = lane_heads(values.shape[0], values.shape[1], values.shape[1] // heads)
    zero = jnp.zeros_like(values)
    return jnp.concatenate([jnp.where(head == h, values, zero) for h in range(heads)], 0)


def gather_heads(values, heads):
    rows = values.shape[0] // heads
    head = lane_heads(rows, values.shape[1], values.shape[1] // heads)
    total = jnp.where(head == 0, values[:rows], 0.0)
    for h in range(1, heads):
        total += jnp.where(head == h, values[h * rows : (h + 1) * rows], 0.0)
    return total


def key_base(group, atoms):
    start = group * SPAN * QBLOCK - KWIN // 2
    return pl.multiple_of(jnp.clip(start, 0, atoms - KWIN - (SPAN - 1) * QBLOCK - QBLOCK), QBLOCK)


def atom_front_kernel(
    atoms_ref, gain_ref, qkv_w_ref, out_w_ref, agg_w_ref, rel_ref, ids_ref, inv_ref,
    qkv_ref, probs_ref, mixed_ref, tokens_ref,
    total,
):
    atoms, width = atoms_ref.shape[1], atoms_ref.shape[2]
    groups, keys_in = probs_ref.shape[1], probs_ref.shape[2]
    queries_in = SPAN * QBLOCK
    scale = (width // ATOM_HEADS) ** (-0.5)
    wide = atoms_ref[0].astype(WIDE)
    normed, _ = layer_norm(wide)
    hidden = (normed * gain_ref[...].astype(WIDE)).astype(LOW)
    qkv_ref[0] = mul(hidden, qkv_w_ref[...]).astype(LOW)
    place = lax.broadcasted_iota(jnp.int32, (keys_in, ATOM_HEADS * queries_in), 0)

    def attend(group, carry):
        base = key_base(group, atoms)
        first = pl.multiple_of(group * queries_in, queries_in)
        queries = spread(qkv_ref[0, pl.ds(first, queries_in), :width], ATOM_HEADS)
        keys = qkv_ref[0, pl.ds(base, keys_in), width : 2 * width]
        values = qkv_ref[0, pl.ds(base, keys_in), 2 * width :]
        offset = place - rel_ref[group]
        scores = mul_nt(keys, queries) * scale
        scores = jnp.where((offset >= 0) & (offset < KWIN), scores, -1e30)
        exps = jnp.exp(scores - jnp.max(scores, 0, keepdims=True))
        probs = (exps * (1.0 / jnp.sum(exps, 0, keepdims=True))).astype(LOW)
        probs_ref[0, group] = probs
        mixed_ref[0, pl.ds(first, queries_in), :] = gather_heads(
            mul_tn(probs, values), ATOM_HEADS
        ).astype(LOW)
        return carry

    lax.fori_loop(0, groups, attend, 0)
    chunk = 256
    ids = lax.broadcasted_iota(jnp.int32, (total.shape[0], chunk), 0)
    for i in range(atoms // chunk):
        rows = slice(i * chunk, (i + 1) * chunk)
        after = wide[rows] + mul(mixed_ref[0, rows, :], out_w_ref[...])
        pre = mul(after.astype(LOW), agg_w_ref[...])
        units = (pre * sigmoid(pre)).astype(LOW)
        member = jnp.where(ids == ids_ref[:, rows], 1.0, 0.0).astype(LOW)
        part = mul(member, units)
        if i == 0:
            total[...] = part
        else:
            total[...] += part
    tokens_ref[0] = (total[...] * inv_ref[...]).astype(LOW)


def atom_front(atoms, gain, qkv_w, out_w, agg_w, rel, ids, inverse_counts):
    samples, count, width = atoms.shape
    groups = count // (SPAN * QBLOCK)
    keys_in = KWIN + SPAN * QBLOCK
    lanes = ATOM_HEADS * SPAN * QBLOCK
    tokens, wide = inverse_counts.shape[0], agg_w.shape[1]

    def whole(array):
        return pl.BlockSpec(array.shape, lambda i: (0,) * array.ndim)

    def sample(*shape):
        return pl.BlockSpec((1,) + shape, lambda i: (i,) + (0,) * len(shape))

    return pl.pallas_call(
        atom_front_kernel,
        grid=(samples,),
        in_specs=[sample(count, width)]
        + [whole(a) for a in (gain, qkv_w, out_w, agg_w, rel, ids, inverse_counts)],
        out_specs=[
            sample(count, 3 * width),
            sample(groups, keys_in, lanes),
            sample(count, width),
            sample(tokens, wide),
        ],
        out_shape=[
            sds((samples, count, 3 * width), LOW),
            sds((samples, groups, keys_in, lanes), LOW),
            sds((samples, count, width), LOW),
            sds((samples, tokens, wide), LOW),
        ],
        scratch_shapes=[pltpu.VMEM((tokens, wide), WIDE)],
        compiler_params=params(48),
        cost_estimate=cost(20e9, 12e6),
        name="atom_front",
    )(atoms, gain, qkv_w, out_w, agg_w, rel, ids, inverse_counts)


def atom_back_kernel(
    atoms_ref, gain_ref, qkv_w_ref, out_w_ref, agg_w_ref, ids_ref, inv_ref,
    qkv_ref, probs_ref, mixed_ref, grad_ref,
    atoms_grad_ref, gain_grad_ref, qkv_grad_ref, out_grad_ref, agg_grad_ref,
    after_grad, mixed_grad, key_grad, value_grad, proj_grad,
):
    atoms, width = atoms_ref.shape[1], atoms_ref.shape[2]
    groups, keys_in = probs_ref.shape[1], probs_ref.shape[2]
    queries_in = SPAN * QBLOCK
    scale = (width // ATOM_HEADS) ** (-0.5)

    @pl.when(pl.program_id(0) == 0)
    def _():
        for ref in (gain_grad_ref, qkv_grad_ref, out_grad_ref, agg_grad_ref):
            ref[...] = jnp.zeros_like(ref)

    grad = (grad_ref[0].astype(WIDE) * inv_ref[...]).astype(LOW)
    chunk = 256
    token_ids = lax.broadcasted_iota(jnp.int32, (chunk, grad.shape[0]), 1)
    for i in range(atoms // chunk):
        rows = slice(i * chunk, (i + 1) * chunk)
        mixed = mixed_ref[0, rows, :]
        after = atoms_ref[0, rows, :].astype(WIDE) + mul(mixed, out_w_ref[...])
        after_low = after.astype(LOW)
        pre = mul(after_low, agg_w_ref[...])
        sigma = sigmoid(pre)
        member = jnp.where(token_ids == ids_ref[rows, :], 1.0, 0.0).astype(LOW)
        unit_grad = mul(member, grad)
        pre_grad = (unit_grad * (sigma * (1.0 + pre * (1.0 - sigma)))).astype(LOW)
        agg_grad_ref[...] += mul_tn(after_low, pre_grad)
        after_back = mul_nt(pre_grad, agg_w_ref[...])
        after_grad[rows, :] = after_back
        branch = after_back.astype(LOW)
        out_grad_ref[...] += mul_tn(mixed, branch)
        mixed_grad[rows, :] = mul_nt(branch, out_w_ref[...]).astype(LOW)
    key_grad[...] = jnp.zeros_like(key_grad)
    value_grad[...] = jnp.zeros_like(value_grad)

    def attend(group, carry):
        base = key_base(group, atoms)
        first = pl.multiple_of(group * queries_in, queries_in)
        queries = spread(qkv_ref[0, pl.ds(first, queries_in), :width], ATOM_HEADS)
        grads = spread(mixed_grad[pl.ds(first, queries_in), :], ATOM_HEADS)
        keys = qkv_ref[0, pl.ds(base, keys_in), width : 2 * width]
        values = qkv_ref[0, pl.ds(base, keys_in), 2 * width :]
        probs_low = probs_ref[0, group]
        probs = probs_low.astype(WIDE)
        probs_grad = mul_nt(values, grads)
        mean = jnp.sum(probs * probs_grad, 0, keepdims=True)
        scores_grad = (probs * (probs_grad - mean)).astype(LOW)
        query_grad = gather_heads(mul_tn(scores_grad, keys), ATOM_HEADS)
        proj_grad[pl.ds(first, queries_in), :width] = (query_grad * scale).astype(LOW)
        key_grad[pl.ds(base, keys_in), :] += mul(scores_grad, queries)
        value_grad[pl.ds(base, keys_in), :] += mul(probs_low, grads)
        return carry

    lax.fori_loop(0, groups, attend, 0)
    proj_grad[:, width : 2 * width] = (key_grad[...] * scale).astype(LOW)
    proj_grad[:, 2 * width :] = value_grad[...].astype(LOW)
    gain = gain_ref[...].astype(WIDE)
    normed, inverse = layer_norm(atoms_ref[0].astype(WIDE))
    hidden = (normed * gain).astype(LOW)
    proj = proj_grad[...]
    qkv_grad_ref[...] += mul_tn(hidden, proj)
    hidden_grad = mul_nt(proj, qkv_w_ref[...])
    gain_grad_ref[...] += jnp.sum(hidden_grad * normed, 0, keepdims=True)
    atoms_grad_ref[0] = after_grad[...] + norm_back(normed, inverse, hidden_grad * gain)


def atom_back(atoms, gain, qkv_w, out_w, agg_w, ids, inverse_counts, qkv, probs, mixed, grad):
    samples, count, width = atoms.shape
    wide = agg_w.shape[1]

    def whole(shape):
        return pl.BlockSpec(shape, lambda i: (0,) * len(shape))

    def sample(array):
        return pl.BlockSpec((1,) + array.shape[1:], lambda i: (i,) + (0,) * (array.ndim - 1))

    fixed = (gain, qkv_w, out_w, agg_w, ids, inverse_counts)
    return pl.pallas_call(
        atom_back_kernel,
        grid=(samples,),
        in_specs=[sample(atoms)]
        + [whole(a.shape) for a in fixed]
        + [sample(a) for a in (qkv, probs, mixed, grad)],
        out_specs=[
            sample(atoms),
            whole((1, width)),
            whole((width, 3 * width)),
            whole((width, width)),
            whole((width, wide)),
        ],
        out_shape=[
            sds(atoms.shape, WIDE),
            sds((1, width), WIDE),
            sds((width, 3 * width), WIDE),
            sds((width, width), WIDE),
            sds((width, wide), WIDE),
        ],
        scratch_shapes=[
            pltpu.VMEM((count, width), WIDE),
            pltpu.VMEM((count, width), LOW),
            pltpu.VMEM((count, width), WIDE),
            pltpu.VMEM((count, width), WIDE),
            pltpu.VMEM((count, 3 * width), LOW),
        ],
        compiler_params=params(48),
        cost_estimate=cost(40e9, 12e6),
        name="atom_back",
    )(atoms, *fixed, qkv, probs, mixed, grad)


def token_attention_kernel(
    tokens_ref, scale_ref, shift_ref, gate_ref, bias_ref, in_a_ref, in_b_ref, out_a_ref, out_b_ref,
    inner_ref, qkv_ref, sig_ref, heads_ref, gated_ref, probs_ref, attn_ref, middle_ref,
):
    rows, width = tokens_ref.shape
    samples, heads, count = probs_ref.shape[0], probs_ref.shape[1], probs_ref.shape[2]
    local = in_a_ref.shape[1] // 4
    size = 2 * local // heads
    scale = size ** (-0.5)
    wide = tokens_ref[...].astype(WIDE)
    normed, _ = layer_norm(wide)
    inner = (normed * scale_ref[0] + shift_ref[0]).astype(LOW)
    inner_ref[...] = inner
    for half, weight_ref in enumerate((in_a_ref, in_b_ref)):
        qkv_ref[half] = mul(inner, weight_ref[:, : 3 * local]).astype(LOW)
        sig_ref[half] = sigmoid(mul(inner, weight_ref[:, 3 * local :]))
        for s in range(samples):
            at = slice(s * count, (s + 1) * count)
            outs = []
            for h in range(heads // 2):
                col = h * size
                query = qkv_ref[half, at, col : col + size]
                key = qkv_ref[half, at, local + col : local + col + size]
                value = qkv_ref[half, at, 2 * local + col : 2 * local + col + size]
                scores = mul_nt(query, key) * scale + bias_ref[half * (heads // 2) + h]
                exps = jnp.exp(scores - jnp.max(scores, -1, keepdims=True))
                probs = (exps * (1.0 / jnp.sum(exps, -1, keepdims=True))).astype(LOW)
                probs_ref[s, half * (heads // 2) + h] = probs
                outs.append(mul(probs, value))
            heads_ref[half, at, :] = jnp.concatenate(outs, 1)
        gated_ref[half] = (heads_ref[half] * sig_ref[half]).astype(LOW)
    attn = mul(gated_ref[0], out_a_ref[...]) + mul(gated_ref[1], out_b_ref[...])
    attn_ref[...] = attn
    middle_ref[...] = wide + gate_ref[0] * attn


def vmem(count):
    return [pl.BlockSpec(memory_space=pltpu.VMEM)] * count


def part(index, shape):
    return pl.BlockSpec((1,) + shape, lambda i: (index,) + (0,) * len(shape))


def token_attention(tokens, cond, bias, in_a, in_b, out_a, out_b):
    rows, width = tokens.shape
    heads, count = bias.shape[0], bias.shape[1]
    samples, local = rows // count, in_a.shape[1] // 4

    def whole(shape):
        return pl.BlockSpec(shape, lambda i: (0,) * len(shape))

    outs = [
        ((rows, width), LOW),
        ((2, rows, 3 * local), LOW),
        ((2, rows, local), WIDE),
        ((2, rows, local), WIDE),
        ((2, rows, local), LOW),
        ((samples, heads, count, count), LOW),
        ((rows, width), WIDE),
        ((rows, width), WIDE),
    ]
    return pl.pallas_call(
        token_attention_kernel,
        grid=(1,),
        in_specs=[whole(tokens.shape)]
        + [part(i, (rows, width)) for i in (0, 1, 2)]
        + [whole(a.shape) for a in (bias, in_a, in_b, out_a, out_b)],
        out_specs=[whole(shape) for shape, _ in outs],
        out_shape=[sds(*out) for out in outs],
        compiler_params=params(56),
        cost_estimate=cost(40e9, 20e6),
        name="token_attention",
    )(tokens, cond, cond, cond, bias, in_a, in_b, out_a, out_b)


def transition_kernel(
    middle_ref, scale_ref, shift_ref, gate_ref, grad_ref, low_ref,
    up_a_ref, up_b_ref, down_a_ref, down_b_ref,
    result_ref, middle_grad_ref, weight_grad_ref, cond_grad_ref, cond_bias_ref,
    up_ref, hidden_ref,
):
    local = down_a_ref.shape[0]
    width = middle_ref.shape[1]
    half_rows, half_cols = width // 2, width // 2
    middle = middle_ref[...]
    normed, inverse = layer_norm(middle)
    scale = scale_ref[0]
    inner = (normed * scale + shift_ref[0]).astype(LOW)
    mlp = None
    for half, (weight_ref, down_ref) in enumerate(((up_a_ref, down_a_ref), (up_b_ref, down_b_ref))):
        up_ref[half] = mul(inner, weight_ref[...])
        gate_in = up_ref[half, :, :local]
        hidden = (gate_in * sigmoid(gate_in) * up_ref[half, :, local:]).astype(LOW)
        hidden_ref[half] = hidden
        add = mul(hidden, down_ref[...])
        mlp = add if mlp is None else mlp + add
    gate = gate_ref[0]
    result_ref[...] = (middle + gate * mlp).astype(LOW)
    grad = grad_ref[...].astype(WIDE)
    mlp_grad = (grad * gate).astype(LOW)
    inner_t = inner.T
    inner_grad = None
    for half, (weight_ref, down_ref) in enumerate(((up_a_ref, down_a_ref), (up_b_ref, down_b_ref))):
        hidden_t = hidden_ref[half].T
        for sec in range(2):
            weight_grad_ref[half, sec, 4 * half_rows :, :] = mul(
                hidden_t, mlp_grad[:, sec * half_cols : (sec + 1) * half_cols]
            ).astype(LOW)
        hidden_grad = mul_nt(mlp_grad, down_ref[...])
        gate_in = up_ref[half, :, :local]
        sigma = sigmoid(gate_in)
        first = (
            hidden_grad * up_ref[half, :, local:] * (sigma * (1.0 + gate_in * (1.0 - sigma)))
        ).astype(LOW)
        second = (hidden_grad * (gate_in * sigma)).astype(LOW)
        up_grad = jnp.concatenate([first, second], 1)
        for sec in range(2):
            rows = slice(sec * half_rows, (sec + 1) * half_rows)
            for block in range(4):
                weight_grad_ref[
                    half, sec, block * half_rows : (block + 1) * half_rows, :
                ] = mul(
                    inner_t[rows], up_grad[:, block * half_cols : (block + 1) * half_cols]
                ).astype(LOW)
        add = mul_nt(up_grad, weight_ref[...])
        inner_grad = add if inner_grad is None else inner_grad + add
    middle_grad_ref[...] = grad + norm_back(normed, inverse, inner_grad * scale)
    low_t = low_ref[...].T
    pieces = (
        inner_grad * normed * (scale * (1.0 - scale)),
        inner_grad,
        grad * mlp * (gate * (1.0 - gate)),
    )
    for k, piece in enumerate(pieces):
        piece = piece.astype(LOW)
        cond_grad_ref[k] = mul(low_t, piece).astype(LOW)
        cond_bias_ref[k] = jnp.sum(piece.astype(WIDE), 0, keepdims=True)


def transition(middle, cond, grad, low, up_a, up_b, down_a, down_b):
    rows, width = middle.shape
    local, half = down_a.shape[0], width // 2

    def whole(shape):
        return pl.BlockSpec(shape, lambda i: (0,) * len(shape))

    outs = [
        ((rows, width), LOW),
        ((rows, width), WIDE),
        ((2, 2, 4 * half + local, half), LOW),
        ((3, low.shape[1], width), LOW),
        ((3, 1, width), WIDE),
    ]
    return pl.pallas_call(
        transition_kernel,
        grid=(1,),
        in_specs=[whole(middle.shape)]
        + [part(i, (rows, width)) for i in (3, 4, 5)]
        + [whole(a.shape) for a in (grad, low, up_a, up_b, down_a, down_b)],
        out_specs=[whole(shape) for shape, _ in outs],
        out_shape=[sds(*out) for out in outs],
        scratch_shapes=[
            pltpu.VMEM((2, rows, 2 * local), WIDE),
            pltpu.VMEM((2, rows, local), LOW),
        ],
        compiler_params=params(56),
        cost_estimate=cost(60e9, 20e6),
        name="transition",
    )(middle, cond, cond, cond, grad, low, up_a, up_b, down_a, down_b)


def attention_back_kernel(
    middle_grad_ref, tokens_ref, scale_ref, gate_ref, attn_ref, low_ref, inner_ref, qkv_ref,
    sig_ref, heads_ref, gated_ref, probs_ref, in_a_ref, in_b_ref, out_a_ref, out_b_ref,
    token_grad_ref, weight_grad_ref, cond_grad_ref, cond_bias_ref, bias_grad_ref,
    proj_ref, heads_grad_ref,
):
    rows, width = tokens_ref.shape
    samples, heads, count = probs_ref.shape[0], probs_ref.shape[1], probs_ref.shape[2]
    local = in_a_ref.shape[1] // 4
    size = 2 * local // heads
    head_scale = size ** (-0.5)
    half_rows = width // 2
    middle_grad = middle_grad_ref[...]
    gate = gate_ref[0]
    attn_grad = (middle_grad * gate).astype(LOW)
    inner_t = inner_ref[...].T
    inner_grad = None
    for half, (weight_ref, out_ref) in enumerate(((in_a_ref, out_a_ref), (in_b_ref, out_b_ref))):
        gated_t = gated_ref[half].T
        for sec in range(2):
            weight_grad_ref[half, sec, 4 * half_rows :, :] = mul(
                gated_t, attn_grad[:, sec * half_rows : (sec + 1) * half_rows]
            ).astype(LOW)
        gated_grad = mul_nt(attn_grad, out_ref[...])
        sig = sig_ref[half]
        with_sig = gated_grad * sig
        heads_grad_ref[...] = with_sig.astype(LOW)
        proj_ref[:, 3 * local :] = (with_sig * heads_ref[half] * (1.0 - sig)).astype(LOW)
        for s in range(samples):
            at = slice(s * count, (s + 1) * count)
            grads = ([], [], [])
            for h in range(heads // 2):
                col, index = h * size, half * (heads // 2) + h
                query = qkv_ref[half, at, col : col + size]
                key = qkv_ref[half, at, local + col : local + col + size]
                value = qkv_ref[half, at, 2 * local + col : 2 * local + col + size]
                grad = heads_grad_ref[at, col : col + size]
                probs_low = probs_ref[s, index]
                probs = probs_low.astype(WIDE)
                probs_grad = mul_nt(grad, value)
                mean = jnp.sum(probs * probs_grad, -1, keepdims=True)
                scores_grad = (probs * (probs_grad - mean)).astype(LOW)
                if s == 0:
                    bias_grad_ref[index] = scores_grad.astype(WIDE)
                else:
                    bias_grad_ref[index] += scores_grad.astype(WIDE)
                grads[0].append(mul(scores_grad, key) * head_scale)
                grads[1].append(mul_tn(scores_grad, query) * head_scale)
                grads[2].append(mul_tn(probs_low, grad))
            for k in range(3):
                proj_ref[at, k * local : (k + 1) * local] = jnp.concatenate(grads[k], 1).astype(LOW)
        proj = proj_ref[...]
        for sec in range(2):
            for k in range(4):
                weight_grad_ref[half, sec, k * half_rows : (k + 1) * half_rows, :] = mul(
                    inner_t[sec * half_rows : (sec + 1) * half_rows],
                    proj[:, k * local : (k + 1) * local],
                ).astype(LOW)
        add = mul_nt(proj, weight_ref[...])
        inner_grad = add if inner_grad is None else inner_grad + add
    scale = scale_ref[0]
    normed, inverse = layer_norm(tokens_ref[...].astype(WIDE))
    token_grad_ref[...] = (middle_grad + norm_back(normed, inverse, inner_grad * scale)).astype(LOW)
    low_t = low_ref[...].T
    pieces = (
        inner_grad * normed * (scale * (1.0 - scale)),
        inner_grad,
        middle_grad * attn_ref[...] * (gate * (1.0 - gate)),
    )
    for k, piece in enumerate(pieces):
        piece = piece.astype(LOW)
        cond_grad_ref[k] = mul(low_t, piece).astype(LOW)
        cond_bias_ref[k] = jnp.sum(piece.astype(WIDE), 0, keepdims=True)


def attention_back(
    middle_grad, tokens, cond, attn, low, inner, qkv, sig, heads_out, gated, probs,
    in_a, in_b, out_a, out_b,
):
    rows, width = tokens.shape
    heads, count = probs.shape[1], probs.shape[2]
    local, half = in_a.shape[1] // 4, width // 2

    def whole(shape):
        return pl.BlockSpec(shape, lambda i: (0,) * len(shape))

    outs = [
        ((rows, width), LOW),
        ((2, 2, 4 * half + local, half), LOW),
        ((3, low.shape[1], width), LOW),
        ((3, 1, width), WIDE),
        ((heads, count, count), WIDE),
    ]
    after = (attn, low, inner, qkv, sig, heads_out, gated, probs, in_a, in_b, out_a, out_b)
    return pl.pallas_call(
        attention_back_kernel,
        grid=(1,),
        in_specs=[whole(middle_grad.shape), whole(tokens.shape)]
        + [part(i, (rows, width)) for i in (0, 2)]
        + [whole(a.shape) for a in after],
        out_specs=[whole(shape) for shape, _ in outs],
        out_shape=[sds(*out) for out in outs],
        scratch_shapes=[pltpu.VMEM((rows, 4 * local), LOW), pltpu.VMEM((rows, local), LOW)],
        compiler_params=params(56),
        cost_estimate=cost(60e9, 24e6),
        name="attention_back",
    )(middle_grad, tokens, cond, cond, *after)


def swap(array, axis, bit=0):
    size = lax.axis_size(axis)
    return lax.ppermute(array, axis, [(i, i ^ (1 << bit)) for i in range(size)])


def side(axis, bit=0):
    return (lax.axis_index(axis) >> bit) & 1


def sum_half(array, axis, bit, dim):
    size, me = array.shape[dim] // 2, side(axis, bit)
    other = lax.dynamic_slice_in_dim(array, (1 - me) * size, size, dim)
    mine = lax.dynamic_slice_in_dim(array, me * size, size, dim)
    return (mine.astype(WIDE) + swap(other, axis, bit).astype(WIDE)).astype(array.dtype)


def both_halves(array, axis, bit, dim):
    other, me = swap(array, axis, bit), side(axis, bit)
    first, second = jnp.where(me == 0, array, other), jnp.where(me == 0, other, array)
    return jnp.concatenate([first, second], dim)


def far_bits():
    return range(1, lax.axis_size("dp").bit_length() - 1)


def sum_far(array, dim):
    for bit in far_bits():
        array = sum_half(array, "dp", bit, dim)
    for bit in reversed(far_bits()):
        array = both_halves(array, "dp", bit, dim)
    return array


def fetch(weight):
    size = weight.shape[0] // 2
    own = lax.dynamic_slice_in_dim(weight, side("dp") * size, size, 0)
    return both_halves(swap(own, "mp"), "dp", 0, 0)


def sum_split(grads):
    part = sum_half(grads, "dp", 0, 2)
    part = (part[0].astype(WIDE) + swap(part[1], "mp").astype(WIDE)).astype(LOW)
    part = sum_half(part, "section", 0, 0)[0]
    return both_halves(sum_far(part, 0), "dp", 0, 0)


def sum_copied(grads):
    part = sum_half(grads, "dp", 0, 1)
    part = sum_half(part, "section", 0, 0)[0]
    part = sum_half(part, "mp", 0, 0)
    part = sum_far(part, 0)
    part = both_halves(part, "mp", 0, 0)
    return both_halves(part, "dp", 0, 0)


def local(
    atoms_in,
    atom_token,
    window_start,
    noise_level,
    level_table,
    single_trunk,
    pair,
    atom_gain,
    atom_qkv,
    atom_out,
    atom_agg,
    cond_weight,
    cond_bias,
    pair_weight,
    attn_in,
    attn_out,
    mlp_up,
    mlp_down,
    cotangent,
):
    section, mp = lax.axis_index("section"), lax.axis_index("mp")
    batch, half_atoms, atom_width = atoms_in.shape
    batch //= MICRO
    samples = batch // 2
    atoms = 2 * half_atoms
    tokens, width = cotangent.shape[1], cotangent.shape[2]
    single = single_trunk.shape[1]
    own_first = section * batch + mp * samples
    other_first = section * batch + (1 - mp) * samples

    own_atoms = lax.dynamic_slice_in_dim(atoms_in, own_first, samples, 0)
    other_atoms = swap(lax.dynamic_slice_in_dim(atoms_in, other_first, samples, 0), "mp")
    all_atoms = jnp.concatenate(
        [jnp.where(mp == 0, own_atoms, other_atoms), jnp.where(mp == 0, other_atoms, own_atoms)], 1
    )
    other_start = swap(window_start, "mp")
    starts = jnp.concatenate(
        [jnp.where(mp == 0, window_start, other_start), jnp.where(mp == 0, other_start, window_start)]
    )
    in_a = attn_in.reshape(width, -1)
    up_a = mlp_up.reshape(width, -1)
    in_b, out_b = fetch(in_a), fetch(attn_out)
    up_b, down_b = fetch(up_a), fetch(mlp_down)
    pair_w = jnp.concatenate([pair_weight, swap(pair_weight, "mp")], 1).T
    levels = lax.dynamic_slice_in_dim(noise_level, own_first, samples, 0)
    grad_out = lax.dynamic_slice_in_dim(cotangent, own_first, samples, 0).reshape(-1, width)

    token_ids = jnp.arange(tokens, dtype=jnp.int32)
    counts = jnp.sum((atom_token[:, None] == token_ids[None, :]).astype(WIDE), 0)
    inverse_counts = (1.0 / counts)[:, None]
    level_pick = (levels[:, None] == jnp.arange(level_table.shape[0], dtype=jnp.int32)[None, :])
    level_rows = jnp.sum(
        jnp.where(level_pick[:, :, None], level_table.astype(WIDE)[None], 0.0), 1, keepdims=True
    )
    windows = starts.shape[0]
    groups = windows // SPAN
    base = jnp.clip(
        jnp.arange(groups, dtype=jnp.int32) * (SPAN * QBLOCK) - KWIN // 2,
        0,
        atoms - KWIN - SPAN * QBLOCK,
    )
    rel = starts.reshape(groups, SPAN) - base[:, None]
    rel = jnp.broadcast_to(rel[:, None, None, :, None], (groups, 1, ATOM_HEADS, SPAN, QBLOCK))
    rel = rel.reshape(groups, 1, ATOM_HEADS * SPAN * QBLOCK)
    gain = atom_gain[None, :]
    qkv_w = atom_qkv.reshape(atom_width, -1)

    low_pair, bias = pair_bias(pair, pair_w)
    cond_w = jnp.transpose(cond_weight, (0, 2, 1, 3)).reshape(6, single, width)
    low, cond = conditioning(single_trunk, level_rows, cond_w, cond_bias.reshape(6, 1, width))
    qkv, probs, mixed, token_in = atom_front(
        all_atoms, gain, qkv_w, atom_out, atom_agg, rel, atom_token[None, :], inverse_counts
    )
    token_in = token_in.reshape(-1, width)
    inner, token_qkv, sig, heads_out, gated, token_probs, attn, middle = token_attention(
        token_in, cond, bias, in_a, in_b, attn_out, out_b
    )
    result, middle_grad, mlp_grads, cond_grad_1, cond_bias_1 = transition(
        middle, cond, grad_out, low, up_a, up_b, mlp_down, down_b
    )
    mlp_sum = sum_split(mlp_grads)
    other_result = swap(result, "mp")
    token_grad, attn_grads, cond_grad_0, cond_bias_0, bias_grad = attention_back(
        middle_grad, token_in, cond, attn, low, inner, token_qkv, sig, heads_out, gated,
        token_probs, in_a, in_b, attn_out, out_b,
    )
    attn_sum = sum_split(attn_grads)
    cond_sum = sum_copied(
        jnp.stack([cond_grad_0.reshape(-1, width), cond_grad_1.reshape(-1, width)])
    )
    atoms_grad, gain_grad, qkv_grad, out_grad, agg_grad = atom_back(
        all_atoms, gain, qkv_w, atom_out, atom_agg, atom_token[:, None], inverse_counts,
        qkv, probs, mixed, token_grad.reshape(samples, tokens, width),
    )
    pair_grad = pair_back(low_pair, bias_grad)

    lanes = atom_width
    half_width = atom_width // 2
    heads = pair_grad.shape[0]
    own_heads = heads // 2
    pair_ordered = jnp.where(
        mp == 0, pair_grad, jnp.concatenate([pair_grad[own_heads:], pair_grad[:own_heads]], 0)
    )
    pieces = [
        jnp.pad(gain_grad.reshape(2, half_width), ((0, 0), (0, lanes - half_width))).reshape(2, 1, lanes),
        qkv_grad.reshape(2, -1, lanes),
        out_grad.reshape(2, -1, lanes),
        agg_grad.reshape(2, -1, lanes),
        jnp.stack([cond_bias_0.reshape(-1, lanes), cond_bias_1.reshape(-1, lanes)]),
        pair_ordered.T.reshape(2, -1, lanes),
    ]
    sizes = [piece.shape[1] for piece in pieces]
    rows = sum(sizes)
    whole_rows = -(-rows // 512) * 512
    small = jnp.concatenate(pieces + [jnp.zeros((2, whole_rows - rows, lanes), WIDE)], 1)
    small = sum_copied(small)
    cuts = [sum(sizes[:i]) for i in range(len(sizes) + 1)]
    small = [small[cuts[i] : cuts[i + 1]] for i in range(len(sizes))]
    pair_out = small[5].reshape(half_width, heads)
    pair_out = lax.dynamic_slice_in_dim(pair_out, mp * own_heads, own_heads, 1)

    result = result.reshape(samples, tokens, width)
    other_result = other_result.reshape(samples, tokens, width)
    token_out = jnp.concatenate(
        [jnp.where(mp == 0, result, other_result), jnp.where(mp == 0, other_result, result)]
    )
    keep = lax.dynamic_slice_in_dim(atoms_grad, mp * half_atoms, half_atoms, 1)
    send = lax.dynamic_slice_in_dim(atoms_grad, (1 - mp) * half_atoms, half_atoms, 1)
    got = swap(send.astype(LOW), "mp").astype(WIDE)
    atoms_out = jnp.concatenate([jnp.where(mp == 0, keep, got), jnp.where(mp == 0, got, keep)])
    half = width // 2
    attn_local, mlp_local = attn_in.shape[2], mlp_up.shape[2]
    in_sum = jnp.transpose(attn_sum[: 4 * half].reshape(4, half, attn_local), (1, 0, 2))
    up_sum = jnp.transpose(
        mlp_sum[: 4 * half].reshape(2, mlp_local // half, half, half), (2, 0, 1, 3)
    ).reshape(half, 2, mlp_local)
    return (
        token_out.reshape(1, 1, batch, tokens, width),
        atoms_out.reshape(1, 1, batch, half_atoms, atom_width),
        small[0].reshape(lanes)[:half_width],
        small[1].reshape(half_width, 3, atom_width),
        small[2].reshape(half_width, atom_width),
        small[3].reshape(half_width, width),
        jnp.transpose(cond_sum.reshape(1, 3, single, width), (0, 2, 1, 3)).astype(WIDE),
        small[4].reshape(1, 3, width),
        pair_out,
        in_sum.astype(WIDE),
        attn_sum[4 * half :].astype(WIDE),
        up_sum.astype(WIDE),
        mlp_sum[4 * half :].astype(WIDE),
    )


def solution(mesh):
    in_specs = (
        P("dp", "mp", None),
        P(),
        P("mp"),
        P("dp"),
        P(),
        P(),
        P(),
        P(),
        P(),
        P(),
        P(),
        P(),
        P(),
        P(None, "mp"),
        P(None, None, "mp"),
        P("mp", None),
        P(None, None, "mp"),
        P("mp", None),
        P("dp", None, None),
    )
    out_specs = (
        P("dp", "section", None, None, None),
        P("dp", "section", None, "mp", None),
        P("section"),
        P("section", None, None),
        P("section", None),
        P("section", None),
        P("section", None, None, None),
        P("section", None, None),
        P("section", "mp"),
        P("section", None, "mp"),
        P("mp", "section"),
        P("section", None, "mp"),
        P("mp", "section"),
    )
    return jax.shard_map(local, mesh=mesh, in_specs=in_specs, out_specs=out_specs, check_vma=False)
```

```python
import functools

import jax
import jax.numpy as jnp
from jax import lax
from jax.experimental import pallas as pl
from jax.experimental.pallas import tpu as pltpu
from jax.sharding import PartitionSpec as P

QBLOCK = 32
KWIN = 128
MICRO = 2
ATOM_HEADS = 4
SPAN = 2
EPS = 1e-05
LOW = jnp.bfloat16
WIDE = jnp.float32
MIB = 1 << 20


def mul(left, right):
    return lax.dot_general(left, right, (((1,), (0,)), ((), ())), preferred_element_type=WIDE)


def mul_nt(left, right):
    return lax.dot_general(left, right, (((1,), (1,)), ((), ())), preferred_element_type=WIDE)


def mul_tn(left, right):
    return lax.dot_general(left, right, (((0,), (0,)), ((), ())), preferred_element_type=WIDE)


def layer_norm(values):
    center = values - jnp.mean(values, -1, keepdims=True)
    inverse = lax.rsqrt(jnp.mean(center * center, -1, keepdims=True) + EPS)
    return center * inverse, inverse


def norm_back(normed, inverse, grad):
    return inverse * (
        grad
        - jnp.mean(grad, -1, keepdims=True)
        - normed * jnp.mean(grad * normed, -1, keepdims=True)
    )


def sigmoid(values):
    return 1.0 / (1.0 + jnp.exp(-values))


def params(mib, semantics=None):
    return pltpu.CompilerParams(vmem_limit_bytes=mib * MIB, dimension_semantics=semantics)


def cost(flops, moved, exps=0):
    return pl.CostEstimate(flops=int(flops), bytes_accessed=int(moved), transcendentals=int(exps))


def sds(shape, dtype):
    return jax.ShapeDtypeStruct(shape, dtype)


def pair_kernel(pair_ref, weight_ref, low_ref, bias_ref):
    normed, _ = layer_norm(pair_ref[...].astype(WIDE))
    low = normed.astype(LOW)
    low_ref[...] = low
    for i in range(low.shape[0]):
        bias_ref[:, i, :] = mul_nt(weight_ref[...], low[i])


def pair_bias(pair, weight):
    tokens, width = pair.shape[1], pair.shape[2]
    heads, block = weight.shape[0], 8
    return pl.pallas_call(
        pair_kernel,
        grid=(tokens // block,),
        in_specs=[
            pl.BlockSpec((block, tokens, width), lambda i: (i, 0, 0)),
            pl.BlockSpec((heads, width), lambda i: (0, 0)),
        ],
        out_specs=[
            pl.BlockSpec((block, tokens, width), lambda i: (i, 0, 0)),
            pl.BlockSpec((heads, block, tokens), lambda i: (0, i, 0)),
        ],
        out_shape=[sds(pair.shape, LOW), sds((heads, tokens, tokens), WIDE)],
        compiler_params=params(24),
        cost_estimate=cost(20e9, 16e6),
        name="pair_bias",
    )(pair, weight)


def cond_kernel(trunk_ref, level_ref, weight_ref, bias_ref, low_ref, first_ref, second_ref):
    step = pl.program_id(0)
    samples, tokens = level_ref.shape[0], trunk_ref.shape[0]

    @pl.when(step == 0)
    def _():
        trunk = trunk_ref[...].astype(WIDE)
        for s in range(samples):
            normed, _ = layer_norm(trunk + level_ref[s])
            low_ref[s * tokens : (s + 1) * tokens, :] = normed.astype(LOW)

    value = mul(low_ref[...], weight_ref[0]) + bias_ref[0]
    value = jnp.where(step % 3 == 1, value, sigmoid(value))

    @pl.when(step < 3)
    def _():
        first_ref[0] = value

    @pl.when(step >= 3)
    def _():
        second_ref[0] = value


def conditioning(trunk, levels, weight, bias):
    tokens, width = trunk.shape
    samples, parts, wide = levels.shape[0], weight.shape[0], weight.shape[2]
    rows = samples * tokens
    return pl.pallas_call(
        cond_kernel,
        grid=(parts,),
        in_specs=[
            pl.BlockSpec((tokens, width), lambda i: (0, 0)),
            pl.BlockSpec((samples, 1, width), lambda i: (0, 0, 0)),
            pl.BlockSpec((1, width, wide), lambda i: (i, 0, 0)),
            pl.BlockSpec((1, 1, wide), lambda i: (i, 0, 0)),
        ],
        out_specs=[
            pl.BlockSpec((rows, width), lambda i: (0, 0)),
            pl.BlockSpec((1, rows, wide), lambda i: (jnp.minimum(i, 2), 0, 0)),
            pl.BlockSpec((1, rows, wide), lambda i: (jnp.maximum(i, 3) - 3, 0, 0)),
        ],
        out_shape=[sds((rows, width), LOW)] + [sds((parts // 2, rows, wide), WIDE)] * 2,
        compiler_params=params(24),
        cost_estimate=cost(4e9, 10e6),
        name="conditioning",
    )(trunk, levels, weight, bias)


def lane_heads(rows, width, size):
    return lax.broadcasted_iota(jnp.int32, (rows, width), 1) // size


def spread(values, heads):
    head = lane_heads(values.shape[0], values.shape[1], values.shape[1] // heads)
    zero = jnp.zeros_like(values)
    return jnp.concatenate([jnp.where(head == h, values, zero) for h in range(heads)], 0)


def gather_heads(values, heads):
    rows = values.shape[0] // heads
    head = lane_heads(rows, values.shape[1], values.shape[1] // heads)
    total = jnp.where(head == 0, values[:rows], 0.0)
    for h in range(1, heads):
        total += jnp.where(head == h, values[h * rows : (h + 1) * rows], 0.0)
    return total


def key_base(group, atoms):
    start = group * SPAN * QBLOCK - KWIN // 2
    return pl.multiple_of(jnp.clip(start, 0, atoms - KWIN - (SPAN - 1) * QBLOCK - QBLOCK), QBLOCK)


def atom_front_kernel(
    atoms_ref, gain_ref, qkv_w_ref, out_w_ref, agg_w_ref, rel_ref, ids_ref, inv_ref,
    qkv_ref, probs_ref, mixed_ref, tokens_ref,
    total,
):
    atoms, width = atoms_ref.shape[1], atoms_ref.shape[2]
    groups, keys_in = probs_ref.shape[1], probs_ref.shape[2]
    queries_in = SPAN * QBLOCK
    scale = (width // ATOM_HEADS) ** (-0.5)
    wide = atoms_ref[0].astype(WIDE)
    normed, _ = layer_norm(wide)
    hidden = (normed * gain_ref[...].astype(WIDE)).astype(LOW)
    qkv_ref[0] = mul(hidden, qkv_w_ref[...]).astype(LOW)
    place = lax.broadcasted_iota(jnp.int32, (keys_in, ATOM_HEADS * queries_in), 0)

    def attend(group, carry):
        base = key_base(group, atoms)
        first = pl.multiple_of(group * queries_in, queries_in)
        queries = spread(qkv_ref[0, pl.ds(first, queries_in), :width], ATOM_HEADS)
        keys = qkv_ref[0, pl.ds(base, keys_in), width : 2 * width]
        values = qkv_ref[0, pl.ds(base, keys_in), 2 * width :]
        offset = place - rel_ref[group]
        scores = mul_nt(keys, queries) * scale
        scores = jnp.where((offset >= 0) & (offset < KWIN), scores, -1e30)
        exps = jnp.exp(scores - jnp.max(scores, 0, keepdims=True))
        probs = (exps * (1.0 / jnp.sum(exps, 0, keepdims=True))).astype(LOW)
        probs_ref[0, group] = probs
        mixed_ref[0, pl.ds(first, queries_in), :] = gather_heads(
            mul_tn(probs, values), ATOM_HEADS
        ).astype(LOW)
        return carry

    lax.fori_loop(0, groups, attend, 0)
    chunk = 256
    ids = lax.broadcasted_iota(jnp.int32, (total.shape[0], chunk), 0)
    for i in range(atoms // chunk):
        rows = slice(i * chunk, (i + 1) * chunk)
        after = wide[rows] + mul(mixed_ref[0, rows, :], out_w_ref[...])
        pre = mul(after.astype(LOW), agg_w_ref[...])
        units = (pre * sigmoid(pre)).astype(LOW)
        member = jnp.where(ids == ids_ref[:, rows], 1.0, 0.0).astype(LOW)
        part = mul(member, units)
        if i == 0:
            total[...] = part
        else:
            total[...] += part
    tokens_ref[0] = (total[...] * inv_ref[...]).astype(LOW)


def atom_front(atoms, gain, qkv_w, out_w, agg_w, rel, ids, inverse_counts):
    samples, count, width = atoms.shape
    groups = count // (SPAN * QBLOCK)
    keys_in = KWIN + SPAN * QBLOCK
    lanes = ATOM_HEADS * SPAN * QBLOCK
    tokens, wide = inverse_counts.shape[0], agg_w.shape[1]

    def whole(array):
        return pl.BlockSpec(array.shape, lambda i: (0,) * array.ndim)

    def sample(*shape):
        return pl.BlockSpec((1,) + shape, lambda i: (i,) + (0,) * len(shape))

    return pl.pallas_call(
        atom_front_kernel,
        grid=(samples,),
        in_specs=[sample(count, width)]
        + [whole(a) for a in (gain, qkv_w, out_w, agg_w, rel, ids, inverse_counts)],
        out_specs=[
            sample(count, 3 * width),
            sample(groups, keys_in, lanes),
            sample(count, width),
            sample(tokens, wide),
        ],
        out_shape=[
            sds((samples, count, 3 * width), LOW),
            sds((samples, groups, keys_in, lanes), LOW),
            sds((samples, count, width), LOW),
            sds((samples, tokens, wide), LOW),
        ],
        scratch_shapes=[pltpu.VMEM((tokens, wide), WIDE)],
        compiler_params=params(48),
        cost_estimate=cost(20e9, 12e6),
        name="atom_front",
    )(atoms, gain, qkv_w, out_w, agg_w, rel, ids, inverse_counts)


def token_attention_kernel(
    tokens_ref, scale_ref, shift_ref, gate_ref, bias_ref, in_a_ref, in_b_ref, out_a_ref, out_b_ref,
    inner_ref, qkv_ref, sig_ref, heads_ref, gated_ref, probs_ref, attn_ref, middle_ref,
):
    rows, width = tokens_ref.shape
    samples, heads, count = probs_ref.shape[0], probs_ref.shape[1], probs_ref.shape[2]
    local = in_a_ref.shape[1] // 4
    size = 2 * local // heads
    scale = size ** (-0.5)
    wide = tokens_ref[...].astype(WIDE)
    normed, _ = layer_norm(wide)
    inner = (normed * scale_ref[0] + shift_ref[0]).astype(LOW)
    inner_ref[...] = inner
    for half, weight_ref in enumerate((in_a_ref, in_b_ref)):
        qkv_ref[half] = mul(inner, weight_ref[:, : 3 * local]).astype(LOW)
        sig_ref[half] = sigmoid(mul(inner, weight_ref[:, 3 * local :]))
        for s in range(samples):
            at = slice(s * count, (s + 1) * count)
            outs = []
            for h in range(heads // 2):
                col = h * size
                query = qkv_ref[half, at, col : col + size]
                key = qkv_ref[half, at, local + col : local + col + size]
                value = qkv_ref[half, at, 2 * local + col : 2 * local + col + size]
                scores = mul_nt(query, key) * scale + bias_ref[half * (heads // 2) + h]
                exps = jnp.exp(scores - jnp.max(scores, -1, keepdims=True))
                probs = (exps * (1.0 / jnp.sum(exps, -1, keepdims=True))).astype(LOW)
                probs_ref[s, half * (heads // 2) + h] = probs
                outs.append(mul(probs, value))
            heads_ref[half, at, :] = jnp.concatenate(outs, 1)
        gated_ref[half] = (heads_ref[half] * sig_ref[half]).astype(LOW)
    attn = mul(gated_ref[0], out_a_ref[...]) + mul(gated_ref[1], out_b_ref[...])
    attn_ref[...] = attn
    middle_ref[...] = wide + gate_ref[0] * attn


def vmem(count):
    return [pl.BlockSpec(memory_space=pltpu.VMEM)] * count


def part(index, shape):
    return pl.BlockSpec((1,) + shape, lambda i: (index,) + (0,) * len(shape))


def token_attention(tokens, cond, bias, in_a, in_b, out_a, out_b):
    rows, width = tokens.shape
    heads, count = bias.shape[0], bias.shape[1]
    samples, local = rows // count, in_a.shape[1] // 4

    def whole(shape):
        return pl.BlockSpec(shape, lambda i: (0,) * len(shape))

    outs = [
        ((rows, width), LOW),
        ((2, rows, 3 * local), LOW),
        ((2, rows, local), WIDE),
        ((2, rows, local), WIDE),
        ((2, rows, local), LOW),
        ((samples, heads, count, count), LOW),
        ((rows, width), WIDE),
        ((rows, width), WIDE),
    ]
    return pl.pallas_call(
        token_attention_kernel,
        grid=(1,),
        in_specs=[whole(tokens.shape)]
        + [part(i, (rows, width)) for i in (0, 1, 2)]
        + [whole(a.shape) for a in (bias, in_a, in_b, out_a, out_b)],
        out_specs=[whole(shape) for shape, _ in outs],
        out_shape=[sds(*out) for out in outs],
        compiler_params=params(56),
        cost_estimate=cost(40e9, 20e6),
        name="token_attention",
    )(tokens, cond, cond, cond, bias, in_a, in_b, out_a, out_b)


def transition_kernel(
    middle_ref, scale_ref, shift_ref, gate_ref, grad_ref, low_ref,
    up_a_ref, up_b_ref, down_a_ref, down_b_ref,
    result_ref, middle_grad_ref, weight_grad_ref, cond_grad_ref, cond_bias_ref,
    up_ref, hidden_ref,
):
    local = down_a_ref.shape[0]
    width = middle_ref.shape[1]
    half_rows, half_cols = width // 2, width // 2
    middle = middle_ref[...]
    normed, inverse = layer_norm(middle)
    scale = scale_ref[0]
    inner = (normed * scale + shift_ref[0]).astype(LOW)
    mlp = None
    for half, (weight_ref, down_ref) in enumerate(((up_a_ref, down_a_ref), (up_b_ref, down_b_ref))):
        up_ref[half] = mul(inner, weight_ref[...])
        gate_in = up_ref[half, :, :local]
        hidden = (gate_in * sigmoid(gate_in) * up_ref[half, :, local:]).astype(LOW)
        hidden_ref[half] = hidden
        add = mul(hidden, down_ref[...])
        mlp = add if mlp is None else mlp + add
    gate = gate_ref[0]
    result_ref[...] = (middle + gate * mlp).astype(LOW)
    grad = grad_ref[...].astype(WIDE)
    mlp_grad = (grad * gate).astype(LOW)
    inner_t = inner.T
    inner_grad = None
    for half, (weight_ref, down_ref) in enumerate(((up_a_ref, down_a_ref), (up_b_ref, down_b_ref))):
        hidden_t = hidden_ref[half].T
        for sec in range(2):
            weight_grad_ref[half, sec, 4 * half_rows :, :] = mul(
                hidden_t, mlp_grad[:, sec * half_cols : (sec + 1) * half_cols]
            ).astype(LOW)
        hidden_grad = mul_nt(mlp_grad, down_ref[...])
        gate_in = up_ref[half, :, :local]
        sigma = sigmoid(gate_in)
        first = (
            hidden_grad * up_ref[half, :, local:] * (sigma * (1.0 + gate_in * (1.0 - sigma)))
        ).astype(LOW)
        second = (hidden_grad * (gate_in * sigma)).astype(LOW)
        up_grad = jnp.concatenate([first, second], 1)
        for sec in range(2):
            rows = slice(sec * half_rows, (sec + 1) * half_rows)
            for block in range(4):
                weight_grad_ref[
                    half, sec, block * half_rows : (block + 1) * half_rows, :
                ] = mul(
                    inner_t[rows], up_grad[:, block * half_cols : (block + 1) * half_cols]
                ).astype(LOW)
        add = mul_nt(up_grad, weight_ref[...])
        inner_grad = add if inner_grad is None else inner_grad + add
    middle_grad_ref[...] = grad + norm_back(normed, inverse, inner_grad * scale)
    low_t = low_ref[...].T
    pieces = (
        inner_grad * normed * (scale * (1.0 - scale)),
        inner_grad,
        grad * mlp * (gate * (1.0 - gate)),
    )
    for k, piece in enumerate(pieces):
        piece = piece.astype(LOW)
        rows = slice(k * low_t.shape[0], (k + 1) * low_t.shape[0])
        for h in range(2):
            cond_grad_ref[h, rows, :] = mul(
                low_t, piece[:, h * half_cols : (h + 1) * half_cols]
            ).astype(LOW)
        cond_bias_ref[k] = jnp.sum(piece.astype(WIDE), 0, keepdims=True)


def transition(middle, cond, grad, low, up_a, up_b, down_a, down_b):
    rows, width = middle.shape
    local, half = down_a.shape[0], width // 2

    def whole(shape):
        return pl.BlockSpec(shape, lambda i: (0,) * len(shape))

    outs = [
        ((rows, width), LOW),
        ((rows, width), WIDE),
        ((2, 2, 4 * half + local, half), LOW),
        ((2, 3 * low.shape[1], half), LOW),
        ((3, 1, width), WIDE),
    ]
    return pl.pallas_call(
        transition_kernel,
        grid=(1,),
        in_specs=[whole(middle.shape)]
        + [part(i, (rows, width)) for i in (0, 1, 2)]
        + [whole(a.shape) for a in (grad, low, up_a, up_b, down_a, down_b)],
        out_specs=[whole(shape) for shape, _ in outs],
        out_shape=[sds(*out) for out in outs],
        scratch_shapes=[
            pltpu.VMEM((2, rows, 2 * local), WIDE),
            pltpu.VMEM((2, rows, local), LOW),
        ],
        compiler_params=params(56),
        cost_estimate=cost(60e9, 20e6),
        name="transition",
    )(middle, cond, cond, cond, grad, low, up_a, up_b, down_a, down_b)


def far_bits():
    return range(1, lax.axis_size("dp").bit_length() - 1)


class Links:
    def __init__(self, send_sem, recv_sem):
        self.section, self.mp = lax.axis_index("section"), lax.axis_index("mp")
        self.dp = lax.axis_index("dp")
        self.core = self.dp % 2
        self.far = [self.dp // (1 << b) % 2 for b in far_bits()]
        self.partners = [{"section": 1 - self.section}, {"mp": 1 - self.mp}]
        self.partners.append({"dp": self.dp + 1 - 2 * self.core})
        for b, side_of in zip(far_bits(), self.far):
            self.partners.append({"dp": self.dp + (1 - 2 * side_of) * (1 << b)})
        self.x, self.y, self.twin = self.partners[:3]
        self.z = self.partners[3:]
        self.send_sem, self.recv_sem, self.used = send_sem, recv_sem, 0

    def barrier(self):
        barrier = pltpu.get_barrier_semaphore()
        for partner in self.partners:
            pl.semaphore_signal(
                barrier, inc=1, device_id=partner, device_id_type=pl.DeviceIdType.MESH
            )
        pl.semaphore_wait(barrier, len(self.partners))

    def send(self, source, target, partner):
        copy = pltpu.make_async_remote_copy(
            src_ref=source,
            dst_ref=target,
            send_sem=self.send_sem.at[self.used],
            recv_sem=self.recv_sem.at[self.used],
            device_id=partner,
            device_id_type=pl.DeviceIdType.MESH,
        )
        self.used += 1
        copy.start()
        return copy


def splits_far(rows):
    steps = []
    for _ in far_bits():
        halves = rows % 32 == 0
        rows = rows // 2 if halves else rows
        steps.append((rows, halves))
    return steps


def journey_copies(rows, shared):
    steps = splits_far(rows)
    return 4 + len(steps) + sum(halves for _, halves in steps) + (2 if shared else 0)


def journey_scratch(chunks, rows, cols):
    shapes = [(chunks, 2, 2, rows, cols), (chunks, 2, rows, cols), (chunks, rows, cols)]
    shapes += [(chunks, size, cols) for size, _ in splits_far(rows)]
    return [pltpu.VMEM(shape, LOW) for shape in shapes]


def journey(links, grads, buffers, out, other_out, chunk, rows, x_first, shared):
    near, middle, last = (buffer.at[chunk] for buffer in buffers[:3])
    far = [buffer.at[chunk] for buffer in buffers[3:]]
    total_rows = grads.shape[2]
    start = links.core * (total_rows // 2) + chunk * rows
    twin_start = (1 - links.core) * (total_rows // 2) + chunk * rows
    mine, theirs = pl.ds(pl.multiple_of(start, 16), rows), pl.ds(pl.multiple_of(twin_start, 16), rows)
    me, you = links.section, 1 - links.section
    copy = links.send(grads.at[:, :, theirs, :], near, links.twin)
    yield
    copy.wait()
    if x_first:
        near[:, you] += grads[:, you, mine, :]
        copy = links.send(near.at[:, you], middle, links.x)
        near[:, me] += grads[:, me, mine, :]
        yield
        copy.wait()
        middle[1] += near[1, me]
        copy = links.send(middle.at[1], last, links.y)
        middle[0] += near[0, me]
        yield
        copy.wait()
        last[...] += middle[0]
    else:
        near[1] += grads[1, :, mine, :]
        copy = links.send(near.at[1], middle, links.y)
        near[0] += grads[0, :, mine, :]
        yield
        copy.wait()
        middle[you] += near[0, you]
        copy = links.send(middle.at[you], last, links.x)
        middle[me] += near[0, me]
        yield
        copy.wait()
        last[...] += middle[me]
    held, place, size = last, start, rows
    back = []
    for (count, halves), bit, partner, slot in zip(splits_far(rows), links.far, links.z, far):
        if halves:
            give = pl.ds(pl.multiple_of((1 - bit) * count, 16), count)
            keep = pl.ds(pl.multiple_of(bit * count, 16), count)
            copy = links.send(held.at[give, :], slot, partner)
            back.append((bit, partner))
            place = place + bit * count
        else:
            keep = pl.ds(0, count)
            copy = links.send(held, slot, partner)
        yield
        copy.wait()
        slot[...] += held[keep, :]
        held, size = slot, count
    out[pl.ds(pl.multiple_of(place, 16), size), :] = held[...]
    for bit, partner in reversed(back):
        at = pl.ds(pl.multiple_of(place, 16), size)
        copy = links.send(out.at[at, :], out.at[at, :], partner)
        yield
        copy.wait()
        place, size = place - bit * size, 2 * size
    copies = [links.send(out.at[mine, :], out.at[mine, :], links.twin)]
    if shared:
        across = links.send(out.at[mine, :], other_out.at[mine, :], links.y)
        yield
        across.wait()
        copies.append(links.send(other_out.at[mine, :], other_out.at[mine, :], links.twin))
    yield
    for copy in copies:
        copy.wait()


class Flow:
    def __init__(self, journeys, lag=1):
        self.waiting, self.running, self.lag, self.count = list(journeys), [], lag, 0

    def step(self):
        if self.waiting and self.count % self.lag == 0:
            self.running.append(self.waiting.pop(0))
        self.count += 1
        alive = []
        for one in self.running:
            if next(one, "end") is None:
                alive.append(one)
        self.running = alive

    def finish(self):
        while self.waiting or self.running:
            self.step()


CHUNK = 192


def everywhere(count):
    return [pl.BlockSpec(memory_space=pltpu.VMEM)] * count


def remote_params(mib, number):
    return pltpu.CompilerParams(
        vmem_limit_bytes=mib * MIB, collective_id=number, has_side_effects=True
    )


def relative(half, mp):
    return mp if half == 0 else 1 - mp


def attention_back_kernel(
    middle_grad_ref, tokens_ref, cond_ref, attn_ref, low_ref, inner_ref, qkv_ref,
    sig_ref, heads_ref, gated_ref, probs_ref, in_a_ref, in_b_ref, out_a_ref, out_b_ref,
    mlp_ref, cond_grad_ref,
    token_grad_ref, grads_ref, cond_bias_ref, bias_grad_ref, mlp_out_ref,
    proj_ref, heads_grad_ref, *rest,
):
    *buffers, send_sem, recv_sem = rest
    links = Links(send_sem, recv_sem)
    links.barrier()
    chunks = mlp_ref.shape[2] // 2 // CHUNK
    flow = Flow(
        journey(links, mlp_ref, buffers, mlp_out_ref, None, i, CHUNK, i % 2 == 1, False)
        for i in range(chunks)
    )
    flow.step()
    rows, width = tokens_ref.shape
    samples, heads, count = probs_ref.shape[0], probs_ref.shape[1], probs_ref.shape[2]
    local = in_a_ref.shape[1] // 4
    size = 2 * local // heads
    head_scale = size ** (-0.5)
    half_rows = width // 2
    first_cond = 4 * half_rows + local
    for h in range(2):
        grads_ref[relative(h, links.mp), 1, first_cond:, :] = cond_grad_ref[h]
    middle_grad = middle_grad_ref[...]
    gate = cond_ref[2]
    attn_grad = (middle_grad * gate).astype(LOW)
    inner_t = inner_ref[...].T
    inner_grad = None
    for half, (weight_ref, out_ref) in enumerate(((in_a_ref, out_a_ref), (in_b_ref, out_b_ref))):
        gated_t = gated_ref[half].T
        for sec in range(2):
            grads_ref[half, sec, 4 * half_rows : first_cond, :] = mul(
                gated_t, attn_grad[:, sec * half_rows : (sec + 1) * half_rows]
            ).astype(LOW)
        gated_grad = mul_nt(attn_grad, out_ref[...])
        sig = sig_ref[half]
        with_sig = gated_grad * sig
        heads_grad_ref[...] = with_sig.astype(LOW)
        proj_ref[:, 3 * local :] = (with_sig * heads_ref[half] * (1.0 - sig)).astype(LOW)
        flow.step()
        for s in range(samples):
            at = slice(s * count, (s + 1) * count)
            grads = ([], [], [])
            for h in range(heads // 2):
                col, index = h * size, half * (heads // 2) + h
                query = qkv_ref[half, at, col : col + size]
                key = qkv_ref[half, at, local + col : local + col + size]
                value = qkv_ref[half, at, 2 * local + col : 2 * local + col + size]
                grad = heads_grad_ref[at, col : col + size]
                probs_low = probs_ref[s, index]
                probs = probs_low.astype(WIDE)
                probs_grad = mul_nt(grad, value)
                mean = jnp.sum(probs * probs_grad, -1, keepdims=True)
                scores_grad = (probs * (probs_grad - mean)).astype(LOW)
                if s == 0:
                    bias_grad_ref[index] = scores_grad.astype(WIDE)
                else:
                    bias_grad_ref[index] += scores_grad.astype(WIDE)
                grads[0].append(mul(scores_grad, key) * head_scale)
                grads[1].append(mul_tn(scores_grad, query) * head_scale)
                grads[2].append(mul_tn(probs_low, grad))
                if h % 4 == 3:
                    flow.step()
            for k in range(3):
                proj_ref[at, k * local : (k + 1) * local] = jnp.concatenate(grads[k], 1).astype(LOW)
        proj = proj_ref[...]
        for sec in range(2):
            for k in range(4):
                grads_ref[half, sec, k * half_rows : (k + 1) * half_rows, :] = mul(
                    inner_t[sec * half_rows : (sec + 1) * half_rows],
                    proj[:, k * local : (k + 1) * local],
                ).astype(LOW)
        add = mul_nt(proj, weight_ref[...])
        inner_grad = add if inner_grad is None else inner_grad + add
        flow.step()
    scale = cond_ref[0]
    normed, inverse = layer_norm(tokens_ref[...].astype(WIDE))
    token_grad_ref[...] = (middle_grad + norm_back(normed, inverse, inner_grad * scale)).astype(LOW)
    flow.step()
    low_t = low_ref[...].T
    pieces = (
        inner_grad * normed * (scale * (1.0 - scale)),
        inner_grad,
        middle_grad * attn_ref[...] * (gate * (1.0 - gate)),
    )
    for k, piece in enumerate(pieces):
        piece = piece.astype(LOW)
        place = first_cond + k * low_t.shape[0]
        for h in range(2):
            grads_ref[relative(h, links.mp), 0, place : place + low_t.shape[0], :] = mul(
                low_t, piece[:, h * half_rows : (h + 1) * half_rows]
            ).astype(LOW)
        cond_bias_ref[k] = jnp.sum(piece.astype(WIDE), 0, keepdims=True)
    flow.finish()


def attention_back(
    middle_grad, tokens, cond, attn, low, inner, qkv, sig, heads_out, gated, probs,
    in_a, in_b, out_a, out_b, mlp_grads, cond_grads,
):
    rows, width = tokens.shape
    heads, count = probs.shape[1], probs.shape[2]
    local, half = in_a.shape[1] // 4, width // 2
    chunks = mlp_grads.shape[2] // 2 // CHUNK
    copies = chunks * journey_copies(CHUNK, False)
    outs = [
        sds((rows, width), LOW),
        sds((2, 2, 4 * half + local + 3 * low.shape[1], half), LOW),
        sds((3, 1, width), WIDE),
        sds((heads, count, count), WIDE),
        sds(mlp_grads.shape[2:], LOW),
    ]
    return pl.pallas_call(
        attention_back_kernel,
        in_specs=everywhere(17),
        out_specs=everywhere(len(outs)),
        out_shape=outs,
        scratch_shapes=[
            pltpu.VMEM((rows, 4 * local), LOW),
            pltpu.VMEM((rows, local), LOW),
            *journey_scratch(chunks, CHUNK, half),
            pltpu.SemaphoreType.DMA((copies,)),
            pltpu.SemaphoreType.DMA((copies,)),
        ],
        compiler_params=remote_params(60, 1),
        cost_estimate=cost(60e9, 24e6),
        name="attention_back",
    )(
        middle_grad, tokens, cond, attn, low, inner, qkv, sig, heads_out, gated, probs,
        in_a, in_b, out_a, out_b, mlp_grads, cond_grads,
    )


SMALL_ROWS = 160


def atom_back_kernel(
    atoms_ref, gain_ref, qkv_w_ref, out_w_ref, agg_w_ref, ids_ref, inv_ref,
    qkv_ref, probs_ref, mixed_ref, grad_ref, pair_ref, bias_grad_ref,
    grads_ref, result_ref, cond_bias_a_ref, cond_bias_b_ref,
    keep_ref, got_ref, other_result_ref, attn_out_ref, cond_out_ref, cond_other_ref,
    small_out_ref, small_other_ref,
    after_grad, mixed_grad, key_grad, value_grad, proj_grad, atoms_grad, send_buffer,
    gain_grad, qkv_grad, out_grad, agg_grad, pair_grad, small, *rest,
):
    *buffers, send_sem, recv_sem = rest
    links = Links(send_sem, recv_sem)
    links.barrier()
    samples, atoms, width = atoms_ref.shape
    groups, keys_in = probs_ref.shape[1], probs_ref.shape[2]
    queries_in = SPAN * QBLOCK
    scale = (width // ATOM_HEADS) ** (-0.5)
    cond_rows = cond_out_ref.shape[0]
    attn_rows = grads_ref.shape[2] - cond_rows
    attn_grads = grads_ref.at[:, :, :attn_rows, :]
    cond_grads = grads_ref.at[:, :, attn_rows:, :]
    number = len(buffers) // 3
    first, second, third = (buffers[i * number : (i + 1) * number] for i in range(3))
    journeys = [
        journey(links, attn_grads, first, attn_out_ref, None, i, CHUNK, i % 2 == 1, False)
        for i in range(attn_rows // 2 // CHUNK)
    ]
    journeys += [
        journey(links, cond_grads, second, cond_out_ref, cond_other_ref, i, CHUNK, i % 2 == 0, True)
        for i in range(cond_rows // 2 // CHUNK)
    ]
    flow = Flow(journeys)
    flow.step()
    result_copy = links.send(result_ref, other_result_ref, links.y)

    heads = bias_grad_ref.shape[0]
    total = jnp.zeros_like(pair_grad)
    for i in range(pair_ref.shape[0]):
        grad = bias_grad_ref[:, i, :]
        high = grad.astype(LOW)
        tail = (grad - high.astype(WIDE)).astype(LOW)
        both = mul(jnp.concatenate([high, tail], 0), pair_ref[i])
        total += both[:heads] + both[heads:]
        if i % 40 == 39:
            flow.step()
    pair_grad[...] = total

    for ref in (gain_grad, qkv_grad, out_grad, agg_grad):
        ref[...] = jnp.zeros_like(ref)
    chunk = 256
    token_ids = lax.broadcasted_iota(jnp.int32, (chunk, grad_ref.shape[1]), 1)
    atom_copies = []
    for s in range(samples):
        token_grad = (grad_ref[s].astype(WIDE) * inv_ref[...]).astype(LOW)
        for i in range(atoms // chunk):
            rows = slice(i * chunk, (i + 1) * chunk)
            mixed = mixed_ref[s, rows, :]
            after = atoms_ref[s, rows, :].astype(WIDE) + mul(mixed, out_w_ref[...])
            after_low = after.astype(LOW)
            pre = mul(after_low, agg_w_ref[...])
            sigma = sigmoid(pre)
            member = jnp.where(token_ids == ids_ref[rows, :], 1.0, 0.0).astype(LOW)
            unit_grad = mul(member, token_grad)
            pre_grad = (unit_grad * (sigma * (1.0 + pre * (1.0 - sigma)))).astype(LOW)
            agg_grad[...] += mul_tn(after_low, pre_grad)
            after_back = mul_nt(pre_grad, agg_w_ref[...])
            after_grad[rows, :] = after_back
            branch = after_back.astype(LOW)
            out_grad[...] += mul_tn(mixed, branch)
            mixed_grad[rows, :] = mul_nt(branch, out_w_ref[...]).astype(LOW)
            if i % 2 == 1:
                flow.step()
        key_grad[...] = jnp.zeros_like(key_grad)
        value_grad[...] = jnp.zeros_like(value_grad)

        def attend(group, carry, s=s):
            base = key_base(group, atoms)
            start = pl.multiple_of(group * queries_in, queries_in)
            queries = spread(qkv_ref[s, pl.ds(start, queries_in), :width], ATOM_HEADS)
            grads = spread(mixed_grad[pl.ds(start, queries_in), :], ATOM_HEADS)
            keys = qkv_ref[s, pl.ds(base, keys_in), width : 2 * width]
            values = qkv_ref[s, pl.ds(base, keys_in), 2 * width :]
            probs_low = probs_ref[s, group]
            probs = probs_low.astype(WIDE)
            probs_grad = mul_nt(values, grads)
            mean = jnp.sum(probs * probs_grad, 0, keepdims=True)
            scores_grad = (probs * (probs_grad - mean)).astype(LOW)
            query_grad = gather_heads(mul_tn(scores_grad, keys), ATOM_HEADS)
            proj_grad[pl.ds(start, queries_in), :width] = (query_grad * scale).astype(LOW)
            key_grad[pl.ds(base, keys_in), :] += mul(scores_grad, queries)
            value_grad[pl.ds(base, keys_in), :] += mul(probs_low, grads)
            return carry

        cuts = 4
        for i in range(cuts):
            lax.fori_loop(groups * i // cuts, groups * (i + 1) // cuts, attend, 0)
            flow.step()
        proj_grad[:, width : 2 * width] = (key_grad[...] * scale).astype(LOW)
        proj_grad[:, 2 * width :] = value_grad[...].astype(LOW)
        gain = gain_ref[...].astype(WIDE)
        normed, inverse = layer_norm(atoms_ref[s].astype(WIDE))
        hidden = (normed * gain).astype(LOW)
        proj = proj_grad[...]
        qkv_grad[...] += mul_tn(hidden, proj)
        hidden_grad = mul_nt(proj, qkv_w_ref[...])
        gain_grad[...] += jnp.sum(hidden_grad * normed, 0, keepdims=True)
        atoms_grad[...] = after_grad[...] + norm_back(normed, inverse, hidden_grad * gain)
        half = atoms // 2
        theirs = pl.ds(pl.multiple_of((1 - links.mp) * half, 16), half)
        send_buffer[s] = atoms_grad[theirs, :].astype(LOW)
        atom_copies.append(links.send(send_buffer.at[s], got_ref.at[s], links.y))
        keep_ref[s] = atoms_grad[pl.ds(pl.multiple_of(links.mp * half, 16), half), :]
        flow.step()

    wide = agg_grad.shape[1] // 2
    rows, part_rows = width // 2, width // 4

    def fill(values, cols):
        if values.shape[1] == cols:
            return values
        empty = jnp.zeros((values.shape[0], cols - values.shape[1]), WIDE)
        return jnp.concatenate([values, empty], 1)

    for h in range(2):
        to = relative(h, links.mp)
        cols = slice(h * wide, (h + 1) * wide)
        own_pair = jnp.where(links.mp == h, pair_grad[: heads // 2], pair_grad[heads // 2 :])
        for sec, cond_bias_ref in enumerate((cond_bias_a_ref, cond_bias_b_ref)):
            at = slice(sec * rows, (sec + 1) * rows)
            small[to, sec, :rows, :] = agg_grad[at, cols].astype(LOW)
            first_row = sec * rows + h * part_rows
            part_at = slice(first_row, first_row + part_rows)
            small[to, sec, rows : rows + part_rows, :] = fill(qkv_grad[part_at], wide).astype(LOW)
            small[to, sec, rows + part_rows : 2 * rows, :] = fill(out_grad[part_at], wide).astype(LOW)
            block = [fill(gain_grad[...], wide)]
            block += [cond_bias_ref[k, :, cols] for k in range(3)]
            block += [jnp.zeros((4, wide), WIDE), fill(own_pair, wide)]
            block += [jnp.zeros((16, wide), WIDE)]
            small[to, sec, 2 * rows :, :] = jnp.concatenate(block, 0).astype(LOW)
    flow.waiting.append(
        journey(
            links, small, third, small_out_ref, small_other_ref, 0, SMALL_ROWS // 2, False, True
        )
    )
    flow.finish()
    result_copy.wait()
    for copy in atom_copies:
        copy.wait()


def atom_back(
    atoms, gain, qkv_w, out_w, agg_w, ids, inverse_counts, qkv, probs, mixed, grad,
    low_pair, bias_grad, grads, result, cond_bias_a, cond_bias_b, cond_rows,
):
    samples, count, width = atoms.shape
    wide = agg_w.shape[1]
    cols = grads.shape[3]
    attn_rows = grads.shape[2] - cond_rows
    attn_chunks, cond_chunks = attn_rows // 2 // CHUNK, cond_rows // 2 // CHUNK
    copies = attn_chunks * journey_copies(CHUNK, False) + cond_chunks * journey_copies(CHUNK, True)
    copies += journey_copies(SMALL_ROWS // 2, True) + 1 + samples
    outs = [
        sds((samples, count // 2, width), WIDE),
        sds((samples, count // 2, width), LOW),
        sds(result.shape, LOW),
        sds((attn_rows, cols), LOW),
        sds((cond_rows, cols), LOW),
        sds((cond_rows, cols), LOW),
        sds((SMALL_ROWS, cols), LOW),
        sds((SMALL_ROWS, cols), LOW),
    ]
    args = (
        atoms, gain, qkv_w, out_w, agg_w, ids, inverse_counts, qkv, probs, mixed, grad,
        low_pair, bias_grad, grads, result, cond_bias_a, cond_bias_b,
    )
    return pl.pallas_call(
        atom_back_kernel,
        in_specs=everywhere(len(args)),
        out_specs=everywhere(len(outs)),
        out_shape=outs,
        scratch_shapes=[
            pltpu.VMEM((count, width), WIDE),
            pltpu.VMEM((count, width), LOW),
            pltpu.VMEM((count, width), WIDE),
            pltpu.VMEM((count, width), WIDE),
            pltpu.VMEM((count, 3 * width), LOW),
            pltpu.VMEM((count, width), WIDE),
            pltpu.VMEM((samples, count // 2, width), LOW),
            pltpu.VMEM((1, width), WIDE),
            pltpu.VMEM((width, 3 * width), WIDE),
            pltpu.VMEM((width, width), WIDE),
            pltpu.VMEM((width, wide), WIDE),
            pltpu.VMEM((bias_grad.shape[0], width), WIDE),
            pltpu.VMEM((2, 2, SMALL_ROWS, cols), LOW),
            *journey_scratch(attn_chunks, CHUNK, cols),
            *journey_scratch(cond_chunks, CHUNK, cols),
            *journey_scratch(1, SMALL_ROWS // 2, cols),
            pltpu.SemaphoreType.DMA((copies,)),
            pltpu.SemaphoreType.DMA((copies,)),
        ],
        compiler_params=remote_params(60, 2),
        cost_estimate=cost(60e9, 24e6),
        name="atom_back",
    )(*args)


def swap(array, axis, bit=0):
    size = lax.axis_size(axis)
    return lax.ppermute(array, axis, [(i, i ^ (1 << bit)) for i in range(size)])


def side(axis, bit=0):
    return (lax.axis_index(axis) >> bit) & 1


def both_halves(array, axis, bit, dim):
    other, me = swap(array, axis, bit), side(axis, bit)
    first, second = jnp.where(me == 0, array, other), jnp.where(me == 0, other, array)
    return jnp.concatenate([first, second], dim)


def fetch(weight):
    size = weight.shape[0] // 2
    own = lax.dynamic_slice_in_dim(weight, side("dp") * size, size, 0)
    return both_halves(swap(own, "mp"), "dp", 0, 0)


def local(
    atoms_in,
    atom_token,
    window_start,
    noise_level,
    level_table,
    single_trunk,
    pair,
    atom_gain,
    atom_qkv,
    atom_out,
    atom_agg,
    cond_weight,
    cond_bias,
    pair_weight,
    attn_in,
    attn_out,
    mlp_up,
    mlp_down,
    cotangent,
):
    section, mp = lax.axis_index("section"), lax.axis_index("mp")
    batch, half_atoms, atom_width = atoms_in.shape
    batch //= MICRO
    samples = batch // 2
    atoms = 2 * half_atoms
    tokens, width = cotangent.shape[1], cotangent.shape[2]
    single = single_trunk.shape[1]
    own_first = section * batch + mp * samples
    other_first = section * batch + (1 - mp) * samples

    own_atoms = lax.dynamic_slice_in_dim(atoms_in, own_first, samples, 0)
    other_atoms = swap(lax.dynamic_slice_in_dim(atoms_in, other_first, samples, 0), "mp")
    all_atoms = jnp.concatenate(
        [jnp.where(mp == 0, own_atoms, other_atoms), jnp.where(mp == 0, other_atoms, own_atoms)], 1
    )
    other_start = swap(window_start, "mp")
    starts = jnp.concatenate(
        [jnp.where(mp == 0, window_start, other_start), jnp.where(mp == 0, other_start, window_start)]
    )
    in_a = attn_in.reshape(width, -1)
    up_a = mlp_up.reshape(width, -1)
    in_b, out_b = fetch(in_a), fetch(attn_out)
    up_b, down_b = fetch(up_a), fetch(mlp_down)
    pair_w = jnp.concatenate([pair_weight, swap(pair_weight, "mp")], 1).T
    levels = lax.dynamic_slice_in_dim(noise_level, own_first, samples, 0)
    grad_out = lax.dynamic_slice_in_dim(cotangent, own_first, samples, 0).reshape(-1, width)

    token_ids = jnp.arange(tokens, dtype=jnp.int32)
    counts = jnp.sum((atom_token[:, None] == token_ids[None, :]).astype(WIDE), 0)
    inverse_counts = (1.0 / counts)[:, None]
    level_pick = (levels[:, None] == jnp.arange(level_table.shape[0], dtype=jnp.int32)[None, :])
    level_rows = jnp.sum(
        jnp.where(level_pick[:, :, None], level_table.astype(WIDE)[None], 0.0), 1, keepdims=True
    )
    windows = starts.shape[0]
    groups = windows // SPAN
    base = jnp.clip(
        jnp.arange(groups, dtype=jnp.int32) * (SPAN * QBLOCK) - KWIN // 2,
        0,
        atoms - KWIN - SPAN * QBLOCK,
    )
    rel = starts.reshape(groups, SPAN) - base[:, None]
    rel = jnp.broadcast_to(rel[:, None, None, :, None], (groups, 1, ATOM_HEADS, SPAN, QBLOCK))
    rel = rel.reshape(groups, 1, ATOM_HEADS * SPAN * QBLOCK)
    gain = atom_gain[None, :]
    qkv_w = atom_qkv.reshape(atom_width, -1)

    low_pair, bias = pair_bias(pair, pair_w)
    cond_w = jnp.transpose(cond_weight, (0, 2, 1, 3)).reshape(6, single, width)
    low, cond_a, cond_b = conditioning(
        single_trunk, level_rows, cond_w, cond_bias.reshape(6, 1, width)
    )
    qkv, probs, mixed, token_in = atom_front(
        all_atoms, gain, qkv_w, atom_out, atom_agg, rel, atom_token[None, :], inverse_counts
    )
    token_in = token_in.reshape(-1, width)
    inner, token_qkv, sig, heads_out, gated, token_probs, attn, middle = token_attention(
        token_in, cond_a, bias, in_a, in_b, attn_out, out_b
    )
    result, middle_grad, mlp_grads, cond_grad, cond_bias_b = transition(
        middle, cond_b, grad_out, low, up_a, up_b, mlp_down, down_b
    )
    token_grad, attn_grads, cond_bias_a, bias_grad, mlp_sum = attention_back(
        middle_grad, token_in, cond_a, attn, low, inner, token_qkv, sig, heads_out, gated,
        token_probs, in_a, in_b, attn_out, out_b, mlp_grads, cond_grad,
    )
    keep, got, other_result, attn_sum, cond_sum, cond_other, small, small_other = atom_back(
        all_atoms, gain, qkv_w, atom_out, atom_agg, atom_token[:, None], inverse_counts,
        qkv, probs, mixed, token_grad.reshape(samples, tokens, width),
        low_pair, bias_grad, attn_grads, result, cond_bias_a, cond_bias_b, cond_grad.shape[1],
    )

    result = result.reshape(samples, tokens, width)
    other_result = other_result.reshape(samples, tokens, width)
    token_out = jnp.concatenate(
        [jnp.where(mp == 0, result, other_result), jnp.where(mp == 0, other_result, result)]
    )
    got = got.astype(WIDE)
    atoms_out = jnp.concatenate([jnp.where(mp == 0, keep, got), jnp.where(mp == 0, got, keep)])
    half = width // 2
    attn_local, mlp_local = attn_in.shape[2], mlp_up.shape[2]
    in_sum = jnp.transpose(attn_sum[: 4 * half].reshape(4, half, attn_local), (1, 0, 2))
    up_sum = jnp.transpose(
        mlp_sum[: 4 * half].reshape(2, mlp_local // half, half, half), (2, 0, 1, 3)
    ).reshape(half, 2, mlp_local)
    small, small_other = small.astype(WIDE), small_other.astype(WIDE)
    small_pair = (
        jnp.where(mp == 0, small, small_other),
        jnp.where(mp == 0, small_other, small),
    )
    rows, part_rows = atom_width // 2, atom_width // 4
    lanes = lax.dynamic_slice_in_dim(small[2 * rows :, :atom_width], section * rows, rows, 1)
    cond_pair = [
        jnp.where(mp == 0, cond_sum, cond_other).reshape(3, single, half),
        jnp.where(mp == 0, cond_other, cond_sum).reshape(3, single, half),
    ]
    cond_total = jnp.transpose(jnp.concatenate(cond_pair, 2), (1, 0, 2))
    return (
        token_out.reshape(1, 1, batch, tokens, width),
        atoms_out.reshape(1, 1, batch, half_atoms, atom_width),
        lanes[0],
        jnp.concatenate([a[rows : rows + part_rows] for a in small_pair], 0).reshape(
            rows, 3, atom_width
        ),
        jnp.concatenate([a[rows + part_rows : 2 * rows, :atom_width] for a in small_pair], 0),
        jnp.concatenate([a[:rows] for a in small_pair], 1),
        cond_total[None].astype(WIDE),
        jnp.concatenate([a[2 * rows + 1 : 2 * rows + 4] for a in small_pair], 1)[None],
        lanes[8:16].T,
        in_sum.astype(WIDE),
        attn_sum[4 * half :].astype(WIDE),
        up_sum.astype(WIDE),
        mlp_sum[4 * half :].astype(WIDE),
    )


def solution(mesh):
    in_specs = (
        P("dp", "mp", None),
        P(),
        P("mp"),
        P("dp"),
        P(),
        P(),
        P(),
        P(),
        P(),
        P(),
        P(),
        P(),
        P(),
        P(None, "mp"),
        P(None, None, "mp"),
        P("mp", None),
        P(None, None, "mp"),
        P("mp", None),
        P("dp", None, None),
    )
    out_specs = (
        P("dp", "section", None, None, None),
        P("dp", "section", None, "mp", None),
        P("section"),
        P("section", None, None),
        P("section", None),
        P("section", None),
        P("section", None, None, None),
        P("section", None, None),
        P("section", "mp"),
        P("section", None, "mp"),
        P("mp", "section"),
        P("section", None, "mp"),
        P("mp", "section"),
    )
    return jax.shard_map(local, mesh=mesh, in_specs=in_specs, out_specs=out_specs, check_vma=False)
```

```python
import functools

import jax
import jax.numpy as jnp
from jax import lax
from jax.experimental import pallas as pl
from jax.experimental.pallas import tpu as pltpu
from jax.sharding import PartitionSpec as P

QBLOCK = 32
KWIN = 128
MICRO = 2
ATOM_HEADS = 4
SPAN = 2
EPS = 1e-05
LOW = jnp.bfloat16
WIDE = jnp.float32
MIB = 1 << 20


def mul(left, right):
    return lax.dot_general(left, right, (((1,), (0,)), ((), ())), preferred_element_type=WIDE)


def mul_nt(left, right):
    return lax.dot_general(left, right, (((1,), (1,)), ((), ())), preferred_element_type=WIDE)


def mul_tn(left, right):
    return lax.dot_general(left, right, (((0,), (0,)), ((), ())), preferred_element_type=WIDE)


def layer_norm(values):
    center = values - jnp.mean(values, -1, keepdims=True)
    inverse = lax.rsqrt(jnp.mean(center * center, -1, keepdims=True) + EPS)
    return center * inverse, inverse


def norm_back(normed, inverse, grad):
    return inverse * (
        grad
        - jnp.mean(grad, -1, keepdims=True)
        - normed * jnp.mean(grad * normed, -1, keepdims=True)
    )


def sigmoid(values):
    return 1.0 / (1.0 + jnp.exp(-values))


def params(mib, semantics=None):
    return pltpu.CompilerParams(vmem_limit_bytes=mib * MIB, dimension_semantics=semantics)


def cost(flops, moved, exps=0):
    return pl.CostEstimate(flops=int(flops), bytes_accessed=int(moved), transcendentals=int(exps))


def sds(shape, dtype):
    return jax.ShapeDtypeStruct(shape, dtype)


def lane_heads(rows, width, size):
    return lax.broadcasted_iota(jnp.int32, (rows, width), 1) // size


def spread(values, heads):
    head = lane_heads(values.shape[0], values.shape[1], values.shape[1] // heads)
    zero = jnp.zeros_like(values)
    return jnp.concatenate([jnp.where(head == h, values, zero) for h in range(heads)], 0)


def gather_heads(values, heads):
    rows = values.shape[0] // heads
    head = lane_heads(rows, values.shape[1], values.shape[1] // heads)
    total = jnp.where(head == 0, values[:rows], 0.0)
    for h in range(1, heads):
        total += jnp.where(head == h, values[h * rows : (h + 1) * rows], 0.0)
    return total


def key_base(group, atoms):
    start = group * SPAN * QBLOCK - KWIN // 2
    return pl.multiple_of(jnp.clip(start, 0, atoms - KWIN - (SPAN - 1) * QBLOCK - QBLOCK), QBLOCK)


def far_bits():
    return range(1, lax.axis_size("dp").bit_length() - 1)


class Links:
    def __init__(self, send_sem, recv_sem, far=True):
        self.section, self.mp = lax.axis_index("section"), lax.axis_index("mp")
        self.dp = lax.axis_index("dp")
        self.core = self.dp % 2
        self.far = [self.dp // (1 << b) % 2 for b in far_bits()]
        self.partners = [{"section": 1 - self.section}, {"mp": 1 - self.mp}]
        self.partners.append({"dp": self.dp + 1 - 2 * self.core})
        for b, side_of in zip(far_bits() if far else (), self.far):
            self.partners.append({"dp": self.dp + (1 - 2 * side_of) * (1 << b)})
        self.x, self.y, self.twin = self.partners[:3]
        self.z = self.partners[3:]
        self.send_sem, self.recv_sem, self.used = send_sem, recv_sem, 0

    def barrier(self):
        barrier = pltpu.get_barrier_semaphore()
        for partner in self.partners:
            pl.semaphore_signal(
                barrier, inc=1, device_id=partner, device_id_type=pl.DeviceIdType.MESH
            )
        pl.semaphore_wait(barrier, len(self.partners))

    def send(self, source, target, partner):
        copy = pltpu.make_async_remote_copy(
            src_ref=source,
            dst_ref=target,
            send_sem=self.send_sem.at[self.used],
            recv_sem=self.recv_sem.at[self.used],
            device_id=partner,
            device_id_type=pl.DeviceIdType.MESH,
        )
        self.used += 1
        copy.start()
        return copy


def splits_far(rows):
    steps = []
    for _ in far_bits():
        halves = rows % 32 == 0
        rows = rows // 2 if halves else rows
        steps.append((rows, halves))
    return steps


def journey_copies(rows, shared):
    steps = splits_far(rows)
    return 4 + len(steps) + sum(halves for _, halves in steps) + (2 if shared else 0)


def journey_scratch(chunks, rows, cols):
    shapes = [(chunks, 2, 2, rows, cols), (chunks, 2, rows, cols), (chunks, rows, cols)]
    shapes += [(chunks, size, cols) for size, _ in splits_far(rows)]
    return [pltpu.VMEM(shape, LOW) for shape in shapes]


def journey(links, grads, kept, buffers, out, other_out, chunk, rows, x_first, shared):
    near, middle, last = (buffer.at[chunk] for buffer in buffers[:3])
    far = [buffer.at[chunk] for buffer in buffers[3:]]
    total_rows = grads.shape[2]
    start = links.core * (total_rows // 2) + chunk * rows
    twin_start = (1 - links.core) * (total_rows // 2) + chunk * rows
    mine, theirs = pl.ds(pl.multiple_of(start, 16), rows), pl.ds(pl.multiple_of(twin_start, 16), rows)
    me, you = links.section, 1 - links.section
    if kept is None:
        own = grads.at[:, :, mine, :]
    else:
        own = kept.at[:, :, pl.ds(chunk * rows, rows), :]
    block = rows * grads.shape[3] * 2
    copy = links.send(grads.at[:, :, theirs, :], near, links.twin)
    yield [("core", 4 * block)]
    copy.wait()
    if x_first:
        near[:, you] += own[:, you]
        copy = links.send(near.at[:, you], middle, links.x)
        near[:, me] += own[:, me]
        yield [("x", 2 * block)]
        copy.wait()
        middle[1] += near[1, me]
        copy = links.send(middle.at[1], last, links.y)
        middle[0] += near[0, me]
        yield [("y", block)]
        copy.wait()
        last[...] += middle[0]
    else:
        near[1] += own[1]
        copy = links.send(near.at[1], middle, links.y)
        near[0] += own[0]
        yield [("y", 2 * block)]
        copy.wait()
        middle[you] += near[0, you]
        copy = links.send(middle.at[you], last, links.x)
        middle[me] += near[0, me]
        yield [("x", block)]
        copy.wait()
        last[...] += middle[me]
    held, place, size = last, start, rows
    back = []
    names = ["z"] + ["far" + str(i) for i in range(1, len(far))]
    for (count, halves), bit, partner, slot, name in zip(
        splits_far(rows), links.far, links.z, far, names
    ):
        if halves:
            give = pl.ds(pl.multiple_of((1 - bit) * count, 16), count)
            keep = pl.ds(pl.multiple_of(bit * count, 16), count)
            copy = links.send(held.at[give, :], slot, partner)
            back.append((bit, partner, name))
            place = place + bit * count
        else:
            keep = pl.ds(0, count)
            copy = links.send(held, slot, partner)
        yield [(name, block * count // rows)]
        copy.wait()
        slot[...] += held[keep, :]
        held, size = slot, count
    out[pl.ds(pl.multiple_of(place, 16), size), :] = held[...]
    for bit, partner, name in reversed(back):
        at = pl.ds(pl.multiple_of(place, 16), size)
        copy = links.send(out.at[at, :], out.at[at, :], partner)
        yield [(name, block * size // rows)]
        copy.wait()
        place, size = place - bit * size, 2 * size
    copies = [links.send(out.at[mine, :], out.at[mine, :], links.twin)]
    if shared:
        across = links.send(out.at[mine, :], other_out.at[mine, :], links.y)
        yield [("y", block)]
        across.wait()
        copies.append(links.send(other_out.at[mine, :], other_out.at[mine, :], links.twin))
    yield [("core", block)]
    for copy in copies:
        copy.wait()


class Flow:
    RATES = {"core": 400e3, "x": 43e3, "y": 43e3, "z": 43e3, "far": 21e3}
    DELAY = 1.5

    def __init__(self, journeys):
        self.clock, self.free, self.queue, self.count = 0.0, {}, [], 0
        for one in journeys:
            self.add(one)

    def add(self, one):
        copies = next(one, None)
        if copies is None:
            return
        ready = self.clock
        for link, count in copies:
            finish = max(self.clock, self.free.get(link, 0.0)) + count / self.RATES[link.rstrip("0123456789")]
            self.free[link] = finish
            ready = max(ready, finish + self.DELAY)
        self.queue.append((ready, self.count, one))
        self.queue.sort(key=lambda entry: entry[:2])
        self.count += 1

    def after(self, duration):
        self.clock += duration
        while self.queue and self.queue[0][0] <= self.clock:
            self.add(self.queue.pop(0)[2])

    def finish(self):
        while self.queue:
            self.clock = max(self.clock, self.queue[0][0])
            self.add(self.queue.pop(0)[2])


def everywhere(count):
    return [pl.BlockSpec(memory_space=pltpu.VMEM)] * count


def remote_params(mib, number):
    return pltpu.CompilerParams(
        vmem_limit_bytes=mib * MIB, collective_id=number, has_side_effects=True
    )


class Local:
    def __init__(self, sem):
        self.sem, self.used, self.open = sem, 0, []

    def start(self, source, target):
        copy = pltpu.make_async_copy(source, target, self.sem.at[self.used])
        self.used += 1
        copy.start()
        return copy

    def store(self, source, target):
        self.open.append(self.start(source, target))

    def finish(self):
        for copy in self.open:
            copy.wait()


def fetch_journey(links, own, other, chunk, rows):
    quarter = own.shape[0] // 4
    block = rows * own.shape[1] * 2

    def at(core, section):
        start = (2 * core + section) * quarter + chunk * rows
        return pl.ds(pl.multiple_of(start, 16), rows)

    mine = at(links.core, links.section)
    across = at(links.core, 1 - links.section)
    copy = links.send(own.at[mine, :], other.at[mine, :], links.y)
    yield [("y", block)]
    copy.wait()
    first = links.send(other.at[mine, :], other.at[mine, :], links.x)
    second = links.send(other.at[mine, :], other.at[mine, :], links.twin)
    yield [("x", block), ("core", block)]
    first.wait()
    third = links.send(other.at[across, :], other.at[across, :], links.twin)
    yield [("core", block)]
    second.wait()
    third.wait()


def front_kernel(
    trunk_ref, level_ref, cond_w_ref, cond_b_ref, pair_ref, pair_w_ref, atoms_ref, gain_ref,
    qkv_w_ref, out_w_ref, agg_w_ref, rel_ref, ids_ref, inv_ref, in_a_ref, out_a_ref, up_a_ref,
    low_ref, cond_a_ref, cond_b_out_ref, low_pair_ref, bias_ref, atoms_out_ref, qkv_ref, probs_ref,
    mixed_ref, tokens_ref, in_b_ref, out_b_ref, up_b_ref,
    cond_w, cond_out, pair, pair_w, bias, atoms, rel, qkv, probs, mixed, total, tokens,
    local_sem, send_sem, recv_sem,
):
    links = Links(send_sem, recv_sem, far=False)
    local = Local(local_sem)
    samples, count, width = atoms.shape
    half_atoms = count // 2
    batch = atoms_ref.shape[0] // MICRO
    parts = cond_w.shape[0]
    loads = [local.start(cond_w_ref.at[i], cond_w.at[i]) for i in range(parts)]
    pieces = 4
    each = pair.shape[0] // pieces
    pair_loads = [
        local.start(pair_ref.at[pl.ds(i * each, each)], pair.at[pl.ds(i * each, each)])
        for i in range(pieces)
    ]
    own_first = links.section * batch + links.mp * samples
    other_first = links.section * batch + (1 - links.mp) * samples
    own_half = pl.ds(pl.multiple_of(links.mp * half_atoms, 16), half_atoms)
    own_groups = pl.ds(links.mp * rel_ref.shape[0], rel_ref.shape[0])
    heads = pair_w_ref.shape[0]
    atom_loads = [
        local.start(atoms_ref.at[pl.ds(own_first, samples)], atoms.at[:, own_half, :]),
        local.start(rel_ref, rel.at[own_groups]),
        local.start(pair_w_ref, pair_w.at[0]),
    ]
    links.barrier()
    pair_w_copy = links.send(pair_w_ref, pair_w.at[1], links.y)
    rel_copy = links.send(rel_ref, rel.at[own_groups], links.y)
    atom_copy = links.send(
        atoms_ref.at[pl.ds(other_first, samples)], atoms.at[:, own_half, :], links.y
    )
    flow = Flow([])
    flow.free["y"] = samples * half_atoms * width * 2 / Flow.RATES["y"]
    for own, other, chunks in (
        (in_a_ref, in_b_ref, 4),
        (out_a_ref, out_b_ref, 1),
        (up_a_ref, up_b_ref, 4),
    ):
        rows = own.shape[0] // 4 // chunks
        for i in range(chunks):
            flow.add(fetch_journey(links, own, other, i, rows))

    trunk = trunk_ref[...].astype(WIDE)
    rows = trunk.shape[0]
    for s in range(samples):
        normed, _ = layer_norm(trunk + level_ref[s])
        low_ref[s * rows : (s + 1) * rows, :] = normed.astype(LOW)
    for i in range(parts):
        loads[i].wait()
        value = mul(low_ref[...], cond_w[i]) + cond_b_ref[i]
        cond_out[i] = value if i % 3 == 1 else sigmoid(value)
        target = (cond_a_ref, cond_b_out_ref)[i // 3]
        local.store(cond_out.at[i], target.at[i % 3])
    flow.after(4.0)

    atom_loads[2].wait()
    pair_w_copy.wait()
    weight = jnp.concatenate([pair_w[0], pair_w[1]], 0)
    block = 8
    for piece in range(pieces):
        pair_loads[piece].wait()

        def pair_rows(i, carry):
            at = pl.multiple_of(i * block, block)
            normed, _ = layer_norm(pair[pl.ds(at, block)].astype(WIDE))
            low = normed.astype(LOW)
            pair[pl.ds(at, block)] = low
            for j in range(block):
                bias[:, pl.ds(at + j, 1), :] = mul_nt(weight, low[j])[:, None, :]
            return carry

        lax.fori_loop(piece * each // block, (piece + 1) * each // block, pair_rows, 0)
        at = pl.ds(piece * each, each)
        local.store(pair.at[at], low_pair_ref.at[at])
        local.store(bias.at[:, at, :], bias_ref.at[:, at, :])
        flow.after(3.0)

    for copy in (atom_loads[0], atom_loads[1], rel_copy, atom_copy):
        copy.wait()
    local.store(atoms, atoms_out_ref)
    groups, keys_in = probs.shape[1], probs.shape[2]
    queries_in = SPAN * QBLOCK
    scale = (width // ATOM_HEADS) ** (-0.5)
    place = lax.broadcasted_iota(jnp.int32, (keys_in, ATOM_HEADS * queries_in), 0)
    chunk = 256
    ids = lax.broadcasted_iota(jnp.int32, (total.shape[0], chunk), 0)
    for s in range(samples):
        normed, _ = layer_norm(atoms[s].astype(WIDE))
        hidden = (normed * gain_ref[...].astype(WIDE)).astype(LOW)
        qkv[s] = mul(hidden, qkv_w_ref[...]).astype(LOW)
        local.store(qkv.at[s], qkv_ref.at[s])

        def attend(group, carry, s=s):
            base = key_base(group, count)
            first = pl.multiple_of(group * queries_in, queries_in)
            queries = spread(qkv[s, pl.ds(first, queries_in), :width], ATOM_HEADS)
            keys = qkv[s, pl.ds(base, keys_in), width : 2 * width]
            values = qkv[s, pl.ds(base, keys_in), 2 * width :]
            offset = place - rel[group]
            scores = mul_nt(keys, queries) * scale
            scores = jnp.where((offset >= 0) & (offset < KWIN), scores, -1e30)
            exps = jnp.exp(scores - jnp.max(scores, 0, keepdims=True))
            low = (exps * (1.0 / jnp.sum(exps, 0, keepdims=True))).astype(LOW)
            probs[s, group] = low
            mixed[s, pl.ds(first, queries_in), :] = gather_heads(
                mul_tn(low, values), ATOM_HEADS
            ).astype(LOW)
            return carry

        cuts = 4
        for i in range(cuts):
            lax.fori_loop(groups * i // cuts, groups * (i + 1) // cuts, attend, 0)
            flow.after(2.0)
        local.store(probs.at[s], probs_ref.at[s])
        local.store(mixed.at[s], mixed_ref.at[s])
        for i in range(count // chunk):
            rows = slice(i * chunk, (i + 1) * chunk)
            after = atoms[s, rows, :].astype(WIDE) + mul(mixed[s, rows, :], out_w_ref[...])
            pre = mul(after.astype(LOW), agg_w_ref[...])
            units = (pre * sigmoid(pre)).astype(LOW)
            member = jnp.where(ids == ids_ref[:, rows], 1.0, 0.0).astype(LOW)
            part_sum = mul(member, units)
            if i == 0:
                total[...] = part_sum
            else:
                total[...] += part_sum
            flow.after(0.9)
        tokens[s] = (total[...] * inv_ref[...]).astype(LOW)
        local.store(tokens.at[s], tokens_ref.at[s])
    flow.finish()
    local.finish()


def front(
    trunk, levels, cond_w, cond_b, pair, pair_w, atoms, gain, qkv_w, out_w, agg_w, rel, ids,
    inverse_counts, in_a, out_a, up_a,
):
    tokens_in, width = trunk.shape
    samples, parts, wide = levels.shape[0], cond_w.shape[0], cond_w.shape[2]
    rows = samples * tokens_in
    count, atom_width = 2 * atoms.shape[1], atoms.shape[2]
    heads = 2 * pair_w.shape[0]
    groups = count // (SPAN * QBLOCK)
    keys_in, lanes = KWIN + SPAN * QBLOCK, ATOM_HEADS * SPAN * QBLOCK
    probs_shape = (samples, groups, keys_in, lanes)
    hbm, near = pl.BlockSpec(memory_space=pl.ANY), pl.BlockSpec(memory_space=pltpu.VMEM)
    outs = [
        (near, (rows, width), LOW),
        (hbm, (parts // 2, rows, wide), WIDE),
        (hbm, (parts // 2, rows, wide), WIDE),
        (hbm, pair.shape, LOW),
        (hbm, (heads, tokens_in, tokens_in), WIDE),
        (hbm, (samples, count, atom_width), LOW),
        (hbm, (samples, count, 3 * atom_width), LOW),
        (hbm, probs_shape, LOW),
        (hbm, (samples, count, atom_width), LOW),
        (hbm, (samples, tokens_in, wide), LOW),
        (hbm, in_a.shape, LOW),
        (hbm, out_a.shape, LOW),
        (hbm, up_a.shape, LOW),
    ]
    copies = 3 + 9 * 4
    return pl.pallas_call(
        front_kernel,
        in_specs=[near, near, hbm, near, hbm, near, hbm] + [near] * 4 + [near] * 3 + [hbm] * 3,
        out_specs=[spec for spec, _, _ in outs],
        out_shape=[sds(shape, dtype) for _, shape, dtype in outs],
        scratch_shapes=[
            pltpu.VMEM(cond_w.shape, LOW),
            pltpu.VMEM((parts, rows, wide), WIDE),
            pltpu.VMEM(pair.shape, LOW),
            pltpu.VMEM((2,) + pair_w.shape, LOW),
            pltpu.VMEM((heads, tokens_in, tokens_in), WIDE),
            pltpu.VMEM((samples, count, atom_width), LOW),
            pltpu.VMEM((2 * rel.shape[0],) + rel.shape[1:], jnp.int32),
            pltpu.VMEM((samples, count, 3 * atom_width), LOW),
            pltpu.VMEM(probs_shape, LOW),
            pltpu.VMEM((samples, count, atom_width), LOW),
            pltpu.VMEM((tokens_in, wide), WIDE),
            pltpu.VMEM((samples, tokens_in, wide), LOW),
            pltpu.SemaphoreType.DMA((64,)),
            pltpu.SemaphoreType.DMA((copies,)),
            pltpu.SemaphoreType.DMA((copies,)),
        ],
        compiler_params=remote_params(60, 3),
        cost_estimate=cost(40e9, 40e6),
        name="front",
    )(
        trunk, levels, cond_w, cond_b, pair, pair_w, atoms, gain, qkv_w, out_w, agg_w, rel, ids,
        inverse_counts, in_a, out_a, up_a,
    )


def token_attention_kernel(
    tokens_ref, cond_ref, bias_ref, in_a_ref, in_b_ref, out_a_ref, out_b_ref, down_a_ref,
    inner_ref, qkv_ref, sig_ref, heads_ref, gated_ref, probs_ref, attn_ref, middle_ref, down_b_ref,
    tokens, cond, bias, in_a, in_b, out_a, out_b, inner, qkv, sig, heads_out, gated, probs, attn,
    middle, local_sem, send_sem, recv_sem,
):
    links = Links(send_sem, recv_sem, far=False)
    local = Local(local_sem)
    load_tokens = local.start(tokens_ref, tokens)
    load_cond = local.start(cond_ref, cond)
    load_in = [local.start(in_a_ref, in_a)]
    load_bias = local.start(bias_ref, bias)
    load_in.append(local.start(in_b_ref, in_b))
    load_out = [local.start(out_a_ref, out_a), local.start(out_b_ref, out_b)]
    links.barrier()
    chunks = 2
    flow = Flow(
        fetch_journey(links, down_a_ref, down_b_ref, i, down_a_ref.shape[0] // 4 // chunks)
        for i in range(chunks)
    )
    samples, heads, count = probs.shape[0], probs.shape[1], probs.shape[2]
    width_in = in_a.shape[1] // 4
    size = 2 * width_in // heads
    scale = size ** (-0.5)
    load_tokens.wait()
    load_cond.wait()
    wide = tokens[...].astype(WIDE)
    normed, _ = layer_norm(wide)
    inner[...] = (normed * cond[0] + cond[1]).astype(LOW)
    local.store(inner, inner_ref)
    for half, weight in enumerate((in_a, in_b)):
        load_in[half].wait()
        qkv[half] = mul(inner[...], weight[:, : 3 * width_in]).astype(LOW)
        local.store(qkv.at[half], qkv_ref.at[half])
        sig[half] = sigmoid(mul(inner[...], weight[:, 3 * width_in :]))
        local.store(sig.at[half], sig_ref.at[half])
        if half == 0:
            load_bias.wait()
        flow.after(1.5)
        for s in range(samples):
            at = slice(s * count, (s + 1) * count)
            outs = []
            for h in range(heads // 2):
                col = h * size
                query = qkv[half, at, col : col + size]
                key = qkv[half, at, width_in + col : width_in + col + size]
                value = qkv[half, at, 2 * width_in + col : 2 * width_in + col + size]
                scores = mul_nt(query, key) * scale + bias[half * (heads // 2) + h]
                exps = jnp.exp(scores - jnp.max(scores, -1, keepdims=True))
                low = (exps * (1.0 / jnp.sum(exps, -1, keepdims=True))).astype(LOW)
                probs[s, half * (heads // 2) + h] = low
                outs.append(mul(low, value))
                if h % 4 == 3:
                    flow.after(1.2)
            heads_out[half, at, :] = jnp.concatenate(outs, 1)
        gated[half] = (heads_out[half] * sig[half]).astype(LOW)
        local.store(heads_out.at[half], heads_ref.at[half])
        local.store(gated.at[half], gated_ref.at[half])
    local.store(probs, probs_ref)
    load_out[0].wait()
    load_out[1].wait()
    attn[...] = mul(gated[0], out_a[...]) + mul(gated[1], out_b[...])
    local.store(attn, attn_ref)
    middle[...] = wide + cond[2] * attn[...]
    local.store(middle, middle_ref)
    flow.finish()
    local.finish()


def token_attention(tokens, cond, bias, in_a, in_b, out_a, out_b, down_a):
    rows, width = tokens.shape
    heads, count = bias.shape[0], bias.shape[1]
    samples, width_in = rows // count, in_a.shape[1] // 4
    hbm = pl.BlockSpec(memory_space=pl.ANY)
    outs = [
        sds((rows, width), LOW),
        sds((2, rows, 3 * width_in), LOW),
        sds((2, rows, width_in), WIDE),
        sds((2, rows, width_in), WIDE),
        sds((2, rows, width_in), LOW),
        sds((samples, heads, count, count), LOW),
        sds((rows, width), WIDE),
        sds((rows, width), WIDE),
    ]
    args = (tokens, cond, bias, in_a, in_b, out_a, out_b)
    copies = 4 * 2
    return pl.pallas_call(
        token_attention_kernel,
        in_specs=[hbm] * (len(args) + 1),
        out_specs=[hbm] * (len(outs) + 1),
        out_shape=outs + [sds(down_a.shape, LOW)],
        scratch_shapes=[
            *(pltpu.VMEM(a.shape, a.dtype) for a in args),
            *(pltpu.VMEM(a.shape, a.dtype) for a in outs),
            pltpu.SemaphoreType.DMA((32,)),
            pltpu.SemaphoreType.DMA((copies,)),
            pltpu.SemaphoreType.DMA((copies,)),
        ],
        compiler_params=remote_params(60, 4),
        cost_estimate=cost(40e9, 20e6),
        name="token_attention",
    )(*args, down_a)


CHUNK = 192


def relative(half, mp):
    return mp if half == 0 else 1 - mp


def token_back_kernel(
    middle_ref, cond_b_ref, cotangent_ref, low_ref, up_a_ref, up_b_ref, down_a_ref, down_b_ref,
    tokens_ref, cond_a_ref, attn_ref, inner_ref, qkv_ref, sig_ref, heads_ref, gated_ref, probs_ref,
    in_a_ref, in_b_ref, out_a_ref, out_b_ref, pair_ref,
    result_ref, other_result_ref, token_grad_ref, grads_ref, cond_bias_a_ref, cond_bias_b_ref,
    pair_grad_ref, mlp_out_ref,
    middle, cond, grad, low, weight, out_weight, up, hidden, mlp_grads, middle_grad, result,
    tokens, inner, qkv, sig, heads_out, gated, probs, grads, bias_grad, proj, heads_grad, pair, *rest,
):
    *buffers, local_sem, send_sem, recv_sem = rest
    links = Links(send_sem, recv_sem)
    local = Local(local_sem)
    load_first = [
        local.start(a, b)
        for a, b in ((middle_ref, middle), (cond_b_ref, cond), (up_a_ref, weight.at[0]))
    ]
    load_up_b = local.start(up_b_ref, weight.at[1])
    load_down = [local.start(down_a_ref, out_weight.at[0])]
    load_down.append(local.start(down_b_ref, out_weight.at[1]))
    load_grad = [local.start(cotangent_ref, grad), local.start(low_ref, low)]
    load_later = [
        local.start(a, b)
        for a, b in (
            (gated_ref, gated), (sig_ref, sig), (heads_ref, heads_out), (qkv_ref, qkv),
            (probs_ref, probs), (inner_ref, inner), (tokens_ref, tokens),
        )
    ]
    links.barrier()
    flow = Flow([])
    rows, width = middle.shape
    half_cols = width // 2
    samples, heads, count = probs.shape[0], probs.shape[1], probs.shape[2]

    for copy in load_first:
        copy.wait()
    middle_value = middle[...]
    normed, inverse = layer_norm(middle_value)
    scale, gate = cond[0], cond[2]
    inner_mlp = (normed * scale + cond[1]).astype(LOW)
    mlp_width = hidden.shape[2]
    mlp = None
    for half in range(2):
        if half == 1:
            load_up_b.wait()
        gate_in = mul(inner_mlp, weight[half, :, :mlp_width])
        up_in = mul(inner_mlp, weight[half, :, mlp_width:])
        up[half, :, :mlp_width] = gate_in.astype(LOW)
        up[half, :, mlp_width:] = up_in.astype(LOW)
        hidden[half] = (gate_in * sigmoid(gate_in) * up_in).astype(LOW)
        load_down[half].wait()
        add = mul(hidden[half], out_weight[half])
        mlp = add if mlp is None else mlp + add
    result[...] = (middle_value + gate * mlp).astype(LOW)
    local.store(result, result_ref)
    result_copy = links.send(result, other_result_ref, links.y)
    flow.free["y"] = rows * width * 2 / Flow.RATES["y"]

    load_grad[0].wait()
    load_grad[1].wait()
    grad_value = grad[...].astype(WIDE)
    mlp_grad = (grad_value * gate).astype(LOW)
    core_rows = mlp_grads.shape[2] // 2
    down_rows = mlp_width // 2
    for half in range(2):
        hidden_t = hidden[half].T
        for core in range(2):
            for sec in range(2):
                mlp_grads[half, sec, core * core_rows : core * core_rows + down_rows, :] = mul(
                    hidden_t[core * down_rows : (core + 1) * down_rows],
                    mlp_grad[:, sec * half_cols : (sec + 1) * half_cols],
                ).astype(LOW)

    def launch(chunks):
        for i in chunks:
            flow.add(
                journey(links, mlp_grads, None, buffers, mlp_out_ref, None, i, CHUNK, i % 2 == 0, False)
            )

    launch(range(down_rows // CHUNK))
    inner_t = inner_mlp.T
    inner_grad = None
    for half in range(2):
        hidden_grad = mul_nt(mlp_grad, out_weight[half])
        gate_in = up[half, :, :mlp_width].astype(WIDE)
        up_in = up[half, :, mlp_width:].astype(WIDE)
        sigma = sigmoid(gate_in)
        first = (hidden_grad * up_in * (sigma * (1.0 + gate_in * (1.0 - sigma)))).astype(LOW)
        second = (hidden_grad * (gate_in * sigma)).astype(LOW)
        up_grad = jnp.concatenate([first, second], 1)
        for sec in range(2):
            at = slice(sec * half_cols, (sec + 1) * half_cols)
            for block in range(4):
                place = block // 2 * core_rows + down_rows + block % 2 * half_cols
                mlp_grads[half, sec, place : place + half_cols, :] = mul(
                    inner_t[at], up_grad[:, block * half_cols : (block + 1) * half_cols]
                ).astype(LOW)
        add = mul_nt(up_grad, weight[half])
        inner_grad = add if inner_grad is None else inner_grad + add
        flow.after(3.0)
    load_weight = [local.start(in_a_ref, weight.at[0]), local.start(in_b_ref, weight.at[1])]
    out_rows = out_a_ref.shape[0]
    load_out = [
        local.start(a, out_weight.at[h, :out_rows, :]) for h, a in enumerate((out_a_ref, out_b_ref))
    ]
    launch(range(down_rows // CHUNK, core_rows // CHUNK))
    middle_grad[...] = grad_value + norm_back(normed, inverse, inner_grad * scale)
    low_t = low[...].T
    first_cond = grads.shape[2] - 3 * low_t.shape[0]

    def cond_back(sec, pieces, bias_out):
        for k, piece in enumerate(pieces):
            piece = piece.astype(LOW)
            place = first_cond + k * low_t.shape[0]
            for h in range(2):
                grads[relative(h, links.mp), sec, place : place + low_t.shape[0], :] = mul(
                    low_t, piece[:, h * half_cols : (h + 1) * half_cols]
                ).astype(LOW)
            bias_out[k] = jnp.sum(piece.astype(WIDE), 0, keepdims=True)

    cond_back(
        1,
        (
            inner_grad * normed * (scale * (1.0 - scale)),
            inner_grad,
            grad_value * mlp * (gate * (1.0 - gate)),
        ),
        cond_bias_b_ref,
    )
    load_cond = local.start(cond_a_ref, cond)
    load_attn = local.start(attn_ref, middle)
    flow.after(3.0)

    local_cols = out_rows
    size = 2 * local_cols // heads
    head_scale = size ** (-0.5)
    load_cond.wait()
    for copy in load_later:
        copy.wait()
    scale, gate = cond[0], cond[2]
    attn_grad = (middle_grad[...] * gate).astype(LOW)
    inner_t = inner[...].T
    inner_grad = None
    for half in range(2):
        load_out[half].wait()
        gated_t = gated[half].T
        for sec in range(2):
            grads[half, sec, 4 * half_cols : first_cond, :] = mul(
                gated_t, attn_grad[:, sec * half_cols : (sec + 1) * half_cols]
            ).astype(LOW)
        gated_grad = mul_nt(attn_grad, out_weight[half, :out_rows, :])
        sig_half = sig[half]
        with_sig = gated_grad * sig_half
        heads_grad[...] = with_sig.astype(LOW)
        proj[:, 3 * local_cols :] = (with_sig * heads_out[half] * (1.0 - sig_half)).astype(LOW)
        flow.after(1.5)
        for s in range(samples):
            at = slice(s * count, (s + 1) * count)
            parts = ([], [], [])
            for h in range(heads // 2):
                col, index = h * size, half * (heads // 2) + h
                query = qkv[half, at, col : col + size]
                key = qkv[half, at, local_cols + col : local_cols + col + size]
                value = qkv[half, at, 2 * local_cols + col : 2 * local_cols + col + size]
                one_grad = heads_grad[at, col : col + size]
                probs_low = probs[s, index]
                wide_probs = probs_low.astype(WIDE)
                probs_grad = mul_nt(one_grad, value)
                mean = jnp.sum(wide_probs * probs_grad, -1, keepdims=True)
                scores_grad = (wide_probs * (probs_grad - mean)).astype(LOW)
                if s == 0:
                    bias_grad[index] = scores_grad.astype(WIDE)
                else:
                    bias_grad[index] += scores_grad.astype(WIDE)
                parts[0].append(mul(scores_grad, key) * head_scale)
                parts[1].append(mul_tn(scores_grad, query) * head_scale)
                parts[2].append(mul_tn(probs_low, one_grad))
                if h % 2 == 1:
                    flow.after(1.0)
            for k in range(3):
                proj[at, k * local_cols : (k + 1) * local_cols] = jnp.concatenate(
                    parts[k], 1
                ).astype(LOW)
        load_weight[half].wait()
        for sec in range(2):
            for k in range(4):
                grads[half, sec, k * half_cols : (k + 1) * half_cols, :] = mul(
                    inner_t[sec * half_cols : (sec + 1) * half_cols],
                    proj[:, k * local_cols : (k + 1) * local_cols],
                ).astype(LOW)
        local.store(grads.at[half, :, :first_cond, :], grads_ref.at[half, :, :first_cond, :])
        add = mul_nt(proj[...], weight[half])
        inner_grad = add if inner_grad is None else inner_grad + add
        flow.after(2.5)
    normed, inverse = layer_norm(tokens[...].astype(WIDE))
    tokens[...] = (middle_grad[...] + norm_back(normed, inverse, inner_grad * scale)).astype(LOW)
    local.store(tokens, token_grad_ref)
    flow.after(1.0)
    load_attn.wait()
    cond_back(
        0,
        (
            inner_grad * normed * (scale * (1.0 - scale)),
            inner_grad,
            middle_grad[...] * middle[...] * (gate * (1.0 - gate)),
        ),
        cond_bias_a_ref,
    )
    local.store(grads.at[:, :, first_cond:, :], grads_ref.at[:, :, first_cond:, :])

    slots = pair.shape[0]
    block = pair.shape[1]
    blocks = pair_ref.shape[0] // block

    def load_pair(i):
        return local.start(pair_ref.at[pl.ds(i * block, block)], pair.at[i % slots])

    loads = [load_pair(i) for i in range(slots)]
    total = jnp.zeros(pair_grad_ref.shape, WIDE)
    for i in range(blocks):
        loads[i].wait()
        for j in range(block):
            one = bias_grad[:, i * block + j, :]
            high = one.astype(LOW)
            tail = (one - high.astype(WIDE)).astype(LOW)
            both = mul(jnp.concatenate([high, tail], 0), pair[i % slots, j])
            total += both[:heads] + both[heads:]
        if i + slots < blocks:
            loads.append(load_pair(i + slots))
        flow.after(0.06 * block)
    pair_grad_ref[...] = total
    flow.finish()
    result_copy.wait()
    local.finish()


def token_back(
    middle, cond_b, cotangent, low, up_a, up_b, down_a, down_b, tokens, cond_a, attn, inner, qkv,
    sig, heads_out, gated, probs, in_a, in_b, out_a, out_b, low_pair,
):
    rows, width = tokens.shape
    heads, count = probs.shape[1], probs.shape[2]
    mlp_width, local_cols, half = down_a.shape[0], out_a.shape[0], width // 2
    mlp_rows = 4 * half + mlp_width
    grad_rows = 4 * half + local_cols + 3 * low.shape[1]
    chunks = mlp_rows // 2 // CHUNK
    copies = chunks * journey_copies(CHUNK, False) + 1
    hbm, near = pl.BlockSpec(memory_space=pl.ANY), pl.BlockSpec(memory_space=pltpu.VMEM)
    args = (
        middle, cond_b, cotangent, low, up_a, up_b, down_a, down_b, tokens, cond_a, attn, inner,
        qkv, sig, heads_out, gated, probs, in_a, in_b, out_a, out_b, low_pair,
    )
    outs = [
        (hbm, (rows, width), LOW),
        (hbm, (rows, width), LOW),
        (hbm, (rows, width), LOW),
        (hbm, (2, 2, grad_rows, half), LOW),
        (near, (3, 1, width), WIDE),
        (near, (3, 1, width), WIDE),
        (near, (heads, low_pair.shape[2]), WIDE),
        (near, (mlp_rows, half), LOW),
    ]
    scratch = [
        (middle.shape, WIDE),
        (cond_b.shape, WIDE),
        (cotangent.shape, LOW),
        (low.shape, LOW),
        ((2,) + up_a.shape, LOW),
        ((2,) + down_a.shape, LOW),
        ((2, rows, 2 * mlp_width), LOW),
        ((2, rows, mlp_width), LOW),
        ((2, 2, mlp_rows, half), LOW),
        (middle.shape, WIDE),
        ((rows, width), LOW),
        *((a.shape, a.dtype) for a in (tokens, inner, qkv, sig, heads_out, gated, probs)),
        ((2, 2, grad_rows, half), LOW),
        ((heads, count, count), WIDE),
        ((rows, 4 * local_cols), LOW),
        ((rows, local_cols), LOW),
        ((2, 8) + low_pair.shape[1:], LOW),
    ]
    return pl.pallas_call(
        token_back_kernel,
        in_specs=[hbm] * len(args),
        out_specs=[spec for spec, _, _ in outs],
        out_shape=[sds(shape, dtype) for _, shape, dtype in outs],
        scratch_shapes=[
            *(pltpu.VMEM(shape, dtype) for shape, dtype in scratch),
            *journey_scratch(chunks, CHUNK, half),
            pltpu.SemaphoreType.DMA((64,)),
            pltpu.SemaphoreType.DMA((copies,)),
            pltpu.SemaphoreType.DMA((copies,)),
        ],
        compiler_params=remote_params(62, 1),
        cost_estimate=cost(90e9, 50e6),
        name="token_back",
    )(*args)


SMALL_ROWS = 160


def atom_back_kernel(
    atoms_hbm, gain_ref, qkv_w_ref, out_w_ref, agg_w_ref, ids_ref, inv_ref,
    qkv_hbm, probs_hbm, mixed_hbm, grad_ref, pair_grad, grads_ref, cond_bias_a_ref,
    cond_bias_b_ref,
    keep_ref, got_ref, attn_out_ref, cond_out_ref, cond_other_ref,
    small_out_ref, small_other_ref,
    atoms_ref, qkv_ref, probs_ref, mixed_ref, kept_attn, kept_cond,
    after_grad, mixed_grad, key_grad, value_grad, proj_grad, atoms_grad, send_buffer,
    gain_grad, qkv_grad, out_grad, agg_grad, small, *rest,
):
    *buffers, local_sem, send_sem, recv_sem = rest
    links = Links(send_sem, recv_sem)
    local = Local(local_sem)
    samples, atoms, width = atoms_ref.shape
    groups, keys_in = probs_ref.shape[1], probs_ref.shape[2]
    queries_in = SPAN * QBLOCK
    scale = (width // ATOM_HEADS) ** (-0.5)
    cond_rows = cond_out_ref.shape[0]
    attn_rows = grads_ref.shape[2] - cond_rows
    attn_grads = grads_ref.at[:, :, :attn_rows, :]
    cond_grads = grads_ref.at[:, :, attn_rows:, :]
    loads = [local.start(mixed_hbm, mixed_ref), local.start(atoms_hbm, atoms_ref)]

    def load_kept(source, target):
        start = links.core * (source.shape[2] // 2)
        at = pl.ds(pl.multiple_of(start, 16), target.shape[2])
        return local.start(source.at[:, :, at, :], target)

    kept_loads = [load_kept(attn_grads, kept_attn), load_kept(cond_grads, kept_cond)]
    later = [
        (local.start(qkv_hbm.at[s], qkv_ref.at[s]), local.start(probs_hbm.at[s], probs_ref.at[s]))
        for s in range(samples)
    ]
    links.barrier()
    number = len(buffers) // 3
    first, second, third = (buffers[i * number : (i + 1) * number] for i in range(3))
    flow = Flow(
        journey(links, attn_grads, kept_attn, first, attn_out_ref, None, i, CHUNK, i % 2 == 1, False)
        for i in range(attn_rows // 2 // CHUNK)
    )
    for i in range(cond_rows // 2 // CHUNK):
        flow.add(
            journey(
                links, cond_grads, kept_cond, second, cond_out_ref, cond_other_ref, i, CHUNK, True, True
            )
        )
    for copy in kept_loads + loads:
        copy.wait()

    for ref in (gain_grad, qkv_grad, out_grad, agg_grad):
        ref[...] = jnp.zeros_like(ref)
    chunk = 256
    token_ids = lax.broadcasted_iota(jnp.int32, (chunk, grad_ref.shape[1]), 1)
    atom_copies = []
    for s in range(samples):
        token_grad = (grad_ref[s].astype(WIDE) * inv_ref[...]).astype(LOW)
        for i in range(atoms // chunk):
            rows = slice(i * chunk, (i + 1) * chunk)
            mixed = mixed_ref[s, rows, :]
            after = atoms_ref[s, rows, :].astype(WIDE) + mul(mixed, out_w_ref[...])
            after_low = after.astype(LOW)
            pre = mul(after_low, agg_w_ref[...])
            sigma = sigmoid(pre)
            member = jnp.where(token_ids == ids_ref[rows, :], 1.0, 0.0).astype(LOW)
            unit_grad = mul(member, token_grad)
            pre_grad = (unit_grad * (sigma * (1.0 + pre * (1.0 - sigma)))).astype(LOW)
            agg_grad[...] += mul_tn(after_low, pre_grad)
            after_back = mul_nt(pre_grad, agg_w_ref[...])
            after_grad[rows, :] = after_back
            branch = after_back.astype(LOW)
            out_grad[...] += mul_tn(mixed, branch)
            mixed_grad[rows, :] = mul_nt(branch, out_w_ref[...]).astype(LOW)
            flow.after(1.2)
        for copy in later[s]:
            copy.wait()
        key_grad[...] = jnp.zeros_like(key_grad)
        value_grad[...] = jnp.zeros_like(value_grad)

        def attend(group, carry, s=s):
            base = key_base(group, atoms)
            start = pl.multiple_of(group * queries_in, queries_in)
            queries = spread(qkv_ref[s, pl.ds(start, queries_in), :width], ATOM_HEADS)
            grads = spread(mixed_grad[pl.ds(start, queries_in), :], ATOM_HEADS)
            keys = qkv_ref[s, pl.ds(base, keys_in), width : 2 * width]
            values = qkv_ref[s, pl.ds(base, keys_in), 2 * width :]
            probs_low = probs_ref[s, group]
            probs = probs_low.astype(WIDE)
            probs_grad = mul_nt(values, grads)
            mean = jnp.sum(probs * probs_grad, 0, keepdims=True)
            scores_grad = (probs * (probs_grad - mean)).astype(LOW)
            query_grad = gather_heads(mul_tn(scores_grad, keys), ATOM_HEADS)
            proj_grad[pl.ds(start, queries_in), :width] = (query_grad * scale).astype(LOW)
            key_grad[pl.ds(base, keys_in), :] += mul(scores_grad, queries)
            value_grad[pl.ds(base, keys_in), :] += mul(probs_low, grads)
            return carry

        cuts = 5
        for i in range(cuts):
            lax.fori_loop(groups * i // cuts, groups * (i + 1) // cuts, attend, 0)
            flow.after(2.0)
        proj_grad[:, width : 2 * width] = (key_grad[...] * scale).astype(LOW)
        proj_grad[:, 2 * width :] = value_grad[...].astype(LOW)
        gain = gain_ref[...].astype(WIDE)
        normed, inverse = layer_norm(atoms_ref[s].astype(WIDE))
        hidden = (normed * gain).astype(LOW)
        proj = proj_grad[...]
        qkv_grad[...] += mul_tn(hidden, proj)
        hidden_grad = mul_nt(proj, qkv_w_ref[...])
        gain_grad[...] += jnp.sum(hidden_grad * normed, 0, keepdims=True)
        atoms_grad[...] = after_grad[...] + norm_back(normed, inverse, hidden_grad * gain)
        half = atoms // 2
        theirs = pl.ds(pl.multiple_of((1 - links.mp) * half, 16), half)
        send_buffer[s] = atoms_grad[theirs, :].astype(LOW)
        atom_copies.append(links.send(send_buffer.at[s], got_ref.at[s], links.y))
        keep_ref[s] = atoms_grad[pl.ds(pl.multiple_of(links.mp * half, 16), half), :]
        flow.after(1.5)

    heads = pair_grad.shape[0]
    wide = agg_grad.shape[1] // 2
    rows, part_rows = width // 2, width // 4

    def fill(values, cols):
        if values.shape[1] == cols:
            return values
        empty = jnp.zeros((values.shape[0], cols - values.shape[1]), WIDE)
        return jnp.concatenate([values, empty], 1)

    for h in range(2):
        to = relative(h, links.mp)
        cols = slice(h * wide, (h + 1) * wide)
        own_pair = jnp.where(links.mp == h, pair_grad[: heads // 2], pair_grad[heads // 2 :])
        for sec, cond_bias_ref in enumerate((cond_bias_a_ref, cond_bias_b_ref)):
            at = slice(sec * rows, (sec + 1) * rows)
            small[to, sec, :rows, :] = agg_grad[at, cols].astype(LOW)
            first_row = sec * rows + h * part_rows
            part_at = slice(first_row, first_row + part_rows)
            small[to, sec, rows : rows + part_rows, :] = fill(qkv_grad[part_at], wide).astype(LOW)
            small[to, sec, rows + part_rows : 2 * rows, :] = fill(out_grad[part_at], wide).astype(LOW)
            block = [fill(gain_grad[...], wide)]
            block += [cond_bias_ref[k, :, cols] for k in range(3)]
            block += [jnp.zeros((4, wide), WIDE), fill(own_pair, wide)]
            block += [jnp.zeros((16, wide), WIDE)]
            small[to, sec, 2 * rows :, :] = jnp.concatenate(block, 0).astype(LOW)
    flow.add(
        journey(
            links, small, None, third, small_out_ref, small_other_ref, 0, SMALL_ROWS // 2, False, True
        )
    )
    flow.finish()
    for copy in atom_copies:
        copy.wait()


def atom_back(
    atoms, gain, qkv_w, out_w, agg_w, ids, inverse_counts, qkv, probs, mixed, grad,
    pair_grad, grads, cond_bias_a, cond_bias_b, cond_rows,
):
    samples, count, width = atoms.shape
    wide = agg_w.shape[1]
    cols = grads.shape[3]
    attn_rows = grads.shape[2] - cond_rows
    attn_chunks, cond_chunks = attn_rows // 2 // CHUNK, cond_rows // 2 // CHUNK
    copies = attn_chunks * journey_copies(CHUNK, False) + cond_chunks * journey_copies(CHUNK, True)
    copies += journey_copies(SMALL_ROWS // 2, True) + samples
    outs = [
        sds((samples, count // 2, width), WIDE),
        sds((samples, count // 2, width), LOW),
        sds((attn_rows, cols), LOW),
        sds((cond_rows, cols), LOW),
        sds((cond_rows, cols), LOW),
        sds((SMALL_ROWS, cols), LOW),
        sds((SMALL_ROWS, cols), LOW),
    ]
    args = (
        atoms, gain, qkv_w, out_w, agg_w, ids, inverse_counts, qkv, probs, mixed, grad,
        pair_grad, grads, cond_bias_a, cond_bias_b,
    )
    hbm, near = pl.BlockSpec(memory_space=pl.ANY), pl.BlockSpec(memory_space=pltpu.VMEM)
    return pl.pallas_call(
        atom_back_kernel,
        in_specs=[hbm] + [near] * 6 + [hbm] * 3 + [near] * 2 + [hbm] + [near] * 2,
        out_specs=everywhere(len(outs)),
        out_shape=outs,
        scratch_shapes=[
            *(pltpu.VMEM(a.shape, a.dtype) for a in (atoms, qkv, probs, mixed)),
            pltpu.VMEM((2, 2, attn_rows // 2, cols), LOW),
            pltpu.VMEM((2, 2, cond_rows // 2, cols), LOW),
            pltpu.VMEM((count, width), WIDE),
            pltpu.VMEM((count, width), LOW),
            pltpu.VMEM((count, width), WIDE),
            pltpu.VMEM((count, width), WIDE),
            pltpu.VMEM((count, 3 * width), LOW),
            pltpu.VMEM((count, width), WIDE),
            pltpu.VMEM((samples, count // 2, width), LOW),
            pltpu.VMEM((1, width), WIDE),
            pltpu.VMEM((width, 3 * width), WIDE),
            pltpu.VMEM((width, width), WIDE),
            pltpu.VMEM((width, wide), WIDE),
            pltpu.VMEM((2, 2, SMALL_ROWS, cols), LOW),
            *journey_scratch(attn_chunks, CHUNK, cols),
            *journey_scratch(cond_chunks, CHUNK, cols),
            *journey_scratch(1, SMALL_ROWS // 2, cols),
            pltpu.SemaphoreType.DMA((16,)),
            pltpu.SemaphoreType.DMA((copies,)),
            pltpu.SemaphoreType.DMA((copies,)),
        ],
        compiler_params=remote_params(60, 2),
        cost_estimate=cost(60e9, 24e6),
        name="atom_back",
    )(*args)


def swap(array, axis, bit=0):
    size = lax.axis_size(axis)
    return lax.ppermute(array, axis, [(i, i ^ (1 << bit)) for i in range(size)])


def side(axis, bit=0):
    return (lax.axis_index(axis) >> bit) & 1


def local(
    atoms_in,
    atom_token,
    window_start,
    noise_level,
    level_table,
    single_trunk,
    pair,
    atom_gain,
    atom_qkv,
    atom_out,
    atom_agg,
    cond_weight,
    cond_bias,
    pair_weight,
    attn_in,
    attn_out,
    mlp_up,
    mlp_down,
    cotangent,
):
    section, mp = lax.axis_index("section"), lax.axis_index("mp")
    batch, half_atoms, atom_width = atoms_in.shape
    batch //= MICRO
    samples = batch // 2
    atoms = 2 * half_atoms
    tokens, width = cotangent.shape[1], cotangent.shape[2]
    single = single_trunk.shape[1]
    own_first = section * batch + mp * samples

    in_a = attn_in.reshape(width, -1)
    up_a = mlp_up.reshape(width, -1)
    levels = lax.dynamic_slice_in_dim(noise_level, own_first, samples, 0)
    grad_out = lax.dynamic_slice_in_dim(cotangent, own_first, samples, 0).reshape(-1, width)

    token_ids = jnp.arange(tokens, dtype=jnp.int32)
    counts = jnp.sum((atom_token[:, None] == token_ids[None, :]).astype(WIDE), 0)
    inverse_counts = (1.0 / counts)[:, None]
    level_pick = (levels[:, None] == jnp.arange(level_table.shape[0], dtype=jnp.int32)[None, :])
    level_rows = jnp.sum(
        jnp.where(level_pick[:, :, None], level_table.astype(WIDE)[None], 0.0), 1, keepdims=True
    )
    groups = window_start.shape[0] // SPAN
    own_groups = mp * groups + jnp.arange(groups, dtype=jnp.int32)
    base = jnp.clip(
        own_groups * (SPAN * QBLOCK) - KWIN // 2, 0, atoms - KWIN - SPAN * QBLOCK
    )
    rel = window_start.reshape(groups, SPAN) - base[:, None]
    rel = jnp.broadcast_to(rel[:, None, None, :, None], (groups, 1, ATOM_HEADS, SPAN, QBLOCK))
    rel = rel.reshape(groups, 1, ATOM_HEADS * SPAN * QBLOCK)
    gain = atom_gain[None, :]
    qkv_w = atom_qkv.reshape(atom_width, -1)

    cond_w = jnp.transpose(cond_weight, (0, 2, 1, 3)).reshape(6, single, width)
    (
        low, cond_a, cond_b, low_pair, bias, all_atoms, qkv, probs, mixed, token_in,
        in_b, out_b, up_b,
    ) = front(
        single_trunk, level_rows, cond_w, cond_bias.reshape(6, 1, width), pair, pair_weight.T,
        atoms_in, gain, qkv_w, atom_out, atom_agg, rel, atom_token[None, :], inverse_counts,
        in_a, attn_out, up_a,
    )
    token_in = token_in.reshape(-1, width)
    inner, token_qkv, sig, heads_out, gated, token_probs, attn, middle, down_b = token_attention(
        token_in, cond_a, bias, in_a, in_b, attn_out, out_b, mlp_down
    )
    result, other_result, token_grad, attn_grads, cond_bias_a, cond_bias_b, pair_grad, mlp_sum = (
        token_back(
            middle, cond_b, grad_out, low, up_a, up_b, mlp_down, down_b, token_in, cond_a, attn,
            inner, token_qkv, sig, heads_out, gated, token_probs, in_a, in_b, attn_out, out_b,
            low_pair,
        )
    )
    keep, got, attn_sum, cond_sum, cond_other, small, small_other = atom_back(
        all_atoms, gain, qkv_w, atom_out, atom_agg, atom_token[:, None], inverse_counts,
        qkv, probs, mixed, token_grad.reshape(samples, tokens, width),
        pair_grad, attn_grads, cond_bias_a, cond_bias_b, 3 * single,
    )

    result = result.reshape(samples, tokens, width)
    other_result = other_result.reshape(samples, tokens, width)
    token_out = jnp.concatenate(
        [jnp.where(mp == 0, result, other_result), jnp.where(mp == 0, other_result, result)]
    )
    got = got.astype(WIDE)
    atoms_out = jnp.concatenate([jnp.where(mp == 0, keep, got), jnp.where(mp == 0, got, keep)])
    half = width // 2
    attn_local, mlp_local = attn_in.shape[2], mlp_up.shape[2]
    in_sum = jnp.transpose(attn_sum[: 4 * half].reshape(4, half, attn_local), (1, 0, 2))
    mlp_sum = mlp_sum.reshape(2, -1, half)
    down_rows = mlp_local // 2
    up_sum = jnp.transpose(mlp_sum[:, down_rows:].reshape(2, 2, half, half), (2, 0, 1, 3)).reshape(
        half, 2, mlp_local
    )
    down_sum = mlp_sum[:, :down_rows].reshape(mlp_local, half)
    small, small_other = small.astype(WIDE), small_other.astype(WIDE)
    small_pair = (
        jnp.where(mp == 0, small, small_other),
        jnp.where(mp == 0, small_other, small),
    )
    rows, part_rows = atom_width // 2, atom_width // 4
    lanes = lax.dynamic_slice_in_dim(small[2 * rows :, :atom_width], section * rows, rows, 1)
    cond_pair = [
        jnp.where(mp == 0, cond_sum, cond_other).reshape(3, single, half),
        jnp.where(mp == 0, cond_other, cond_sum).reshape(3, single, half),
    ]
    cond_total = jnp.transpose(jnp.concatenate(cond_pair, 2), (1, 0, 2))
    return (
        token_out.reshape(1, 1, batch, tokens, width),
        atoms_out.reshape(1, 1, batch, half_atoms, atom_width),
        lanes[0],
        jnp.concatenate([a[rows : rows + part_rows] for a in small_pair], 0).reshape(
            rows, 3, atom_width
        ),
        jnp.concatenate([a[rows + part_rows : 2 * rows, :atom_width] for a in small_pair], 0),
        jnp.concatenate([a[:rows] for a in small_pair], 1),
        cond_total[None].astype(WIDE),
        jnp.concatenate([a[2 * rows + 1 : 2 * rows + 4] for a in small_pair], 1)[None],
        lanes[8:16].T,
        in_sum.astype(WIDE),
        attn_sum[4 * half :].astype(WIDE),
        up_sum.astype(WIDE),
        down_sum.astype(WIDE),
    )


def solution(mesh):
    in_specs = (
        P("dp", "mp", None),
        P(),
        P("mp"),
        P("dp"),
        P(),
        P(),
        P(),
        P(),
        P(),
        P(),
        P(),
        P(),
        P(),
        P(None, "mp"),
        P(None, None, "mp"),
        P("mp", None),
        P(None, None, "mp"),
        P("mp", None),
        P("dp", None, None),
    )
    out_specs = (
        P("dp", "section", None, None, None),
        P("dp", "section", None, "mp", None),
        P("section"),
        P("section", None, None),
        P("section", None),
        P("section", None),
        P("section", None, None, None),
        P("section", None, None),
        P("section", "mp"),
        P("section", None, "mp"),
        P("mp", "section"),
        P("section", None, "mp"),
        P("mp", "section"),
    )
    return jax.shard_map(local, mesh=mesh, in_specs=in_specs, out_specs=out_specs, check_vma=False)
```

```python
import functools

import jax
import jax.numpy as jnp
from jax import lax
from jax.experimental import pallas as pl
from jax.experimental.pallas import tpu as pltpu
from jax.sharding import PartitionSpec as P

QBLOCK = 32
KWIN = 128
MICRO = 2
ATOM_HEADS = 4
SPAN = 2
EPS = 1e-05
LOW = jnp.bfloat16
WIDE = jnp.float32
MIB = 1 << 20


def mul(left, right):
    return lax.dot_general(left, right, (((1,), (0,)), ((), ())), preferred_element_type=WIDE)


def mul_nt(left, right):
    return lax.dot_general(left, right, (((1,), (1,)), ((), ())), preferred_element_type=WIDE)


def mul_tn(left, right):
    return lax.dot_general(left, right, (((0,), (0,)), ((), ())), preferred_element_type=WIDE)


def layer_norm(values):
    center = values - jnp.mean(values, -1, keepdims=True)
    inverse = lax.rsqrt(jnp.mean(center * center, -1, keepdims=True) + EPS)
    return center * inverse, inverse


def norm_back(normed, inverse, grad):
    return inverse * (
        grad
        - jnp.mean(grad, -1, keepdims=True)
        - normed * jnp.mean(grad * normed, -1, keepdims=True)
    )


def sigmoid(values):
    return 1.0 / (1.0 + jnp.exp(-values))


def params(mib, semantics=None):
    return pltpu.CompilerParams(vmem_limit_bytes=mib * MIB, dimension_semantics=semantics)


def cost(flops, moved, exps=0):
    return pl.CostEstimate(flops=int(flops), bytes_accessed=int(moved), transcendentals=int(exps))


def sds(shape, dtype):
    return jax.ShapeDtypeStruct(shape, dtype)


def lane_heads(rows, width, size):
    return lax.broadcasted_iota(jnp.int32, (rows, width), 1) // size


def spread(values, heads):
    head = lane_heads(values.shape[0], values.shape[1], values.shape[1] // heads)
    zero = jnp.zeros_like(values)
    return jnp.concatenate([jnp.where(head == h, values, zero) for h in range(heads)], 0)


def gather_heads(values, heads):
    rows = values.shape[0] // heads
    head = lane_heads(rows, values.shape[1], values.shape[1] // heads)
    total = jnp.where(head == 0, values[:rows], 0.0)
    for h in range(1, heads):
        total += jnp.where(head == h, values[h * rows : (h + 1) * rows], 0.0)
    return total


def key_base(group, atoms):
    start = group * SPAN * QBLOCK - KWIN // 2
    return pl.multiple_of(jnp.clip(start, 0, atoms - KWIN - (SPAN - 1) * QBLOCK - QBLOCK), QBLOCK)


def far_lines():
    bits = lax.axis_size("dp").bit_length() - 2
    return [(1 + b, 4 if b + 1 < bits else 2) for b in range(0, bits, 2)]


class Links:
    def __init__(self, send_sem, recv_sem, far=True):
        self.section, self.mp = lax.axis_index("section"), lax.axis_index("mp")
        self.dp = lax.axis_index("dp")
        self.core = self.dp % 2
        self.partners = [{"section": 1 - self.section}, {"mp": 1 - self.mp}]
        self.partners.append({"dp": self.dp + 1 - 2 * self.core})
        self.x, self.y, self.twin = self.partners
        self.lines = []
        for bit, count in far_lines() if far else ():
            place = self.dp // (1 << bit) % count
            beside = {"dp": self.dp + (1 - 2 * (place % 2)) * (1 << bit)}
            across = {"dp": self.dp + (count - 1 - 2 * place) * (1 << bit)}
            self.lines.append((count, place, beside, across))
            self.partners += [beside, across] if count == 4 else [beside]
        self.send_sem, self.recv_sem, self.used = send_sem, recv_sem, 0

    def barrier(self):
        barrier = pltpu.get_barrier_semaphore()
        for partner in self.partners:
            pl.semaphore_signal(
                barrier, inc=1, device_id=partner, device_id_type=pl.DeviceIdType.MESH
            )
        pl.semaphore_wait(barrier, len(self.partners))

    def copy(self, source, target, partner):
        copy = pltpu.make_async_remote_copy(
            src_ref=source,
            dst_ref=target,
            send_sem=self.send_sem.at[self.used],
            recv_sem=self.recv_sem.at[self.used],
            device_id=partner,
            device_id_type=pl.DeviceIdType.MESH,
        )
        self.used += 1
        return copy

    def send(self, source, target, partner):
        copy = self.copy(source, target, partner)
        copy.start()
        return copy


def far_copies():
    return sum(3 if count == 4 else 1 for _, count in far_lines())


def journey_copies(shared, near=3):
    return near + far_copies() + 1 + (2 if shared else 0)


def far_slots():
    return sum(count // 2 for _, count in far_lines())


def far_scratch(rows, cols):
    return [pltpu.VMEM((rows, cols), LOW)] * far_slots()


def near_scratch(rows, cols):
    return [pltpu.VMEM(shape + (rows, cols), LOW) for shape in ((2, 2), (2,), ())]


def journey_scratch(rows, cols):
    return near_scratch(rows, cols) + far_scratch(rows, cols)


class Pool:
    def __init__(self, buffers):
        self.buffers, self.used = buffers, 0

    def take(self, count):
        self.used += count
        return self.buffers[self.used - count : self.used]


def offsets(sizes):
    return [sum(sizes[:i]) for i in range(len(sizes))]


def journey(links, grads, kept, buffers, out, other_out, offset, rows, x_first, shared, part=None):
    near, middle, last, *far = buffers
    total_rows = grads.shape[2]
    start = links.core * (total_rows // 2) + offset
    twin_start = (1 - links.core) * (total_rows // 2) + offset
    mine, theirs = pl.ds(pl.multiple_of(start, 16), rows), pl.ds(pl.multiple_of(twin_start, 16), rows)
    me, you = links.section, 1 - links.section
    if kept is None:
        own = grads.at[:, :, mine, :]
    else:
        own = kept.at[:, :, pl.ds(offset, rows), :]
    block = rows * grads.shape[3] * 2
    copy = links.send(grads.at[:, :, theirs, :], near, links.twin)
    yield [("core", 4 * block)]
    copy.wait()
    if x_first:
        near[:, you] += own[:, you]
        copy = links.send(near.at[:, you], middle, links.x)
        near[:, me] += own[:, me]
        yield [("x", 2 * block)]
        copy.wait()
        middle[1] += near[1, me]
        copy = links.send(middle.at[1], last, links.y)
        middle[0] += near[0, me]
        yield [("y", block)]
        copy.wait()
        last[...] += middle[0]
    else:
        near[1] += own[1]
        copy = links.send(near.at[1], middle, links.y)
        near[0] += own[0]
        yield [("y", 2 * block)]
        copy.wait()
        middle[you] += near[0, you]
        copy = links.send(middle.at[you], last, links.x)
        middle[me] += near[0, me]
        yield [("x", block)]
        copy.wait()
        last[...] += middle[me]
    if part is not None:
        part[...] = last[...]
        return
    yield from far_journey(links, last, far, out, other_out, offset, shared)


def far_journey(links, held, far, out, other_out, offset, shared):
    rows = held.shape[0]
    start = links.core * (out.shape[0] // 2) + offset
    mine = pl.ds(pl.multiple_of(start, 16), rows)
    block = rows * held.shape[1] * 2
    far = list(far)
    for count, place, beside, across in links.lines:
        if count == 2:
            slot = far.pop(0)
            copy = links.send(held, slot, beside)
            yield [("z", block)]
            copy.wait()
            held[...] += slot[...]
            continue
        inner = (place == 1) | (place == 2)
        outer = (place == 0) | (place == 3)
        slot, second = far.pop(0), far.pop(0)
        gather = links.copy(held, slot, beside)
        exchange = links.copy(held, second, across)
        spread_back = links.copy(held, slot, beside)

        @pl.when(outer)
        def _():
            gather.start()

        yield [("z", block)]

        @pl.when(outer)
        def _():
            gather.wait_send()

        @pl.when(inner)
        def _():
            gather.wait_recv()
            held[...] += slot[...]
            exchange.start()

        yield [("mid", block)]

        @pl.when(inner)
        def _():
            exchange.wait()
            held[...] += second[...]
            spread_back.start()

        yield [("back", block)]

        @pl.when(inner)
        def _():
            spread_back.wait_send()

        @pl.when(outer)
        def _():
            spread_back.wait_recv()
            held[...] = slot[...]

    out[mine, :] = held[...]
    copies = [links.send(out.at[mine, :], out.at[mine, :], links.twin)]
    if shared:
        across = links.send(out.at[mine, :], other_out.at[mine, :], links.y)
        yield [("y", block)]
        across.wait()
        copies.append(links.send(other_out.at[mine, :], other_out.at[mine, :], links.twin))
    yield [("core", block)]
    for copy in copies:
        copy.wait()


class Flow:
    RATES = {"core": 400e3, "x": 43e3, "y": 43e3, "z": 43e3, "mid": 43e3, "back": 43e3}
    DELAYS = {"core": 0.4}

    def __init__(self, journeys):
        self.clock, self.free, self.queue, self.count = 0.0, {}, [], 0
        for one in journeys:
            self.add(one)

    def add(self, one):
        copies = next(one, None)
        if copies is None:
            return
        ready = self.clock
        for link, count in copies:
            finish = max(self.clock, self.free.get(link, 0.0)) + count / self.RATES[link]
            self.free[link] = finish
            ready = max(ready, finish + self.DELAYS.get(link, 1.5))
        self.queue.append((ready, self.count, one))
        self.queue.sort(key=lambda entry: entry[:2])
        self.count += 1

    def after(self, duration):
        self.clock += duration
        while self.queue and self.queue[0][0] <= self.clock:
            self.add(self.queue.pop(0)[2])

    def finish(self):
        while self.queue:
            self.clock = max(self.clock, self.queue[0][0])
            self.add(self.queue.pop(0)[2])


def everywhere(count):
    return [pl.BlockSpec(memory_space=pltpu.VMEM)] * count


def remote_params(mib, number):
    return pltpu.CompilerParams(
        vmem_limit_bytes=mib * MIB, collective_id=number, has_side_effects=True
    )


class Local:
    def __init__(self, sem):
        self.sem, self.used, self.open = sem, 0, []

    def start(self, source, target):
        copy = pltpu.make_async_copy(source, target, self.sem.at[self.used])
        self.used += 1
        copy.start()
        return copy

    def store(self, source, target):
        self.open.append(self.start(source, target))

    def finish(self):
        for copy in self.open:
            copy.wait()


def fetch_journey(links, own, other, chunk, rows):
    quarter = own.shape[0] // 4
    block = rows * own.shape[1] * 2

    def at(core, section):
        start = (2 * core + section) * quarter + chunk * rows
        return pl.ds(pl.multiple_of(start, 16), rows)

    mine = at(links.core, links.section)
    across = at(links.core, 1 - links.section)
    copy = links.send(own.at[mine, :], other.at[mine, :], links.y)
    yield [("y", block)]
    copy.wait()
    first = links.send(other.at[mine, :], other.at[mine, :], links.x)
    second = links.send(other.at[mine, :], other.at[mine, :], links.twin)
    yield [("x", block), ("core", block)]
    first.wait()
    third = links.send(other.at[across, :], other.at[across, :], links.twin)
    yield [("core", block)]
    second.wait()
    third.wait()


def front_kernel(
    trunk_ref, noise_ref, level_ref, cond_w_ref, cond_b_ref, pair_ref, pair_w_ref, atoms_ref,
    gain_ref, qkv_w_ref, out_w_ref, agg_w_ref, start_ref, ids_ref, in_a_ref, out_a_ref, up_a_ref,
    low_ref, cond_a_ref, cond_b_out_ref, low_pair_ref, bias_ref, atoms_out_ref, qkv_ref, probs_ref,
    mixed_ref, tokens_ref, in_b_ref, out_b_ref, up_b_ref, inv_ref,
    cond_w, cond_out, pair, pair_w, bias, atoms, rel_own, rel, qkv, probs, mixed, total, tokens,
    local_sem, send_sem, recv_sem,
):
    links = Links(send_sem, recv_sem, far=False)
    local = Local(local_sem)
    samples, count, width = atoms.shape
    half_atoms = count // 2
    batch = atoms_ref.shape[0] // MICRO
    parts = cond_w.shape[0]
    loads = [local.start(cond_w_ref.at[i], cond_w.at[i]) for i in range(parts)]
    pieces = 2
    pair_rows_in = pair.shape[0]
    each = pair_rows_in // pieces
    pair_first = links.core * pair_rows_in
    pair_loads = [
        local.start(
            pair_ref.at[pl.ds(pair_first + i * each, each)], pair.at[pl.ds(i * each, each)]
        )
        for i in range(pieces)
    ]
    own_first = links.section * batch + links.mp * samples
    other_first = links.section * batch + (1 - links.mp) * samples
    own_half = pl.ds(pl.multiple_of(links.mp * half_atoms, 16), half_atoms)
    groups_in = rel_own.shape[0]
    own_groups = pl.ds(links.mp * groups_in, groups_in)
    lane = lax.broadcasted_iota(jnp.int32, rel_own.shape[1:], 1) % (SPAN * QBLOCK)
    for i in range(groups_in):
        starts = jnp.where(lane < QBLOCK, start_ref[SPAN * i], start_ref[SPAN * i + 1])
        rel_own[i] = starts - key_base(links.mp * groups_in + i, count)
    heads = pair_w_ref.shape[0]
    atom_loads = [
        local.start(atoms_ref.at[pl.ds(own_first, samples)], atoms.at[:, own_half, :]),
        local.start(rel_own, rel.at[own_groups]),
        local.start(pair_w_ref, pair_w.at[0]),
    ]
    links.barrier()
    pair_w_copy = links.send(pair_w_ref, pair_w.at[1], links.y)
    rel_copy = links.send(rel_own, rel.at[own_groups], links.y)
    atom_copy = links.send(
        atoms_ref.at[pl.ds(other_first, samples)], atoms.at[:, own_half, :], links.y
    )
    flow = Flow([])
    flow.free["y"] = samples * half_atoms * width * 2 / Flow.RATES["y"]
    for own, other, chunks in (
        (in_a_ref, in_b_ref, 4),
        (out_a_ref, out_b_ref, 1),
        (up_a_ref, up_b_ref, 4),
    ):
        rows = own.shape[0] // 4 // chunks
        for i in range(chunks):
            flow.add(fetch_journey(links, own, other, i, rows))

    trunk = trunk_ref[...].astype(WIDE)
    rows = trunk.shape[0]
    for s in range(samples):
        level_rows = lax.broadcasted_iota(jnp.int32, level_ref.shape, 0)
        level = jnp.where(level_rows == noise_ref[own_first + s], level_ref[...].astype(WIDE), 0.0)
        normed, _ = layer_norm(trunk + jnp.sum(level, 0, keepdims=True))
        low_ref[s * rows : (s + 1) * rows, :] = normed.astype(LOW)
    for i in range(parts):
        loads[i].wait()
        value = mul(low_ref[...], cond_w[i]) + cond_b_ref[i // 3, i % 3 : i % 3 + 1, :].astype(WIDE)
        cond_out[i] = value if i % 3 == 1 else sigmoid(value)
        target = (cond_a_ref, cond_b_out_ref)[i // 3]
        local.store(cond_out.at[i], target.at[i % 3])
    flow.after(5.0)

    atom_loads[2].wait()
    pair_w_copy.wait()
    weight = jnp.concatenate([pair_w[0], pair_w[1]], 0)
    block = 8
    for piece in range(pieces):
        pair_loads[piece].wait()

        def pair_rows(i, carry):
            at = pl.multiple_of(i * block, block)
            normed, _ = layer_norm(pair[pl.ds(at, block)].astype(WIDE))
            low = normed.astype(LOW)
            pair[pl.ds(at, block)] = low
            for j in range(block):
                bias[:, pl.ds(pair_first + at + j, 1), :] = mul_nt(weight, low[j])[:, None, :]
            return carry

        lax.fori_loop(piece * each // block, (piece + 1) * each // block, pair_rows, 0)
        at = pl.ds(piece * each, each)
        local.store(pair.at[at], low_pair_ref.at[at])
        flow.after(3.6)
    own_rows = pl.ds(pl.multiple_of(pair_first, 8), pair_rows_in)
    bias_copy = links.send(bias.at[:, own_rows, :], bias.at[:, own_rows, :], links.twin)

    for copy in (atom_loads[0], atom_loads[1], rel_copy, atom_copy):
        copy.wait()
    local.store(atoms, atoms_out_ref)
    bias_copy.wait()
    local.store(bias, bias_ref)
    groups, keys_in = probs.shape[1], probs.shape[2]
    queries_in = SPAN * QBLOCK
    scale = (width // ATOM_HEADS) ** (-0.5)
    place = lax.broadcasted_iota(jnp.int32, (keys_in, ATOM_HEADS * queries_in), 0)
    chunk = 256
    ids = lax.broadcasted_iota(jnp.int32, (total.shape[0], chunk), 0)
    for s in range(samples):
        normed, _ = layer_norm(atoms[s].astype(WIDE))
        hidden = (normed * gain_ref[...].astype(WIDE)).astype(LOW)
        qkv[s] = mul(hidden, qkv_w_ref[...]).astype(LOW)
        local.store(qkv.at[s], qkv_ref.at[s])
        flow.after(1.7)

        def attend(group, carry, s=s):
            base = key_base(group, count)
            first = pl.multiple_of(group * queries_in, queries_in)
            queries = spread(qkv[s, pl.ds(first, queries_in), :width], ATOM_HEADS)
            keys = qkv[s, pl.ds(base, keys_in), width : 2 * width]
            values = qkv[s, pl.ds(base, keys_in), 2 * width :]
            offset = place - rel[group]
            scores = mul_nt(keys, queries) * scale
            scores = jnp.where((offset >= 0) & (offset < KWIN), scores, -1e30)
            exps = jnp.exp(scores - jnp.max(scores, 0, keepdims=True))
            low = (exps * (1.0 / jnp.sum(exps, 0, keepdims=True))).astype(LOW)
            probs[s, group] = low
            mixed[s, pl.ds(first, queries_in), :] = gather_heads(
                mul_tn(low, values), ATOM_HEADS
            ).astype(LOW)
            return carry

        cuts = 4
        for i in range(cuts):
            lax.fori_loop(groups * i // cuts, groups * (i + 1) // cuts, attend, 0)
            flow.after(2.5)
        local.store(probs.at[s], probs_ref.at[s])
        local.store(mixed.at[s], mixed_ref.at[s])
        for i in range(count // chunk):
            rows = slice(i * chunk, (i + 1) * chunk)
            after = atoms[s, rows, :].astype(WIDE) + mul(mixed[s, rows, :], out_w_ref[...])
            pre = mul(after.astype(LOW), agg_w_ref[...])
            units = (pre * sigmoid(pre)).astype(LOW)
            member = jnp.where(ids == ids_ref[:, rows], 1.0, 0.0).astype(LOW)
            part_sum = mul(member, units)
            if i == 0:
                total[...] = part_sum
            else:
                total[...] += part_sum
            if s == 0:
                number = jnp.sum(member.astype(WIDE), 1, keepdims=True)
                counts = number if i == 0 else counts + number
            flow.after(1.2)
        if s == 0:
            inv_ref[...] = 1.0 / counts
        tokens[s] = (total[...] * inv_ref[...]).astype(LOW)
        local.store(tokens.at[s], tokens_ref.at[s])
    flow.finish()
    local.finish()


def front(
    trunk, noise, levels, cond_w, cond_b, pair, pair_w, atoms, gain, qkv_w, out_w, agg_w, starts,
    ids, in_a, out_a, up_a,
):
    tokens_in, width = trunk.shape
    parts, wide = cond_w.shape[0], cond_w.shape[2]
    samples = atoms.shape[0] // MICRO // 2
    rows = samples * tokens_in
    count, atom_width = 2 * atoms.shape[1], atoms.shape[2]
    heads = 2 * pair_w.shape[0]
    groups = count // (SPAN * QBLOCK)
    keys_in, lanes = KWIN + SPAN * QBLOCK, ATOM_HEADS * SPAN * QBLOCK
    probs_shape = (samples, groups, keys_in, lanes)
    half_pair = (pair.shape[0] // 2,) + pair.shape[1:]
    hbm, near = pl.BlockSpec(memory_space=pl.ANY), pl.BlockSpec(memory_space=pltpu.VMEM)
    smem = pl.BlockSpec(memory_space=pltpu.SMEM)
    outs = [
        (near, (rows, width), LOW),
        (hbm, (parts // 2, rows, wide), WIDE),
        (hbm, (parts // 2, rows, wide), WIDE),
        (hbm, half_pair, LOW),
        (hbm, (heads, tokens_in, tokens_in), WIDE),
        (hbm, (samples, count, atom_width), LOW),
        (hbm, (samples, count, 3 * atom_width), LOW),
        (hbm, probs_shape, LOW),
        (hbm, (samples, count, atom_width), LOW),
        (hbm, (samples, tokens_in, wide), LOW),
        (hbm, in_a.shape, LOW),
        (hbm, out_a.shape, LOW),
        (hbm, up_a.shape, LOW),
        (near, (tokens_in, 1), WIDE),
    ]
    copies = 4 + 9 * 4
    return pl.pallas_call(
        front_kernel,
        in_specs=[near, smem, near, hbm, near, hbm, near, hbm] + [near] * 4 + [smem, near] + [hbm] * 3,
        out_specs=[spec for spec, _, _ in outs],
        out_shape=[sds(shape, dtype) for _, shape, dtype in outs],
        scratch_shapes=[
            pltpu.VMEM(cond_w.shape, LOW),
            pltpu.VMEM((parts, rows, wide), WIDE),
            pltpu.VMEM(half_pair, LOW),
            pltpu.VMEM((2,) + pair_w.shape, LOW),
            pltpu.VMEM((heads, tokens_in, tokens_in), WIDE),
            pltpu.VMEM((samples, count, atom_width), LOW),
            pltpu.VMEM((groups // 2, 1, lanes), jnp.int32),
            pltpu.VMEM((groups, 1, lanes), jnp.int32),
            pltpu.VMEM((samples, count, 3 * atom_width), LOW),
            pltpu.VMEM(probs_shape, LOW),
            pltpu.VMEM((samples, count, atom_width), LOW),
            pltpu.VMEM((tokens_in, wide), WIDE),
            pltpu.VMEM((samples, tokens_in, wide), LOW),
            pltpu.SemaphoreType.DMA((64,)),
            pltpu.SemaphoreType.DMA((copies,)),
            pltpu.SemaphoreType.DMA((copies,)),
        ],
        compiler_params=remote_params(60, 3),
        cost_estimate=cost(40e9, 40e6),
        name="front",
    )(
        trunk, noise, levels, cond_w, cond_b, pair, pair_w, atoms, gain, qkv_w, out_w, agg_w,
        starts, ids, in_a, out_a, up_a,
    )


def token_attention_kernel(
    tokens_ref, cond_ref, bias_ref, in_a_ref, in_b_ref, out_a_ref, out_b_ref, down_a_ref,
    inner_ref, qkv_ref, sig_ref, heads_ref, gated_ref, probs_ref, attn_ref, middle_ref, down_b_ref,
    tokens, cond, bias, in_a, in_b, out_a, out_b, inner, qkv, sig, heads_out, gated, probs, attn,
    middle, local_sem, send_sem, recv_sem,
):
    links = Links(send_sem, recv_sem, far=False)
    local = Local(local_sem)
    load_tokens = local.start(tokens_ref, tokens)
    load_cond = local.start(cond_ref, cond)
    load_in = [local.start(in_a_ref, in_a)]
    load_bias = local.start(bias_ref, bias)
    load_in.append(local.start(in_b_ref, in_b))
    load_out = [local.start(out_a_ref, out_a), local.start(out_b_ref, out_b)]
    links.barrier()
    chunks = 2
    flow = Flow(
        fetch_journey(links, down_a_ref, down_b_ref, i, down_a_ref.shape[0] // 4 // chunks)
        for i in range(chunks)
    )
    samples, heads, count = probs.shape[0], probs.shape[1], probs.shape[2]
    width_in = in_a.shape[1] // 4
    size = 2 * width_in // heads
    scale = size ** (-0.5)
    load_tokens.wait()
    load_cond.wait()
    wide = tokens[...].astype(WIDE)
    normed, _ = layer_norm(wide)
    inner[...] = (normed * cond[0] + cond[1]).astype(LOW)
    local.store(inner, inner_ref)
    for half, weight in enumerate((in_a, in_b)):
        load_in[half].wait()
        qkv[half] = mul(inner[...], weight[:, : 3 * width_in]).astype(LOW)
        local.store(qkv.at[half], qkv_ref.at[half])
        sig[half] = sigmoid(mul(inner[...], weight[:, 3 * width_in :]))
        local.store(sig.at[half], sig_ref.at[half])
        if half == 0:
            load_bias.wait()
        flow.after(2.0)
        for s in range(samples):
            at = slice(s * count, (s + 1) * count)
            outs = []
            for h in range(heads // 2):
                col = h * size
                query = qkv[half, at, col : col + size]
                key = qkv[half, at, width_in + col : width_in + col + size]
                value = qkv[half, at, 2 * width_in + col : 2 * width_in + col + size]
                scores = mul_nt(query, key) * scale + bias[half * (heads // 2) + h]
                exps = jnp.exp(scores - jnp.max(scores, -1, keepdims=True))
                low = (exps * (1.0 / jnp.sum(exps, -1, keepdims=True))).astype(LOW)
                probs[s, half * (heads // 2) + h] = low
                outs.append(mul(low, value))
                if h % 4 == 3:
                    flow.after(1.4)
            heads_out[half, at, :] = jnp.concatenate(outs, 1)
        gated[half] = (heads_out[half] * sig[half]).astype(LOW)
        local.store(heads_out.at[half], heads_ref.at[half])
        local.store(gated.at[half], gated_ref.at[half])
    local.store(probs, probs_ref)
    load_out[0].wait()
    load_out[1].wait()
    attn[...] = mul(gated[0], out_a[...]) + mul(gated[1], out_b[...])
    local.store(attn, attn_ref)
    middle[...] = wide + cond[2] * attn[...]
    local.store(middle, middle_ref)
    flow.finish()
    local.finish()


def token_attention(tokens, cond, bias, in_a, in_b, out_a, out_b, down_a):
    rows, width = tokens.shape
    heads, count = bias.shape[0], bias.shape[1]
    samples, width_in = rows // count, in_a.shape[1] // 4
    hbm = pl.BlockSpec(memory_space=pl.ANY)
    outs = [
        sds((rows, width), LOW),
        sds((2, rows, 3 * width_in), LOW),
        sds((2, rows, width_in), WIDE),
        sds((2, rows, width_in), WIDE),
        sds((2, rows, width_in), LOW),
        sds((samples, heads, count, count), LOW),
        sds((rows, width), WIDE),
        sds((rows, width), WIDE),
    ]
    args = (tokens, cond, bias, in_a, in_b, out_a, out_b)
    copies = 4 * 2
    return pl.pallas_call(
        token_attention_kernel,
        in_specs=[hbm] * (len(args) + 1),
        out_specs=[hbm] * (len(outs) + 1),
        out_shape=outs + [sds(down_a.shape, LOW)],
        scratch_shapes=[
            *(pltpu.VMEM(a.shape, a.dtype) for a in args),
            *(pltpu.VMEM(a.shape, a.dtype) for a in outs),
            pltpu.SemaphoreType.DMA((32,)),
            pltpu.SemaphoreType.DMA((copies,)),
            pltpu.SemaphoreType.DMA((copies,)),
        ],
        compiler_params=remote_params(60, 4),
        cost_estimate=cost(40e9, 20e6),
        name="token_attention",
    )(*args, down_a)


CHUNK = 192
MLP_CHUNKS = (192,) * 6
EARLY = 2
COND_CHUNKS = (192,) * 3
ATTN_CHUNKS = (192, 192, 192, 192, 96, 96)


def relative(half, mp):
    return mp if half == 0 else 1 - mp


def token_back_kernel(
    middle_ref, cond_b_ref, cotangent_ref, low_ref, up_a_ref, up_b_ref, down_a_ref, down_b_ref,
    tokens_ref, cond_a_ref, attn_ref, inner_ref, qkv_ref, sig_ref, heads_ref, gated_ref, probs_ref,
    in_a_ref, in_b_ref, out_a_ref, out_b_ref,
    result_ref, other_result_ref, token_grad_ref, grads_ref, cond_bias_a_ref, cond_bias_b_ref,
    bias_grad_ref, mlp_out_ref, mlp_part_ref,
    middle, cond, grad, low, weight, out_weight, up, hidden, mlp_grads, middle_grad, result,
    tokens, inner, qkv, sig, heads_out, gated, probs, grads, bias_grad, proj, heads_grad, *rest,
):
    *buffers, local_sem, send_sem, recv_sem = rest
    links = Links(send_sem, recv_sem)
    local = Local(local_sem)
    load_first = [
        local.start(a, b)
        for a, b in ((middle_ref, middle), (cond_b_ref, cond), (up_a_ref, weight.at[0]))
    ]
    load_up_b = local.start(up_b_ref, weight.at[1])
    load_down = [local.start(down_a_ref, out_weight.at[0])]
    load_down.append(local.start(down_b_ref, out_weight.at[1]))
    samples, tokens_in = probs.shape[0], probs.shape[2]
    batch = cotangent_ref.shape[0] // MICRO
    load_grad = [local.start(low_ref, low)]
    for s in range(samples):
        sample = links.section * batch + links.mp * samples + s
        at = pl.ds(s * tokens_in, tokens_in)
        load_grad.append(local.start(cotangent_ref.at[sample], grad.at[at, :]))
    load_later = [
        local.start(a, b)
        for a, b in (
            (gated_ref, gated), (sig_ref, sig), (heads_ref, heads_out), (qkv_ref, qkv),
            (probs_ref, probs), (inner_ref, inner), (tokens_ref, tokens),
        )
    ]
    links.barrier()
    flow = Flow([])
    rows, width = middle.shape
    half_cols = width // 2
    samples, heads, count = probs.shape[0], probs.shape[1], probs.shape[2]

    for copy in load_first:
        copy.wait()
    middle_value = middle[...]
    normed, inverse = layer_norm(middle_value)
    scale, gate = cond[0], cond[2]
    inner_mlp = (normed * scale + cond[1]).astype(LOW)
    mlp_width = hidden.shape[2]
    mlp = None
    for half in range(2):
        if half == 1:
            load_up_b.wait()
        gate_in = mul(inner_mlp, weight[half, :, :mlp_width])
        up_in = mul(inner_mlp, weight[half, :, mlp_width:])
        up[half, :, :mlp_width] = gate_in.astype(LOW)
        up[half, :, mlp_width:] = up_in.astype(LOW)
        hidden[half] = (gate_in * sigmoid(gate_in) * up_in).astype(LOW)
        load_down[half].wait()
        add = mul(hidden[half], out_weight[half])
        mlp = add if mlp is None else mlp + add
    result[...] = (middle_value + gate * mlp).astype(LOW)
    local.store(result, result_ref)
    result_copy = links.send(result, other_result_ref, links.y)
    flow.free["y"] = rows * width * 2 / Flow.RATES["y"]

    for copy in load_grad:
        copy.wait()
    grad_value = grad[...].astype(WIDE)
    mlp_grad = (grad_value * gate).astype(LOW)
    core_rows = mlp_grads.shape[2] // 2
    down_rows = mlp_width // 2
    for half in range(2):
        hidden_t = hidden[half].T
        for core in range(2):
            for sec in range(2):
                mlp_grads[half, sec, core * core_rows : core * core_rows + down_rows, :] = mul(
                    hidden_t[core * down_rows : (core + 1) * down_rows],
                    mlp_grad[:, sec * half_cols : (sec + 1) * half_cols],
                ).astype(LOW)

    pool = Pool(buffers)

    def launch(first, last):
        for i in range(first, last):
            early = i < EARLY
            taken = pool.take(3 + (far_slots() if early else 0))
            part = None if early else mlp_part_ref.at[i - EARLY]
            flow.add(
                journey(
                    links, mlp_grads, None, taken, mlp_out_ref, None,
                    offsets(MLP_CHUNKS)[i], MLP_CHUNKS[i], i % 3 != 2, False, part,
                )
            )

    launch(0, down_rows // CHUNK)
    inner_t = inner_mlp.T
    inner_grad = None
    for half in range(2):
        hidden_grad = mul_nt(mlp_grad, out_weight[half])
        gate_in = up[half, :, :mlp_width].astype(WIDE)
        up_in = up[half, :, mlp_width:].astype(WIDE)
        sigma = sigmoid(gate_in)
        first = (hidden_grad * up_in * (sigma * (1.0 + gate_in * (1.0 - sigma)))).astype(LOW)
        second = (hidden_grad * (gate_in * sigma)).astype(LOW)
        up_grad = jnp.concatenate([first, second], 1)
        for sec in range(2):
            at = slice(sec * half_cols, (sec + 1) * half_cols)
            for block in range(4):
                place = block // 2 * core_rows + down_rows + block % 2 * half_cols
                mlp_grads[half, sec, place : place + half_cols, :] = mul(
                    inner_t[at], up_grad[:, block * half_cols : (block + 1) * half_cols]
                ).astype(LOW)
        add = mul_nt(up_grad, weight[half])
        inner_grad = add if inner_grad is None else inner_grad + add
        flow.after(3.0)
    load_weight = [local.start(in_a_ref, weight.at[0]), local.start(in_b_ref, weight.at[1])]
    out_rows = out_a_ref.shape[0]
    load_out = [
        local.start(a, out_weight.at[h, :out_rows, :]) for h, a in enumerate((out_a_ref, out_b_ref))
    ]
    launch(down_rows // CHUNK, core_rows // CHUNK)
    middle_grad[...] = grad_value + norm_back(normed, inverse, inner_grad * scale)
    low_t = low[...].T
    first_cond = grads.shape[2] - 3 * low_t.shape[0]

    def cond_back(sec, pieces, bias_out):
        for k, piece in enumerate(pieces):
            piece = piece.astype(LOW)
            place = first_cond + k * low_t.shape[0]
            for h in range(2):
                grads[relative(h, links.mp), sec, place : place + low_t.shape[0], :] = mul(
                    low_t, piece[:, h * half_cols : (h + 1) * half_cols]
                ).astype(LOW)
            bias_out[k] = jnp.sum(piece.astype(WIDE), 0, keepdims=True)

    cond_back(
        1,
        (
            inner_grad * normed * (scale * (1.0 - scale)),
            inner_grad,
            grad_value * mlp * (gate * (1.0 - gate)),
        ),
        cond_bias_b_ref,
    )
    load_cond = local.start(cond_a_ref, cond)
    load_attn = local.start(attn_ref, middle)
    flow.after(3.0)

    local_cols = out_rows
    size = 2 * local_cols // heads
    head_scale = size ** (-0.5)
    load_cond.wait()
    for copy in load_later:
        copy.wait()
    scale, gate = cond[0], cond[2]
    attn_grad = (middle_grad[...] * gate).astype(LOW)
    inner_t = inner[...].T
    inner_grad = None
    for half in range(2):
        load_out[half].wait()
        gated_t = gated[half].T
        for sec in range(2):
            grads[half, sec, 4 * half_cols : first_cond, :] = mul(
                gated_t, attn_grad[:, sec * half_cols : (sec + 1) * half_cols]
            ).astype(LOW)
        gated_grad = mul_nt(attn_grad, out_weight[half, :out_rows, :])
        sig_half = sig[half]
        with_sig = gated_grad * sig_half
        heads_grad[...] = with_sig.astype(LOW)
        proj[:, 3 * local_cols :] = (with_sig * heads_out[half] * (1.0 - sig_half)).astype(LOW)
        flow.after(1.5)
        for s in range(samples):
            at = slice(s * count, (s + 1) * count)
            parts = ([], [], [])
            for h in range(heads // 2):
                col, index = h * size, half * (heads // 2) + h
                query = qkv[half, at, col : col + size]
                key = qkv[half, at, local_cols + col : local_cols + col + size]
                value = qkv[half, at, 2 * local_cols + col : 2 * local_cols + col + size]
                one_grad = heads_grad[at, col : col + size]
                probs_low = probs[s, index]
                wide_probs = probs_low.astype(WIDE)
                probs_grad = mul_nt(one_grad, value)
                mean = jnp.sum(wide_probs * probs_grad, -1, keepdims=True)
                scores_grad = (wide_probs * (probs_grad - mean)).astype(LOW)
                if s == 0:
                    bias_grad[index] = scores_grad.astype(WIDE)
                else:
                    bias_grad[index] += scores_grad.astype(WIDE)
                parts[0].append(mul(scores_grad, key) * head_scale)
                parts[1].append(mul_tn(scores_grad, query) * head_scale)
                parts[2].append(mul_tn(probs_low, one_grad))
                if h % 2 == 1:
                    flow.after(1.0)
            for k in range(3):
                proj[at, k * local_cols : (k + 1) * local_cols] = jnp.concatenate(
                    parts[k], 1
                ).astype(LOW)
        load_weight[half].wait()
        for sec in range(2):
            for k in range(4):
                grads[half, sec, k * half_cols : (k + 1) * half_cols, :] = mul(
                    inner_t[sec * half_cols : (sec + 1) * half_cols],
                    proj[:, k * local_cols : (k + 1) * local_cols],
                ).astype(LOW)
        local.store(grads.at[half, :, :first_cond, :], grads_ref.at[half, :, :first_cond, :])
        some = pl.ds(half * (heads // 2), heads // 2)
        local.store(bias_grad.at[some], bias_grad_ref.at[some])
        add = mul_nt(proj[...], weight[half])
        inner_grad = add if inner_grad is None else inner_grad + add
        flow.after(2.5)
    normed, inverse = layer_norm(tokens[...].astype(WIDE))
    tokens[...] = (middle_grad[...] + norm_back(normed, inverse, inner_grad * scale)).astype(LOW)
    local.store(tokens, token_grad_ref)
    flow.after(1.0)
    load_attn.wait()
    cond_back(
        0,
        (
            inner_grad * normed * (scale * (1.0 - scale)),
            inner_grad,
            middle_grad[...] * middle[...] * (gate * (1.0 - gate)),
        ),
        cond_bias_a_ref,
    )
    local.store(grads.at[:, :, first_cond:, :], grads_ref.at[:, :, first_cond:, :])

    flow.finish()
    result_copy.wait()
    local.finish()


def token_back(
    middle, cond_b, cotangent, low, up_a, up_b, down_a, down_b, tokens, cond_a, attn, inner, qkv,
    sig, heads_out, gated, probs, in_a, in_b, out_a, out_b,
):
    rows, width = tokens.shape
    heads, count = probs.shape[1], probs.shape[2]
    mlp_width, local_cols, half = down_a.shape[0], out_a.shape[0], width // 2
    mlp_rows = 4 * half + mlp_width
    grad_rows = 4 * half + local_cols + 3 * low.shape[1]
    chunks = mlp_rows // 2 // CHUNK
    copies = chunks * journey_copies(False) + 1
    hbm, near = pl.BlockSpec(memory_space=pl.ANY), pl.BlockSpec(memory_space=pltpu.VMEM)
    args = (
        middle, cond_b, cotangent, low, up_a, up_b, down_a, down_b, tokens, cond_a, attn, inner,
        qkv, sig, heads_out, gated, probs, in_a, in_b, out_a, out_b,
    )
    outs = [
        (hbm, (rows, width), LOW),
        (hbm, (rows, width), LOW),
        (hbm, (rows, width), LOW),
        (hbm, (2, 2, grad_rows, half), LOW),
        (near, (3, 1, width), WIDE),
        (near, (3, 1, width), WIDE),
        (hbm, (heads, count, count), WIDE),
        (near, (2 * EARLY * CHUNK, half), LOW),
        (near, (chunks - EARLY, CHUNK, half), LOW),
    ]
    scratch = [
        (middle.shape, WIDE),
        (cond_b.shape, WIDE),
        ((rows, width), LOW),
        (low.shape, LOW),
        ((2,) + up_a.shape, LOW),
        ((2,) + down_a.shape, LOW),
        ((2, rows, 2 * mlp_width), LOW),
        ((2, rows, mlp_width), LOW),
        ((2, 2, mlp_rows, half), LOW),
        (middle.shape, WIDE),
        ((rows, width), LOW),
        *((a.shape, a.dtype) for a in (tokens, inner, qkv, sig, heads_out, gated, probs)),
        ((2, 2, grad_rows, half), LOW),
        ((heads, count, count), WIDE),
        ((rows, 4 * local_cols), LOW),
        ((rows, local_cols), LOW),
    ]
    return pl.pallas_call(
        token_back_kernel,
        in_specs=[hbm] * len(args),
        out_specs=[spec for spec, _, _ in outs],
        out_shape=[sds(shape, dtype) for _, shape, dtype in outs],
        scratch_shapes=[
            *(pltpu.VMEM(shape, dtype) for shape, dtype in scratch),
            *journey_scratch(CHUNK, half) * EARLY,
            *near_scratch(CHUNK, half) * (chunks - EARLY),
            pltpu.SemaphoreType.DMA((64,)),
            pltpu.SemaphoreType.DMA((copies,)),
            pltpu.SemaphoreType.DMA((copies,)),
        ],
        compiler_params=remote_params(62, 1),
        cost_estimate=cost(90e9, 50e6),
        name="token_back",
    )(*args)


FIRST_ROWS, LAST_ROWS = 128, 64


def atom_back_kernel(
    atoms_hbm, gain_ref, qkv_w_ref, out_w_ref, agg_w_ref, ids_ref, inv_ref,
    qkv_hbm, probs_hbm, mixed_hbm, grad_ref, pair_ref, bias_grad_hbm, grads_ref, cond_bias_a_ref,
    cond_bias_b_ref, mlp_part_ref,
    keep_ref, got_ref, attn_out_ref, cond_out_ref, cond_other_ref,
    first_out_ref, first_other_ref, last_out_ref, last_other_ref, mlp_out_ref,
    pair, bias_grad, twin_bias, pair_grad, atoms_ref, qkv_ref, probs_ref, mixed_ref, kept_attn, kept_cond,
    after_grad, mixed_grad, key_grad, value_grad, proj_grad, atoms_grad, send_buffer,
    gain_grad, qkv_grad, out_grad, agg_grad, first_small, last_small, *rest,
):
    *buffers, local_sem, send_sem, recv_sem = rest
    links = Links(send_sem, recv_sem)
    local = Local(local_sem)
    samples, atoms, width = atoms_ref.shape
    groups, keys_in = probs_ref.shape[1], probs_ref.shape[2]
    queries_in = SPAN * QBLOCK
    scale = (width // ATOM_HEADS) ** (-0.5)
    cond_rows = cond_out_ref.shape[0]
    attn_rows = grads_ref.shape[2] - cond_rows
    attn_grads = grads_ref.at[:, :, :attn_rows, :]
    cond_grads = grads_ref.at[:, :, attn_rows:, :]
    pair_half = bias_grad.shape[1]
    own_rows = pl.ds(pl.multiple_of(links.core * pair_half, 8), pair_half)
    twin_rows = pl.ds(pl.multiple_of((1 - links.core) * pair_half, 8), pair_half)
    load_bias = local.start(bias_grad_hbm.at[:, own_rows, :], bias_grad)

    def load_kept(source, target):
        start = links.core * (source.shape[2] // 2)
        at = pl.ds(pl.multiple_of(start, 16), target.shape[2])
        return local.start(source.at[:, :, at, :], target)

    kept_loads = [load_kept(attn_grads, kept_attn), load_kept(cond_grads, kept_cond)]
    loads = [local.start(mixed_hbm, mixed_ref), local.start(atoms_hbm, atoms_ref)]
    later = [
        (local.start(qkv_hbm.at[s], qkv_ref.at[s]), local.start(probs_hbm.at[s], probs_ref.at[s]))
        for s in range(samples)
    ]
    links.barrier()
    bias_copy = links.send(bias_grad_hbm.at[:, twin_rows, :], twin_bias, links.twin)
    pool, each = Pool(buffers), 3 + far_slots()
    flow = Flow([])
    for i in range(mlp_part_ref.shape[0]):
        held, *slots = pool.take(each - 2)
        held[...] = mlp_part_ref[i]
        offset = i * mlp_part_ref.shape[1]
        flow.add(far_journey(links, held, slots, mlp_out_ref, None, offset, False))
    for offset, rows in zip(offsets(COND_CHUNKS), COND_CHUNKS):
        flow.add(
            journey(
                links, cond_grads, kept_cond, pool.take(each), cond_out_ref, cond_other_ref,
                offset, rows, True, True,
            )
        )
    for i, (offset, rows) in enumerate(zip(offsets(ATTN_CHUNKS), ATTN_CHUNKS)):
        flow.add(
            journey(
                links, attn_grads, kept_attn, pool.take(each), attn_out_ref, None,
                offset, rows, i != 3, False,
            )
        )
    for copy in kept_loads:
        copy.wait()

    load_bias.wait()
    bias_copy.wait()
    heads = pair_grad.shape[0]
    slots = pair.shape[0]
    block = pair.shape[1]
    blocks = pair_ref.shape[0] // block

    def load_pair(i):
        return local.start(pair_ref.at[pl.ds(i * block, block)], pair.at[i % slots])

    pair_loads = [load_pair(i) for i in range(slots)]
    total = jnp.zeros(pair_grad.shape, WIDE)
    for i in range(blocks):
        pair_loads[i].wait()
        for j in range(block):
            one = bias_grad[:, i * block + j, :] + twin_bias[:, i * block + j, :]
            high = one.astype(LOW)
            tail = (one - high.astype(WIDE)).astype(LOW)
            both = mul(jnp.concatenate([high, tail], 0), pair[i % slots, j])
            total += both[:heads] + both[heads:]
        if i + slots < blocks:
            pair_loads.append(load_pair(i + slots))
        flow.after(0.08 * block)
    pair_grad[...] = total
    for copy in loads:
        copy.wait()

    for ref in (gain_grad, qkv_grad, out_grad, agg_grad):
        ref[...] = jnp.zeros_like(ref)
    chunk = 256
    token_ids = lax.broadcasted_iota(jnp.int32, (grad_ref.shape[1], chunk), 0)
    atom_copies = []
    for s in range(samples):
        token_grad = (grad_ref[s].astype(WIDE) * inv_ref[...]).astype(LOW)
        for i in range(atoms // chunk):
            rows = slice(i * chunk, (i + 1) * chunk)
            mixed = mixed_ref[s, rows, :]
            after = atoms_ref[s, rows, :].astype(WIDE) + mul(mixed, out_w_ref[...])
            after_low = after.astype(LOW)
            pre = mul(after_low, agg_w_ref[...])
            sigma = sigmoid(pre)
            member = jnp.where(token_ids == ids_ref[:, rows], 1.0, 0.0).astype(LOW)
            unit_grad = mul_tn(member, token_grad)
            pre_grad = (unit_grad * (sigma * (1.0 + pre * (1.0 - sigma)))).astype(LOW)
            agg_grad[...] += mul_tn(after_low, pre_grad)
            after_back = mul_nt(pre_grad, agg_w_ref[...])
            after_grad[s, rows, :] = after_back
            branch = after_back.astype(LOW)
            out_grad[...] += mul_tn(mixed, branch)
            mixed_grad[s, rows, :] = mul_nt(branch, out_w_ref[...]).astype(LOW)
            flow.after(1.7)
    heads = pair_grad.shape[0]
    wide = agg_grad.shape[1] // 2
    rows, part_rows = width // 2, width // 4

    def fill(values, cols):
        if values.shape[1] == cols:
            return values
        empty = jnp.zeros((values.shape[0], cols - values.shape[1]), WIDE)
        return jnp.concatenate([values, empty], 1)

    for h in range(2):
        to = relative(h, links.mp)
        cols = slice(h * wide, (h + 1) * wide)
        own_pair = jnp.where(links.mp == h, pair_grad[: heads // 2], pair_grad[heads // 2 :])
        for sec, cond_bias_ref in enumerate((cond_bias_a_ref, cond_bias_b_ref)):
            first_small[to, sec, :rows, :] = agg_grad[sec * rows : (sec + 1) * rows, cols].astype(LOW)
            first_row = sec * rows + h * part_rows
            block = fill(out_grad[first_row : first_row + part_rows], wide)
            first_small[to, sec, rows : rows + part_rows, :] = block.astype(LOW)
            block = [cond_bias_ref[k, :, cols] for k in range(3)]
            block += [jnp.zeros((5, wide), WIDE), fill(own_pair, wide)]
            block += [jnp.zeros((part_rows - 16, wide), WIDE)]
            first_small[to, sec, rows + part_rows :, :] = jnp.concatenate(block, 0).astype(LOW)
    flow.add(
        journey(
            links, first_small, None, pool.take(each), first_out_ref, first_other_ref,
            0, FIRST_ROWS // 2, False, True,
        )
    )
    for s in range(samples):
        for copy in later[s]:
            copy.wait()
        key_grad[...] = jnp.zeros_like(key_grad)
        value_grad[...] = jnp.zeros_like(value_grad)

        def attend(group, carry, s=s):
            base = key_base(group, atoms)
            start = pl.multiple_of(group * queries_in, queries_in)
            queries = spread(qkv_ref[s, pl.ds(start, queries_in), :width], ATOM_HEADS)
            grads = spread(mixed_grad[s, pl.ds(start, queries_in), :], ATOM_HEADS)
            keys = qkv_ref[s, pl.ds(base, keys_in), width : 2 * width]
            values = qkv_ref[s, pl.ds(base, keys_in), 2 * width :]
            probs_low = probs_ref[s, group]
            probs = probs_low.astype(WIDE)
            probs_grad = mul_nt(values, grads)
            mean = jnp.sum(probs * probs_grad, 0, keepdims=True)
            scores_grad = (probs * (probs_grad - mean)).astype(LOW)
            query_grad = gather_heads(mul_tn(scores_grad, keys), ATOM_HEADS)
            proj_grad[pl.ds(start, queries_in), :width] = (query_grad * scale).astype(LOW)
            key_grad[pl.ds(base, keys_in), :] += mul(scores_grad, queries)
            value_grad[pl.ds(base, keys_in), :] += mul(probs_low, grads)
            return carry

        cuts = 5
        for i in range(cuts):
            lax.fori_loop(groups * i // cuts, groups * (i + 1) // cuts, attend, 0)
            flow.after(2.3)
        proj_grad[:, width : 2 * width] = (key_grad[...] * scale).astype(LOW)
        proj_grad[:, 2 * width :] = value_grad[...].astype(LOW)
        gain = gain_ref[...].astype(WIDE)
        normed, inverse = layer_norm(atoms_ref[s].astype(WIDE))
        hidden = (normed * gain).astype(LOW)
        proj = proj_grad[...]
        qkv_grad[...] += mul_tn(hidden, proj)
        hidden_grad = mul_nt(proj, qkv_w_ref[...])
        gain_grad[...] += jnp.sum(hidden_grad * normed, 0, keepdims=True)
        atoms_grad[...] = after_grad[s] + norm_back(normed, inverse, hidden_grad * gain)
        half = atoms // 2
        theirs = pl.ds(pl.multiple_of((1 - links.mp) * half, 16), half)
        send_buffer[s] = atoms_grad[theirs, :].astype(LOW)
        atom_copies.append(links.send(send_buffer.at[s], got_ref.at[s], links.y))
        keep_ref[s] = atoms_grad[pl.ds(pl.multiple_of(links.mp * half, 16), half), :]
        flow.after(2.5)

    for h in range(2):
        to = relative(h, links.mp)
        for sec in range(2):
            first_row = sec * rows + h * part_rows
            part = fill(qkv_grad[first_row : first_row + part_rows], wide)
            last_small[to, sec, :part_rows, :] = part.astype(LOW)
            block = [fill(gain_grad[...], wide), jnp.zeros((part_rows - 1, wide), WIDE)]
            last_small[to, sec, part_rows:, :] = jnp.concatenate(block, 0).astype(LOW)
    flow.add(
        journey(
            links, last_small, None, pool.take(each), last_out_ref, last_other_ref,
            0, LAST_ROWS // 2, False, True,
        )
    )
    flow.finish()
    for copy in atom_copies:
        copy.wait()


def atom_back(
    atoms, gain, qkv_w, out_w, agg_w, ids, inverse_counts, qkv, probs, mixed, grad,
    low_pair, bias_grad, grads, cond_bias_a, cond_bias_b, mlp_part, cond_rows,
):
    samples, count, width = atoms.shape
    wide = agg_w.shape[1]
    cols = grads.shape[3]
    attn_rows = grads.shape[2] - cond_rows
    copies = len(ATTN_CHUNKS) * journey_copies(False)
    copies += len(COND_CHUNKS) * journey_copies(True)
    copies += 2 * journey_copies(True) + samples + 1
    half_bias = (bias_grad.shape[0], bias_grad.shape[1] // 2, bias_grad.shape[2])
    copies += mlp_part.shape[0] * journey_copies(False, near=0)
    outs = [
        sds((samples, count // 2, width), WIDE),
        sds((samples, count // 2, width), LOW),
        sds((attn_rows, cols), LOW),
        sds((cond_rows, cols), LOW),
        sds((cond_rows, cols), LOW),
        sds((FIRST_ROWS, cols), LOW),
        sds((FIRST_ROWS, cols), LOW),
        sds((LAST_ROWS, cols), LOW),
        sds((LAST_ROWS, cols), LOW),
        sds((2 * mlp_part.shape[0] * CHUNK, cols), LOW),
    ]
    args = (
        atoms, gain, qkv_w, out_w, agg_w, ids, inverse_counts, qkv, probs, mixed, grad,
        low_pair, bias_grad, grads, cond_bias_a, cond_bias_b, mlp_part,
    )
    hbm, near = pl.BlockSpec(memory_space=pl.ANY), pl.BlockSpec(memory_space=pltpu.VMEM)
    return pl.pallas_call(
        atom_back_kernel,
        in_specs=[hbm] + [near] * 6 + [hbm] * 3 + [near] + [hbm] * 3 + [near] * 3,
        out_specs=everywhere(len(outs)),
        out_shape=outs,
        scratch_shapes=[
            pltpu.VMEM((2, 8) + low_pair.shape[1:], LOW),
            pltpu.VMEM(half_bias, WIDE),
            pltpu.VMEM(half_bias, WIDE),
            pltpu.VMEM((bias_grad.shape[0], width), WIDE),
            *(pltpu.VMEM(a.shape, a.dtype) for a in (atoms, qkv, probs, mixed)),
            pltpu.VMEM((2, 2, attn_rows // 2, cols), LOW),
            pltpu.VMEM((2, 2, cond_rows // 2, cols), LOW),
            pltpu.VMEM((samples, count, width), WIDE),
            pltpu.VMEM((samples, count, width), LOW),
            pltpu.VMEM((count, width), WIDE),
            pltpu.VMEM((count, width), WIDE),
            pltpu.VMEM((count, 3 * width), LOW),
            pltpu.VMEM((count, width), WIDE),
            pltpu.VMEM((samples, count // 2, width), LOW),
            pltpu.VMEM((1, width), WIDE),
            pltpu.VMEM((width, 3 * width), WIDE),
            pltpu.VMEM((width, width), WIDE),
            pltpu.VMEM((width, wide), WIDE),
            pltpu.VMEM((2, 2, FIRST_ROWS, cols), LOW),
            pltpu.VMEM((2, 2, LAST_ROWS, cols), LOW),
            *([pltpu.VMEM((CHUNK, cols), LOW)] + far_scratch(CHUNK, cols)) * mlp_part.shape[0],
            *(b for rows in COND_CHUNKS + ATTN_CHUNKS for b in journey_scratch(rows, cols)),
            *journey_scratch(FIRST_ROWS // 2, cols),
            *journey_scratch(LAST_ROWS // 2, cols),
            pltpu.SemaphoreType.DMA((32,)),
            pltpu.SemaphoreType.DMA((copies,)),
            pltpu.SemaphoreType.DMA((copies,)),
        ],
        compiler_params=remote_params(60, 2),
        cost_estimate=cost(60e9, 24e6),
        name="atom_back",
    )(*args)


def results_kernel(*refs):
    number, count = 13, 13
    hbm_in, hbm_out = refs[:number], refs[number : number + count]
    scratch, sem = refs[number + count : -1], refs[-1]
    near_in, near_out = scratch[:number], scratch[number:]
    local = Local(sem)
    loads = [local.start(a, b) for a, b in zip(hbm_in, near_in)]
    (
        cond_ref, cond_other_ref, attn_ref, mlp_first_ref, mlp_late_ref, keep_ref, got_ref,
        result_ref, other_result_ref, first_ref, first_other_ref, last_ref, last_other_ref,
    ) = near_in
    (
        token_out, atoms_out, gain_out, qkv_out, out_out, agg_out, cond_out, cond_bias_out,
        pair_out, in_out, attn_out, up_out, down_out,
    ) = near_out
    mp, section = lax.axis_index("mp"), lax.axis_index("section")

    def wait(*indices):
        for index in indices:
            loads[index].wait()

    def store(*outs):
        for out in outs:
            index = [i for i, ref in enumerate(near_out) if ref is out][0]
            local.store(out, hbm_out[index])

    half = cond_ref.shape[1]
    size = cond_out.shape[1]
    wait(0, 1)
    for h in range(2):
        cols = slice(h * half, (h + 1) * half)
        for k in range(3):
            at = slice(k * size, (k + 1) * size)
            value = jnp.where(mp == h, cond_ref[at, :], cond_other_ref[at, :])
            cond_out[k, :, cols] = value.astype(WIDE)
    store(cond_out)
    wait(2)
    blocks = in_out.shape[1]
    for k in range(blocks):
        in_out[:, k, :] = attn_ref[k * half : (k + 1) * half, :].astype(WIDE)
    store(in_out)
    attn_out[...] = attn_ref[blocks * half :, :].astype(WIDE)
    store(attn_out)
    wait(3, 4)
    core_first, core_late = mlp_first_ref.shape[0] // 2, mlp_late_ref.shape[0] // 2
    down_rows = down_out.shape[0] // 2
    for core in range(2):
        at = slice(core * down_rows, (core + 1) * down_rows)
        start = core * core_first
        down_out[at, :] = mlp_first_ref[start : start + down_rows, :].astype(WIDE)
        row = 0
        for ref, begin, end in (
            (mlp_first_ref, start + down_rows, start + core_first),
            (mlp_late_ref, core * core_late, (core + 1) * core_late),
        ):
            while begin < end:
                block, within = row // half, row % half
                some = min(end - begin, half - within)
                up_out[within : within + some, core, block * half : (block + 1) * half] = ref[
                    begin : begin + some, :
                ].astype(WIDE)
                begin, row = begin + some, row + some
    store(up_out, down_out)
    wait(5, 6)
    samples = keep_ref.shape[0]
    here, there = pl.ds(mp * samples, samples), pl.ds((1 - mp) * samples, samples)
    atoms_out[here] = keep_ref[...]
    atoms_out[there] = got_ref[...].astype(WIDE)
    store(atoms_out)
    wait(7, 8)
    token_out[here] = result_ref[...]
    token_out[there] = other_result_ref[...]
    store(token_out)
    wait(9, 10, 11, 12)
    width, rows = atoms_out.shape[2], out_out.shape[0]
    part_rows = rows // 2

    def own_lanes(values):
        return jnp.where(section == 0, values[:, :rows], values[:, rows:width])

    gain_out[...] = own_lanes(last_ref[part_rows : part_rows + 16, :].astype(WIDE))[:1]
    pair = first_ref[rows + part_rows : rows + part_rows + 16, :].astype(WIDE)
    pair_out[...] = own_lanes(pair[8:])
    for h in range(2):
        first = jnp.where(mp == h, first_ref[...], first_other_ref[...]).astype(WIDE)
        last = jnp.where(mp == h, last_ref[...], last_other_ref[...]).astype(WIDE)
        cols = slice(h * half, (h + 1) * half)
        part_at = slice(h * part_rows, (h + 1) * part_rows)
        agg_out[:, cols] = first[:rows]
        out_out[part_at, :] = first[rows : rows + part_rows, :width]
        cond_bias_out[:, cols] = first[rows + part_rows : rows + part_rows + 3]
        for k in range(3):
            qkv_out[k, part_at, :] = last[:part_rows, k * width : (k + 1) * width]
    store(gain_out, pair_out, agg_out, out_out, cond_bias_out, qkv_out)
    local.finish()


def results(
    result, other_result, keep, got, first, first_other, last, last_other, cond, cond_other, attn,
    mlp_first, mlp_late, width, mlp_local,
):
    samples, half_atoms, atom_width = keep.shape
    half, rows = width // 2, atom_width // 2
    attn_local = attn.shape[0] - 4 * half
    hbm = pl.BlockSpec(memory_space=pl.ANY)
    outs = [
        sds((2 * samples,) + result.shape[1:], LOW),
        sds((2 * samples, half_atoms, atom_width), WIDE),
        sds((1, rows), WIDE),
        sds((3, rows, atom_width), WIDE),
        sds((rows, atom_width), WIDE),
        sds((rows, width), WIDE),
        sds((3, cond.shape[0] // 3, width), WIDE),
        sds((3, width), WIDE),
        sds((8, rows), WIDE),
        sds((half, 4, attn_local), WIDE),
        sds((attn_local, half), WIDE),
        sds((half, 2, mlp_local), WIDE),
        sds((mlp_local, half), WIDE),
    ]
    args = (
        cond, cond_other, attn, mlp_first, mlp_late, keep, got, result, other_result, first,
        first_other, last, last_other,
    )
    return pl.pallas_call(
        results_kernel,
        in_specs=[hbm] * len(args),
        out_specs=[hbm] * len(outs),
        out_shape=outs,
        scratch_shapes=[
            *(pltpu.VMEM(a.shape, a.dtype) for a in args),
            *(pltpu.VMEM(a.shape, a.dtype) for a in outs),
            pltpu.SemaphoreType.DMA((32,)),
        ],
        compiler_params=params(60),
        cost_estimate=cost(1e8, 20e6),
        name="results",
    )(*args)


def local(
    atoms_in,
    atom_token,
    window_start,
    noise_level,
    level_table,
    single_trunk,
    pair,
    atom_gain,
    atom_qkv,
    atom_out,
    atom_agg,
    cond_weight,
    cond_bias,
    pair_weight,
    attn_in,
    attn_out,
    mlp_up,
    mlp_down,
    cotangent,
):
    section, mp = lax.axis_index("section"), lax.axis_index("mp")
    batch, half_atoms, atom_width = atoms_in.shape
    batch //= MICRO
    samples = batch // 2
    atoms = 2 * half_atoms
    tokens, width = cotangent.shape[1], cotangent.shape[2]
    single = single_trunk.shape[1]
    in_a = attn_in.reshape(width, -1)
    up_a = mlp_up.reshape(width, -1)
    gain = atom_gain[None, :]
    qkv_w = atom_qkv.reshape(atom_width, -1)

    cond_w = jnp.transpose(cond_weight, (0, 2, 1, 3)).reshape(6, single, width)
    (
        low, cond_a, cond_b, low_pair, bias, all_atoms, qkv, probs, mixed, token_in,
        in_b, out_b, up_b, inverse_counts,
    ) = front(
        single_trunk, noise_level, level_table, cond_w, cond_bias, pair, pair_weight.T,
        atoms_in, gain, qkv_w, atom_out, atom_agg, window_start, atom_token[None, :],
        in_a, attn_out, up_a,
    )
    token_in = token_in.reshape(-1, width)
    inner, token_qkv, sig, heads_out, gated, token_probs, attn, middle, down_b = token_attention(
        token_in, cond_a, bias, in_a, in_b, attn_out, out_b, mlp_down
    )
    (
        result, other_result, token_grad, attn_grads, cond_bias_a, cond_bias_b, bias_grad, mlp_first,
        mlp_part,
    ) = (
        token_back(
            middle, cond_b, cotangent, low, up_a, up_b, mlp_down, down_b, token_in, cond_a, attn,
            inner, token_qkv, sig, heads_out, gated, token_probs, in_a, in_b, attn_out, out_b,
        )
    )
    (
        keep, got, attn_sum, cond_sum, cond_other, first, first_other, last, last_other, mlp_late,
    ) = atom_back(
        all_atoms, gain, qkv_w, atom_out, atom_agg, atom_token[None, :], inverse_counts,
        qkv, probs, mixed, token_grad.reshape(samples, tokens, width),
        low_pair, bias_grad, attn_grads, cond_bias_a, cond_bias_b, mlp_part, 3 * single,
    )

    outs = results(
        result.reshape(samples, tokens, width), other_result.reshape(samples, tokens, width),
        keep, got, first, first_other, last, last_other, cond_sum, cond_other, attn_sum,
        mlp_first, mlp_late, width, mlp_up.shape[2],
    )
    token_out, atoms_out, gain_out, qkv_out, out_out, agg_out, cond_out = outs[:7]
    cond_bias_out, pair_out, in_out, attn_out_grad, up_out, down_out = outs[7:]
    return (
        token_out.reshape(1, 1, batch, tokens, width),
        atoms_out.reshape(1, 1, batch, half_atoms, atom_width),
        gain_out[0],
        jnp.transpose(qkv_out, (1, 0, 2)),
        out_out,
        agg_out,
        jnp.transpose(cond_out, (1, 0, 2))[None],
        cond_bias_out[None],
        pair_out.T,
        in_out,
        attn_out_grad,
        up_out,
        down_out,
    )


def solution(mesh):
    in_specs = (
        P("dp", "mp", None),
        P(),
        P("mp"),
        P("dp"),
        P(),
        P(),
        P(),
        P(),
        P(),
        P(),
        P(),
        P(),
        P(),
        P(None, "mp"),
        P(None, None, "mp"),
        P("mp", None),
        P(None, None, "mp"),
        P("mp", None),
        P("dp", None, None),
    )
    out_specs = (
        P("dp", "section", None, None, None),
        P("dp", "section", None, "mp", None),
        P("section"),
        P("section", None, None),
        P("section", None),
        P("section", None),
        P("section", None, None, None),
        P("section", None, None),
        P("section", "mp"),
        P("section", None, "mp"),
        P("mp", "section"),
        P("section", None, "mp"),
        P("mp", "section"),
    )
    return jax.shard_map(local, mesh=mesh, in_specs=in_specs, out_specs=out_specs, check_vma=False)
```

```python
import functools

import jax
import jax.numpy as jnp
from jax import lax
from jax.experimental import pallas as pl
from jax.experimental.pallas import tpu as pltpu
from jax.sharding import PartitionSpec as P

QBLOCK = 32
KWIN = 128
MICRO = 2
ATOM_HEADS = 4
SPAN = 2
EPS = 1e-05
LOW = jnp.bfloat16
WIDE = jnp.float32
MIB = 1 << 20


def mul(left, right):
    return lax.dot_general(left, right, (((1,), (0,)), ((), ())), preferred_element_type=WIDE)


def mul_nt(left, right):
    return lax.dot_general(left, right, (((1,), (1,)), ((), ())), preferred_element_type=WIDE)


def mul_tn(left, right):
    return lax.dot_general(left, right, (((0,), (0,)), ((), ())), preferred_element_type=WIDE)


def layer_norm(values):
    center = values - jnp.mean(values, -1, keepdims=True)
    inverse = lax.rsqrt(jnp.mean(center * center, -1, keepdims=True) + EPS)
    return center * inverse, inverse


def norm_back(normed, inverse, grad):
    return inverse * (
        grad
        - jnp.mean(grad, -1, keepdims=True)
        - normed * jnp.mean(grad * normed, -1, keepdims=True)
    )


def sigmoid(values):
    return 1.0 / (1.0 + jnp.exp(-values))


def params(mib, semantics=None):
    return pltpu.CompilerParams(vmem_limit_bytes=mib * MIB, dimension_semantics=semantics)


def cost(flops, moved, exps=0):
    return pl.CostEstimate(flops=int(flops), bytes_accessed=int(moved), transcendentals=int(exps))


def sds(shape, dtype):
    return jax.ShapeDtypeStruct(shape, dtype)


def joined(ref):
    return jnp.concatenate([ref[k] for k in range(ref.shape[0])], 1)


def lane_heads(rows, width, size):
    return lax.broadcasted_iota(jnp.int32, (rows, width), 1) // size


def spread(values, heads):
    head = lane_heads(values.shape[0], values.shape[1], values.shape[1] // heads)
    zero = jnp.zeros_like(values)
    return jnp.concatenate([jnp.where(head == h, values, zero) for h in range(heads)], 0)


def gather_heads(values, heads):
    rows = values.shape[0] // heads
    head = lane_heads(rows, values.shape[1], values.shape[1] // heads)
    total = jnp.where(head == 0, values[:rows], 0.0)
    for h in range(1, heads):
        total += jnp.where(head == h, values[h * rows : (h + 1) * rows], 0.0)
    return total


def key_base(group, atoms):
    start = group * SPAN * QBLOCK - KWIN // 2
    return pl.multiple_of(jnp.clip(start, 0, atoms - KWIN - (SPAN - 1) * QBLOCK - QBLOCK), QBLOCK)


def far_lines():
    bits = lax.axis_size("dp").bit_length() - 2
    return [(1 + b, 4 if b + 1 < bits else 2) for b in range(0, bits, 2)]


class Links:
    def __init__(self, send_sem, recv_sem, far=True):
        self.section, self.mp = lax.axis_index("section"), lax.axis_index("mp")
        self.dp = lax.axis_index("dp")
        self.core = self.dp % 2
        self.partners = [{"section": 1 - self.section}, {"mp": 1 - self.mp}]
        self.partners.append({"dp": self.dp + 1 - 2 * self.core})
        self.x, self.y, self.twin = self.partners
        self.lines = []
        for bit, count in far_lines() if far else ():
            place = self.dp // (1 << bit) % count
            beside = {"dp": self.dp + (1 - 2 * (place % 2)) * (1 << bit)}
            across = {"dp": self.dp + (count - 1 - 2 * place) * (1 << bit)}
            self.lines.append((count, place, beside, across))
            self.partners += [beside, across] if count == 4 else [beside]
        self.send_sem, self.recv_sem, self.used = send_sem, recv_sem, 0

    def barrier(self):
        barrier = pltpu.get_barrier_semaphore()
        for partner in self.partners:
            pl.semaphore_signal(
                barrier, inc=1, device_id=partner, device_id_type=pl.DeviceIdType.MESH
            )
        pl.semaphore_wait(barrier, len(self.partners))

    def copy(self, source, target, partner):
        copy = pltpu.make_async_remote_copy(
            src_ref=source,
            dst_ref=target,
            send_sem=self.send_sem.at[self.used],
            recv_sem=self.recv_sem.at[self.used],
            device_id=partner,
            device_id_type=pl.DeviceIdType.MESH,
        )
        self.used += 1
        return copy

    def send(self, source, target, partner):
        copy = self.copy(source, target, partner)
        copy.start()
        return copy


def far_copies():
    return sum(3 if count == 4 else 1 for _, count in far_lines())


def journey_copies(shared, near=3):
    return near + far_copies() + 1 + (2 if shared else 0)


def far_slots():
    return sum(count // 2 for _, count in far_lines())


def far_scratch(rows, cols):
    return [pltpu.VMEM((rows, cols), LOW)] * far_slots()


def near_scratch(rows, cols):
    return [pltpu.VMEM(shape + (rows, cols), LOW) for shape in ((2, 2), (2,), ())]


def journey_scratch(rows, cols):
    return near_scratch(rows, cols) + far_scratch(rows, cols)


class Pool:
    def __init__(self, buffers):
        self.buffers, self.used = buffers, 0

    def take(self, count):
        self.used += count
        return self.buffers[self.used - count : self.used]


def offsets(sizes):
    return [sum(sizes[:i]) for i in range(len(sizes))]


def journey(links, grads, kept, buffers, out, other_out, offset, rows, x_first, shared, part=None):
    near, middle, last, *far = buffers
    total_rows = grads.shape[2]
    start = links.core * (total_rows // 2) + offset
    twin_start = (1 - links.core) * (total_rows // 2) + offset
    mine, theirs = pl.ds(pl.multiple_of(start, 16), rows), pl.ds(pl.multiple_of(twin_start, 16), rows)
    me, you = links.section, 1 - links.section
    if kept is None:
        own = grads.at[:, :, mine, :]
    else:
        own = kept.at[:, :, pl.ds(offset, rows), :]
    block = rows * grads.shape[3] * 2
    copy = links.send(grads.at[:, :, theirs, :], near, links.twin)
    yield [("core", 4 * block)]
    copy.wait()
    if x_first:
        near[:, you] += own[:, you]
        copy = links.send(near.at[:, you], middle, links.x)
        near[:, me] += own[:, me]
        yield [("x", 2 * block)]
        copy.wait()
        middle[1] += near[1, me]
        copy = links.send(middle.at[1], last, links.y)
        middle[0] += near[0, me]
        yield [("y", block)]
        copy.wait()
        last[...] += middle[0]
    else:
        near[1] += own[1]
        copy = links.send(near.at[1], middle, links.y)
        near[0] += own[0]
        yield [("y", 2 * block)]
        copy.wait()
        middle[you] += near[0, you]
        copy = links.send(middle.at[you], last, links.x)
        middle[me] += near[0, me]
        yield [("x", block)]
        copy.wait()
        last[...] += middle[me]
    if part is not None:
        part[...] = last[...]
        return
    yield from far_journey(links, last, far, out, other_out, offset, shared)


def far_journey(links, held, far, out, other_out, offset, shared):
    rows = held.shape[0]
    start = links.core * (out.shape[0] // 2) + offset
    mine = pl.ds(pl.multiple_of(start, 16), rows)
    block = rows * held.shape[1] * 2
    far = list(far)
    for count, place, beside, across in links.lines:
        if count == 2:
            slot = far.pop(0)
            copy = links.send(held, slot, beside)
            yield [("z", block)]
            copy.wait()
            held[...] += slot[...]
            continue
        inner = (place == 1) | (place == 2)
        outer = (place == 0) | (place == 3)
        slot, second = far.pop(0), far.pop(0)
        gather = links.copy(held, slot, beside)
        exchange = links.copy(held, second, across)
        spread_back = links.copy(held, slot, beside)

        @pl.when(outer)
        def _():
            gather.start()

        yield [("z", block)]

        @pl.when(outer)
        def _():
            gather.wait_send()

        @pl.when(inner)
        def _():
            gather.wait_recv()
            held[...] += slot[...]
            exchange.start()

        yield [("mid", block)]

        @pl.when(inner)
        def _():
            exchange.wait()
            held[...] += second[...]
            spread_back.start()

        yield [("back", block)]

        @pl.when(inner)
        def _():
            spread_back.wait_send()

        @pl.when(outer)
        def _():
            spread_back.wait_recv()
            held[...] = slot[...]

    out[mine, :] = held[...]
    copies = [links.send(out.at[mine, :], out.at[mine, :], links.twin)]
    if shared:
        across = links.send(out.at[mine, :], other_out.at[mine, :], links.y)
        yield [("y", block)]
        across.wait()
        copies.append(links.send(other_out.at[mine, :], other_out.at[mine, :], links.twin))
    yield [("core", block)]
    for copy in copies:
        copy.wait()


class Flow:
    RATES = {"core": 400e3, "x": 43e3, "y": 43e3, "z": 43e3, "mid": 43e3, "back": 43e3}
    DELAYS = {"core": 0.4}

    def __init__(self, journeys):
        self.clock, self.free, self.queue, self.count = 0.0, {}, [], 0
        for one in journeys:
            self.add(one)

    def add(self, one):
        copies = next(one, None)
        if copies is None:
            return
        ready = self.clock
        for link, count in copies:
            finish = max(self.clock, self.free.get(link, 0.0)) + count / self.RATES[link]
            self.free[link] = finish
            ready = max(ready, finish + self.DELAYS.get(link, 1.5))
        self.queue.append((ready, self.count, one))
        self.queue.sort(key=lambda entry: entry[:2])
        self.count += 1

    def after(self, duration):
        self.clock += duration
        while self.queue and self.queue[0][0] <= self.clock:
            self.add(self.queue.pop(0)[2])

    def finish(self):
        while self.queue:
            self.clock = max(self.clock, self.queue[0][0])
            self.add(self.queue.pop(0)[2])


def everywhere(count):
    return [pl.BlockSpec(memory_space=pltpu.VMEM)] * count


def remote_params(mib, number):
    return pltpu.CompilerParams(
        vmem_limit_bytes=mib * MIB, collective_id=number, has_side_effects=True
    )


class Local:
    def __init__(self, sem):
        self.sem, self.used, self.open = sem, 0, []

    def start(self, source, target):
        copy = pltpu.make_async_copy(source, target, self.sem.at[self.used])
        self.used += 1
        copy.start()
        return copy

    def store(self, source, target):
        self.open.append(self.start(source, target))

    def finish(self):
        for copy in self.open:
            copy.wait()


def fetch_journey(links, own, other, chunk, rows):
    quarter = own.shape[0] // 4
    block = rows * own.shape[1] * 2

    def at(core, section):
        start = (2 * core + section) * quarter + chunk * rows
        return pl.ds(pl.multiple_of(start, 16), rows)

    mine = at(links.core, links.section)
    across = at(links.core, 1 - links.section)
    copy = links.send(own.at[mine, :], other.at[mine, :], links.y)
    yield [("y", block)]
    copy.wait()
    first = links.send(other.at[mine, :], other.at[mine, :], links.x)
    second = links.send(other.at[mine, :], other.at[mine, :], links.twin)
    yield [("x", block), ("core", block)]
    first.wait()
    third = links.send(other.at[across, :], other.at[across, :], links.twin)
    yield [("core", block)]
    second.wait()
    third.wait()


def fetch_eighths(links, own, other, chunk, rows):
    piece = own.shape[0] // 8
    block = rows * own.shape[1] * 2
    _, place, beside, _ = links.lines[0]
    side = place % 2

    def at(section, z):
        start = ((2 * links.core + section) * 2 + z) * piece + chunk * rows
        return other.at[pl.ds(pl.multiple_of(start, 16), rows), :]

    me, you = links.section, 1 - links.section
    mine, across = at(me, side), at(you, side)
    start = ((2 * links.core + me) * 2 + side) * piece + chunk * rows
    source = own.at[pl.ds(pl.multiple_of(start, 16), rows), :]
    copy = links.send(source, mine, links.y)
    yield [("y", block)]
    copy.wait()
    over_x = links.send(mine, mine, links.x)
    over_z = [links.send(mine, mine, beside)]
    twins = [links.send(mine, mine, links.twin)]
    yield [("x", block)]
    over_x.wait()
    over_z.append(links.send(across, across, beside))
    twins.append(links.send(across, across, links.twin))
    yield [("z", 2 * block)]
    for copy, section in zip(over_z, (me, you)):
        copy.wait()
        far = at(section, 1 - side)
        twins.append(links.send(far, far, links.twin))
    yield [("core", 2 * block)]
    for copy in twins:
        copy.wait()


def front_kernel(
    trunk_ref, noise_ref, level_ref, cond_w_ref, cond_b_ref, pair_ref, pair_w_ref, atoms_ref,
    gain_ref, qkv_w_ref, out_w_ref, agg_w_ref, start_ref, ids_ref, in_a_ref, out_a_ref, up_a_ref,
    down_a_ref,
    low_ref, cond_a_ref, cond_b_out_ref, low_pair_ref, bias_ref, atoms_out_ref, qkv_ref, probs_ref,
    mixed_ref, tokens_ref, in_b_ref, out_b_ref, up_b_ref, down_b_ref, inv_ref,
    cond_w, cond_out, pair, pair_w, bias, atoms, rel_own, rel, qkv, probs, mixed, total, tokens,
    local_sem, send_sem, recv_sem,
):
    links = Links(send_sem, recv_sem)
    local = Local(local_sem)
    samples, count, width = atoms.shape
    half_atoms = count // 2
    batch = atoms_ref.shape[0] // MICRO
    parts = cond_w.shape[0]
    loads = [local.start(cond_w_ref.at[i], cond_w.at[i]) for i in range(parts)]
    pieces = 2
    pair_rows_in = pair.shape[0]
    each = pair_rows_in // pieces
    pair_first = links.core * pair_rows_in
    pair_loads = [
        local.start(
            pair_ref.at[pl.ds(pair_first + i * each, each)], pair.at[pl.ds(i * each, each)]
        )
        for i in range(pieces)
    ]
    own_first = links.section * batch + links.mp * samples
    other_first = links.section * batch + (1 - links.mp) * samples
    own_half = pl.ds(pl.multiple_of(links.mp * half_atoms, 16), half_atoms)
    groups_in = rel_own.shape[0]
    own_groups = pl.ds(links.mp * groups_in, groups_in)
    lane = lax.broadcasted_iota(jnp.int32, rel_own.shape[1:], 1) % (SPAN * QBLOCK)
    for i in range(groups_in):
        starts = jnp.where(lane < QBLOCK, start_ref[SPAN * i], start_ref[SPAN * i + 1])
        rel_own[i] = starts - key_base(links.mp * groups_in + i, count)
    heads = pair_w_ref.shape[0]
    atom_loads = [
        local.start(atoms_ref.at[pl.ds(own_first, samples)], atoms.at[:, own_half, :]),
        local.start(rel_own, rel.at[own_groups]),
        local.start(pair_w_ref, pair_w.at[0]),
    ]
    links.barrier()
    pair_w_copy = links.send(pair_w_ref, pair_w.at[1], links.y)
    rel_copy = links.send(rel_own, rel.at[own_groups], links.y)
    atom_copy = links.send(
        atoms_ref.at[pl.ds(other_first, samples)], atoms.at[:, own_half, :], links.y
    )
    flow = Flow([])
    flow.free["y"] = samples * half_atoms * width * 2 / Flow.RATES["y"]
    for way, parts_in, own, other, chunks in (
        (fetch_eighths, 8, in_a_ref, in_b_ref, 2),
        (fetch_journey, 4, out_a_ref, out_b_ref, 1),
        (fetch_eighths, 8, up_a_ref, up_b_ref, 2),
        (fetch_journey, 4, down_a_ref, down_b_ref, 2),
    ):
        for i in range(chunks):
            flow.add(way(links, own, other, i, own.shape[0] // parts_in // chunks))

    trunk = trunk_ref[...].astype(WIDE)
    rows = trunk.shape[0]
    for s in range(samples):
        level_rows = lax.broadcasted_iota(jnp.int32, level_ref.shape, 0)
        level = jnp.where(level_rows == noise_ref[own_first + s], level_ref[...].astype(WIDE), 0.0)
        normed, _ = layer_norm(trunk + jnp.sum(level, 0, keepdims=True))
        low_ref[s * rows : (s + 1) * rows, :] = normed.astype(LOW)
    for i in range(parts):
        loads[i].wait()
        value = mul(low_ref[...], cond_w[i]) + cond_b_ref[i % 3, i // 3 : i // 3 + 1, :].astype(WIDE)
        cond_out[i] = value if i % 3 == 1 else sigmoid(value)
        target = (cond_a_ref, cond_b_out_ref)[i // 3]
        local.store(cond_out.at[i], target.at[i % 3])
    flow.after(5.0)

    atom_loads[2].wait()
    pair_w_copy.wait()
    weight = jnp.concatenate([pair_w[0], pair_w[1]], 0)
    block = 8
    for piece in range(pieces):
        pair_loads[piece].wait()

        def pair_rows(i, carry):
            at = pl.multiple_of(i * block, block)
            normed, _ = layer_norm(pair[pl.ds(at, block)].astype(WIDE))
            low = normed.astype(LOW)
            pair[pl.ds(at, block)] = low
            for j in range(block):
                bias[:, pl.ds(pair_first + at + j, 1), :] = mul_nt(weight, low[j])[:, None, :]
            return carry

        lax.fori_loop(piece * each // block, (piece + 1) * each // block, pair_rows, 0)
        at = pl.ds(piece * each, each)
        local.store(pair.at[at], low_pair_ref.at[at])
        flow.after(3.6)
    own_rows = pl.ds(pl.multiple_of(pair_first, 8), pair_rows_in)
    bias_copy = links.send(bias.at[:, own_rows, :], bias.at[:, own_rows, :], links.twin)

    for copy in (atom_loads[0], atom_loads[1], rel_copy, atom_copy):
        copy.wait()
    local.store(atoms, atoms_out_ref)
    bias_copy.wait()
    local.store(bias, bias_ref)
    groups, keys_in = probs.shape[1], probs.shape[2]
    queries_in = SPAN * QBLOCK
    scale = (width // ATOM_HEADS) ** (-0.5)
    place = lax.broadcasted_iota(jnp.int32, (keys_in, ATOM_HEADS * queries_in), 0)
    chunk = 256
    ids = lax.broadcasted_iota(jnp.int32, (total.shape[0], chunk), 0)
    for s in range(samples):
        normed, _ = layer_norm(atoms[s].astype(WIDE))
        hidden = (normed * gain_ref[...].astype(WIDE)).astype(LOW)
        qkv[s] = mul(hidden, joined(qkv_w_ref)).astype(LOW)
        local.store(qkv.at[s], qkv_ref.at[s])
        flow.after(1.7)

        def attend(group, carry, s=s):
            base = key_base(group, count)
            first = pl.multiple_of(group * queries_in, queries_in)
            queries = spread(qkv[s, pl.ds(first, queries_in), :width], ATOM_HEADS)
            keys = qkv[s, pl.ds(base, keys_in), width : 2 * width]
            values = qkv[s, pl.ds(base, keys_in), 2 * width :]
            offset = place - rel[group]
            scores = mul_nt(keys, queries) * scale
            scores = jnp.where((offset >= 0) & (offset < KWIN), scores, -1e30)
            exps = jnp.exp(scores - jnp.max(scores, 0, keepdims=True))
            low = (exps * (1.0 / jnp.sum(exps, 0, keepdims=True))).astype(LOW)
            probs[s, group] = low
            mixed[s, pl.ds(first, queries_in), :] = gather_heads(
                mul_tn(low, values), ATOM_HEADS
            ).astype(LOW)
            return carry

        cuts = 4
        for i in range(cuts):
            lax.fori_loop(groups * i // cuts, groups * (i + 1) // cuts, attend, 0)
            flow.after(2.5)
        local.store(probs.at[s], probs_ref.at[s])
        local.store(mixed.at[s], mixed_ref.at[s])
        for i in range(count // chunk):
            rows = slice(i * chunk, (i + 1) * chunk)
            after = atoms[s, rows, :].astype(WIDE) + mul(mixed[s, rows, :], out_w_ref[...])
            pre = mul(after.astype(LOW), agg_w_ref[...])
            units = (pre * sigmoid(pre)).astype(LOW)
            member = jnp.where(ids == ids_ref[:, rows], 1.0, 0.0).astype(LOW)
            part_sum = mul(member, units)
            if i == 0:
                total[...] = part_sum
            else:
                total[...] += part_sum
            if s == 0:
                number = jnp.sum(member.astype(WIDE), 1, keepdims=True)
                counts = number if i == 0 else counts + number
            flow.after(1.2)
        if s == 0:
            inv_ref[...] = 1.0 / counts
        tokens[s] = (total[...] * inv_ref[...]).astype(LOW)
        local.store(tokens.at[s], tokens_ref.at[s])
    flow.finish()
    local.finish()


def front(
    trunk, noise, levels, cond_w, cond_b, pair, pair_w, atoms, gain, qkv_w, out_w, agg_w, starts,
    ids, in_a, out_a, up_a, down_a,
):
    tokens_in, width = trunk.shape
    parts, wide = cond_w.shape[0], cond_w.shape[2]
    samples = atoms.shape[0] // MICRO // 2
    rows = samples * tokens_in
    count, atom_width = 2 * atoms.shape[1], atoms.shape[2]
    heads = 2 * pair_w.shape[0]
    groups = count // (SPAN * QBLOCK)
    keys_in, lanes = KWIN + SPAN * QBLOCK, ATOM_HEADS * SPAN * QBLOCK
    probs_shape = (samples, groups, keys_in, lanes)
    half_pair = (pair.shape[0] // 2,) + pair.shape[1:]
    hbm, near = pl.BlockSpec(memory_space=pl.ANY), pl.BlockSpec(memory_space=pltpu.VMEM)
    smem = pl.BlockSpec(memory_space=pltpu.SMEM)
    outs = [
        (near, (rows, width), LOW),
        (hbm, (parts // 2, rows, wide), WIDE),
        (hbm, (parts // 2, rows, wide), WIDE),
        (hbm, half_pair, LOW),
        (hbm, (heads, tokens_in, tokens_in), WIDE),
        (hbm, (samples, count, atom_width), LOW),
        (hbm, (samples, count, 3 * atom_width), LOW),
        (hbm, probs_shape, LOW),
        (hbm, (samples, count, atom_width), LOW),
        (hbm, (samples, tokens_in, wide), LOW),
        (hbm, in_a.shape, LOW),
        (hbm, out_a.shape, LOW),
        (hbm, up_a.shape, LOW),
        (hbm, down_a.shape, LOW),
        (near, (tokens_in, 1), WIDE),
    ]
    copies = 4 + 4 * 8 + 3 * 4
    return pl.pallas_call(
        front_kernel,
        in_specs=[near, smem, near, hbm, near, hbm, near, hbm] + [near] * 4 + [smem, near] + [hbm] * 4,
        out_specs=[spec for spec, _, _ in outs],
        out_shape=[sds(shape, dtype) for _, shape, dtype in outs],
        scratch_shapes=[
            pltpu.VMEM(cond_w.shape, LOW),
            pltpu.VMEM((parts, rows, wide), WIDE),
            pltpu.VMEM(half_pair, LOW),
            pltpu.VMEM((2,) + pair_w.shape, LOW),
            pltpu.VMEM((heads, tokens_in, tokens_in), WIDE),
            pltpu.VMEM((samples, count, atom_width), LOW),
            pltpu.VMEM((groups // 2, 1, lanes), jnp.int32),
            pltpu.VMEM((groups, 1, lanes), jnp.int32),
            pltpu.VMEM((samples, count, 3 * atom_width), LOW),
            pltpu.VMEM(probs_shape, LOW),
            pltpu.VMEM((samples, count, atom_width), LOW),
            pltpu.VMEM((tokens_in, wide), WIDE),
            pltpu.VMEM((samples, tokens_in, wide), LOW),
            pltpu.SemaphoreType.DMA((64,)),
            pltpu.SemaphoreType.DMA((copies,)),
            pltpu.SemaphoreType.DMA((copies,)),
        ],
        compiler_params=remote_params(60, 3),
        cost_estimate=cost(40e9, 40e6),
        name="front",
    )(
        trunk, noise, levels, cond_w, cond_b, pair, pair_w, atoms, gain, qkv_w, out_w, agg_w,
        starts, ids, in_a, out_a, up_a, down_a,
    )


def token_attention_kernel(
    tokens_ref, cond_ref, bias_ref, in_a_ref, in_b_ref, out_a_ref, out_b_ref,
    inner_ref, qkv_ref, sig_ref, heads_ref, gated_ref, probs_ref, attn_ref, middle_ref,
    tokens, cond, bias, in_a, in_b, out_a, out_b, inner, qkv, sig, heads_out, gated, probs, attn,
    middle, local_sem,
):
    local = Local(local_sem)
    load_tokens = local.start(tokens_ref, tokens)
    load_cond = local.start(cond_ref, cond)
    load_in = [local.start(in_a_ref, in_a)]
    load_bias = local.start(bias_ref, bias)
    load_in.append(local.start(in_b_ref, in_b))
    load_out = [local.start(out_a_ref, out_a), local.start(out_b_ref, out_b)]
    samples, heads, count = probs.shape[0], probs.shape[1], probs.shape[2]
    width_in = in_a.shape[1] // 4
    size = 2 * width_in // heads
    scale = size ** (-0.5)
    load_tokens.wait()
    load_cond.wait()
    wide = tokens[...].astype(WIDE)
    normed, _ = layer_norm(wide)
    inner[...] = (normed * cond[0] + cond[1]).astype(LOW)
    local.store(inner, inner_ref)
    for half, weight in enumerate((in_a, in_b)):
        load_in[half].wait()
        qkv[half] = mul(inner[...], weight[:, : 3 * width_in]).astype(LOW)
        local.store(qkv.at[half], qkv_ref.at[half])
        sig[half] = sigmoid(mul(inner[...], weight[:, 3 * width_in :]))
        local.store(sig.at[half], sig_ref.at[half])
        if half == 0:
            load_bias.wait()
        for s in range(samples):
            at = slice(s * count, (s + 1) * count)
            outs = []
            for h in range(heads // 2):
                col = h * size
                query = qkv[half, at, col : col + size]
                key = qkv[half, at, width_in + col : width_in + col + size]
                value = qkv[half, at, 2 * width_in + col : 2 * width_in + col + size]
                scores = mul_nt(query, key) * scale + bias[half * (heads // 2) + h]
                exps = jnp.exp(scores - jnp.max(scores, -1, keepdims=True))
                low = (exps * (1.0 / jnp.sum(exps, -1, keepdims=True))).astype(LOW)
                probs[s, half * (heads // 2) + h] = low
                outs.append(mul(low, value))
            heads_out[half, at, :] = jnp.concatenate(outs, 1)
        gated[half] = (heads_out[half] * sig[half]).astype(LOW)
        local.store(heads_out.at[half], heads_ref.at[half])
        local.store(gated.at[half], gated_ref.at[half])
    local.store(probs, probs_ref)
    load_out[0].wait()
    load_out[1].wait()
    attn[...] = mul(gated[0], out_a[...]) + mul(gated[1], out_b[...])
    local.store(attn, attn_ref)
    middle[...] = wide + cond[2] * attn[...]
    local.store(middle, middle_ref)
    local.finish()


def token_attention(tokens, cond, bias, in_a, in_b, out_a, out_b):
    rows, width = tokens.shape
    heads, count = bias.shape[0], bias.shape[1]
    samples, width_in = rows // count, in_a.shape[1] // 4
    hbm = pl.BlockSpec(memory_space=pl.ANY)
    outs = [
        sds((rows, width), LOW),
        sds((2, rows, 3 * width_in), LOW),
        sds((2, rows, width_in), WIDE),
        sds((2, rows, width_in), WIDE),
        sds((2, rows, width_in), LOW),
        sds((samples, heads, count, count), LOW),
        sds((rows, width), WIDE),
        sds((rows, width), WIDE),
    ]
    args = (tokens, cond, bias, in_a, in_b, out_a, out_b)
    return pl.pallas_call(
        token_attention_kernel,
        in_specs=[hbm] * len(args),
        out_specs=[hbm] * len(outs),
        out_shape=outs,
        scratch_shapes=[
            *(pltpu.VMEM(a.shape, a.dtype) for a in args),
            *(pltpu.VMEM(a.shape, a.dtype) for a in outs),
            pltpu.SemaphoreType.DMA((32,)),
        ],
        compiler_params=params(60),
        cost_estimate=cost(40e9, 20e6),
        name="token_attention",
    )(*args)


CHUNK = 192
MLP_CHUNKS = (192,) * 6
MLP_X_FIRST = (True, True, False, True, True, True)
EARLY = 2
COND_CHUNKS = (192,) * 3
ATTN_CHUNKS = (192,) * 5
ORDER = (
    ("attn", False), ("attn", True), ("cond", True), ("cond", True), ("attn", True),
    ("cond", False), ("attn", True), ("attn", True),
)


def relative(half, mp):
    return mp if half == 0 else 1 - mp


def token_back_kernel(
    middle_ref, cond_b_ref, cotangent_ref, low_ref, up_a_ref, up_b_ref, down_a_ref, down_b_ref,
    tokens_ref, cond_a_ref, attn_ref, inner_ref, qkv_ref, sig_ref, heads_ref, gated_ref, probs_ref,
    in_a_ref, in_b_ref, out_a_ref, out_b_ref,
    result_ref, other_result_ref, token_grad_ref, grads_ref, cond_bias_a_ref, cond_bias_b_ref,
    bias_grad_ref, mlp_out_ref, mlp_part_ref,
    middle, cond, grad, low, weight, out_weight, up, hidden, mlp_grads, middle_grad, result,
    tokens, inner, qkv, sig, heads_out, gated, probs, grads, bias_grad, proj, heads_grad, *rest,
):
    *buffers, local_sem, send_sem, recv_sem = rest
    links = Links(send_sem, recv_sem)
    local = Local(local_sem)
    load_first = [
        local.start(a, b)
        for a, b in ((middle_ref, middle), (cond_b_ref, cond), (up_a_ref, weight.at[0]))
    ]
    load_up_b = local.start(up_b_ref, weight.at[1])
    load_down = [local.start(down_a_ref, out_weight.at[0])]
    load_down.append(local.start(down_b_ref, out_weight.at[1]))
    samples, tokens_in = probs.shape[0], probs.shape[2]
    batch = cotangent_ref.shape[0] // MICRO
    load_grad = [local.start(low_ref, low)]
    for s in range(samples):
        sample = links.section * batch + links.mp * samples + s
        at = pl.ds(s * tokens_in, tokens_in)
        load_grad.append(local.start(cotangent_ref.at[sample], grad.at[at, :]))
    load_later = [
        local.start(a, b)
        for a, b in (
            (gated_ref, gated), (sig_ref, sig), (heads_ref, heads_out), (qkv_ref, qkv),
            (probs_ref, probs), (inner_ref, inner), (tokens_ref, tokens),
        )
    ]
    links.barrier()
    flow = Flow([])
    rows, width = middle.shape
    half_cols = width // 2
    samples, heads, count = probs.shape[0], probs.shape[1], probs.shape[2]

    for copy in load_first:
        copy.wait()
    middle_value = middle[...]
    normed, inverse = layer_norm(middle_value)
    scale, gate = cond[0], cond[2]
    inner_mlp = (normed * scale + cond[1]).astype(LOW)
    mlp_width = hidden.shape[2]
    mlp = None
    for half in range(2):
        if half == 1:
            load_up_b.wait()
        gate_in = mul(inner_mlp, weight[half, :, :mlp_width])
        up_in = mul(inner_mlp, weight[half, :, mlp_width:])
        up[half, :, :mlp_width] = gate_in.astype(LOW)
        up[half, :, mlp_width:] = up_in.astype(LOW)
        hidden[half] = (gate_in * sigmoid(gate_in) * up_in).astype(LOW)
        load_down[half].wait()
        add = mul(hidden[half], out_weight[half])
        mlp = add if mlp is None else mlp + add
    result[...] = (middle_value + gate * mlp).astype(LOW)
    local.store(result, result_ref)
    result_copy = links.send(result, other_result_ref, links.y)
    flow.free["y"] = rows * width * 2 / Flow.RATES["y"]

    for copy in load_grad:
        copy.wait()
    grad_value = grad[...].astype(WIDE)
    mlp_grad = (grad_value * gate).astype(LOW)
    core_rows = mlp_grads.shape[2] // 2
    down_rows = mlp_width // 2
    for half in range(2):
        hidden_t = hidden[half].T
        for core in range(2):
            for sec in range(2):
                mlp_grads[half, sec, core * core_rows : core * core_rows + down_rows, :] = mul(
                    hidden_t[core * down_rows : (core + 1) * down_rows],
                    mlp_grad[:, sec * half_cols : (sec + 1) * half_cols],
                ).astype(LOW)

    pool = Pool(buffers)

    def launch(first, last):
        for i in range(first, last):
            early = i < EARLY
            taken = pool.take(3 + (far_slots() if early else 0))
            part = None if early else mlp_part_ref.at[i - EARLY]
            flow.add(
                journey(
                    links, mlp_grads, None, taken, mlp_out_ref, None,
                    offsets(MLP_CHUNKS)[i], MLP_CHUNKS[i], MLP_X_FIRST[i], False, part,
                )
            )

    launch(0, down_rows // CHUNK)
    inner_t = inner_mlp.T
    inner_grad = None
    for half in range(2):
        hidden_grad = mul_nt(mlp_grad, out_weight[half])
        gate_in = up[half, :, :mlp_width].astype(WIDE)
        up_in = up[half, :, mlp_width:].astype(WIDE)
        sigma = sigmoid(gate_in)
        first = (hidden_grad * up_in * (sigma * (1.0 + gate_in * (1.0 - sigma)))).astype(LOW)
        second = (hidden_grad * (gate_in * sigma)).astype(LOW)
        up_grad = jnp.concatenate([first, second], 1)
        for sec in range(2):
            at = slice(sec * half_cols, (sec + 1) * half_cols)
            for block in range(4):
                place = block // 2 * core_rows + down_rows + block % 2 * half_cols
                mlp_grads[half, sec, place : place + half_cols, :] = mul(
                    inner_t[at], up_grad[:, block * half_cols : (block + 1) * half_cols]
                ).astype(LOW)
        add = mul_nt(up_grad, weight[half])
        inner_grad = add if inner_grad is None else inner_grad + add
        flow.after(3.0)
    load_weight = [local.start(in_a_ref, weight.at[0]), local.start(in_b_ref, weight.at[1])]
    out_rows = out_a_ref.shape[0]
    load_out = [
        local.start(a, out_weight.at[h, :out_rows, :]) for h, a in enumerate((out_a_ref, out_b_ref))
    ]
    launch(down_rows // CHUNK, core_rows // CHUNK)
    middle_grad[...] = grad_value + norm_back(normed, inverse, inner_grad * scale)
    low_t = low[...].T
    first_cond = grads.shape[2] - 3 * low_t.shape[0]

    def cond_back(sec, pieces, bias_out):
        for k, piece in enumerate(pieces):
            piece = piece.astype(LOW)
            place = first_cond + k * low_t.shape[0]
            for h in range(2):
                grads[relative(h, links.mp), sec, place : place + low_t.shape[0], :] = mul(
                    low_t, piece[:, h * half_cols : (h + 1) * half_cols]
                ).astype(LOW)
            bias_out[k] = jnp.sum(piece.astype(WIDE), 0, keepdims=True)

    cond_back(
        1,
        (
            inner_grad * normed * (scale * (1.0 - scale)),
            inner_grad,
            grad_value * mlp * (gate * (1.0 - gate)),
        ),
        cond_bias_b_ref,
    )
    load_cond = local.start(cond_a_ref, cond)
    load_attn = local.start(attn_ref, middle)
    flow.after(3.0)

    local_cols = out_rows
    size = 2 * local_cols // heads
    head_scale = size ** (-0.5)
    load_cond.wait()
    for copy in load_later:
        copy.wait()
    scale, gate = cond[0], cond[2]
    attn_grad = (middle_grad[...] * gate).astype(LOW)
    inner_t = inner[...].T
    inner_grad = None
    for half in range(2):
        load_out[half].wait()
        gated_t = gated[half].T
        for sec in range(2):
            grads[half, sec, 4 * half_cols : first_cond, :] = mul(
                gated_t, attn_grad[:, sec * half_cols : (sec + 1) * half_cols]
            ).astype(LOW)
        gated_grad = mul_nt(attn_grad, out_weight[half, :out_rows, :])
        sig_half = sig[half]
        with_sig = gated_grad * sig_half
        heads_grad[...] = with_sig.astype(LOW)
        proj[:, 3 * local_cols :] = (with_sig * heads_out[half] * (1.0 - sig_half)).astype(LOW)
        flow.after(1.5)
        for s in range(samples):
            at = slice(s * count, (s + 1) * count)
            parts = ([], [], [])
            for h in range(heads // 2):
                col, index = h * size, half * (heads // 2) + h
                query = qkv[half, at, col : col + size]
                key = qkv[half, at, local_cols + col : local_cols + col + size]
                value = qkv[half, at, 2 * local_cols + col : 2 * local_cols + col + size]
                one_grad = heads_grad[at, col : col + size]
                probs_low = probs[s, index]
                wide_probs = probs_low.astype(WIDE)
                probs_grad = mul_nt(one_grad, value)
                mean = jnp.sum(wide_probs * probs_grad, -1, keepdims=True)
                scores_grad = (wide_probs * (probs_grad - mean)).astype(LOW)
                if s == 0:
                    bias_grad[index] = scores_grad.astype(WIDE)
                else:
                    bias_grad[index] += scores_grad.astype(WIDE)
                parts[0].append(mul(scores_grad, key) * head_scale)
                parts[1].append(mul_tn(scores_grad, query) * head_scale)
                parts[2].append(mul_tn(probs_low, one_grad))
                if h % 2 == 1:
                    flow.after(1.0)
            for k in range(3):
                proj[at, k * local_cols : (k + 1) * local_cols] = jnp.concatenate(
                    parts[k], 1
                ).astype(LOW)
        load_weight[half].wait()
        for sec in range(2):
            for k in range(4):
                grads[half, sec, k * half_cols : (k + 1) * half_cols, :] = mul(
                    inner_t[sec * half_cols : (sec + 1) * half_cols],
                    proj[:, k * local_cols : (k + 1) * local_cols],
                ).astype(LOW)
        local.store(grads.at[half, :, :first_cond, :], grads_ref.at[half, :, :first_cond, :])
        some = pl.ds(half * (heads // 2), heads // 2)
        local.store(bias_grad.at[some], bias_grad_ref.at[some])
        add = mul_nt(proj[...], weight[half])
        inner_grad = add if inner_grad is None else inner_grad + add
        flow.after(2.5)
    normed, inverse = layer_norm(tokens[...].astype(WIDE))
    tokens[...] = (middle_grad[...] + norm_back(normed, inverse, inner_grad * scale)).astype(LOW)
    local.store(tokens, token_grad_ref)
    flow.after(1.0)
    load_attn.wait()
    cond_back(
        0,
        (
            inner_grad * normed * (scale * (1.0 - scale)),
            inner_grad,
            middle_grad[...] * middle[...] * (gate * (1.0 - gate)),
        ),
        cond_bias_a_ref,
    )
    local.store(grads.at[:, :, first_cond:, :], grads_ref.at[:, :, first_cond:, :])

    flow.finish()
    result_copy.wait()
    local.finish()


def token_back(
    middle, cond_b, cotangent, low, up_a, up_b, down_a, down_b, tokens, cond_a, attn, inner, qkv,
    sig, heads_out, gated, probs, in_a, in_b, out_a, out_b,
):
    rows, width = tokens.shape
    heads, count = probs.shape[1], probs.shape[2]
    mlp_width, local_cols, half = down_a.shape[0], out_a.shape[0], width // 2
    mlp_rows = 4 * half + mlp_width
    grad_rows = 4 * half + local_cols + 3 * low.shape[1]
    chunks = mlp_rows // 2 // CHUNK
    copies = chunks * journey_copies(False) + 1
    hbm, near = pl.BlockSpec(memory_space=pl.ANY), pl.BlockSpec(memory_space=pltpu.VMEM)
    args = (
        middle, cond_b, cotangent, low, up_a, up_b, down_a, down_b, tokens, cond_a, attn, inner,
        qkv, sig, heads_out, gated, probs, in_a, in_b, out_a, out_b,
    )
    outs = [
        (hbm, (rows, width), LOW),
        (hbm, (rows, width), LOW),
        (hbm, (rows, width), LOW),
        (hbm, (2, 2, grad_rows, half), LOW),
        (near, (3, 1, width), WIDE),
        (near, (3, 1, width), WIDE),
        (hbm, (heads, count, count), WIDE),
        (near, (2 * EARLY * CHUNK, half), LOW),
        (near, (chunks - EARLY, CHUNK, half), LOW),
    ]
    scratch = [
        (middle.shape, WIDE),
        (cond_b.shape, WIDE),
        ((rows, width), LOW),
        (low.shape, LOW),
        ((2,) + up_a.shape, LOW),
        ((2,) + down_a.shape, LOW),
        ((2, rows, 2 * mlp_width), LOW),
        ((2, rows, mlp_width), LOW),
        ((2, 2, mlp_rows, half), LOW),
        (middle.shape, WIDE),
        ((rows, width), LOW),
        *((a.shape, a.dtype) for a in (tokens, inner, qkv, sig, heads_out, gated, probs)),
        ((2, 2, grad_rows, half), LOW),
        ((heads, count, count), WIDE),
        ((rows, 4 * local_cols), LOW),
        ((rows, local_cols), LOW),
    ]
    return pl.pallas_call(
        token_back_kernel,
        in_specs=[hbm] * len(args),
        out_specs=[spec for spec, _, _ in outs],
        out_shape=[sds(shape, dtype) for _, shape, dtype in outs],
        scratch_shapes=[
            *(pltpu.VMEM(shape, dtype) for shape, dtype in scratch),
            *journey_scratch(CHUNK, half) * EARLY,
            *near_scratch(CHUNK, half) * (chunks - EARLY),
            pltpu.SemaphoreType.DMA((64,)),
            pltpu.SemaphoreType.DMA((copies,)),
            pltpu.SemaphoreType.DMA((copies,)),
        ],
        compiler_params=remote_params(62, 1),
        cost_estimate=cost(90e9, 50e6),
        name="token_back",
    )(*args)


FIRST_ROWS, LAST_ROWS = 128, 64


def atom_back_kernel(
    atoms_hbm, gain_ref, qkv_w_ref, out_w_ref, agg_w_ref, ids_ref, inv_ref,
    qkv_hbm, probs_hbm, mixed_hbm, grad_ref, pair_ref, bias_grad_hbm, grads_ref, cond_bias_a_ref,
    cond_bias_b_ref, mlp_part_ref,
    keep_ref, got_ref, attn_out_ref, cond_out_ref, cond_other_ref,
    first_out_ref, first_other_ref, last_out_ref, last_other_ref, mlp_out_ref,
    pair, bias_grad, twin_bias, pair_grad, atoms_ref, qkv_ref, probs_ref, mixed_ref, kept_attn, kept_cond,
    after_grad, mixed_grad, key_grad, value_grad, proj_grad, atoms_grad, send_buffer,
    gain_grad, qkv_grad, out_grad, agg_grad, first_small, last_small, *rest,
):
    *buffers, local_sem, send_sem, recv_sem = rest
    links = Links(send_sem, recv_sem)
    local = Local(local_sem)
    samples, atoms, width = atoms_ref.shape
    groups, keys_in = probs_ref.shape[1], probs_ref.shape[2]
    queries_in = SPAN * QBLOCK
    scale = (width // ATOM_HEADS) ** (-0.5)
    cond_rows = cond_out_ref.shape[0]
    attn_rows = grads_ref.shape[2] - cond_rows
    attn_grads = grads_ref.at[:, :, :attn_rows, :]
    cond_grads = grads_ref.at[:, :, attn_rows:, :]
    pair_half = bias_grad.shape[1]
    own_rows = pl.ds(pl.multiple_of(links.core * pair_half, 8), pair_half)
    twin_rows = pl.ds(pl.multiple_of((1 - links.core) * pair_half, 8), pair_half)
    load_bias = local.start(bias_grad_hbm.at[:, own_rows, :], bias_grad)

    def load_kept(source, target):
        start = links.core * (source.shape[2] // 2)
        at = pl.ds(pl.multiple_of(start, 16), target.shape[2])
        return local.start(source.at[:, :, at, :], target)

    kept_loads = [load_kept(attn_grads, kept_attn), load_kept(cond_grads, kept_cond)]
    loads = [local.start(mixed_hbm, mixed_ref), local.start(atoms_hbm, atoms_ref)]
    later = [
        (local.start(qkv_hbm.at[s], qkv_ref.at[s]), local.start(probs_hbm.at[s], probs_ref.at[s]))
        for s in range(samples)
    ]
    links.barrier()
    bias_copy = links.send(bias_grad_hbm.at[:, twin_rows, :], twin_bias, links.twin)
    pool, each = Pool(buffers), 3 + far_slots()
    flow = Flow([])
    for i in range(mlp_part_ref.shape[0]):
        held, *slots = pool.take(each - 2)
        held[...] = mlp_part_ref[i]
        offset = i * mlp_part_ref.shape[1]
        flow.add(far_journey(links, held, slots, mlp_out_ref, None, offset, False))
    sums = {
        "attn": (attn_grads, kept_attn, attn_out_ref, None, ATTN_CHUNKS),
        "cond": (cond_grads, kept_cond, cond_out_ref, cond_other_ref, COND_CHUNKS),
    }
    taken = {"attn": 0, "cond": 0}
    for kind, x_first in ORDER:
        source, kept, out, other, sizes = sums[kind]
        i = taken[kind]
        taken[kind] += 1
        flow.add(
            journey(
                links, source, kept, pool.take(each), out, other, offsets(sizes)[i], sizes[i],
                x_first, other is not None,
            )
        )
    for copy in kept_loads:
        copy.wait()

    load_bias.wait()
    bias_copy.wait()
    heads = pair_grad.shape[0]
    slots = pair.shape[0]
    block = pair.shape[1]
    blocks = pair_ref.shape[0] // block

    def load_pair(i):
        return local.start(pair_ref.at[pl.ds(i * block, block)], pair.at[i % slots])

    pair_loads = [load_pair(i) for i in range(slots)]
    total = jnp.zeros(pair_grad.shape, WIDE)
    for i in range(blocks):
        pair_loads[i].wait()
        for j in range(block):
            one = bias_grad[:, i * block + j, :] + twin_bias[:, i * block + j, :]
            high = one.astype(LOW)
            tail = (one - high.astype(WIDE)).astype(LOW)
            both = mul(jnp.concatenate([high, tail], 0), pair[i % slots, j])
            total += both[:heads] + both[heads:]
        if i + slots < blocks:
            pair_loads.append(load_pair(i + slots))
        flow.after(0.08 * block)
    pair_grad[...] = total
    for copy in loads:
        copy.wait()

    for ref in (gain_grad, qkv_grad, out_grad, agg_grad):
        ref[...] = jnp.zeros_like(ref)
    chunk = 256
    token_ids = lax.broadcasted_iota(jnp.int32, (grad_ref.shape[1], chunk), 0)
    atom_copies = []
    for s in range(samples):
        token_grad = (grad_ref[s].astype(WIDE) * inv_ref[...]).astype(LOW)
        for i in range(atoms // chunk):
            rows = slice(i * chunk, (i + 1) * chunk)
            mixed = mixed_ref[s, rows, :]
            after = atoms_ref[s, rows, :].astype(WIDE) + mul(mixed, out_w_ref[...])
            after_low = after.astype(LOW)
            pre = mul(after_low, agg_w_ref[...])
            sigma = sigmoid(pre)
            member = jnp.where(token_ids == ids_ref[:, rows], 1.0, 0.0).astype(LOW)
            unit_grad = mul_tn(member, token_grad)
            pre_grad = (unit_grad * (sigma * (1.0 + pre * (1.0 - sigma)))).astype(LOW)
            agg_grad[...] += mul_tn(after_low, pre_grad)
            after_back = mul_nt(pre_grad, agg_w_ref[...])
            after_grad[s, rows, :] = after_back
            branch = after_back.astype(LOW)
            out_grad[...] += mul_tn(mixed, branch)
            mixed_grad[s, rows, :] = mul_nt(branch, out_w_ref[...]).astype(LOW)
            flow.after(1.7)
    heads = pair_grad.shape[0]
    wide = agg_grad.shape[1] // 2
    rows, part_rows = width // 2, width // 4

    def fill(values, cols):
        if values.shape[1] == cols:
            return values
        empty = jnp.zeros((values.shape[0], cols - values.shape[1]), WIDE)
        return jnp.concatenate([values, empty], 1)

    for h in range(2):
        to = relative(h, links.mp)
        cols = slice(h * wide, (h + 1) * wide)
        own_pair = jnp.where(links.mp == h, pair_grad[: heads // 2], pair_grad[heads // 2 :])
        for sec, cond_bias_ref in enumerate((cond_bias_a_ref, cond_bias_b_ref)):
            first_small[to, sec, :rows, :] = agg_grad[sec * rows : (sec + 1) * rows, cols].astype(LOW)
            first_row = sec * rows + h * part_rows
            block = fill(out_grad[first_row : first_row + part_rows], wide)
            first_small[to, sec, rows : rows + part_rows, :] = block.astype(LOW)
            block = [cond_bias_ref[k, :, cols] for k in range(3)]
            block += [jnp.zeros((5, wide), WIDE), fill(own_pair, wide)]
            block += [jnp.zeros((part_rows - 16, wide), WIDE)]
            first_small[to, sec, rows + part_rows :, :] = jnp.concatenate(block, 0).astype(LOW)
    flow.add(
        journey(
            links, first_small, None, pool.take(each), first_out_ref, first_other_ref,
            0, FIRST_ROWS // 2, False, True,
        )
    )
    for s in range(samples):
        for copy in later[s]:
            copy.wait()
        key_grad[...] = jnp.zeros_like(key_grad)
        value_grad[...] = jnp.zeros_like(value_grad)

        def attend(group, carry, s=s):
            base = key_base(group, atoms)
            start = pl.multiple_of(group * queries_in, queries_in)
            queries = spread(qkv_ref[s, pl.ds(start, queries_in), :width], ATOM_HEADS)
            grads = spread(mixed_grad[s, pl.ds(start, queries_in), :], ATOM_HEADS)
            keys = qkv_ref[s, pl.ds(base, keys_in), width : 2 * width]
            values = qkv_ref[s, pl.ds(base, keys_in), 2 * width :]
            probs_low = probs_ref[s, group]
            probs = probs_low.astype(WIDE)
            probs_grad = mul_nt(values, grads)
            mean = jnp.sum(probs * probs_grad, 0, keepdims=True)
            scores_grad = (probs * (probs_grad - mean)).astype(LOW)
            query_grad = gather_heads(mul_tn(scores_grad, keys), ATOM_HEADS)
            proj_grad[pl.ds(start, queries_in), :width] = (query_grad * scale).astype(LOW)
            key_grad[pl.ds(base, keys_in), :] += mul(scores_grad, queries)
            value_grad[pl.ds(base, keys_in), :] += mul(probs_low, grads)
            return carry

        cuts = 5
        for i in range(cuts):
            lax.fori_loop(groups * i // cuts, groups * (i + 1) // cuts, attend, 0)
            flow.after(2.3)
        proj_grad[:, width : 2 * width] = (key_grad[...] * scale).astype(LOW)
        proj_grad[:, 2 * width :] = value_grad[...].astype(LOW)
        gain = gain_ref[...].astype(WIDE)
        normed, inverse = layer_norm(atoms_ref[s].astype(WIDE))
        hidden = (normed * gain).astype(LOW)
        proj = proj_grad[...]
        qkv_grad[...] += mul_tn(hidden, proj)
        hidden_grad = mul_nt(proj, joined(qkv_w_ref))
        gain_grad[...] += jnp.sum(hidden_grad * normed, 0, keepdims=True)
        atoms_grad[...] = after_grad[s] + norm_back(normed, inverse, hidden_grad * gain)
        half = atoms // 2
        theirs = pl.ds(pl.multiple_of((1 - links.mp) * half, 16), half)
        send_buffer[s] = atoms_grad[theirs, :].astype(LOW)
        atom_copies.append(links.send(send_buffer.at[s], got_ref.at[s], links.y))
        keep_ref[s] = atoms_grad[pl.ds(pl.multiple_of(links.mp * half, 16), half), :]
        flow.after(2.5)

    for h in range(2):
        to = relative(h, links.mp)
        for sec in range(2):
            first_row = sec * rows + h * part_rows
            part = fill(qkv_grad[first_row : first_row + part_rows], wide)
            last_small[to, sec, :part_rows, :] = part.astype(LOW)
            block = [fill(gain_grad[...], wide), jnp.zeros((part_rows - 1, wide), WIDE)]
            last_small[to, sec, part_rows:, :] = jnp.concatenate(block, 0).astype(LOW)
    flow.add(
        journey(
            links, last_small, None, pool.take(each), last_out_ref, last_other_ref,
            0, LAST_ROWS // 2, False, True,
        )
    )
    flow.finish()
    for copy in atom_copies:
        copy.wait()


def atom_back(
    atoms, gain, qkv_w, out_w, agg_w, ids, inverse_counts, qkv, probs, mixed, grad,
    low_pair, bias_grad, grads, cond_bias_a, cond_bias_b, mlp_part, cond_rows,
):
    samples, count, width = atoms.shape
    wide = agg_w.shape[1]
    cols = grads.shape[3]
    attn_rows = grads.shape[2] - cond_rows
    copies = len(ATTN_CHUNKS) * journey_copies(False)
    copies += len(COND_CHUNKS) * journey_copies(True)
    copies += 2 * journey_copies(True) + samples + 1
    half_bias = (bias_grad.shape[0], bias_grad.shape[1] // 2, bias_grad.shape[2])
    copies += mlp_part.shape[0] * journey_copies(False, near=0)
    outs = [
        sds((samples, count // 2, width), WIDE),
        sds((samples, count // 2, width), LOW),
        sds((attn_rows, cols), LOW),
        sds((cond_rows, cols), LOW),
        sds((cond_rows, cols), LOW),
        sds((FIRST_ROWS, cols), LOW),
        sds((FIRST_ROWS, cols), LOW),
        sds((LAST_ROWS, cols), LOW),
        sds((LAST_ROWS, cols), LOW),
        sds((2 * mlp_part.shape[0] * CHUNK, cols), LOW),
    ]
    args = (
        atoms, gain, qkv_w, out_w, agg_w, ids, inverse_counts, qkv, probs, mixed, grad,
        low_pair, bias_grad, grads, cond_bias_a, cond_bias_b, mlp_part,
    )
    hbm, near = pl.BlockSpec(memory_space=pl.ANY), pl.BlockSpec(memory_space=pltpu.VMEM)
    return pl.pallas_call(
        atom_back_kernel,
        in_specs=[hbm] + [near] * 6 + [hbm] * 3 + [near] + [hbm] * 3 + [near] * 3,
        out_specs=everywhere(len(outs)),
        out_shape=outs,
        scratch_shapes=[
            pltpu.VMEM((2, 8) + low_pair.shape[1:], LOW),
            pltpu.VMEM(half_bias, WIDE),
            pltpu.VMEM(half_bias, WIDE),
            pltpu.VMEM((bias_grad.shape[0], width), WIDE),
            *(pltpu.VMEM(a.shape, a.dtype) for a in (atoms, qkv, probs, mixed)),
            pltpu.VMEM((2, 2, attn_rows // 2, cols), LOW),
            pltpu.VMEM((2, 2, cond_rows // 2, cols), LOW),
            pltpu.VMEM((samples, count, width), WIDE),
            pltpu.VMEM((samples, count, width), LOW),
            pltpu.VMEM((count, width), WIDE),
            pltpu.VMEM((count, width), WIDE),
            pltpu.VMEM((count, 3 * width), LOW),
            pltpu.VMEM((count, width), WIDE),
            pltpu.VMEM((samples, count // 2, width), LOW),
            pltpu.VMEM((1, width), WIDE),
            pltpu.VMEM((width, 3 * width), WIDE),
            pltpu.VMEM((width, width), WIDE),
            pltpu.VMEM((width, wide), WIDE),
            pltpu.VMEM((2, 2, FIRST_ROWS, cols), LOW),
            pltpu.VMEM((2, 2, LAST_ROWS, cols), LOW),
            *([pltpu.VMEM((CHUNK, cols), LOW)] + far_scratch(CHUNK, cols)) * mlp_part.shape[0],
            *(b for _ in ORDER for b in journey_scratch(CHUNK, cols)),
            *journey_scratch(FIRST_ROWS // 2, cols),
            *journey_scratch(LAST_ROWS // 2, cols),
            pltpu.SemaphoreType.DMA((32,)),
            pltpu.SemaphoreType.DMA((copies,)),
            pltpu.SemaphoreType.DMA((copies,)),
        ],
        compiler_params=remote_params(60, 2),
        cost_estimate=cost(60e9, 24e6),
        name="atom_back",
    )(*args)


def results_kernel(*refs):
    number, count = 13, 13
    hbm_in, hbm_out = refs[:number], refs[number : number + count]
    scratch, sem = refs[number + count : -1], refs[-1]
    near_in, near_out = scratch[:number], scratch[number:]
    local = Local(sem)
    loads = [local.start(a, b) for a, b in zip(hbm_in, near_in)]
    (
        cond_ref, cond_other_ref, attn_ref, mlp_first_ref, mlp_late_ref, keep_ref, got_ref,
        result_ref, other_result_ref, first_ref, first_other_ref, last_ref, last_other_ref,
    ) = near_in
    (
        token_out, atoms_out, gain_out, qkv_out, out_out, agg_out, cond_out, cond_bias_out,
        pair_out, in_out, attn_out, up_out, down_out,
    ) = near_out
    mp, section = lax.axis_index("mp"), lax.axis_index("section")

    def wait(*indices):
        for index in indices:
            loads[index].wait()

    def store(*outs):
        for out in outs:
            index = [i for i, ref in enumerate(near_out) if ref is out][0]
            local.store(out, hbm_out[index])

    half = cond_ref.shape[1]
    size = cond_out.shape[1]
    wait(0, 1)
    for h in range(2):
        cols = slice(h * half, (h + 1) * half)
        for k in range(3):
            at = slice(k * size, (k + 1) * size)
            value = jnp.where(mp == h, cond_ref[at, :], cond_other_ref[at, :])
            cond_out[k, :, cols] = value.astype(WIDE)
    store(cond_out)
    wait(2)
    blocks = in_out.shape[1]
    for k in range(blocks):
        in_out[:, k, :] = attn_ref[k * half : (k + 1) * half, :].astype(WIDE)
    store(in_out)
    attn_out[...] = attn_ref[blocks * half :, :].astype(WIDE)
    store(attn_out)
    wait(3, 4)
    core_first, core_late = mlp_first_ref.shape[0] // 2, mlp_late_ref.shape[0] // 2
    down_rows = down_out.shape[0] // 2
    for core in range(2):
        at = slice(core * down_rows, (core + 1) * down_rows)
        start = core * core_first
        down_out[at, :] = mlp_first_ref[start : start + down_rows, :].astype(WIDE)
        row = 0
        for ref, begin, end in (
            (mlp_first_ref, start + down_rows, start + core_first),
            (mlp_late_ref, core * core_late, (core + 1) * core_late),
        ):
            while begin < end:
                block, within = row // half, row % half
                some = min(end - begin, half - within)
                up_out[within : within + some, core, block * half : (block + 1) * half] = ref[
                    begin : begin + some, :
                ].astype(WIDE)
                begin, row = begin + some, row + some
    store(up_out, down_out)
    wait(5, 6)
    samples = keep_ref.shape[0]
    here, there = pl.ds(mp * samples, samples), pl.ds((1 - mp) * samples, samples)
    atoms_out[here] = keep_ref[...]
    atoms_out[there] = got_ref[...].astype(WIDE)
    store(atoms_out)
    wait(7, 8)
    token_out[here] = result_ref[...]
    token_out[there] = other_result_ref[...]
    store(token_out)
    wait(9, 10, 11, 12)
    width, rows = atoms_out.shape[2], out_out.shape[0]
    part_rows = rows // 2

    def own_lanes(values):
        return jnp.where(section == 0, values[:, :rows], values[:, rows:width])

    gain_out[...] = own_lanes(last_ref[part_rows : part_rows + 16, :].astype(WIDE))[:1]
    pair = first_ref[rows + part_rows : rows + part_rows + 16, :].astype(WIDE)
    pair_out[...] = own_lanes(pair[8:])
    for h in range(2):
        first = jnp.where(mp == h, first_ref[...], first_other_ref[...]).astype(WIDE)
        last = jnp.where(mp == h, last_ref[...], last_other_ref[...]).astype(WIDE)
        cols = slice(h * half, (h + 1) * half)
        part_at = slice(h * part_rows, (h + 1) * part_rows)
        agg_out[:, cols] = first[:rows]
        out_out[part_at, :] = first[rows : rows + part_rows, :width]
        for k in range(3):
            row = rows + part_rows + k
            cond_bias_out[k, :, cols] = first[row : row + 1]
        for k in range(3):
            qkv_out[k, part_at, :] = last[:part_rows, k * width : (k + 1) * width]
    store(gain_out, pair_out, agg_out, out_out, cond_bias_out, qkv_out)
    local.finish()


def results(
    result, other_result, keep, got, first, first_other, last, last_other, cond, cond_other, attn,
    mlp_first, mlp_late, width, mlp_local,
):
    samples, half_atoms, atom_width = keep.shape
    half, rows = width // 2, atom_width // 2
    attn_local = attn.shape[0] - 4 * half
    hbm = pl.BlockSpec(memory_space=pl.ANY)
    outs = [
        sds((2 * samples,) + result.shape[1:], LOW),
        sds((2 * samples, half_atoms, atom_width), WIDE),
        sds((1, rows), WIDE),
        sds((3, rows, atom_width), WIDE),
        sds((rows, atom_width), WIDE),
        sds((rows, width), WIDE),
        sds((3, cond.shape[0] // 3, width), WIDE),
        sds((3, 1, width), WIDE),
        sds((8, rows), WIDE),
        sds((half, 4, attn_local), WIDE),
        sds((attn_local, half), WIDE),
        sds((half, 2, mlp_local), WIDE),
        sds((mlp_local, half), WIDE),
    ]
    args = (
        cond, cond_other, attn, mlp_first, mlp_late, keep, got, result, other_result, first,
        first_other, last, last_other,
    )
    return pl.pallas_call(
        results_kernel,
        in_specs=[hbm] * len(args),
        out_specs=[hbm] * len(outs),
        out_shape=outs,
        scratch_shapes=[
            *(pltpu.VMEM(a.shape, a.dtype) for a in args),
            *(pltpu.VMEM(a.shape, a.dtype) for a in outs),
            pltpu.SemaphoreType.DMA((32,)),
        ],
        compiler_params=params(60),
        cost_estimate=cost(1e8, 20e6),
        name="results",
    )(*args)


def local(
    atoms_in,
    atom_token,
    window_start,
    noise_level,
    level_table,
    single_trunk,
    pair,
    atom_gain,
    atom_qkv,
    atom_out,
    atom_agg,
    cond_weight,
    cond_bias,
    pair_weight,
    attn_in,
    attn_out,
    mlp_up,
    mlp_down,
    cotangent,
):
    section, mp = lax.axis_index("section"), lax.axis_index("mp")
    batch, half_atoms, atom_width = atoms_in.shape
    batch //= MICRO
    samples = batch // 2
    atoms = 2 * half_atoms
    tokens, width = cotangent.shape[1], cotangent.shape[2]
    single = single_trunk.shape[1]
    in_a = attn_in.reshape(width, -1)
    up_a = mlp_up.reshape(width, -1)
    gain = atom_gain[None, :]
    qkv_w = jnp.transpose(atom_qkv, (1, 0, 2))

    cond_w = jnp.transpose(cond_weight, (0, 2, 1, 3)).reshape(6, single, width)
    (
        low, cond_a, cond_b, low_pair, bias, all_atoms, qkv, probs, mixed, token_in,
        in_b, out_b, up_b, down_b, inverse_counts,
    ) = front(
        single_trunk, noise_level, level_table, cond_w, jnp.transpose(cond_bias, (1, 0, 2)), pair,
        pair_weight.T,
        atoms_in, gain, qkv_w, atom_out, atom_agg, window_start, atom_token[None, :],
        in_a, attn_out, up_a, mlp_down,
    )
    token_in = token_in.reshape(-1, width)
    inner, token_qkv, sig, heads_out, gated, token_probs, attn, middle = token_attention(
        token_in, cond_a, bias, in_a, in_b, attn_out, out_b
    )
    (
        result, other_result, token_grad, attn_grads, cond_bias_a, cond_bias_b, bias_grad, mlp_first,
        mlp_part,
    ) = (
        token_back(
            middle, cond_b, cotangent, low, up_a, up_b, mlp_down, down_b, token_in, cond_a, attn,
            inner, token_qkv, sig, heads_out, gated, token_probs, in_a, in_b, attn_out, out_b,
        )
    )
    (
        keep, got, attn_sum, cond_sum, cond_other, first, first_other, last, last_other, mlp_late,
    ) = atom_back(
        all_atoms, gain, qkv_w, atom_out, atom_agg, atom_token[None, :], inverse_counts,
        qkv, probs, mixed, token_grad.reshape(samples, tokens, width),
        low_pair, bias_grad, attn_grads, cond_bias_a, cond_bias_b, mlp_part, 3 * single,
    )

    outs = results(
        result.reshape(samples, tokens, width), other_result.reshape(samples, tokens, width),
        keep, got, first, first_other, last, last_other, cond_sum, cond_other, attn_sum,
        mlp_first, mlp_late, width, mlp_up.shape[2],
    )
    token_out, atoms_out, gain_out, qkv_out, out_out, agg_out, cond_out = outs[:7]
    cond_bias_out, pair_out, in_out, attn_out_grad, up_out, down_out = outs[7:]
    return (
        token_out.reshape(1, 1, batch, tokens, width),
        atoms_out.reshape(1, 1, batch, half_atoms, atom_width),
        gain_out[0],
        jnp.transpose(qkv_out, (1, 0, 2)),
        out_out,
        agg_out,
        jnp.transpose(cond_out, (1, 0, 2))[None],
        jnp.transpose(cond_bias_out, (1, 0, 2)),
        pair_out.T,
        in_out,
        attn_out_grad,
        up_out,
        down_out,
    )


def solution(mesh):
    in_specs = (
        P("dp", "mp", None),
        P(),
        P("mp"),
        P("dp"),
        P(),
        P(),
        P(),
        P(),
        P(),
        P(),
        P(),
        P(),
        P(),
        P(None, "mp"),
        P(None, None, "mp"),
        P("mp", None),
        P(None, None, "mp"),
        P("mp", None),
        P("dp", None, None),
    )
    out_specs = (
        P("dp", "section", None, None, None),
        P("dp", "section", None, "mp", None),
        P("section"),
        P("section", None, None),
        P("section", None),
        P("section", None),
        P("section", None, None, None),
        P("section", None, None),
        P("section", "mp"),
        P("section", None, "mp"),
        P("mp", "section"),
        P("section", None, "mp"),
        P("mp", "section"),
    )
    return jax.shard_map(local, mesh=mesh, in_specs=in_specs, out_specs=out_specs, check_vma=False)
```

```python
import functools

import jax
import jax.numpy as jnp
from jax import lax
from jax.experimental import pallas as pl
from jax.experimental.pallas import tpu as pltpu
from jax.sharding import PartitionSpec as P

QBLOCK = 32
KWIN = 128
MICRO = 2
ATOM_HEADS = 4
SPAN = 2
EPS = 1e-05
LOW = jnp.bfloat16
WIDE = jnp.float32
MIB = 1 << 20


def mul(left, right):
    return lax.dot_general(left, right, (((1,), (0,)), ((), ())), preferred_element_type=WIDE)


def mul_nt(left, right):
    return lax.dot_general(left, right, (((1,), (1,)), ((), ())), preferred_element_type=WIDE)


def mul_tn(left, right):
    return lax.dot_general(left, right, (((0,), (0,)), ((), ())), preferred_element_type=WIDE)


def layer_norm(values):
    center = values - jnp.mean(values, -1, keepdims=True)
    inverse = lax.rsqrt(jnp.mean(center * center, -1, keepdims=True) + EPS)
    return center * inverse, inverse


def norm_back(normed, inverse, grad):
    return inverse * (
        grad
        - jnp.mean(grad, -1, keepdims=True)
        - normed * jnp.mean(grad * normed, -1, keepdims=True)
    )


def sigmoid(values):
    return 1.0 / (1.0 + jnp.exp(-values))


def params(mib, semantics=None):
    return pltpu.CompilerParams(vmem_limit_bytes=mib * MIB, dimension_semantics=semantics)


def cost(flops, moved, exps=0):
    return pl.CostEstimate(flops=int(flops), bytes_accessed=int(moved), transcendentals=int(exps))


def sds(shape, dtype):
    return jax.ShapeDtypeStruct(shape, dtype)


def joined(ref):
    return jnp.concatenate([ref[k] for k in range(ref.shape[0])], 1)


def lane_heads(rows, width, size):
    return lax.broadcasted_iota(jnp.int32, (rows, width), 1) // size


def spread(values, heads):
    head = lane_heads(values.shape[0], values.shape[1], values.shape[1] // heads)
    zero = jnp.zeros_like(values)
    return jnp.concatenate([jnp.where(head == h, values, zero) for h in range(heads)], 0)


def gather_heads(values, heads):
    rows = values.shape[0] // heads
    head = lane_heads(rows, values.shape[1], values.shape[1] // heads)
    total = jnp.where(head == 0, values[:rows], 0.0)
    for h in range(1, heads):
        total += jnp.where(head == h, values[h * rows : (h + 1) * rows], 0.0)
    return total


def pairs(first, last, body):
    def step(i, carry):
        body(first + 2 * i, carry)
        body(first + 2 * i + 1, carry)
        return carry

    lax.fori_loop(0, (last - first) // 2, step, 0)
    if (last - first) % 2:
        body(last - 1, 0)


def key_base(group, atoms):
    start = group * SPAN * QBLOCK - KWIN // 2
    return pl.multiple_of(jnp.clip(start, 0, atoms - KWIN - (SPAN - 1) * QBLOCK - QBLOCK), QBLOCK)


def far_lines():
    bits = lax.axis_size("dp").bit_length() - 2
    return [(1 + b, 4 if b + 1 < bits else 2) for b in range(0, bits, 2)]


class Links:
    def __init__(self, send_sem, recv_sem, far=True):
        self.section, self.mp = lax.axis_index("section"), lax.axis_index("mp")
        self.dp = lax.axis_index("dp")
        self.core = self.dp % 2
        self.partners = [{"section": 1 - self.section}, {"mp": 1 - self.mp}]
        self.partners.append({"dp": self.dp + 1 - 2 * self.core})
        self.x, self.y, self.twin = self.partners
        self.lines = []
        for bit, count in far_lines() if far else ():
            place = self.dp // (1 << bit) % count
            beside = {"dp": self.dp + (1 - 2 * (place % 2)) * (1 << bit)}
            across = {"dp": self.dp + (count - 1 - 2 * place) * (1 << bit)}
            self.lines.append((count, place, beside, across))
            self.partners += [beside, across] if count == 4 else [beside]
        self.send_sem, self.recv_sem, self.used = send_sem, recv_sem, 0

    def barrier(self):
        barrier = pltpu.get_barrier_semaphore()
        for partner in self.partners:
            pl.semaphore_signal(
                barrier, inc=1, device_id=partner, device_id_type=pl.DeviceIdType.MESH
            )
        pl.semaphore_wait(barrier, len(self.partners))

    def copy(self, source, target, partner):
        copy = pltpu.make_async_remote_copy(
            src_ref=source,
            dst_ref=target,
            send_sem=self.send_sem.at[self.used],
            recv_sem=self.recv_sem.at[self.used],
            device_id=partner,
            device_id_type=pl.DeviceIdType.MESH,
        )
        self.used += 1
        return copy

    def send(self, source, target, partner):
        copy = self.copy(source, target, partner)
        copy.start()
        return copy


def far_copies():
    return sum(3 if count == 4 else 1 for _, count in far_lines())


def journey_copies(shared, near=3):
    return near + far_copies() + 1 + (2 if shared else 0)


def far_slots():
    return sum(count // 2 for _, count in far_lines())


def far_scratch(rows, cols):
    return [pltpu.VMEM((rows, cols), LOW)] * far_slots()


def near_scratch(rows, cols):
    return [pltpu.VMEM(shape + (rows, cols), LOW) for shape in ((2, 2), (2,), ())]


def journey_scratch(rows, cols):
    return near_scratch(rows, cols) + far_scratch(rows, cols)


class Pool:
    def __init__(self, buffers):
        self.buffers, self.used = buffers, 0

    def take(self, count):
        self.used += count
        return self.buffers[self.used - count : self.used]


def offsets(sizes):
    return [sum(sizes[:i]) for i in range(len(sizes))]


def journey(links, grads, kept, buffers, out, other_out, offset, rows, x_first, shared, part=None):
    near, middle, last, *far = buffers
    total_rows = grads.shape[2]
    start = links.core * (total_rows // 2) + offset
    twin_start = (1 - links.core) * (total_rows // 2) + offset
    mine, theirs = pl.ds(pl.multiple_of(start, 16), rows), pl.ds(pl.multiple_of(twin_start, 16), rows)
    me, you = links.section, 1 - links.section
    if kept is None:
        own = grads.at[:, :, mine, :]
    else:
        own = kept.at[:, :, pl.ds(offset, rows), :]
    block = rows * grads.shape[3] * 2
    copy = links.send(grads.at[:, :, theirs, :], near, links.twin)
    yield [("core", 4 * block)]
    copy.wait()
    if x_first:
        near[:, you] += own[:, you]
        copy = links.send(near.at[:, you], middle, links.x)
        near[:, me] += own[:, me]
        yield [("x", 2 * block)]
        copy.wait()
        middle[1] += near[1, me]
        copy = links.send(middle.at[1], last, links.y)
        middle[0] += near[0, me]
        yield [("y", block)]
        copy.wait()
        last[...] += middle[0]
    else:
        near[1] += own[1]
        copy = links.send(near.at[1], middle, links.y)
        near[0] += own[0]
        yield [("y", 2 * block)]
        copy.wait()
        middle[you] += near[0, you]
        copy = links.send(middle.at[you], last, links.x)
        middle[me] += near[0, me]
        yield [("x", block)]
        copy.wait()
        last[...] += middle[me]
    if part is not None:
        part[...] = last[...]
        return
    yield from far_journey(links, last, far, out, other_out, offset, shared)


def far_journey(links, held, far, out, other_out, offset, shared):
    rows = held.shape[0]
    start = links.core * (out.shape[0] // 2) + offset
    mine = pl.ds(pl.multiple_of(start, 16), rows)
    block = rows * held.shape[1] * 2
    far = list(far)
    for count, place, beside, across in links.lines:
        if count == 2:
            slot = far.pop(0)
            copy = links.send(held, slot, beside)
            yield [("z", block)]
            copy.wait()
            held[...] += slot[...]
            continue
        inner = (place == 1) | (place == 2)
        outer = (place == 0) | (place == 3)
        slot, second = far.pop(0), far.pop(0)
        gather = links.copy(held, slot, beside)
        exchange = links.copy(held, second, across)
        spread_back = links.copy(held, slot, beside)

        @pl.when(outer)
        def _():
            gather.start()

        yield [("z", block)]

        @pl.when(outer)
        def _():
            gather.wait_send()

        @pl.when(inner)
        def _():
            gather.wait_recv()
            held[...] += slot[...]
            exchange.start()

        yield [("mid", block)]

        @pl.when(inner)
        def _():
            exchange.wait()
            held[...] += second[...]
            spread_back.start()

        yield [("back", block)]

        @pl.when(inner)
        def _():
            spread_back.wait_send()

        @pl.when(outer)
        def _():
            spread_back.wait_recv()
            held[...] = slot[...]

    out[mine, :] = held[...]
    copies = [links.send(out.at[mine, :], out.at[mine, :], links.twin)]
    if shared:
        across = links.send(out.at[mine, :], other_out.at[mine, :], links.y)
        yield [("y", block)]
        across.wait()
        copies.append(links.send(other_out.at[mine, :], other_out.at[mine, :], links.twin))
    yield [("core", block)]
    for copy in copies:
        copy.wait()


class Flow:
    RATES = {"core": 400e3, "x": 42e3, "y": 42e3, "z": 42e3, "mid": 42e3, "back": 42e3}
    DELAYS = {"core": 0.4}

    def __init__(self, journeys):
        self.clock, self.free, self.queue, self.count = 0.0, {}, [], 0
        for one in journeys:
            self.add(one)

    def add(self, one):
        self.clock += 0.2
        copies = next(one, None)
        if copies is None:
            return
        ready = self.clock
        for link, count in copies:
            finish = max(self.clock, self.free.get(link, 0.0)) + count / self.RATES[link]
            self.free[link] = finish
            ready = max(ready, finish + self.DELAYS.get(link, 1.5))
        self.queue.append((ready, self.count, one))
        self.queue.sort(key=lambda entry: entry[:2])
        self.count += 1

    def after(self, duration):
        self.clock += duration
        while self.queue and self.queue[0][0] <= self.clock:
            self.add(self.queue.pop(0)[2])

    def finish(self):
        while self.queue:
            self.clock = max(self.clock, self.queue[0][0])
            self.add(self.queue.pop(0)[2])


def everywhere(count):
    return [pl.BlockSpec(memory_space=pltpu.VMEM)] * count


def remote_params(mib, number):
    return pltpu.CompilerParams(
        vmem_limit_bytes=mib * MIB, collective_id=number, has_side_effects=True
    )


class Local:
    def __init__(self, sem):
        self.sem, self.used, self.open = sem, 0, []

    def start(self, source, target):
        copy = pltpu.make_async_copy(source, target, self.sem.at[self.used])
        self.used += 1
        copy.start()
        return copy

    def store(self, source, target):
        self.open.append(self.start(source, target))

    def finish(self):
        for copy in self.open:
            copy.wait()


def fetch_journey(links, own, other, chunk, rows):
    quarter = own.shape[0] // 4
    block = rows * own.shape[1] * 2

    def at(core, section):
        start = (2 * core + section) * quarter + chunk * rows
        return pl.ds(pl.multiple_of(start, 16), rows)

    mine = at(links.core, links.section)
    across = at(links.core, 1 - links.section)
    copy = links.send(own.at[mine, :], other.at[mine, :], links.y)
    yield [("y", block)]
    copy.wait()
    first = links.send(other.at[mine, :], other.at[mine, :], links.x)
    second = links.send(other.at[mine, :], other.at[mine, :], links.twin)
    yield [("x", block), ("core", block)]
    first.wait()
    third = links.send(other.at[across, :], other.at[across, :], links.twin)
    yield [("core", block)]
    second.wait()
    third.wait()


def fetch_eighths(links, own, other, chunk, rows):
    piece = own.shape[0] // 8
    block = rows * own.shape[1] * 2
    _, place, beside, _ = links.lines[0]
    side = place % 2

    def at(section, z):
        start = ((2 * links.core + section) * 2 + z) * piece + chunk * rows
        return other.at[pl.ds(pl.multiple_of(start, 16), rows), :]

    me, you = links.section, 1 - links.section
    mine, across = at(me, side), at(you, side)
    start = ((2 * links.core + me) * 2 + side) * piece + chunk * rows
    source = own.at[pl.ds(pl.multiple_of(start, 16), rows), :]
    copy = links.send(source, mine, links.y)
    yield [("y", block)]
    copy.wait()
    over_x = links.send(mine, mine, links.x)
    over_z = [links.send(mine, mine, beside)]
    twins = [links.send(mine, mine, links.twin)]
    yield [("x", block)]
    over_x.wait()
    over_z.append(links.send(across, across, beside))
    twins.append(links.send(across, across, links.twin))
    yield [("z", 2 * block)]
    for copy, section in zip(over_z, (me, you)):
        copy.wait()
        far = at(section, 1 - side)
        twins.append(links.send(far, far, links.twin))
    yield [("core", 2 * block)]
    for copy in twins:
        copy.wait()


def front_kernel(
    trunk_ref, noise_ref, level_ref, cond_w_ref, cond_b_ref, pair_ref, pair_w_ref, atoms_ref,
    gain_ref, qkv_w_ref, out_w_ref, agg_w_ref, start_ref, ids_ref, in_a_ref, out_a_ref, up_a_ref,
    down_a_ref,
    low_ref, cond_a_ref, cond_b_out_ref, low_pair_ref, bias_ref, atoms_out_ref, qkv_ref, probs_ref,
    mixed_ref, tokens_ref, in_b_ref, out_b_ref, up_b_ref, down_b_ref, inv_ref,
    in_flat_ref, up_flat_ref,
    cond_w, cond_out, pair, pair_w, bias, atoms, rel_own, rel, qkv, probs, mixed, total, tokens,
    in_raw, up_raw, in_flat, up_flat,
    local_sem, send_sem, recv_sem,
):
    links = Links(send_sem, recv_sem)
    local = Local(local_sem)
    samples, count, width = atoms.shape
    half_atoms = count // 2
    batch = atoms_ref.shape[0] // MICRO
    parts = cond_w.shape[0]
    raw_loads = [local.start(in_a_ref, in_raw), local.start(up_a_ref, up_raw)]
    loads = [local.start(cond_w_ref.at[i], cond_w.at[i]) for i in range(parts)]
    pieces = 2
    pair_rows_in = pair.shape[0]
    each = pair_rows_in // pieces
    pair_first = links.core * pair_rows_in
    pair_loads = [
        local.start(
            pair_ref.at[pl.ds(pair_first + i * each, each)], pair.at[pl.ds(i * each, each)]
        )
        for i in range(pieces)
    ]
    own_first = links.section * batch + links.mp * samples
    other_first = links.section * batch + (1 - links.mp) * samples
    own_half = pl.ds(pl.multiple_of(links.mp * half_atoms, 16), half_atoms)
    groups_in = rel_own.shape[0]
    own_groups = pl.ds(links.mp * groups_in, groups_in)
    lane = lax.broadcasted_iota(jnp.int32, rel_own.shape[1:], 1) % (SPAN * QBLOCK)
    for i in range(groups_in):
        starts = jnp.where(lane < QBLOCK, start_ref[SPAN * i], start_ref[SPAN * i + 1])
        rel_own[i] = starts - key_base(links.mp * groups_in + i, count)
    heads = pair_w_ref.shape[0]
    atom_loads = [
        local.start(atoms_ref.at[pl.ds(own_first, samples)], atoms.at[:, own_half, :]),
        local.start(rel_own, rel.at[own_groups]),
        local.start(pair_w_ref, pair_w.at[0]),
    ]
    links.barrier()
    pair_w_copy = links.send(pair_w_ref, pair_w.at[1], links.y)
    rel_copy = links.send(rel_own, rel.at[own_groups], links.y)
    atom_copy = links.send(
        atoms_ref.at[pl.ds(other_first, samples)], atoms.at[:, own_half, :], links.y
    )
    flow = Flow([])
    flow.free["y"] = samples * half_atoms * width * 2 / Flow.RATES["y"]
    for copy, raw, flat, target in (
        (raw_loads[0], in_raw, in_flat, in_flat_ref),
        (raw_loads[1], up_raw, up_flat, up_flat_ref),
    ):
        copy.wait()
        step = 64
        for row in range(0, raw.shape[0], step):
            block = raw[row : row + step]
            flat[row : row + step, :] = block.reshape(step, flat.shape[1])
        local.store(flat, target)
    for way, parts_in, own, other, chunks in (
        (fetch_eighths, 8, in_flat, in_b_ref, 2),
        (fetch_journey, 4, out_a_ref, out_b_ref, 1),
        (fetch_eighths, 8, up_flat, up_b_ref, 2),
        (fetch_journey, 4, down_a_ref, down_b_ref, 2),
    ):
        for i in range(chunks):
            flow.add(way(links, own, other, i, own.shape[0] // parts_in // chunks))

    trunk = trunk_ref[...].astype(WIDE)
    rows = trunk.shape[0]
    for s in range(samples):
        level_rows = lax.broadcasted_iota(jnp.int32, level_ref.shape, 0)
        level = jnp.where(level_rows == noise_ref[own_first + s], level_ref[...].astype(WIDE), 0.0)
        normed, _ = layer_norm(trunk + jnp.sum(level, 0, keepdims=True))
        low_ref[s * rows : (s + 1) * rows, :] = normed.astype(LOW)
    for i in range(parts):
        loads[i].wait()
        value = mul(low_ref[...], cond_w[i]) + cond_b_ref[i % 3, i // 3 : i // 3 + 1, :].astype(WIDE)
        cond_out[i] = value if i % 3 == 1 else sigmoid(value)
        target = (cond_a_ref, cond_b_out_ref)[i // 3]
        local.store(cond_out.at[i], target.at[i % 3])
    flow.after(4.0)

    atom_loads[2].wait()
    pair_w_copy.wait()
    weight = jnp.concatenate([pair_w[0], pair_w[1]], 0)
    block = 8
    for piece in range(pieces):
        pair_loads[piece].wait()

        def pair_rows(i, carry):
            at = pl.multiple_of(i * block, block)
            normed, _ = layer_norm(pair[pl.ds(at, block)].astype(WIDE))
            low = normed.astype(LOW)
            pair[pl.ds(at, block)] = low
            for j in range(block):
                bias[:, pl.ds(pair_first + at + j, 1), :] = mul_nt(weight, low[j])[:, None, :]
            return carry

        lax.fori_loop(piece * each // block, (piece + 1) * each // block, pair_rows, 0)
        at = pl.ds(piece * each, each)
        local.store(pair.at[at], low_pair_ref.at[at])
        flow.after(2.8)
    own_rows = pl.ds(pl.multiple_of(pair_first, 8), pair_rows_in)
    bias_copy = links.send(bias.at[:, own_rows, :], bias.at[:, own_rows, :], links.twin)

    for copy in (atom_loads[0], atom_loads[1], rel_copy, atom_copy):
        copy.wait()
    local.store(atoms, atoms_out_ref)
    bias_copy.wait()
    local.store(bias, bias_ref)
    groups, keys_in = probs.shape[1], probs.shape[2]
    queries_in = SPAN * QBLOCK
    scale = (width // ATOM_HEADS) ** (-0.5)
    place = lax.broadcasted_iota(jnp.int32, (keys_in, ATOM_HEADS * queries_in), 0)
    chunk = 256
    ids = lax.broadcasted_iota(jnp.int32, (total.shape[0], chunk), 0)
    for s in range(samples):
        normed, _ = layer_norm(atoms[s].astype(WIDE))
        hidden = (normed * gain_ref[...].astype(WIDE)).astype(LOW)
        qkv[s] = mul(hidden, joined(qkv_w_ref)).astype(LOW)
        local.store(qkv.at[s], qkv_ref.at[s])
        flow.after(1.2)

        def attend(group, carry, s=s):
            base = key_base(group, count)
            first = pl.multiple_of(group * queries_in, queries_in)
            queries = spread(qkv[s, pl.ds(first, queries_in), :width], ATOM_HEADS)
            keys = qkv[s, pl.ds(base, keys_in), width : 2 * width]
            values = qkv[s, pl.ds(base, keys_in), 2 * width :]
            offset = place - rel[group]
            scores = mul_nt(keys, queries) * scale
            scores = jnp.where((offset >= 0) & (offset < KWIN), scores, -1e30)
            exps = jnp.exp(scores - jnp.max(scores, 0, keepdims=True))
            low = (exps * (1.0 / jnp.sum(exps, 0, keepdims=True))).astype(LOW)
            probs[s, group] = low
            mixed[s, pl.ds(first, queries_in), :] = gather_heads(
                mul_tn(low, values), ATOM_HEADS
            ).astype(LOW)
            return carry

        cuts = 5
        for i in range(cuts):
            pairs(groups * i // cuts, groups * (i + 1) // cuts, attend)
            flow.after(1.3)
        local.store(probs.at[s], probs_ref.at[s])
        local.store(mixed.at[s], mixed_ref.at[s])
        for i in range(count // chunk):
            rows = slice(i * chunk, (i + 1) * chunk)
            after = atoms[s, rows, :].astype(WIDE) + mul(mixed[s, rows, :], out_w_ref[...])
            pre = mul(after.astype(LOW), agg_w_ref[...])
            units = (pre * sigmoid(pre)).astype(LOW)
            member = jnp.where(ids == ids_ref[:, rows], 1.0, 0.0).astype(LOW)
            part_sum = mul(member, units)
            if i == 0:
                total[...] = part_sum
            else:
                total[...] += part_sum
            if s == 0:
                number = jnp.sum(member.astype(WIDE), 1, keepdims=True)
                counts = number if i == 0 else counts + number
            flow.after(0.9)
        if s == 0:
            inv_ref[...] = 1.0 / counts
        tokens[s] = (total[...] * inv_ref[...]).astype(LOW)
        local.store(tokens.at[s], tokens_ref.at[s])
    flow.finish()
    local.finish()


def front(
    trunk, noise, levels, cond_w, cond_b, pair, pair_w, atoms, gain, qkv_w, out_w, agg_w, starts,
    ids, in_a, out_a, up_a, down_a,
):
    tokens_in, width = trunk.shape
    parts, wide = cond_w.shape[0], cond_w.shape[2]
    samples = atoms.shape[0] // MICRO // 2
    rows = samples * tokens_in
    count, atom_width = 2 * atoms.shape[1], atoms.shape[2]
    heads = 2 * pair_w.shape[0]
    groups = count // (SPAN * QBLOCK)
    keys_in, lanes = KWIN + SPAN * QBLOCK, ATOM_HEADS * SPAN * QBLOCK
    probs_shape = (samples, groups, keys_in, lanes)
    flat_in, flat_up = ((a.shape[0], a.shape[1] * a.shape[2]) for a in (in_a, up_a))
    half_pair = (pair.shape[0] // 2,) + pair.shape[1:]
    hbm, near = pl.BlockSpec(memory_space=pl.ANY), pl.BlockSpec(memory_space=pltpu.VMEM)
    smem = pl.BlockSpec(memory_space=pltpu.SMEM)
    outs = [
        (near, (rows, width), LOW),
        (hbm, (parts // 2, rows, wide), WIDE),
        (hbm, (parts // 2, rows, wide), WIDE),
        (hbm, half_pair, LOW),
        (hbm, (heads, tokens_in, tokens_in), WIDE),
        (hbm, (samples, count, atom_width), LOW),
        (hbm, (samples, count, 3 * atom_width), LOW),
        (hbm, probs_shape, LOW),
        (hbm, (samples, count, atom_width), LOW),
        (hbm, (samples, tokens_in, wide), LOW),
        (hbm, flat_in, LOW),
        (hbm, out_a.shape, LOW),
        (hbm, flat_up, LOW),
        (hbm, down_a.shape, LOW),
        (near, (tokens_in, 1), WIDE),
        (hbm, flat_in, LOW),
        (hbm, flat_up, LOW),
    ]
    copies = 4 + 4 * 8 + 3 * 4
    return pl.pallas_call(
        front_kernel,
        in_specs=[near, smem, near, hbm, near, hbm, near, hbm] + [near] * 4 + [smem, near] + [hbm] * 4,
        out_specs=[spec for spec, _, _ in outs],
        out_shape=[sds(shape, dtype) for _, shape, dtype in outs],
        scratch_shapes=[
            pltpu.VMEM(cond_w.shape, LOW),
            pltpu.VMEM((parts, rows, wide), WIDE),
            pltpu.VMEM(half_pair, LOW),
            pltpu.VMEM((2,) + pair_w.shape, LOW),
            pltpu.VMEM((heads, tokens_in, tokens_in), WIDE),
            pltpu.VMEM((samples, count, atom_width), LOW),
            pltpu.VMEM((groups // 2, 1, lanes), jnp.int32),
            pltpu.VMEM((groups, 1, lanes), jnp.int32),
            pltpu.VMEM((samples, count, 3 * atom_width), LOW),
            pltpu.VMEM(probs_shape, LOW),
            pltpu.VMEM((samples, count, atom_width), LOW),
            pltpu.VMEM((tokens_in, wide), WIDE),
            pltpu.VMEM((samples, tokens_in, wide), LOW),
            *(pltpu.VMEM(shape, LOW) for shape in (in_a.shape, up_a.shape, flat_in, flat_up)),
            pltpu.SemaphoreType.DMA((64,)),
            pltpu.SemaphoreType.DMA((copies,)),
            pltpu.SemaphoreType.DMA((copies,)),
        ],
        compiler_params=remote_params(60, 3),
        cost_estimate=cost(40e9, 40e6),
        name="front",
    )(
        trunk, noise, levels, cond_w, cond_b, pair, pair_w, atoms, gain, qkv_w, out_w, agg_w,
        starts, ids, in_a, out_a, up_a, down_a,
    )


def token_attention_kernel(
    tokens_ref, cond_ref, bias_ref, in_a_ref, in_b_ref, out_a_ref, out_b_ref,
    inner_ref, qkv_ref, sig_ref, heads_ref, gated_ref, probs_ref, attn_ref, middle_ref,
    tokens, cond, bias, in_a, in_b, out_a, out_b, inner, qkv, sig, heads_out, gated, probs, attn,
    middle, local_sem,
):
    local = Local(local_sem)
    load_tokens = local.start(tokens_ref, tokens)
    load_cond = local.start(cond_ref, cond)
    load_in = [local.start(in_a_ref, in_a)]
    load_bias = local.start(bias_ref, bias)
    load_in.append(local.start(in_b_ref, in_b))
    load_out = [local.start(out_a_ref, out_a), local.start(out_b_ref, out_b)]
    samples, heads, count = probs.shape[0], probs.shape[1], probs.shape[2]
    width_in = in_a.shape[1] // 4
    size = 2 * width_in // heads
    scale = size ** (-0.5)
    load_tokens.wait()
    load_cond.wait()
    wide = tokens[...].astype(WIDE)
    normed, _ = layer_norm(wide)
    inner[...] = (normed * cond[0] + cond[1]).astype(LOW)
    local.store(inner, inner_ref)
    for half, weight in enumerate((in_a, in_b)):
        load_in[half].wait()
        qkv[half] = mul(inner[...], weight[:, : 3 * width_in]).astype(LOW)
        local.store(qkv.at[half], qkv_ref.at[half])
        sig[half] = sigmoid(mul(inner[...], weight[:, 3 * width_in :]))
        local.store(sig.at[half], sig_ref.at[half])
        if half == 0:
            load_bias.wait()
        for s in range(samples):
            at = slice(s * count, (s + 1) * count)
            outs = []
            for h in range(heads // 2):
                col = h * size
                query = qkv[half, at, col : col + size]
                key = qkv[half, at, width_in + col : width_in + col + size]
                value = qkv[half, at, 2 * width_in + col : 2 * width_in + col + size]
                scores = mul_nt(query, key) * scale + bias[half * (heads // 2) + h]
                exps = jnp.exp(scores - jnp.max(scores, -1, keepdims=True))
                low = (exps * (1.0 / jnp.sum(exps, -1, keepdims=True))).astype(LOW)
                probs[s, half * (heads // 2) + h] = low
                outs.append(mul(low, value))
            heads_out[half, at, :] = jnp.concatenate(outs, 1)
        gated[half] = (heads_out[half] * sig[half]).astype(LOW)
        local.store(heads_out.at[half], heads_ref.at[half])
        local.store(gated.at[half], gated_ref.at[half])
    local.store(probs, probs_ref)
    load_out[0].wait()
    load_out[1].wait()
    attn[...] = mul(gated[0], out_a[...]) + mul(gated[1], out_b[...])
    local.store(attn, attn_ref)
    middle[...] = wide + cond[2] * attn[...]
    local.store(middle, middle_ref)
    local.finish()


def token_attention(tokens, cond, bias, in_a, in_b, out_a, out_b):
    rows, width = tokens.shape
    heads, count = bias.shape[0], bias.shape[1]
    samples, width_in = rows // count, in_a.shape[1] // 4
    hbm = pl.BlockSpec(memory_space=pl.ANY)
    outs = [
        sds((rows, width), LOW),
        sds((2, rows, 3 * width_in), LOW),
        sds((2, rows, width_in), WIDE),
        sds((2, rows, width_in), WIDE),
        sds((2, rows, width_in), LOW),
        sds((samples, heads, count, count), LOW),
        sds((rows, width), WIDE),
        sds((rows, width), WIDE),
    ]
    args = (tokens, cond, bias, in_a, in_b, out_a, out_b)
    return pl.pallas_call(
        token_attention_kernel,
        in_specs=[hbm] * len(args),
        out_specs=[hbm] * len(outs),
        out_shape=outs,
        scratch_shapes=[
            *(pltpu.VMEM(a.shape, a.dtype) for a in args),
            *(pltpu.VMEM(a.shape, a.dtype) for a in outs),
            pltpu.SemaphoreType.DMA((32,)),
        ],
        compiler_params=params(60),
        cost_estimate=cost(40e9, 20e6),
        name="token_attention",
    )(*args)


CHUNK = 192
MLP_CHUNKS = (192,) * 6
MLP_X_FIRST = (True, True, False, True, True, True)
EARLY = 2
COND_CHUNKS = (192,) * 3
ATTN_CHUNKS = (192,) * 5
ORDER = (
    ("attn", False), ("attn", True), ("cond", True), ("cond", True), ("attn", True),
    ("cond", False), ("attn", True), ("attn", True),
)


def relative(half, mp):
    return mp if half == 0 else 1 - mp


def token_back_kernel(
    middle_ref, cond_b_ref, cotangent_ref, low_ref, up_a_ref, up_b_ref, down_a_ref, down_b_ref,
    tokens_ref, cond_a_ref, attn_ref, inner_ref, qkv_ref, sig_ref, heads_ref, gated_ref, probs_ref,
    in_a_ref, in_b_ref, out_a_ref, out_b_ref,
    result_ref, other_result_ref, token_grad_ref, grads_ref, cond_bias_a_ref, cond_bias_b_ref,
    bias_grad_ref, mlp_out_ref, mlp_part_ref,
    middle, cond, grad, low, weight, out_weight, up, hidden, mlp_grads, middle_grad, result,
    tokens, inner, qkv, sig, heads_out, gated, probs, grads, bias_grad, proj, heads_grad, *rest,
):
    *buffers, local_sem, send_sem, recv_sem = rest
    links = Links(send_sem, recv_sem)
    local = Local(local_sem)
    load_first = [
        local.start(a, b)
        for a, b in ((middle_ref, middle), (cond_b_ref, cond), (up_a_ref, weight.at[0]))
    ]
    load_up_b = local.start(up_b_ref, weight.at[1])
    load_down = [local.start(down_a_ref, out_weight.at[0])]
    load_down.append(local.start(down_b_ref, out_weight.at[1]))
    samples, tokens_in = probs.shape[0], probs.shape[2]
    batch = cotangent_ref.shape[0] // MICRO
    load_grad = [local.start(low_ref, low)]
    for s in range(samples):
        sample = links.section * batch + links.mp * samples + s
        at = pl.ds(s * tokens_in, tokens_in)
        load_grad.append(local.start(cotangent_ref.at[sample], grad.at[at, :]))
    load_later = [
        local.start(a, b)
        for a, b in (
            (gated_ref, gated), (sig_ref, sig), (heads_ref, heads_out), (qkv_ref, qkv),
            (probs_ref, probs), (inner_ref, inner), (tokens_ref, tokens),
        )
    ]
    links.barrier()
    flow = Flow([])
    rows, width = middle.shape
    half_cols = width // 2
    samples, heads, count = probs.shape[0], probs.shape[1], probs.shape[2]

    for copy in load_first:
        copy.wait()
    middle_value = middle[...]
    normed, inverse = layer_norm(middle_value)
    scale, gate = cond[0], cond[2]
    inner_mlp = (normed * scale + cond[1]).astype(LOW)
    mlp_width = hidden.shape[2]
    mlp = None
    for half in range(2):
        if half == 1:
            load_up_b.wait()
        gate_in = mul(inner_mlp, weight[half, :, :mlp_width])
        up_in = mul(inner_mlp, weight[half, :, mlp_width:])
        up[half, :, :mlp_width] = gate_in.astype(LOW)
        up[half, :, mlp_width:] = up_in.astype(LOW)
        hidden[half] = (gate_in * sigmoid(gate_in) * up_in).astype(LOW)
        load_down[half].wait()
        add = mul(hidden[half], out_weight[half])
        mlp = add if mlp is None else mlp + add
    result[...] = (middle_value + gate * mlp).astype(LOW)
    local.store(result, result_ref)
    result_copy = links.send(result, other_result_ref, links.y)
    flow.free["y"] = rows * width * 2 / Flow.RATES["y"]

    for copy in load_grad:
        copy.wait()
    grad_value = grad[...].astype(WIDE)
    mlp_grad = (grad_value * gate).astype(LOW)
    core_rows = mlp_grads.shape[2] // 2
    down_rows = mlp_width // 2
    for half in range(2):
        hidden_t = hidden[half].T
        for core in range(2):
            for sec in range(2):
                mlp_grads[half, sec, core * core_rows : core * core_rows + down_rows, :] = mul(
                    hidden_t[core * down_rows : (core + 1) * down_rows],
                    mlp_grad[:, sec * half_cols : (sec + 1) * half_cols],
                ).astype(LOW)

    pool = Pool(buffers)

    def launch(first, last):
        for i in range(first, last):
            early = i < EARLY
            taken = pool.take(3 + (far_slots() if early else 0))
            part = None if early else mlp_part_ref.at[i - EARLY]
            flow.add(
                journey(
                    links, mlp_grads, None, taken, mlp_out_ref, None,
                    offsets(MLP_CHUNKS)[i], MLP_CHUNKS[i], MLP_X_FIRST[i], False, part,
                )
            )

    launch(0, down_rows // CHUNK)
    inner_t = inner_mlp.T
    inner_grad = None
    for half in range(2):
        hidden_grad = mul_nt(mlp_grad, out_weight[half])
        gate_in = up[half, :, :mlp_width].astype(WIDE)
        up_in = up[half, :, mlp_width:].astype(WIDE)
        sigma = sigmoid(gate_in)
        first = (hidden_grad * up_in * (sigma * (1.0 + gate_in * (1.0 - sigma)))).astype(LOW)
        second = (hidden_grad * (gate_in * sigma)).astype(LOW)
        up_grad = jnp.concatenate([first, second], 1)
        for sec in range(2):
            at = slice(sec * half_cols, (sec + 1) * half_cols)
            for block in range(4):
                place = block // 2 * core_rows + down_rows + block % 2 * half_cols
                mlp_grads[half, sec, place : place + half_cols, :] = mul(
                    inner_t[at], up_grad[:, block * half_cols : (block + 1) * half_cols]
                ).astype(LOW)
        add = mul_nt(up_grad, weight[half])
        inner_grad = add if inner_grad is None else inner_grad + add
        flow.after(3.0)
    load_weight = [local.start(in_a_ref, weight.at[0]), local.start(in_b_ref, weight.at[1])]
    out_rows = out_a_ref.shape[0]
    load_out = [
        local.start(a, out_weight.at[h, :out_rows, :]) for h, a in enumerate((out_a_ref, out_b_ref))
    ]
    launch(down_rows // CHUNK, core_rows // CHUNK)
    middle_grad[...] = grad_value + norm_back(normed, inverse, inner_grad * scale)
    low_t = low[...].T
    first_cond = grads.shape[2] - 3 * low_t.shape[0]

    def cond_back(sec, pieces, bias_out):
        for k, piece in enumerate(pieces):
            piece = piece.astype(LOW)
            place = first_cond + k * low_t.shape[0]
            for h in range(2):
                grads[relative(h, links.mp), sec, place : place + low_t.shape[0], :] = mul(
                    low_t, piece[:, h * half_cols : (h + 1) * half_cols]
                ).astype(LOW)
            bias_out[k] = jnp.sum(piece.astype(WIDE), 0, keepdims=True)

    cond_back(
        1,
        (
            inner_grad * normed * (scale * (1.0 - scale)),
            inner_grad,
            grad_value * mlp * (gate * (1.0 - gate)),
        ),
        cond_bias_b_ref,
    )
    load_cond = local.start(cond_a_ref, cond)
    load_attn = local.start(attn_ref, middle)
    flow.after(3.0)

    local_cols = out_rows
    size = 2 * local_cols // heads
    head_scale = size ** (-0.5)
    load_cond.wait()
    for copy in load_later:
        copy.wait()
    scale, gate = cond[0], cond[2]
    attn_grad = (middle_grad[...] * gate).astype(LOW)
    inner_t = inner[...].T
    inner_grad = None
    for half in range(2):
        load_out[half].wait()
        gated_t = gated[half].T
        for sec in range(2):
            grads[half, sec, 4 * half_cols : first_cond, :] = mul(
                gated_t, attn_grad[:, sec * half_cols : (sec + 1) * half_cols]
            ).astype(LOW)
        gated_grad = mul_nt(attn_grad, out_weight[half, :out_rows, :])
        sig_half = sig[half]
        with_sig = gated_grad * sig_half
        heads_grad[...] = with_sig.astype(LOW)
        proj[:, 3 * local_cols :] = (with_sig * heads_out[half] * (1.0 - sig_half)).astype(LOW)
        flow.after(1.5)
        for s in range(samples):
            at = slice(s * count, (s + 1) * count)
            parts = ([], [], [])
            for h in range(heads // 2):
                col, index = h * size, half * (heads // 2) + h
                query = qkv[half, at, col : col + size]
                key = qkv[half, at, local_cols + col : local_cols + col + size]
                value = qkv[half, at, 2 * local_cols + col : 2 * local_cols + col + size]
                one_grad = heads_grad[at, col : col + size]
                probs_low = probs[s, index]
                wide_probs = probs_low.astype(WIDE)
                probs_grad = mul_nt(one_grad, value)
                mean = jnp.sum(wide_probs * probs_grad, -1, keepdims=True)
                scores_grad = (wide_probs * (probs_grad - mean)).astype(LOW)
                if s == 0:
                    bias_grad[index] = scores_grad.astype(WIDE)
                else:
                    bias_grad[index] += scores_grad.astype(WIDE)
                parts[0].append(mul(scores_grad, key) * head_scale)
                parts[1].append(mul_tn(scores_grad, query) * head_scale)
                parts[2].append(mul_tn(probs_low, one_grad))
                if h % 2 == 1:
                    flow.after(1.0)
            for k in range(3):
                proj[at, k * local_cols : (k + 1) * local_cols] = jnp.concatenate(
                    parts[k], 1
                ).astype(LOW)
        load_weight[half].wait()
        for sec in range(2):
            for k in range(4):
                grads[half, sec, k * half_cols : (k + 1) * half_cols, :] = mul(
                    inner_t[sec * half_cols : (sec + 1) * half_cols],
                    proj[:, k * local_cols : (k + 1) * local_cols],
                ).astype(LOW)
        local.store(grads.at[half, :, :first_cond, :], grads_ref.at[half, :, :first_cond, :])
        some = pl.ds(half * (heads // 2), heads // 2)
        local.store(bias_grad.at[some], bias_grad_ref.at[some])
        add = mul_nt(proj[...], weight[half])
        inner_grad = add if inner_grad is None else inner_grad + add
        flow.after(2.5)
    normed, inverse = layer_norm(tokens[...].astype(WIDE))
    tokens[...] = (middle_grad[...] + norm_back(normed, inverse, inner_grad * scale)).astype(LOW)
    local.store(tokens, token_grad_ref)
    flow.after(1.0)
    load_attn.wait()
    cond_back(
        0,
        (
            inner_grad * normed * (scale * (1.0 - scale)),
            inner_grad,
            middle_grad[...] * middle[...] * (gate * (1.0 - gate)),
        ),
        cond_bias_a_ref,
    )
    local.store(grads.at[:, :, first_cond:, :], grads_ref.at[:, :, first_cond:, :])

    flow.finish()
    result_copy.wait()
    local.finish()


def token_back(
    middle, cond_b, cotangent, low, up_a, up_b, down_a, down_b, tokens, cond_a, attn, inner, qkv,
    sig, heads_out, gated, probs, in_a, in_b, out_a, out_b,
):
    rows, width = tokens.shape
    heads, count = probs.shape[1], probs.shape[2]
    mlp_width, local_cols, half = down_a.shape[0], out_a.shape[0], width // 2
    mlp_rows = 4 * half + mlp_width
    grad_rows = 4 * half + local_cols + 3 * low.shape[1]
    chunks = mlp_rows // 2 // CHUNK
    copies = chunks * journey_copies(False) + 1
    hbm, near = pl.BlockSpec(memory_space=pl.ANY), pl.BlockSpec(memory_space=pltpu.VMEM)
    args = (
        middle, cond_b, cotangent, low, up_a, up_b, down_a, down_b, tokens, cond_a, attn, inner,
        qkv, sig, heads_out, gated, probs, in_a, in_b, out_a, out_b,
    )
    outs = [
        (hbm, (rows, width), LOW),
        (hbm, (rows, width), LOW),
        (hbm, (rows, width), LOW),
        (hbm, (2, 2, grad_rows, half), LOW),
        (near, (3, 1, width), WIDE),
        (near, (3, 1, width), WIDE),
        (hbm, (heads, count, count), WIDE),
        (near, (2 * EARLY * CHUNK, half), LOW),
        (near, (chunks - EARLY, CHUNK, half), LOW),
    ]
    scratch = [
        (middle.shape, WIDE),
        (cond_b.shape, WIDE),
        ((rows, width), LOW),
        (low.shape, LOW),
        ((2,) + up_a.shape, LOW),
        ((2,) + down_a.shape, LOW),
        ((2, rows, 2 * mlp_width), LOW),
        ((2, rows, mlp_width), LOW),
        ((2, 2, mlp_rows, half), LOW),
        (middle.shape, WIDE),
        ((rows, width), LOW),
        *((a.shape, a.dtype) for a in (tokens, inner, qkv, sig, heads_out, gated, probs)),
        ((2, 2, grad_rows, half), LOW),
        ((heads, count, count), WIDE),
        ((rows, 4 * local_cols), LOW),
        ((rows, local_cols), LOW),
    ]
    return pl.pallas_call(
        token_back_kernel,
        in_specs=[hbm] * len(args),
        out_specs=[spec for spec, _, _ in outs],
        out_shape=[sds(shape, dtype) for _, shape, dtype in outs],
        scratch_shapes=[
            *(pltpu.VMEM(shape, dtype) for shape, dtype in scratch),
            *journey_scratch(CHUNK, half) * EARLY,
            *near_scratch(CHUNK, half) * (chunks - EARLY),
            pltpu.SemaphoreType.DMA((64,)),
            pltpu.SemaphoreType.DMA((copies,)),
            pltpu.SemaphoreType.DMA((copies,)),
        ],
        compiler_params=remote_params(62, 1),
        cost_estimate=cost(90e9, 50e6),
        name="token_back",
    )(*args)


FIRST_ROWS, LAST_ROWS = 128, 64


def atom_back_kernel(
    atoms_hbm, gain_ref, qkv_w_ref, out_w_ref, agg_w_ref, ids_ref, inv_ref,
    qkv_hbm, probs_hbm, mixed_hbm, grad_ref, pair_ref, bias_grad_hbm, grads_ref, cond_bias_a_ref,
    cond_bias_b_ref, mlp_part_ref,
    keep_ref, got_ref, attn_out_ref, cond_out_ref, cond_other_ref,
    first_out_ref, first_other_ref, last_out_ref, last_other_ref, mlp_out_ref,
    pair, bias_grad, twin_bias, pair_grad, atoms_ref, qkv_ref, probs_ref, mixed_ref, kept_attn, kept_cond,
    after_grad, mixed_grad, key_grad, value_grad, proj_grad, atoms_grad, send_buffer,
    gain_grad, qkv_grad, out_grad, agg_grad, first_small, last_small, *rest,
):
    *buffers, local_sem, send_sem, recv_sem = rest
    links = Links(send_sem, recv_sem)
    local = Local(local_sem)
    samples, atoms, width = atoms_ref.shape
    groups, keys_in = probs_ref.shape[1], probs_ref.shape[2]
    queries_in = SPAN * QBLOCK
    scale = (width // ATOM_HEADS) ** (-0.5)
    cond_rows = cond_out_ref.shape[0]
    attn_rows = grads_ref.shape[2] - cond_rows
    attn_grads = grads_ref.at[:, :, :attn_rows, :]
    cond_grads = grads_ref.at[:, :, attn_rows:, :]
    pair_half = bias_grad.shape[1]
    own_rows = pl.ds(pl.multiple_of(links.core * pair_half, 8), pair_half)
    twin_rows = pl.ds(pl.multiple_of((1 - links.core) * pair_half, 8), pair_half)
    load_bias = local.start(bias_grad_hbm.at[:, own_rows, :], bias_grad)

    def load_kept(source, target):
        start = links.core * (source.shape[2] // 2)
        at = pl.ds(pl.multiple_of(start, 16), target.shape[2])
        return local.start(source.at[:, :, at, :], target)

    kept_loads = [load_kept(attn_grads, kept_attn), load_kept(cond_grads, kept_cond)]
    loads = [local.start(mixed_hbm, mixed_ref), local.start(atoms_hbm, atoms_ref)]
    later = [
        (local.start(qkv_hbm.at[s], qkv_ref.at[s]), local.start(probs_hbm.at[s], probs_ref.at[s]))
        for s in range(samples)
    ]
    links.barrier()
    bias_copy = links.send(bias_grad_hbm.at[:, twin_rows, :], twin_bias, links.twin)
    pool, each = Pool(buffers), 3 + far_slots()
    flow = Flow([])
    for i in range(mlp_part_ref.shape[0]):
        held, *slots = pool.take(each - 2)
        held[...] = mlp_part_ref[i]
        offset = i * mlp_part_ref.shape[1]
        flow.add(far_journey(links, held, slots, mlp_out_ref, None, offset, False))
    sums = {
        "attn": (attn_grads, kept_attn, attn_out_ref, None, ATTN_CHUNKS),
        "cond": (cond_grads, kept_cond, cond_out_ref, cond_other_ref, COND_CHUNKS),
    }
    taken = {"attn": 0, "cond": 0}
    for kind, x_first in ORDER:
        source, kept, out, other, sizes = sums[kind]
        i = taken[kind]
        taken[kind] += 1
        flow.add(
            journey(
                links, source, kept, pool.take(each), out, other, offsets(sizes)[i], sizes[i],
                x_first, other is not None,
            )
        )
    for copy in kept_loads:
        copy.wait()

    load_bias.wait()
    bias_copy.wait()
    heads = pair_grad.shape[0]
    slots = pair.shape[0]
    block = pair.shape[1]
    blocks = pair_ref.shape[0] // block

    def load_pair(i):
        return local.start(pair_ref.at[pl.ds(i * block, block)], pair.at[i % slots])

    pair_loads = [load_pair(i) for i in range(slots)]
    total = jnp.zeros(pair_grad.shape, WIDE)
    for i in range(blocks):
        pair_loads[i].wait()
        for j in range(block):
            one = bias_grad[:, i * block + j, :] + twin_bias[:, i * block + j, :]
            high = one.astype(LOW)
            tail = (one - high.astype(WIDE)).astype(LOW)
            both = mul(jnp.concatenate([high, tail], 0), pair[i % slots, j])
            total += both[:heads] + both[heads:]
        if i + slots < blocks:
            pair_loads.append(load_pair(i + slots))
        flow.after(0.08 * block)
    pair_grad[...] = total
    for copy in loads:
        copy.wait()

    for ref in (gain_grad, qkv_grad, out_grad, agg_grad):
        ref[...] = jnp.zeros_like(ref)
    chunk = 256
    token_ids = lax.broadcasted_iota(jnp.int32, (grad_ref.shape[1], chunk), 0)
    atom_copies = []
    for s in range(samples):
        token_grad = (grad_ref[s].astype(WIDE) * inv_ref[...]).astype(LOW)
        for i in range(atoms // chunk):
            rows = slice(i * chunk, (i + 1) * chunk)
            mixed = mixed_ref[s, rows, :]
            after = atoms_ref[s, rows, :].astype(WIDE) + mul(mixed, out_w_ref[...])
            after_low = after.astype(LOW)
            pre = mul(after_low, agg_w_ref[...])
            sigma = sigmoid(pre)
            member = jnp.where(token_ids == ids_ref[:, rows], 1.0, 0.0).astype(LOW)
            unit_grad = mul_tn(member, token_grad)
            pre_grad = (unit_grad * (sigma * (1.0 + pre * (1.0 - sigma)))).astype(LOW)
            agg_grad[...] += mul_tn(after_low, pre_grad)
            after_back = mul_nt(pre_grad, agg_w_ref[...])
            after_grad[s, rows, :] = after_back
            branch = after_back.astype(LOW)
            out_grad[...] += mul_tn(mixed, branch)
            mixed_grad[s, rows, :] = mul_nt(branch, out_w_ref[...]).astype(LOW)
            flow.after(1.7)
    heads = pair_grad.shape[0]
    wide = agg_grad.shape[1] // 2
    rows, part_rows = width // 2, width // 4

    def fill(values, cols):
        if values.shape[1] == cols:
            return values
        empty = jnp.zeros((values.shape[0], cols - values.shape[1]), WIDE)
        return jnp.concatenate([values, empty], 1)

    for h in range(2):
        to = relative(h, links.mp)
        cols = slice(h * wide, (h + 1) * wide)
        own_pair = jnp.where(links.mp == h, pair_grad[: heads // 2], pair_grad[heads // 2 :])
        for sec, cond_bias_ref in enumerate((cond_bias_a_ref, cond_bias_b_ref)):
            first_small[to, sec, :rows, :] = agg_grad[sec * rows : (sec + 1) * rows, cols].astype(LOW)
            first_row = sec * rows + h * part_rows
            block = fill(out_grad[first_row : first_row + part_rows], wide)
            first_small[to, sec, rows : rows + part_rows, :] = block.astype(LOW)
            block = [cond_bias_ref[k, :, cols] for k in range(3)]
            block += [jnp.zeros((5, wide), WIDE), fill(own_pair, wide)]
            block += [jnp.zeros((part_rows - 16, wide), WIDE)]
            first_small[to, sec, rows + part_rows :, :] = jnp.concatenate(block, 0).astype(LOW)
    flow.add(
        journey(
            links, first_small, None, pool.take(each), first_out_ref, first_other_ref,
            0, FIRST_ROWS // 2, False, True,
        )
    )
    for s in range(samples):
        for copy in later[s]:
            copy.wait()
        key_grad[...] = jnp.zeros_like(key_grad)
        value_grad[...] = jnp.zeros_like(value_grad)

        def attend(group, carry, s=s):
            base = key_base(group, atoms)
            start = pl.multiple_of(group * queries_in, queries_in)
            queries = spread(qkv_ref[s, pl.ds(start, queries_in), :width], ATOM_HEADS)
            grads = spread(mixed_grad[s, pl.ds(start, queries_in), :], ATOM_HEADS)
            keys = qkv_ref[s, pl.ds(base, keys_in), width : 2 * width]
            values = qkv_ref[s, pl.ds(base, keys_in), 2 * width :]
            probs_low = probs_ref[s, group]
            probs = probs_low.astype(WIDE)
            probs_grad = mul_nt(values, grads)
            mean = jnp.sum(probs * probs_grad, 0, keepdims=True)
            scores_grad = (probs * (probs_grad - mean)).astype(LOW)
            query_grad = gather_heads(mul_tn(scores_grad, keys), ATOM_HEADS)
            proj_grad[pl.ds(start, queries_in), :width] = (query_grad * scale).astype(LOW)
            key_grad[pl.ds(base, keys_in), :] += mul(scores_grad, queries)
            value_grad[pl.ds(base, keys_in), :] += mul(probs_low, grads)
            return carry

        cuts = 5
        for i in range(cuts):
            pairs(groups * i // cuts, groups * (i + 1) // cuts, attend)
            flow.after(1.7)
        proj_grad[:, width : 2 * width] = (key_grad[...] * scale).astype(LOW)
        proj_grad[:, 2 * width :] = value_grad[...].astype(LOW)
        gain = gain_ref[...].astype(WIDE)
        normed, inverse = layer_norm(atoms_ref[s].astype(WIDE))
        hidden = (normed * gain).astype(LOW)
        proj = proj_grad[...]
        qkv_grad[...] += mul_tn(hidden, proj)
        hidden_grad = mul_nt(proj, joined(qkv_w_ref))
        gain_grad[...] += jnp.sum(hidden_grad * normed, 0, keepdims=True)
        atoms_grad[...] = after_grad[s] + norm_back(normed, inverse, hidden_grad * gain)
        half = atoms // 2
        theirs = pl.ds(pl.multiple_of((1 - links.mp) * half, 16), half)
        send_buffer[s] = atoms_grad[theirs, :].astype(LOW)
        atom_copies.append(links.send(send_buffer.at[s], got_ref.at[s], links.y))
        keep_ref[s] = atoms_grad[pl.ds(pl.multiple_of(links.mp * half, 16), half), :]
        flow.after(2.5)

    for h in range(2):
        to = relative(h, links.mp)
        for sec in range(2):
            first_row = sec * rows + h * part_rows
            part = fill(qkv_grad[first_row : first_row + part_rows], wide)
            last_small[to, sec, :part_rows, :] = part.astype(LOW)
            block = [fill(gain_grad[...], wide), jnp.zeros((part_rows - 1, wide), WIDE)]
            last_small[to, sec, part_rows:, :] = jnp.concatenate(block, 0).astype(LOW)
    flow.add(
        journey(
            links, last_small, None, pool.take(each), last_out_ref, last_other_ref,
            0, LAST_ROWS // 2, False, True,
        )
    )
    flow.finish()
    for copy in atom_copies:
        copy.wait()


def atom_back(
    atoms, gain, qkv_w, out_w, agg_w, ids, inverse_counts, qkv, probs, mixed, grad,
    low_pair, bias_grad, grads, cond_bias_a, cond_bias_b, mlp_part, cond_rows,
):
    samples, count, width = atoms.shape
    wide = agg_w.shape[1]
    cols = grads.shape[3]
    attn_rows = grads.shape[2] - cond_rows
    copies = len(ATTN_CHUNKS) * journey_copies(False)
    copies += len(COND_CHUNKS) * journey_copies(True)
    copies += 2 * journey_copies(True) + samples + 1
    half_bias = (bias_grad.shape[0], bias_grad.shape[1] // 2, bias_grad.shape[2])
    copies += mlp_part.shape[0] * journey_copies(False, near=0)
    outs = [
        sds((samples, count // 2, width), WIDE),
        sds((samples, count // 2, width), LOW),
        sds((attn_rows, cols), LOW),
        sds((cond_rows, cols), LOW),
        sds((cond_rows, cols), LOW),
        sds((FIRST_ROWS, cols), LOW),
        sds((FIRST_ROWS, cols), LOW),
        sds((LAST_ROWS, cols), LOW),
        sds((LAST_ROWS, cols), LOW),
        sds((2 * mlp_part.shape[0] * CHUNK, cols), LOW),
    ]
    args = (
        atoms, gain, qkv_w, out_w, agg_w, ids, inverse_counts, qkv, probs, mixed, grad,
        low_pair, bias_grad, grads, cond_bias_a, cond_bias_b, mlp_part,
    )
    hbm, near = pl.BlockSpec(memory_space=pl.ANY), pl.BlockSpec(memory_space=pltpu.VMEM)
    return pl.pallas_call(
        atom_back_kernel,
        in_specs=[hbm] + [near] * 6 + [hbm] * 3 + [near] + [hbm] * 3 + [near] * 3,
        out_specs=everywhere(len(outs)),
        out_shape=outs,
        scratch_shapes=[
            pltpu.VMEM((2, 8) + low_pair.shape[1:], LOW),
            pltpu.VMEM(half_bias, WIDE),
            pltpu.VMEM(half_bias, WIDE),
            pltpu.VMEM((bias_grad.shape[0], width), WIDE),
            *(pltpu.VMEM(a.shape, a.dtype) for a in (atoms, qkv, probs, mixed)),
            pltpu.VMEM((2, 2, attn_rows // 2, cols), LOW),
            pltpu.VMEM((2, 2, cond_rows // 2, cols), LOW),
            pltpu.VMEM((samples, count, width), WIDE),
            pltpu.VMEM((samples, count, width), LOW),
            pltpu.VMEM((count, width), WIDE),
            pltpu.VMEM((count, width), WIDE),
            pltpu.VMEM((count, 3 * width), LOW),
            pltpu.VMEM((count, width), WIDE),
            pltpu.VMEM((samples, count // 2, width), LOW),
            pltpu.VMEM((1, width), WIDE),
            pltpu.VMEM((width, 3 * width), WIDE),
            pltpu.VMEM((width, width), WIDE),
            pltpu.VMEM((width, wide), WIDE),
            pltpu.VMEM((2, 2, FIRST_ROWS, cols), LOW),
            pltpu.VMEM((2, 2, LAST_ROWS, cols), LOW),
            *([pltpu.VMEM((CHUNK, cols), LOW)] + far_scratch(CHUNK, cols)) * mlp_part.shape[0],
            *(b for _ in ORDER for b in journey_scratch(CHUNK, cols)),
            *journey_scratch(FIRST_ROWS // 2, cols),
            *journey_scratch(LAST_ROWS // 2, cols),
            pltpu.SemaphoreType.DMA((32,)),
            pltpu.SemaphoreType.DMA((copies,)),
            pltpu.SemaphoreType.DMA((copies,)),
        ],
        compiler_params=remote_params(60, 2),
        cost_estimate=cost(60e9, 24e6),
        name="atom_back",
    )(*args)


def results_kernel(*refs):
    number, count = 13, 13
    hbm_in, hbm_out = refs[:number], refs[number : number + count]
    scratch, sem = refs[number + count : -1], refs[-1]
    near_in, near_out = scratch[:number], scratch[number:]
    local = Local(sem)
    loads = [local.start(a, b) for a, b in zip(hbm_in, near_in)]
    (
        cond_ref, cond_other_ref, attn_ref, mlp_first_ref, mlp_late_ref, keep_ref, got_ref,
        result_ref, other_result_ref, first_ref, first_other_ref, last_ref, last_other_ref,
    ) = near_in
    (
        token_out, atoms_out, gain_out, qkv_out, out_out, agg_out, cond_out, cond_bias_out,
        pair_out, in_out, attn_out, up_out, down_out,
    ) = near_out
    mp, section = lax.axis_index("mp"), lax.axis_index("section")

    def wait(*indices):
        for index in indices:
            loads[index].wait()

    def store(*outs):
        for out in outs:
            index = [i for i, ref in enumerate(near_out) if ref is out][0]
            local.store(out, hbm_out[index])

    half = cond_ref.shape[1]
    size = cond_out.shape[1]
    wait(0, 1)
    for h in range(2):
        cols = slice(h * half, (h + 1) * half)
        for k in range(3):
            at = slice(k * size, (k + 1) * size)
            value = jnp.where(mp == h, cond_ref[at, :], cond_other_ref[at, :])
            cond_out[k, :, cols] = value.astype(WIDE)
    store(cond_out)
    wait(2)
    blocks = in_out.shape[1]
    for k in range(blocks):
        in_out[:, k, :] = attn_ref[k * half : (k + 1) * half, :].astype(WIDE)
    store(in_out)
    attn_out[...] = attn_ref[blocks * half :, :].astype(WIDE)
    store(attn_out)
    wait(3, 4)
    core_first, core_late = mlp_first_ref.shape[0] // 2, mlp_late_ref.shape[0] // 2
    down_rows = down_out.shape[0] // 2
    for core in range(2):
        at = slice(core * down_rows, (core + 1) * down_rows)
        start = core * core_first
        down_out[at, :] = mlp_first_ref[start : start + down_rows, :].astype(WIDE)
        row = 0
        for ref, begin, end in (
            (mlp_first_ref, start + down_rows, start + core_first),
            (mlp_late_ref, core * core_late, (core + 1) * core_late),
        ):
            while begin < end:
                block, within = row // half, row % half
                some = min(end - begin, half - within)
                up_out[within : within + some, core, block * half : (block + 1) * half] = ref[
                    begin : begin + some, :
                ].astype(WIDE)
                begin, row = begin + some, row + some
    store(up_out, down_out)
    wait(5, 6)
    samples = keep_ref.shape[0]
    here, there = pl.ds(mp * samples, samples), pl.ds((1 - mp) * samples, samples)
    atoms_out[here] = keep_ref[...]
    atoms_out[there] = got_ref[...].astype(WIDE)
    store(atoms_out)
    wait(7, 8)
    token_out[here] = result_ref[...]
    token_out[there] = other_result_ref[...]
    store(token_out)
    wait(9, 10, 11, 12)
    width, rows = atoms_out.shape[2], out_out.shape[0]
    part_rows = rows // 2

    def own_lanes(values):
        return jnp.where(section == 0, values[:, :rows], values[:, rows:width])

    gain_out[...] = own_lanes(last_ref[part_rows : part_rows + 16, :].astype(WIDE))[:1]
    pair = first_ref[rows + part_rows : rows + part_rows + 16, :].astype(WIDE)
    pair_out[...] = own_lanes(pair[8:])
    for h in range(2):
        first = jnp.where(mp == h, first_ref[...], first_other_ref[...]).astype(WIDE)
        last = jnp.where(mp == h, last_ref[...], last_other_ref[...]).astype(WIDE)
        cols = slice(h * half, (h + 1) * half)
        part_at = slice(h * part_rows, (h + 1) * part_rows)
        agg_out[:, cols] = first[:rows]
        out_out[part_at, :] = first[rows : rows + part_rows, :width]
        for k in range(3):
            row = rows + part_rows + k
            cond_bias_out[k, :, cols] = first[row : row + 1]
        for k in range(3):
            qkv_out[k, part_at, :] = last[:part_rows, k * width : (k + 1) * width]
    store(gain_out, pair_out, agg_out, out_out, cond_bias_out, qkv_out)
    local.finish()


def results(
    result, other_result, keep, got, first, first_other, last, last_other, cond, cond_other, attn,
    mlp_first, mlp_late, width, mlp_local,
):
    samples, half_atoms, atom_width = keep.shape
    half, rows = width // 2, atom_width // 2
    attn_local = attn.shape[0] - 4 * half
    hbm = pl.BlockSpec(memory_space=pl.ANY)
    outs = [
        sds((2 * samples,) + result.shape[1:], LOW),
        sds((2 * samples, half_atoms, atom_width), WIDE),
        sds((1, rows), WIDE),
        sds((3, rows, atom_width), WIDE),
        sds((rows, atom_width), WIDE),
        sds((rows, width), WIDE),
        sds((3, cond.shape[0] // 3, width), WIDE),
        sds((3, 1, width), WIDE),
        sds((8, rows), WIDE),
        sds((half, 4, attn_local), WIDE),
        sds((attn_local, half), WIDE),
        sds((half, 2, mlp_local), WIDE),
        sds((mlp_local, half), WIDE),
    ]
    args = (
        cond, cond_other, attn, mlp_first, mlp_late, keep, got, result, other_result, first,
        first_other, last, last_other,
    )
    return pl.pallas_call(
        results_kernel,
        in_specs=[hbm] * len(args),
        out_specs=[hbm] * len(outs),
        out_shape=outs,
        scratch_shapes=[
            *(pltpu.VMEM(a.shape, a.dtype) for a in args),
            *(pltpu.VMEM(a.shape, a.dtype) for a in outs),
            pltpu.SemaphoreType.DMA((32,)),
        ],
        compiler_params=params(60),
        cost_estimate=cost(1e8, 20e6),
        name="results",
    )(*args)


def local(
    atoms_in,
    atom_token,
    window_start,
    noise_level,
    level_table,
    single_trunk,
    pair,
    atom_gain,
    atom_qkv,
    atom_out,
    atom_agg,
    cond_weight,
    cond_bias,
    pair_weight,
    attn_in,
    attn_out,
    mlp_up,
    mlp_down,
    cotangent,
):
    section, mp = lax.axis_index("section"), lax.axis_index("mp")
    batch, half_atoms, atom_width = atoms_in.shape
    batch //= MICRO
    samples = batch // 2
    atoms = 2 * half_atoms
    tokens, width = cotangent.shape[1], cotangent.shape[2]
    single = single_trunk.shape[1]
    gain = atom_gain[None, :]
    qkv_w = jnp.transpose(atom_qkv, (1, 0, 2))

    cond_w = jnp.transpose(cond_weight, (0, 2, 1, 3)).reshape(6, single, width)
    (
        low, cond_a, cond_b, low_pair, bias, all_atoms, qkv, probs, mixed, token_in,
        in_b, out_b, up_b, down_b, inverse_counts, in_a, up_a,
    ) = front(
        single_trunk, noise_level, level_table, cond_w, jnp.transpose(cond_bias, (1, 0, 2)), pair,
        pair_weight.T,
        atoms_in, gain, qkv_w, atom_out, atom_agg, window_start, atom_token[None, :],
        attn_in, attn_out, mlp_up, mlp_down,
    )
    token_in = token_in.reshape(-1, width)
    inner, token_qkv, sig, heads_out, gated, token_probs, attn, middle = token_attention(
        token_in, cond_a, bias, in_a, in_b, attn_out, out_b
    )
    (
        result, other_result, token_grad, attn_grads, cond_bias_a, cond_bias_b, bias_grad, mlp_first,
        mlp_part,
    ) = (
        token_back(
            middle, cond_b, cotangent, low, up_a, up_b, mlp_down, down_b, token_in, cond_a, attn,
            inner, token_qkv, sig, heads_out, gated, token_probs, in_a, in_b, attn_out, out_b,
        )
    )
    (
        keep, got, attn_sum, cond_sum, cond_other, first, first_other, last, last_other, mlp_late,
    ) = atom_back(
        all_atoms, gain, qkv_w, atom_out, atom_agg, atom_token[None, :], inverse_counts,
        qkv, probs, mixed, token_grad.reshape(samples, tokens, width),
        low_pair, bias_grad, attn_grads, cond_bias_a, cond_bias_b, mlp_part, 3 * single,
    )

    outs = results(
        result.reshape(samples, tokens, width), other_result.reshape(samples, tokens, width),
        keep, got, first, first_other, last, last_other, cond_sum, cond_other, attn_sum,
        mlp_first, mlp_late, width, mlp_up.shape[2],
    )
    token_out, atoms_out, gain_out, qkv_out, out_out, agg_out, cond_out = outs[:7]
    cond_bias_out, pair_out, in_out, attn_out_grad, up_out, down_out = outs[7:]
    return (
        token_out.reshape(1, 1, batch, tokens, width),
        atoms_out.reshape(1, 1, batch, half_atoms, atom_width),
        gain_out[0],
        jnp.transpose(qkv_out, (1, 0, 2)),
        out_out,
        agg_out,
        jnp.transpose(cond_out, (1, 0, 2))[None],
        jnp.transpose(cond_bias_out, (1, 0, 2)),
        pair_out.T,
        in_out,
        attn_out_grad,
        up_out,
        down_out,
    )


def solution(mesh):
    in_specs = (
        P("dp", "mp", None),
        P(),
        P("mp"),
        P("dp"),
        P(),
        P(),
        P(),
        P(),
        P(),
        P(),
        P(),
        P(),
        P(),
        P(None, "mp"),
        P(None, None, "mp"),
        P("mp", None),
        P(None, None, "mp"),
        P("mp", None),
        P("dp", None, None),
    )
    out_specs = (
        P("dp", "section", None, None, None),
        P("dp", "section", None, "mp", None),
        P("section"),
        P("section", None, None),
        P("section", None),
        P("section", None),
        P("section", None, None, None),
        P("section", None, None),
        P("section", "mp"),
        P("section", None, "mp"),
        P("mp", "section"),
        P("section", None, "mp"),
        P("mp", "section"),
    )
    return jax.shard_map(local, mesh=mesh, in_specs=in_specs, out_specs=out_specs, check_vma=False)
```

```python
import functools

import jax
import jax.numpy as jnp
from jax import lax
from jax.experimental import pallas as pl
from jax.experimental.pallas import tpu as pltpu
from jax.sharding import PartitionSpec as P

QBLOCK = 32
KWIN = 128
MICRO = 2
ATOM_HEADS = 4
SPAN = 2
EPS = 1e-05
LOW = jnp.bfloat16
WIDE = jnp.float32
MIB = 1 << 20


def mul(left, right):
    return lax.dot_general(left, right, (((1,), (0,)), ((), ())), preferred_element_type=WIDE)


def mul_nt(left, right):
    return lax.dot_general(left, right, (((1,), (1,)), ((), ())), preferred_element_type=WIDE)


def mul_tn(left, right):
    return lax.dot_general(left, right, (((0,), (0,)), ((), ())), preferred_element_type=WIDE)


def layer_norm(values):
    center = values - jnp.mean(values, -1, keepdims=True)
    inverse = lax.rsqrt(jnp.mean(center * center, -1, keepdims=True) + EPS)
    return center * inverse, inverse


def norm_back(normed, inverse, grad):
    return inverse * (
        grad
        - jnp.mean(grad, -1, keepdims=True)
        - normed * jnp.mean(grad * normed, -1, keepdims=True)
    )


def sigmoid(values):
    return 1.0 / (1.0 + jnp.exp(-values))


def params(mib, semantics=None):
    return pltpu.CompilerParams(vmem_limit_bytes=mib * MIB, dimension_semantics=semantics)


def cost(flops, moved, exps=0):
    return pl.CostEstimate(flops=int(flops), bytes_accessed=int(moved), transcendentals=int(exps))


def sds(shape, dtype):
    return jax.ShapeDtypeStruct(shape, dtype)


def joined(ref):
    return jnp.concatenate([ref[k] for k in range(ref.shape[0])], 1)


def lane_heads(rows, width, size):
    return lax.broadcasted_iota(jnp.int32, (rows, width), 1) // size


def spread(values, heads):
    head = lane_heads(values.shape[0], values.shape[1], values.shape[1] // heads)
    zero = jnp.zeros_like(values)
    return jnp.concatenate([jnp.where(head == h, values, zero) for h in range(heads)], 0)


def gather_heads(values, heads):
    rows = values.shape[0] // heads
    head = lane_heads(rows, values.shape[1], values.shape[1] // heads)
    total = jnp.where(head == 0, values[:rows], 0.0)
    for h in range(1, heads):
        total += jnp.where(head == h, values[h * rows : (h + 1) * rows], 0.0)
    return total


def pairs(first, last, body):
    def step(i, carry):
        body(first + 2 * i, carry)
        body(first + 2 * i + 1, carry)
        return carry

    lax.fori_loop(0, (last - first) // 2, step, 0)
    if (last - first) % 2:
        body(last - 1, 0)


def key_base(group, atoms):
    start = group * SPAN * QBLOCK - KWIN // 2
    return pl.multiple_of(jnp.clip(start, 0, atoms - KWIN - (SPAN - 1) * QBLOCK - QBLOCK), QBLOCK)


def far_lines():
    bits = lax.axis_size("dp").bit_length() - 2
    return [(1 + b, 4 if b + 1 < bits else 2) for b in range(0, bits, 2)]


class Links:
    def __init__(self, send_sem, recv_sem, far=True):
        self.section, self.mp = lax.axis_index("section"), lax.axis_index("mp")
        self.dp = lax.axis_index("dp")
        self.core = self.dp % 2
        self.partners = [{"section": 1 - self.section}, {"mp": 1 - self.mp}]
        self.partners.append({"dp": self.dp + 1 - 2 * self.core})
        self.x, self.y, self.twin = self.partners
        self.lines = []
        for bit, count in far_lines() if far else ():
            place = self.dp // (1 << bit) % count
            beside = {"dp": self.dp + (1 - 2 * (place % 2)) * (1 << bit)}
            across = {"dp": self.dp + (count - 1 - 2 * place) * (1 << bit)}
            self.lines.append((count, place, beside, across))
            self.partners += [beside, across] if count == 4 else [beside]
        self.send_sem, self.recv_sem, self.used = send_sem, recv_sem, 0

    def barrier(self):
        barrier = pltpu.get_barrier_semaphore()
        for partner in self.partners:
            pl.semaphore_signal(
                barrier, inc=1, device_id=partner, device_id_type=pl.DeviceIdType.MESH
            )
        pl.semaphore_wait(barrier, len(self.partners))

    def copy(self, source, target, partner):
        copy = pltpu.make_async_remote_copy(
            src_ref=source,
            dst_ref=target,
            send_sem=self.send_sem.at[self.used],
            recv_sem=self.recv_sem.at[self.used],
            device_id=partner,
            device_id_type=pl.DeviceIdType.MESH,
        )
        self.used += 1
        return copy

    def send(self, source, target, partner):
        copy = self.copy(source, target, partner)
        copy.start()
        return copy


def far_copies():
    return sum(3 if count == 4 else 1 for _, count in far_lines())


def journey_copies(shared, near=3):
    return near + far_copies() + 1 + (2 if shared else 0)


def far_slots():
    return sum(count // 2 for _, count in far_lines())


def far_scratch(rows, cols):
    return [pltpu.VMEM((rows, cols), LOW)] * far_slots()


def near_scratch(rows, cols):
    return [pltpu.VMEM(shape + (rows, cols), LOW) for shape in ((2, 2), (2,), ())]


def journey_scratch(rows, cols):
    return near_scratch(rows, cols) + far_scratch(rows, cols)


class Pool:
    def __init__(self, buffers):
        self.buffers, self.used = buffers, 0

    def take(self, count):
        self.used += count
        return self.buffers[self.used - count : self.used]


def offsets(sizes):
    return [sum(sizes[:i]) for i in range(len(sizes))]


def journey(links, grads, kept, buffers, out, other_out, offset, rows, x_first, shared, part=None):
    near, middle, last, *far = buffers
    total_rows = grads.shape[2]
    start = links.core * (total_rows // 2) + offset
    twin_start = (1 - links.core) * (total_rows // 2) + offset
    mine, theirs = pl.ds(pl.multiple_of(start, 16), rows), pl.ds(pl.multiple_of(twin_start, 16), rows)
    me, you = links.section, 1 - links.section
    if kept is None:
        own = grads.at[:, :, mine, :]
    else:
        own = kept.at[:, :, pl.ds(offset, rows), :]
    block = rows * grads.shape[3] * 2
    copy = links.send(grads.at[:, :, theirs, :], near, links.twin)
    yield [("core", 4 * block)]
    copy.wait()
    if x_first:
        near[:, you] += own[:, you]
        copy = links.send(near.at[:, you], middle, links.x)
        near[:, me] += own[:, me]
        yield [("x", 2 * block)]
        copy.wait()
        middle[1] += near[1, me]
        copy = links.send(middle.at[1], last, links.y)
        middle[0] += near[0, me]
        yield [("y", block)]
        copy.wait()
        last[...] += middle[0]
    else:
        near[1] += own[1]
        copy = links.send(near.at[1], middle, links.y)
        near[0] += own[0]
        yield [("y", 2 * block)]
        copy.wait()
        middle[you] += near[0, you]
        copy = links.send(middle.at[you], last, links.x)
        middle[me] += near[0, me]
        yield [("x", block)]
        copy.wait()
        last[...] += middle[me]
    if part is not None:
        part[...] = last[...]
        return
    yield from far_journey(links, last, far, out, other_out, offset, shared)


def far_journey(links, held, far, out, other_out, offset, shared):
    rows = held.shape[0]
    start = links.core * (out.shape[0] // 2) + offset
    mine = pl.ds(pl.multiple_of(start, 16), rows)
    block = rows * held.shape[1] * 2
    far = list(far)
    for count, place, beside, across in links.lines:
        if count == 2:
            slot = far.pop(0)
            copy = links.send(held, slot, beside)
            yield [("z", block)]
            copy.wait()
            held[...] += slot[...]
            continue
        inner = (place == 1) | (place == 2)
        outer = (place == 0) | (place == 3)
        slot, second = far.pop(0), far.pop(0)
        gather = links.copy(held, slot, beside)
        exchange = links.copy(held, second, across)
        spread_back = links.copy(held, slot, beside)

        @pl.when(outer)
        def _():
            gather.start()

        yield [("z", block)]

        @pl.when(outer)
        def _():
            gather.wait_send()

        @pl.when(inner)
        def _():
            gather.wait_recv()
            held[...] += slot[...]
            exchange.start()

        yield [("mid", block)]

        @pl.when(inner)
        def _():
            exchange.wait()
            held[...] += second[...]
            spread_back.start()

        yield [("back", block)]

        @pl.when(inner)
        def _():
            spread_back.wait_send()

        @pl.when(outer)
        def _():
            spread_back.wait_recv()
            held[...] = slot[...]

    out[mine, :] = held[...]
    copies = [links.send(out.at[mine, :], out.at[mine, :], links.twin)]
    if shared:
        across = links.send(out.at[mine, :], other_out.at[mine, :], links.y)
        yield [("y", block)]
        across.wait()
        copies.append(links.send(other_out.at[mine, :], other_out.at[mine, :], links.twin))
    yield [("core", block)]
    for copy in copies:
        copy.wait()


class Flow:
    CORE_RATE = 400e3
    DELAYS = {"core": 0.4}

    def __init__(self, journeys, rate=42e3):
        self.rate = rate
        self.clock, self.free, self.queue, self.count = 0.0, {}, [], 0
        for one in journeys:
            self.add(one)

    def add(self, one):
        self.clock += 0.2
        copies = next(one, None)
        if copies is None:
            return
        ready = self.clock
        for link, count in copies:
            finish = max(self.clock, self.free.get(link, 0.0)) + count / (self.CORE_RATE if link == "core" else self.rate)
            self.free[link] = finish
            ready = max(ready, finish + self.DELAYS.get(link, 1.5))
        self.queue.append((ready, self.count, one))
        self.queue.sort(key=lambda entry: entry[:2])
        self.count += 1

    def after(self, duration):
        self.clock += duration
        while self.queue and self.queue[0][0] <= self.clock:
            self.add(self.queue.pop(0)[2])

    def finish(self):
        while self.queue:
            self.clock = max(self.clock, self.queue[0][0])
            self.add(self.queue.pop(0)[2])


def everywhere(count):
    return [pl.BlockSpec(memory_space=pltpu.VMEM)] * count


def remote_params(mib, number):
    return pltpu.CompilerParams(
        vmem_limit_bytes=mib * MIB, collective_id=number, has_side_effects=True
    )


class Local:
    def __init__(self, sem):
        self.sem, self.used, self.open = sem, 0, []

    def start(self, source, target):
        copy = pltpu.make_async_copy(source, target, self.sem.at[self.used])
        self.used += 1
        copy.start()
        return copy

    def store(self, source, target):
        self.open.append(self.start(source, target))

    def finish(self):
        for copy in self.open:
            copy.wait()


def fetch_journey(links, own, other, chunk, rows):
    quarter = own.shape[0] // 4
    block = rows * own.shape[1] * 2

    def at(core, section):
        start = (2 * core + section) * quarter + chunk * rows
        return pl.ds(pl.multiple_of(start, 16), rows)

    mine = at(links.core, links.section)
    across = at(links.core, 1 - links.section)
    copy = links.send(own.at[mine, :], other.at[mine, :], links.y)
    yield [("y", block)]
    copy.wait()
    first = links.send(other.at[mine, :], other.at[mine, :], links.x)
    second = links.send(other.at[mine, :], other.at[mine, :], links.twin)
    yield [("x", block), ("core", block)]
    first.wait()
    third = links.send(other.at[across, :], other.at[across, :], links.twin)
    yield [("core", block)]
    second.wait()
    third.wait()


def fetch_eighths(links, own, other, chunk, rows):
    piece = own.shape[0] // 8
    block = rows * own.shape[1] * 2
    _, place, beside, _ = links.lines[0]
    side = place % 2

    def at(section, z):
        start = ((2 * links.core + section) * 2 + z) * piece + chunk * rows
        return other.at[pl.ds(pl.multiple_of(start, 16), rows), :]

    me, you = links.section, 1 - links.section
    mine, across = at(me, side), at(you, side)
    start = ((2 * links.core + me) * 2 + side) * piece + chunk * rows
    source = own.at[pl.ds(pl.multiple_of(start, 16), rows), :]
    copy = links.send(source, mine, links.y)
    yield [("y", block)]
    copy.wait()
    over_x = links.send(mine, mine, links.x)
    over_z = [links.send(mine, mine, beside)]
    twins = [links.send(mine, mine, links.twin)]
    yield [("x", block)]
    over_x.wait()
    over_z.append(links.send(across, across, beside))
    twins.append(links.send(across, across, links.twin))
    yield [("z", 2 * block)]
    for copy, section in zip(over_z, (me, you)):
        copy.wait()
        far = at(section, 1 - side)
        twins.append(links.send(far, far, links.twin))
    yield [("core", 2 * block)]
    for copy in twins:
        copy.wait()


def front_kernel(
    trunk_ref, noise_ref, level_ref, cond_w_ref, cond_b_ref, pair_ref, pair_w_ref, atoms_ref,
    gain_ref, qkv_w_ref, out_w_ref, agg_w_ref, start_ref, ids_ref, in_a_ref, out_a_ref, up_a_ref,
    down_a_ref,
    low_ref, cond_a_ref, cond_b_out_ref, low_pair_ref, bias_ref, atoms_out_ref, qkv_ref, probs_ref,
    mixed_ref, tokens_ref, in_b_ref, out_b_ref, up_b_ref, down_b_ref, inv_ref,
    in_flat_ref, up_flat_ref,
    cond_w, cond_out, pair, pair_w, bias, atoms, rel_own, rel, qkv, probs, mixed, total, tokens,
    in_raw, up_raw, in_flat, up_flat,
    local_sem, send_sem, recv_sem,
):
    links = Links(send_sem, recv_sem)
    local = Local(local_sem)
    samples, count, width = atoms.shape
    half_atoms = count // 2
    batch = atoms_ref.shape[0] // MICRO
    parts = cond_w.shape[0]
    raw_loads = [local.start(in_a_ref, in_raw), local.start(up_a_ref, up_raw)]
    loads = [local.start(cond_w_ref.at[i], cond_w.at[i]) for i in range(parts)]
    pieces = 2
    pair_rows_in = pair.shape[0]
    each = pair_rows_in // pieces
    pair_first = links.core * pair_rows_in
    pair_loads = [
        local.start(
            pair_ref.at[pl.ds(pair_first + i * each, each)], pair.at[pl.ds(i * each, each)]
        )
        for i in range(pieces)
    ]
    own_first = links.section * batch + links.mp * samples
    other_first = links.section * batch + (1 - links.mp) * samples
    own_half = pl.ds(pl.multiple_of(links.mp * half_atoms, 16), half_atoms)
    groups_in = rel_own.shape[0]
    own_groups = pl.ds(links.mp * groups_in, groups_in)
    lane = lax.broadcasted_iota(jnp.int32, rel_own.shape[1:], 1) % (SPAN * QBLOCK)
    for i in range(groups_in):
        starts = jnp.where(lane < QBLOCK, start_ref[SPAN * i], start_ref[SPAN * i + 1])
        rel_own[i] = starts - key_base(links.mp * groups_in + i, count)
    heads = pair_w_ref.shape[0]
    atom_loads = [
        local.start(atoms_ref.at[pl.ds(own_first, samples)], atoms.at[:, own_half, :]),
        local.start(rel_own, rel.at[own_groups]),
        local.start(pair_w_ref, pair_w.at[0]),
    ]
    links.barrier()
    pair_w_copy = links.send(pair_w_ref, pair_w.at[1], links.y)
    rel_copy = links.send(rel_own, rel.at[own_groups], links.y)
    atom_copy = links.send(
        atoms_ref.at[pl.ds(other_first, samples)], atoms.at[:, own_half, :], links.y
    )
    flow = Flow([], 45e3)
    flow.free["y"] = samples * half_atoms * width * 2 / flow.rate
    for copy, raw, flat, target in (
        (raw_loads[0], in_raw, in_flat, in_flat_ref),
        (raw_loads[1], up_raw, up_flat, up_flat_ref),
    ):
        copy.wait()
        step = 64
        for row in range(0, raw.shape[0], step):
            block = raw[row : row + step]
            flat[row : row + step, :] = block.reshape(step, flat.shape[1])
        local.store(flat, target)
    for way, parts_in, own, other, chunks in (
        (fetch_eighths, 8, in_flat, in_b_ref, 2),
        (fetch_eighths, 8, up_flat, up_b_ref, 2),
        (fetch_journey, 4, out_a_ref, out_b_ref, 1),
        (fetch_journey, 4, down_a_ref, down_b_ref, 2),
    ):
        for i in range(chunks):
            flow.add(way(links, own, other, i, own.shape[0] // parts_in // chunks))

    trunk = trunk_ref[...].astype(WIDE)
    rows = trunk.shape[0]
    for s in range(samples):
        level_rows = lax.broadcasted_iota(jnp.int32, level_ref.shape, 0)
        level = jnp.where(level_rows == noise_ref[own_first + s], level_ref[...].astype(WIDE), 0.0)
        normed, _ = layer_norm(trunk + jnp.sum(level, 0, keepdims=True))
        low_ref[s * rows : (s + 1) * rows, :] = normed.astype(LOW)
    for i in range(parts):
        loads[i].wait()
        value = mul(low_ref[...], cond_w[i]) + cond_b_ref[i % 3, i // 3 : i // 3 + 1, :].astype(WIDE)
        cond_out[i] = value if i % 3 == 1 else sigmoid(value)
        target = (cond_a_ref, cond_b_out_ref)[i // 3]
        local.store(cond_out.at[i], target.at[i % 3])
    flow.after(4.0)

    atom_loads[2].wait()
    pair_w_copy.wait()
    weight = jnp.concatenate([pair_w[0], pair_w[1]], 0)
    block = 8
    for piece in range(pieces):
        pair_loads[piece].wait()

        def pair_rows(i, carry):
            at = pl.multiple_of(i * block, block)
            normed, _ = layer_norm(pair[pl.ds(at, block)].astype(WIDE))
            low = normed.astype(LOW)
            pair[pl.ds(at, block)] = low
            for j in range(block):
                bias[:, pl.ds(pair_first + at + j, 1), :] = mul_nt(weight, low[j])[:, None, :]
            return carry

        lax.fori_loop(piece * each // block, (piece + 1) * each // block, pair_rows, 0)
        at = pl.ds(piece * each, each)
        local.store(pair.at[at], low_pair_ref.at[at])
        flow.after(2.8)
    own_rows = pl.ds(pl.multiple_of(pair_first, 8), pair_rows_in)
    bias_copy = links.send(bias.at[:, own_rows, :], bias.at[:, own_rows, :], links.twin)

    for copy in (atom_loads[0], atom_loads[1], rel_copy, atom_copy):
        copy.wait()
    local.store(atoms, atoms_out_ref)
    bias_copy.wait()
    local.store(bias, bias_ref)
    groups, keys_in = probs.shape[1], probs.shape[2]
    queries_in = SPAN * QBLOCK
    scale = (width // ATOM_HEADS) ** (-0.5)
    place = lax.broadcasted_iota(jnp.int32, (keys_in, ATOM_HEADS * queries_in), 0)
    chunk = 256
    ids = lax.broadcasted_iota(jnp.int32, (total.shape[0], chunk), 0)
    for s in range(samples):
        normed, _ = layer_norm(atoms[s].astype(WIDE))
        hidden = (normed * gain_ref[...].astype(WIDE)).astype(LOW)
        qkv[s] = mul(hidden, joined(qkv_w_ref)).astype(LOW)
        local.store(qkv.at[s], qkv_ref.at[s])
        flow.after(1.2)

        def attend(group, carry, s=s):
            base = key_base(group, count)
            first = pl.multiple_of(group * queries_in, queries_in)
            queries = spread(qkv[s, pl.ds(first, queries_in), :width], ATOM_HEADS)
            keys = qkv[s, pl.ds(base, keys_in), width : 2 * width]
            values = qkv[s, pl.ds(base, keys_in), 2 * width :]
            offset = place - rel[group]
            scores = mul_nt(keys, queries) * scale
            scores = jnp.where((offset >= 0) & (offset < KWIN), scores, -1e30)
            exps = jnp.exp(scores - jnp.max(scores, 0, keepdims=True))
            low = (exps * (1.0 / jnp.sum(exps, 0, keepdims=True))).astype(LOW)
            probs[s, group] = low
            mixed[s, pl.ds(first, queries_in), :] = gather_heads(
                mul_tn(low, values), ATOM_HEADS
            ).astype(LOW)
            return carry

        cuts = 5
        for i in range(cuts):
            pairs(groups * i // cuts, groups * (i + 1) // cuts, attend)
            flow.after(1.3)
        local.store(probs.at[s], probs_ref.at[s])
        local.store(mixed.at[s], mixed_ref.at[s])
        for i in range(count // chunk):
            rows = slice(i * chunk, (i + 1) * chunk)
            after = atoms[s, rows, :].astype(WIDE) + mul(mixed[s, rows, :], out_w_ref[...])
            pre = mul(after.astype(LOW), agg_w_ref[...])
            units = (pre * sigmoid(pre)).astype(LOW)
            member = jnp.where(ids == ids_ref[:, rows], 1.0, 0.0).astype(LOW)
            part_sum = mul(member, units)
            if i == 0:
                total[...] = part_sum
            else:
                total[...] += part_sum
            if s == 0:
                number = jnp.sum(member.astype(WIDE), 1, keepdims=True)
                counts = number if i == 0 else counts + number
            flow.after(0.9)
        if s == 0:
            inv_ref[...] = 1.0 / counts
        tokens[s] = (total[...] * inv_ref[...]).astype(LOW)
        local.store(tokens.at[s], tokens_ref.at[s])
    flow.finish()
    local.finish()


def front(
    trunk, noise, levels, cond_w, cond_b, pair, pair_w, atoms, gain, qkv_w, out_w, agg_w, starts,
    ids, in_a, out_a, up_a, down_a,
):
    tokens_in, width = trunk.shape
    parts, wide = cond_w.shape[0], cond_w.shape[2]
    samples = atoms.shape[0] // MICRO // 2
    rows = samples * tokens_in
    count, atom_width = 2 * atoms.shape[1], atoms.shape[2]
    heads = 2 * pair_w.shape[0]
    groups = count // (SPAN * QBLOCK)
    keys_in, lanes = KWIN + SPAN * QBLOCK, ATOM_HEADS * SPAN * QBLOCK
    probs_shape = (samples, groups, keys_in, lanes)
    flat_in, flat_up = ((a.shape[0], a.shape[1] * a.shape[2]) for a in (in_a, up_a))
    half_pair = (pair.shape[0] // 2,) + pair.shape[1:]
    hbm, near = pl.BlockSpec(memory_space=pl.ANY), pl.BlockSpec(memory_space=pltpu.VMEM)
    smem = pl.BlockSpec(memory_space=pltpu.SMEM)
    outs = [
        (near, (rows, width), LOW),
        (hbm, (parts // 2, rows, wide), WIDE),
        (hbm, (parts // 2, rows, wide), WIDE),
        (hbm, half_pair, LOW),
        (hbm, (heads, tokens_in, tokens_in), WIDE),
        (hbm, (samples, count, atom_width), LOW),
        (hbm, (samples, count, 3 * atom_width), LOW),
        (hbm, probs_shape, LOW),
        (hbm, (samples, count, atom_width), LOW),
        (hbm, (samples, tokens_in, wide), LOW),
        (hbm, flat_in, LOW),
        (hbm, out_a.shape, LOW),
        (hbm, flat_up, LOW),
        (hbm, down_a.shape, LOW),
        (near, (tokens_in, 1), WIDE),
        (hbm, flat_in, LOW),
        (hbm, flat_up, LOW),
    ]
    copies = 4 + 4 * 8 + 3 * 4
    return pl.pallas_call(
        front_kernel,
        in_specs=[near, smem, near, hbm, near, hbm, near, hbm] + [near] * 4 + [smem, near] + [hbm] * 4,
        out_specs=[spec for spec, _, _ in outs],
        out_shape=[sds(shape, dtype) for _, shape, dtype in outs],
        scratch_shapes=[
            pltpu.VMEM(cond_w.shape, LOW),
            pltpu.VMEM((parts, rows, wide), WIDE),
            pltpu.VMEM(half_pair, LOW),
            pltpu.VMEM((2,) + pair_w.shape, LOW),
            pltpu.VMEM((heads, tokens_in, tokens_in), WIDE),
            pltpu.VMEM((samples, count, atom_width), LOW),
            pltpu.VMEM((groups // 2, 1, lanes), jnp.int32),
            pltpu.VMEM((groups, 1, lanes), jnp.int32),
            pltpu.VMEM((samples, count, 3 * atom_width), LOW),
            pltpu.VMEM(probs_shape, LOW),
            pltpu.VMEM((samples, count, atom_width), LOW),
            pltpu.VMEM((tokens_in, wide), WIDE),
            pltpu.VMEM((samples, tokens_in, wide), LOW),
            *(pltpu.VMEM(shape, LOW) for shape in (in_a.shape, up_a.shape, flat_in, flat_up)),
            pltpu.SemaphoreType.DMA((64,)),
            pltpu.SemaphoreType.DMA((copies,)),
            pltpu.SemaphoreType.DMA((copies,)),
        ],
        compiler_params=remote_params(60, 3),
        cost_estimate=cost(40e9, 40e6),
        name="front",
    )(
        trunk, noise, levels, cond_w, cond_b, pair, pair_w, atoms, gain, qkv_w, out_w, agg_w,
        starts, ids, in_a, out_a, up_a, down_a,
    )


def token_attention_kernel(
    tokens_ref, cond_ref, bias_ref, in_a_ref, in_b_ref, out_a_ref, out_b_ref,
    inner_ref, qkv_ref, sig_ref, heads_ref, gated_ref, probs_ref, attn_ref, middle_ref,
    tokens, cond, bias, in_a, in_b, out_a, out_b, inner, qkv, sig, heads_out, gated, probs, attn,
    middle, local_sem,
):
    local = Local(local_sem)
    load_tokens = local.start(tokens_ref, tokens)
    load_cond = local.start(cond_ref, cond)
    load_in = [local.start(in_a_ref, in_a)]
    load_bias = local.start(bias_ref, bias)
    load_in.append(local.start(in_b_ref, in_b))
    load_out = [local.start(out_a_ref, out_a), local.start(out_b_ref, out_b)]
    samples, heads, count = probs.shape[0], probs.shape[1], probs.shape[2]
    width_in = in_a.shape[1] // 4
    size = 2 * width_in // heads
    scale = size ** (-0.5)
    load_tokens.wait()
    load_cond.wait()
    wide = tokens[...].astype(WIDE)
    normed, _ = layer_norm(wide)
    inner[...] = (normed * cond[0] + cond[1]).astype(LOW)
    local.store(inner, inner_ref)
    for half, weight in enumerate((in_a, in_b)):
        load_in[half].wait()
        qkv[half] = mul(inner[...], weight[:, : 3 * width_in]).astype(LOW)
        local.store(qkv.at[half], qkv_ref.at[half])
        sig[half] = sigmoid(mul(inner[...], weight[:, 3 * width_in :]))
        local.store(sig.at[half], sig_ref.at[half])
        if half == 0:
            load_bias.wait()
        for s in range(samples):
            at = slice(s * count, (s + 1) * count)
            outs = []
            for h in range(heads // 2):
                col = h * size
                query = qkv[half, at, col : col + size]
                key = qkv[half, at, width_in + col : width_in + col + size]
                value = qkv[half, at, 2 * width_in + col : 2 * width_in + col + size]
                scores = mul_nt(query, key) * scale + bias[half * (heads // 2) + h]
                exps = jnp.exp(scores - jnp.max(scores, -1, keepdims=True))
                low = (exps * (1.0 / jnp.sum(exps, -1, keepdims=True))).astype(LOW)
                probs[s, half * (heads // 2) + h] = low
                outs.append(mul(low, value))
            heads_out[half, at, :] = jnp.concatenate(outs, 1)
        gated[half] = (heads_out[half] * sig[half]).astype(LOW)
        local.store(heads_out.at[half], heads_ref.at[half])
        local.store(gated.at[half], gated_ref.at[half])
    local.store(probs, probs_ref)
    load_out[0].wait()
    load_out[1].wait()
    attn[...] = mul(gated[0], out_a[...]) + mul(gated[1], out_b[...])
    local.store(attn, attn_ref)
    middle[...] = wide + cond[2] * attn[...]
    local.store(middle, middle_ref)
    local.finish()


def token_attention(tokens, cond, bias, in_a, in_b, out_a, out_b):
    rows, width = tokens.shape
    heads, count = bias.shape[0], bias.shape[1]
    samples, width_in = rows // count, in_a.shape[1] // 4
    hbm = pl.BlockSpec(memory_space=pl.ANY)
    outs = [
        sds((rows, width), LOW),
        sds((2, rows, 3 * width_in), LOW),
        sds((2, rows, width_in), WIDE),
        sds((2, rows, width_in), WIDE),
        sds((2, rows, width_in), LOW),
        sds((samples, heads, count, count), LOW),
        sds((rows, width), WIDE),
        sds((rows, width), WIDE),
    ]
    args = (tokens, cond, bias, in_a, in_b, out_a, out_b)
    return pl.pallas_call(
        token_attention_kernel,
        in_specs=[hbm] * len(args),
        out_specs=[hbm] * len(outs),
        out_shape=outs,
        scratch_shapes=[
            *(pltpu.VMEM(a.shape, a.dtype) for a in args),
            *(pltpu.VMEM(a.shape, a.dtype) for a in outs),
            pltpu.SemaphoreType.DMA((32,)),
        ],
        compiler_params=params(60),
        cost_estimate=cost(40e9, 20e6),
        name="token_attention",
    )(*args)


CHUNK = 192
MLP_CHUNKS = (192,) * 6
MLP_X_FIRST = (True, True, False, True, True, True)
EARLY = 2
COND_CHUNKS = (192,) * 3
ATTN_CHUNKS = (192,) * 5
ORDER = (
    ("attn", False), ("attn", True), ("cond", True), ("cond", True), ("attn", True),
    ("cond", False), ("attn", True), ("attn", True),
)


def relative(half, mp):
    return mp if half == 0 else 1 - mp


def token_back_kernel(
    middle_ref, cond_b_ref, cotangent_ref, low_ref, up_a_ref, up_b_ref, down_a_ref, down_b_ref,
    tokens_ref, cond_a_ref, attn_ref, inner_ref, qkv_ref, sig_ref, heads_ref, gated_ref, probs_ref,
    in_a_ref, in_b_ref, out_a_ref, out_b_ref,
    result_ref, other_result_ref, token_grad_ref, grads_ref, cond_bias_a_ref, cond_bias_b_ref,
    bias_grad_ref, mlp_out_ref, mlp_part_ref,
    middle, cond, grad, low, weight, out_weight, up, hidden, mlp_grads, middle_grad, result,
    tokens, inner, qkv, sig, heads_out, gated, probs, grads, bias_grad, proj, heads_grad, *rest,
):
    *buffers, local_sem, send_sem, recv_sem = rest
    links = Links(send_sem, recv_sem)
    local = Local(local_sem)
    load_first = [
        local.start(a, b)
        for a, b in ((middle_ref, middle), (cond_b_ref, cond), (up_a_ref, weight.at[0]))
    ]
    load_up_b = local.start(up_b_ref, weight.at[1])
    load_down = [local.start(down_a_ref, out_weight.at[0])]
    load_down.append(local.start(down_b_ref, out_weight.at[1]))
    samples, tokens_in = probs.shape[0], probs.shape[2]
    batch = cotangent_ref.shape[0] // MICRO
    load_grad = [local.start(low_ref, low)]
    for s in range(samples):
        sample = links.section * batch + links.mp * samples + s
        at = pl.ds(s * tokens_in, tokens_in)
        load_grad.append(local.start(cotangent_ref.at[sample], grad.at[at, :]))
    load_later = [
        local.start(a, b)
        for a, b in (
            (gated_ref, gated), (sig_ref, sig), (heads_ref, heads_out), (qkv_ref, qkv),
            (probs_ref, probs), (inner_ref, inner), (tokens_ref, tokens),
        )
    ]
    links.barrier()
    flow = Flow([], 39e3)
    rows, width = middle.shape
    half_cols = width // 2
    samples, heads, count = probs.shape[0], probs.shape[1], probs.shape[2]

    for copy in load_first:
        copy.wait()
    middle_value = middle[...]
    normed, inverse = layer_norm(middle_value)
    scale, gate = cond[0], cond[2]
    inner_mlp = (normed * scale + cond[1]).astype(LOW)
    mlp_width = hidden.shape[2]
    mlp = None
    for half in range(2):
        if half == 1:
            load_up_b.wait()
        gate_in = mul(inner_mlp, weight[half, :, :mlp_width])
        up_in = mul(inner_mlp, weight[half, :, mlp_width:])
        up[half, :, :mlp_width] = gate_in.astype(LOW)
        up[half, :, mlp_width:] = up_in.astype(LOW)
        hidden[half] = (gate_in * sigmoid(gate_in) * up_in).astype(LOW)
        load_down[half].wait()
        add = mul(hidden[half], out_weight[half])
        mlp = add if mlp is None else mlp + add
    result[...] = (middle_value + gate * mlp).astype(LOW)
    local.store(result, result_ref)
    result_copy = links.send(result, other_result_ref, links.y)
    flow.free["y"] = rows * width * 2 / flow.rate

    for copy in load_grad:
        copy.wait()
    grad_value = grad[...].astype(WIDE)
    mlp_grad = (grad_value * gate).astype(LOW)
    core_rows = mlp_grads.shape[2] // 2
    down_rows = mlp_width // 2
    for half in range(2):
        hidden_t = hidden[half].T
        for core in range(2):
            for sec in range(2):
                mlp_grads[half, sec, core * core_rows : core * core_rows + down_rows, :] = mul(
                    hidden_t[core * down_rows : (core + 1) * down_rows],
                    mlp_grad[:, sec * half_cols : (sec + 1) * half_cols],
                ).astype(LOW)

    pool = Pool(buffers)

    def launch(first, last):
        for i in range(first, last):
            early = i < EARLY
            taken = pool.take(3 + (far_slots() if early else 0))
            part = None if early else mlp_part_ref.at[i - EARLY]
            flow.add(
                journey(
                    links, mlp_grads, None, taken, mlp_out_ref, None,
                    offsets(MLP_CHUNKS)[i], MLP_CHUNKS[i], MLP_X_FIRST[i], False, part,
                )
            )

    launch(0, down_rows // CHUNK)
    inner_t = inner_mlp.T
    inner_grad = None
    for half in range(2):
        hidden_grad = mul_nt(mlp_grad, out_weight[half])
        gate_in = up[half, :, :mlp_width].astype(WIDE)
        up_in = up[half, :, mlp_width:].astype(WIDE)
        sigma = sigmoid(gate_in)
        first = (hidden_grad * up_in * (sigma * (1.0 + gate_in * (1.0 - sigma)))).astype(LOW)
        second = (hidden_grad * (gate_in * sigma)).astype(LOW)
        up_grad = jnp.concatenate([first, second], 1)
        for sec in range(2):
            at = slice(sec * half_cols, (sec + 1) * half_cols)
            for block in range(4):
                place = block // 2 * core_rows + down_rows + block % 2 * half_cols
                mlp_grads[half, sec, place : place + half_cols, :] = mul(
                    inner_t[at], up_grad[:, block * half_cols : (block + 1) * half_cols]
                ).astype(LOW)
        add = mul_nt(up_grad, weight[half])
        inner_grad = add if inner_grad is None else inner_grad + add
        flow.after(3.0)
    load_weight = [local.start(in_a_ref, weight.at[0]), local.start(in_b_ref, weight.at[1])]
    out_rows = out_a_ref.shape[0]
    load_out = [
        local.start(a, out_weight.at[h, :out_rows, :]) for h, a in enumerate((out_a_ref, out_b_ref))
    ]
    launch(down_rows // CHUNK, core_rows // CHUNK)
    middle_grad[...] = grad_value + norm_back(normed, inverse, inner_grad * scale)
    low_t = low[...].T
    first_cond = grads.shape[2] - 3 * low_t.shape[0]

    def cond_back(sec, pieces, bias_out):
        for k, piece in enumerate(pieces):
            piece = piece.astype(LOW)
            place = first_cond + k * low_t.shape[0]
            for h in range(2):
                grads[relative(h, links.mp), sec, place : place + low_t.shape[0], :] = mul(
                    low_t, piece[:, h * half_cols : (h + 1) * half_cols]
                ).astype(LOW)
            bias_out[k] = jnp.sum(piece.astype(WIDE), 0, keepdims=True)

    cond_back(
        1,
        (
            inner_grad * normed * (scale * (1.0 - scale)),
            inner_grad,
            grad_value * mlp * (gate * (1.0 - gate)),
        ),
        cond_bias_b_ref,
    )
    load_cond = local.start(cond_a_ref, cond)
    load_attn = local.start(attn_ref, middle)
    flow.after(3.0)

    local_cols = out_rows
    size = 2 * local_cols // heads
    head_scale = size ** (-0.5)
    load_cond.wait()
    for copy in load_later:
        copy.wait()
    scale, gate = cond[0], cond[2]
    attn_grad = (middle_grad[...] * gate).astype(LOW)
    inner_t = inner[...].T
    inner_grad = None
    for half in range(2):
        load_out[half].wait()
        gated_t = gated[half].T
        for sec in range(2):
            grads[half, sec, 4 * half_cols : first_cond, :] = mul(
                gated_t, attn_grad[:, sec * half_cols : (sec + 1) * half_cols]
            ).astype(LOW)
        gated_grad = mul_nt(attn_grad, out_weight[half, :out_rows, :])
        sig_half = sig[half]
        with_sig = gated_grad * sig_half
        heads_grad[...] = with_sig.astype(LOW)
        proj[:, 3 * local_cols :] = (with_sig * heads_out[half] * (1.0 - sig_half)).astype(LOW)
        flow.after(1.5)
        for s in range(samples):
            at = slice(s * count, (s + 1) * count)
            parts = ([], [], [])
            for h in range(heads // 2):
                col, index = h * size, half * (heads // 2) + h
                query = qkv[half, at, col : col + size]
                key = qkv[half, at, local_cols + col : local_cols + col + size]
                value = qkv[half, at, 2 * local_cols + col : 2 * local_cols + col + size]
                one_grad = heads_grad[at, col : col + size]
                probs_low = probs[s, index]
                wide_probs = probs_low.astype(WIDE)
                probs_grad = mul_nt(one_grad, value)
                mean = jnp.sum(wide_probs * probs_grad, -1, keepdims=True)
                scores_grad = (wide_probs * (probs_grad - mean)).astype(LOW)
                if s == 0:
                    bias_grad[index] = scores_grad.astype(WIDE)
                else:
                    bias_grad[index] += scores_grad.astype(WIDE)
                parts[0].append(mul(scores_grad, key) * head_scale)
                parts[1].append(mul_tn(scores_grad, query) * head_scale)
                parts[2].append(mul_tn(probs_low, one_grad))
                if h % 2 == 1:
                    flow.after(1.0)
            for k in range(3):
                proj[at, k * local_cols : (k + 1) * local_cols] = jnp.concatenate(
                    parts[k], 1
                ).astype(LOW)
        load_weight[half].wait()
        for sec in range(2):
            for k in range(4):
                grads[half, sec, k * half_cols : (k + 1) * half_cols, :] = mul(
                    inner_t[sec * half_cols : (sec + 1) * half_cols],
                    proj[:, k * local_cols : (k + 1) * local_cols],
                ).astype(LOW)
        local.store(grads.at[half, :, :first_cond, :], grads_ref.at[half, :, :first_cond, :])
        some = pl.ds(half * (heads // 2), heads // 2)
        local.store(bias_grad.at[some], bias_grad_ref.at[some])
        add = mul_nt(proj[...], weight[half])
        inner_grad = add if inner_grad is None else inner_grad + add
        flow.after(2.5)
    normed, inverse = layer_norm(tokens[...].astype(WIDE))
    tokens[...] = (middle_grad[...] + norm_back(normed, inverse, inner_grad * scale)).astype(LOW)
    local.store(tokens, token_grad_ref)
    flow.after(1.0)
    load_attn.wait()
    cond_back(
        0,
        (
            inner_grad * normed * (scale * (1.0 - scale)),
            inner_grad,
            middle_grad[...] * middle[...] * (gate * (1.0 - gate)),
        ),
        cond_bias_a_ref,
    )
    local.store(grads.at[:, :, first_cond:, :], grads_ref.at[:, :, first_cond:, :])

    flow.finish()
    result_copy.wait()
    local.finish()


def token_back(
    middle, cond_b, cotangent, low, up_a, up_b, down_a, down_b, tokens, cond_a, attn, inner, qkv,
    sig, heads_out, gated, probs, in_a, in_b, out_a, out_b,
):
    rows, width = tokens.shape
    heads, count = probs.shape[1], probs.shape[2]
    mlp_width, local_cols, half = down_a.shape[0], out_a.shape[0], width // 2
    mlp_rows = 4 * half + mlp_width
    grad_rows = 4 * half + local_cols + 3 * low.shape[1]
    chunks = mlp_rows // 2 // CHUNK
    copies = chunks * journey_copies(False) + 1
    hbm, near = pl.BlockSpec(memory_space=pl.ANY), pl.BlockSpec(memory_space=pltpu.VMEM)
    args = (
        middle, cond_b, cotangent, low, up_a, up_b, down_a, down_b, tokens, cond_a, attn, inner,
        qkv, sig, heads_out, gated, probs, in_a, in_b, out_a, out_b,
    )
    outs = [
        (hbm, (rows, width), LOW),
        (hbm, (rows, width), LOW),
        (hbm, (rows, width), LOW),
        (hbm, (2, 2, grad_rows, half), LOW),
        (near, (3, 1, width), WIDE),
        (near, (3, 1, width), WIDE),
        (hbm, (heads, count, count), WIDE),
        (near, (2 * EARLY * CHUNK, half), LOW),
        (near, (chunks - EARLY, CHUNK, half), LOW),
    ]
    scratch = [
        (middle.shape, WIDE),
        (cond_b.shape, WIDE),
        ((rows, width), LOW),
        (low.shape, LOW),
        ((2,) + up_a.shape, LOW),
        ((2,) + down_a.shape, LOW),
        ((2, rows, 2 * mlp_width), LOW),
        ((2, rows, mlp_width), LOW),
        ((2, 2, mlp_rows, half), LOW),
        (middle.shape, WIDE),
        ((rows, width), LOW),
        *((a.shape, a.dtype) for a in (tokens, inner, qkv, sig, heads_out, gated, probs)),
        ((2, 2, grad_rows, half), LOW),
        ((heads, count, count), WIDE),
        ((rows, 4 * local_cols), LOW),
        ((rows, local_cols), LOW),
    ]
    return pl.pallas_call(
        token_back_kernel,
        in_specs=[hbm] * len(args),
        out_specs=[spec for spec, _, _ in outs],
        out_shape=[sds(shape, dtype) for _, shape, dtype in outs],
        scratch_shapes=[
            *(pltpu.VMEM(shape, dtype) for shape, dtype in scratch),
            *journey_scratch(CHUNK, half) * EARLY,
            *near_scratch(CHUNK, half) * (chunks - EARLY),
            pltpu.SemaphoreType.DMA((64,)),
            pltpu.SemaphoreType.DMA((copies,)),
            pltpu.SemaphoreType.DMA((copies,)),
        ],
        compiler_params=remote_params(62, 1),
        cost_estimate=cost(90e9, 50e6),
        name="token_back",
    )(*args)


FIRST_ROWS, LAST_ROWS = 128, 64


def atom_back_kernel(
    atoms_hbm, gain_ref, qkv_w_ref, out_w_ref, agg_w_ref, ids_ref, inv_ref,
    qkv_hbm, probs_hbm, mixed_hbm, grad_ref, pair_ref, bias_grad_hbm, grads_ref, cond_bias_a_ref,
    cond_bias_b_ref, mlp_part_ref,
    keep_ref, got_ref, attn_out_ref, cond_out_ref, cond_other_ref,
    first_out_ref, first_other_ref, last_out_ref, last_other_ref, mlp_out_ref,
    pair, bias_grad, twin_bias, pair_grad, atoms_ref, qkv_ref, probs_ref, mixed_ref, kept_attn, kept_cond,
    after_grad, mixed_grad, key_grad, value_grad, proj_grad, atoms_grad, send_buffer,
    gain_grad, qkv_grad, out_grad, agg_grad, first_small, last_small, *rest,
):
    *buffers, local_sem, send_sem, recv_sem = rest
    links = Links(send_sem, recv_sem)
    local = Local(local_sem)
    samples, atoms, width = atoms_ref.shape
    groups, keys_in = probs_ref.shape[1], probs_ref.shape[2]
    queries_in = SPAN * QBLOCK
    scale = (width // ATOM_HEADS) ** (-0.5)
    cond_rows = cond_out_ref.shape[0]
    attn_rows = grads_ref.shape[2] - cond_rows
    attn_grads = grads_ref.at[:, :, :attn_rows, :]
    cond_grads = grads_ref.at[:, :, attn_rows:, :]
    pair_half = bias_grad.shape[1]
    own_rows = pl.ds(pl.multiple_of(links.core * pair_half, 8), pair_half)
    twin_rows = pl.ds(pl.multiple_of((1 - links.core) * pair_half, 8), pair_half)
    load_bias = local.start(bias_grad_hbm.at[:, own_rows, :], bias_grad)

    def load_kept(source, target):
        start = links.core * (source.shape[2] // 2)
        at = pl.ds(pl.multiple_of(start, 16), target.shape[2])
        return local.start(source.at[:, :, at, :], target)

    kept_loads = [load_kept(attn_grads, kept_attn), load_kept(cond_grads, kept_cond)]
    loads = [local.start(mixed_hbm, mixed_ref), local.start(atoms_hbm, atoms_ref)]
    later = [
        (local.start(qkv_hbm.at[s], qkv_ref.at[s]), local.start(probs_hbm.at[s], probs_ref.at[s]))
        for s in range(samples)
    ]
    links.barrier()
    bias_copy = links.send(bias_grad_hbm.at[:, twin_rows, :], twin_bias, links.twin)
    pool, each = Pool(buffers), 3 + far_slots()
    flow = Flow([])
    for i in range(mlp_part_ref.shape[0]):
        held, *slots = pool.take(each - 2)
        held[...] = mlp_part_ref[i]
        offset = i * mlp_part_ref.shape[1]
        flow.add(far_journey(links, held, slots, mlp_out_ref, None, offset, False))
    sums = {
        "attn": (attn_grads, kept_attn, attn_out_ref, None, ATTN_CHUNKS),
        "cond": (cond_grads, kept_cond, cond_out_ref, cond_other_ref, COND_CHUNKS),
    }
    taken = {"attn": 0, "cond": 0}
    for kind, x_first in ORDER:
        source, kept, out, other, sizes = sums[kind]
        i = taken[kind]
        taken[kind] += 1
        flow.add(
            journey(
                links, source, kept, pool.take(each), out, other, offsets(sizes)[i], sizes[i],
                x_first, other is not None,
            )
        )
    for copy in kept_loads:
        copy.wait()

    load_bias.wait()
    bias_copy.wait()
    heads = pair_grad.shape[0]
    slots = pair.shape[0]
    block = pair.shape[1]
    blocks = pair_ref.shape[0] // block

    def load_pair(i):
        return local.start(pair_ref.at[pl.ds(i * block, block)], pair.at[i % slots])

    pair_loads = [load_pair(i) for i in range(slots)]
    total = jnp.zeros(pair_grad.shape, WIDE)
    for i in range(blocks):
        pair_loads[i].wait()
        for j in range(block):
            one = bias_grad[:, i * block + j, :] + twin_bias[:, i * block + j, :]
            high = one.astype(LOW)
            tail = (one - high.astype(WIDE)).astype(LOW)
            both = mul(jnp.concatenate([high, tail], 0), pair[i % slots, j])
            total += both[:heads] + both[heads:]
        if i + slots < blocks:
            pair_loads.append(load_pair(i + slots))
        flow.after(0.08 * block)
    pair_grad[...] = total
    for copy in loads:
        copy.wait()

    for ref in (gain_grad, qkv_grad, out_grad, agg_grad):
        ref[...] = jnp.zeros_like(ref)
    chunk = 256
    token_ids = lax.broadcasted_iota(jnp.int32, (grad_ref.shape[1], chunk), 0)
    atom_copies = []
    for s in range(samples):
        token_grad = (grad_ref[s].astype(WIDE) * inv_ref[...]).astype(LOW)
        for i in range(atoms // chunk):
            rows = slice(i * chunk, (i + 1) * chunk)
            mixed = mixed_ref[s, rows, :]
            after = atoms_ref[s, rows, :].astype(WIDE) + mul(mixed, out_w_ref[...])
            after_low = after.astype(LOW)
            pre = mul(after_low, agg_w_ref[...])
            sigma = sigmoid(pre)
            member = jnp.where(token_ids == ids_ref[:, rows], 1.0, 0.0).astype(LOW)
            unit_grad = mul_tn(member, token_grad)
            pre_grad = (unit_grad * (sigma * (1.0 + pre * (1.0 - sigma)))).astype(LOW)
            agg_grad[...] += mul_tn(after_low, pre_grad)
            after_back = mul_nt(pre_grad, agg_w_ref[...])
            after_grad[s, rows, :] = after_back
            branch = after_back.astype(LOW)
            out_grad[...] += mul_tn(mixed, branch)
            mixed_grad[s, rows, :] = mul_nt(branch, out_w_ref[...]).astype(LOW)
            flow.after(1.7)
    heads = pair_grad.shape[0]
    wide = agg_grad.shape[1] // 2
    rows, part_rows = width // 2, width // 4

    def fill(values, cols):
        if values.shape[1] == cols:
            return values
        empty = jnp.zeros((values.shape[0], cols - values.shape[1]), WIDE)
        return jnp.concatenate([values, empty], 1)

    for h in range(2):
        to = relative(h, links.mp)
        cols = slice(h * wide, (h + 1) * wide)
        own_pair = jnp.where(links.mp == h, pair_grad[: heads // 2], pair_grad[heads // 2 :])
        for sec, cond_bias_ref in enumerate((cond_bias_a_ref, cond_bias_b_ref)):
            first_small[to, sec, :rows, :] = agg_grad[sec * rows : (sec + 1) * rows, cols].astype(LOW)
            first_row = sec * rows + h * part_rows
            block = fill(out_grad[first_row : first_row + part_rows], wide)
            first_small[to, sec, rows : rows + part_rows, :] = block.astype(LOW)
            block = [cond_bias_ref[k, :, cols] for k in range(3)]
            block += [jnp.zeros((5, wide), WIDE), fill(own_pair, wide)]
            block += [jnp.zeros((part_rows - 16, wide), WIDE)]
            first_small[to, sec, rows + part_rows :, :] = jnp.concatenate(block, 0).astype(LOW)
    flow.add(
        journey(
            links, first_small, None, pool.take(each), first_out_ref, first_other_ref,
            0, FIRST_ROWS // 2, False, True,
        )
    )
    for s in range(samples):
        for copy in later[s]:
            copy.wait()
        key_grad[...] = jnp.zeros_like(key_grad)
        value_grad[...] = jnp.zeros_like(value_grad)

        def attend(group, carry, s=s):
            base = key_base(group, atoms)
            start = pl.multiple_of(group * queries_in, queries_in)
            queries = spread(qkv_ref[s, pl.ds(start, queries_in), :width], ATOM_HEADS)
            grads = spread(mixed_grad[s, pl.ds(start, queries_in), :], ATOM_HEADS)
            keys = qkv_ref[s, pl.ds(base, keys_in), width : 2 * width]
            values = qkv_ref[s, pl.ds(base, keys_in), 2 * width :]
            probs_low = probs_ref[s, group]
            probs = probs_low.astype(WIDE)
            probs_grad = mul_nt(values, grads)
            mean = jnp.sum(probs * probs_grad, 0, keepdims=True)
            scores_grad = (probs * (probs_grad - mean)).astype(LOW)
            query_grad = gather_heads(mul_tn(scores_grad, keys), ATOM_HEADS)
            proj_grad[pl.ds(start, queries_in), :width] = (query_grad * scale).astype(LOW)
            key_grad[pl.ds(base, keys_in), :] += mul(scores_grad, queries)
            value_grad[pl.ds(base, keys_in), :] += mul(probs_low, grads)
            return carry

        cuts = 5
        for i in range(cuts):
            pairs(groups * i // cuts, groups * (i + 1) // cuts, attend)
            flow.after(1.7)
        proj_grad[:, width : 2 * width] = (key_grad[...] * scale).astype(LOW)
        proj_grad[:, 2 * width :] = value_grad[...].astype(LOW)
        gain = gain_ref[...].astype(WIDE)
        normed, inverse = layer_norm(atoms_ref[s].astype(WIDE))
        hidden = (normed * gain).astype(LOW)
        proj = proj_grad[...]
        qkv_grad[...] += mul_tn(hidden, proj)
        hidden_grad = mul_nt(proj, joined(qkv_w_ref))
        gain_grad[...] += jnp.sum(hidden_grad * normed, 0, keepdims=True)
        atoms_grad[...] = after_grad[s] + norm_back(normed, inverse, hidden_grad * gain)
        half = atoms // 2
        theirs = pl.ds(pl.multiple_of((1 - links.mp) * half, 16), half)
        send_buffer[s] = atoms_grad[theirs, :].astype(LOW)
        atom_copies.append(links.send(send_buffer.at[s], got_ref.at[s], links.y))
        keep_ref[s] = atoms_grad[pl.ds(pl.multiple_of(links.mp * half, 16), half), :]
        flow.after(2.5)

    for h in range(2):
        to = relative(h, links.mp)
        for sec in range(2):
            first_row = sec * rows + h * part_rows
            part = fill(qkv_grad[first_row : first_row + part_rows], wide)
            last_small[to, sec, :part_rows, :] = part.astype(LOW)
            block = [fill(gain_grad[...], wide), jnp.zeros((part_rows - 1, wide), WIDE)]
            last_small[to, sec, part_rows:, :] = jnp.concatenate(block, 0).astype(LOW)
    flow.add(
        journey(
            links, last_small, None, pool.take(each), last_out_ref, last_other_ref,
            0, LAST_ROWS // 2, False, True,
        )
    )
    flow.finish()
    for copy in atom_copies:
        copy.wait()


def atom_back(
    atoms, gain, qkv_w, out_w, agg_w, ids, inverse_counts, qkv, probs, mixed, grad,
    low_pair, bias_grad, grads, cond_bias_a, cond_bias_b, mlp_part, cond_rows,
):
    samples, count, width = atoms.shape
    wide = agg_w.shape[1]
    cols = grads.shape[3]
    attn_rows = grads.shape[2] - cond_rows
    copies = len(ATTN_CHUNKS) * journey_copies(False)
    copies += len(COND_CHUNKS) * journey_copies(True)
    copies += 2 * journey_copies(True) + samples + 1
    half_bias = (bias_grad.shape[0], bias_grad.shape[1] // 2, bias_grad.shape[2])
    copies += mlp_part.shape[0] * journey_copies(False, near=0)
    outs = [
        sds((samples, count // 2, width), WIDE),
        sds((samples, count // 2, width), LOW),
        sds((attn_rows, cols), LOW),
        sds((cond_rows, cols), LOW),
        sds((cond_rows, cols), LOW),
        sds((FIRST_ROWS, cols), LOW),
        sds((FIRST_ROWS, cols), LOW),
        sds((LAST_ROWS, cols), LOW),
        sds((LAST_ROWS, cols), LOW),
        sds((2 * mlp_part.shape[0] * CHUNK, cols), LOW),
    ]
    args = (
        atoms, gain, qkv_w, out_w, agg_w, ids, inverse_counts, qkv, probs, mixed, grad,
        low_pair, bias_grad, grads, cond_bias_a, cond_bias_b, mlp_part,
    )
    hbm, near = pl.BlockSpec(memory_space=pl.ANY), pl.BlockSpec(memory_space=pltpu.VMEM)
    return pl.pallas_call(
        atom_back_kernel,
        in_specs=[hbm] + [near] * 6 + [hbm] * 3 + [near] + [hbm] * 3 + [near] * 3,
        out_specs=everywhere(len(outs)),
        out_shape=outs,
        scratch_shapes=[
            pltpu.VMEM((2, 8) + low_pair.shape[1:], LOW),
            pltpu.VMEM(half_bias, WIDE),
            pltpu.VMEM(half_bias, WIDE),
            pltpu.VMEM((bias_grad.shape[0], width), WIDE),
            *(pltpu.VMEM(a.shape, a.dtype) for a in (atoms, qkv, probs, mixed)),
            pltpu.VMEM((2, 2, attn_rows // 2, cols), LOW),
            pltpu.VMEM((2, 2, cond_rows // 2, cols), LOW),
            pltpu.VMEM((samples, count, width), WIDE),
            pltpu.VMEM((samples, count, width), LOW),
            pltpu.VMEM((count, width), WIDE),
            pltpu.VMEM((count, width), WIDE),
            pltpu.VMEM((count, 3 * width), LOW),
            pltpu.VMEM((count, width), WIDE),
            pltpu.VMEM((samples, count // 2, width), LOW),
            pltpu.VMEM((1, width), WIDE),
            pltpu.VMEM((width, 3 * width), WIDE),
            pltpu.VMEM((width, width), WIDE),
            pltpu.VMEM((width, wide), WIDE),
            pltpu.VMEM((2, 2, FIRST_ROWS, cols), LOW),
            pltpu.VMEM((2, 2, LAST_ROWS, cols), LOW),
            *([pltpu.VMEM((CHUNK, cols), LOW)] + far_scratch(CHUNK, cols)) * mlp_part.shape[0],
            *(b for _ in ORDER for b in journey_scratch(CHUNK, cols)),
            *journey_scratch(FIRST_ROWS // 2, cols),
            *journey_scratch(LAST_ROWS // 2, cols),
            pltpu.SemaphoreType.DMA((32,)),
            pltpu.SemaphoreType.DMA((copies,)),
            pltpu.SemaphoreType.DMA((copies,)),
        ],
        compiler_params=remote_params(60, 2),
        cost_estimate=cost(60e9, 24e6),
        name="atom_back",
    )(*args)


def results_kernel(*refs):
    number, count = 13, 13
    hbm_in, hbm_out = refs[:number], refs[number : number + count]
    scratch, sem = refs[number + count : -1], refs[-1]
    near_in, near_out = scratch[:number], scratch[number:]
    local = Local(sem)
    loads = [local.start(a, b) for a, b in zip(hbm_in, near_in)]
    (
        cond_ref, cond_other_ref, attn_ref, mlp_first_ref, mlp_late_ref, keep_ref, got_ref,
        result_ref, other_result_ref, first_ref, first_other_ref, last_ref, last_other_ref,
    ) = near_in
    (
        token_out, atoms_out, gain_out, qkv_out, out_out, agg_out, cond_out, cond_bias_out,
        pair_out, in_out, attn_out, up_out, down_out,
    ) = near_out
    mp, section = lax.axis_index("mp"), lax.axis_index("section")

    def wait(*indices):
        for index in indices:
            loads[index].wait()

    def store(*outs):
        for out in outs:
            index = [i for i, ref in enumerate(near_out) if ref is out][0]
            local.store(out, hbm_out[index])

    half = cond_ref.shape[1]
    size = cond_out.shape[1]
    wait(0, 1)
    for h in range(2):
        cols = slice(h * half, (h + 1) * half)
        for k in range(3):
            at = slice(k * size, (k + 1) * size)
            value = jnp.where(mp == h, cond_ref[at, :], cond_other_ref[at, :])
            cond_out[k, :, cols] = value.astype(WIDE)
    store(cond_out)
    wait(2)
    blocks = in_out.shape[1]
    for k in range(blocks):
        in_out[:, k, :] = attn_ref[k * half : (k + 1) * half, :].astype(WIDE)
    store(in_out)
    attn_out[...] = attn_ref[blocks * half :, :].astype(WIDE)
    store(attn_out)
    wait(3, 4)
    core_first, core_late = mlp_first_ref.shape[0] // 2, mlp_late_ref.shape[0] // 2
    down_rows = down_out.shape[0] // 2
    for core in range(2):
        at = slice(core * down_rows, (core + 1) * down_rows)
        start = core * core_first
        down_out[at, :] = mlp_first_ref[start : start + down_rows, :].astype(WIDE)
        row = 0
        for ref, begin, end in (
            (mlp_first_ref, start + down_rows, start + core_first),
            (mlp_late_ref, core * core_late, (core + 1) * core_late),
        ):
            while begin < end:
                block, within = row // half, row % half
                some = min(end - begin, half - within)
                up_out[within : within + some, core, block * half : (block + 1) * half] = ref[
                    begin : begin + some, :
                ].astype(WIDE)
                begin, row = begin + some, row + some
    store(up_out, down_out)
    wait(5, 6)
    samples = keep_ref.shape[0]
    here, there = pl.ds(mp * samples, samples), pl.ds((1 - mp) * samples, samples)
    atoms_out[here] = keep_ref[...]
    atoms_out[there] = got_ref[...].astype(WIDE)
    store(atoms_out)
    wait(7, 8)
    token_out[here] = result_ref[...]
    token_out[there] = other_result_ref[...]
    store(token_out)
    wait(9, 10, 11, 12)
    width, rows = atoms_out.shape[2], out_out.shape[0]
    part_rows = rows // 2

    def own_lanes(values):
        return jnp.where(section == 0, values[:, :rows], values[:, rows:width])

    gain_out[...] = own_lanes(last_ref[part_rows : part_rows + 16, :].astype(WIDE))[:1]
    pair = first_ref[rows + part_rows : rows + part_rows + 16, :].astype(WIDE)
    pair_out[...] = own_lanes(pair[8:])
    for h in range(2):
        first = jnp.where(mp == h, first_ref[...], first_other_ref[...]).astype(WIDE)
        last = jnp.where(mp == h, last_ref[...], last_other_ref[...]).astype(WIDE)
        cols = slice(h * half, (h + 1) * half)
        part_at = slice(h * part_rows, (h + 1) * part_rows)
        agg_out[:, cols] = first[:rows]
        out_out[part_at, :] = first[rows : rows + part_rows, :width]
        for k in range(3):
            row = rows + part_rows + k
            cond_bias_out[k, :, cols] = first[row : row + 1]
        for k in range(3):
            qkv_out[k, part_at, :] = last[:part_rows, k * width : (k + 1) * width]
    store(gain_out, pair_out, agg_out, out_out, cond_bias_out, qkv_out)
    local.finish()


def results(
    result, other_result, keep, got, first, first_other, last, last_other, cond, cond_other, attn,
    mlp_first, mlp_late, width, mlp_local,
):
    samples, half_atoms, atom_width = keep.shape
    half, rows = width // 2, atom_width // 2
    attn_local = attn.shape[0] - 4 * half
    hbm = pl.BlockSpec(memory_space=pl.ANY)
    outs = [
        sds((2 * samples,) + result.shape[1:], LOW),
        sds((2 * samples, half_atoms, atom_width), WIDE),
        sds((1, rows), WIDE),
        sds((3, rows, atom_width), WIDE),
        sds((rows, atom_width), WIDE),
        sds((rows, width), WIDE),
        sds((3, cond.shape[0] // 3, width), WIDE),
        sds((3, 1, width), WIDE),
        sds((8, rows), WIDE),
        sds((half, 4, attn_local), WIDE),
        sds((attn_local, half), WIDE),
        sds((half, 2, mlp_local), WIDE),
        sds((mlp_local, half), WIDE),
    ]
    args = (
        cond, cond_other, attn, mlp_first, mlp_late, keep, got, result, other_result, first,
        first_other, last, last_other,
    )
    return pl.pallas_call(
        results_kernel,
        in_specs=[hbm] * len(args),
        out_specs=[hbm] * len(outs),
        out_shape=outs,
        scratch_shapes=[
            *(pltpu.VMEM(a.shape, a.dtype) for a in args),
            *(pltpu.VMEM(a.shape, a.dtype) for a in outs),
            pltpu.SemaphoreType.DMA((32,)),
        ],
        compiler_params=params(60),
        cost_estimate=cost(1e8, 20e6),
        name="results",
    )(*args)


def local(
    atoms_in,
    atom_token,
    window_start,
    noise_level,
    level_table,
    single_trunk,
    pair,
    atom_gain,
    atom_qkv,
    atom_out,
    atom_agg,
    cond_weight,
    cond_bias,
    pair_weight,
    attn_in,
    attn_out,
    mlp_up,
    mlp_down,
    cotangent,
):
    section, mp = lax.axis_index("section"), lax.axis_index("mp")
    batch, half_atoms, atom_width = atoms_in.shape
    batch //= MICRO
    samples = batch // 2
    atoms = 2 * half_atoms
    tokens, width = cotangent.shape[1], cotangent.shape[2]
    single = single_trunk.shape[1]
    gain = atom_gain[None, :]
    qkv_w = jnp.transpose(atom_qkv, (1, 0, 2))

    cond_w = jnp.transpose(cond_weight, (0, 2, 1, 3)).reshape(6, single, width)
    (
        low, cond_a, cond_b, low_pair, bias, all_atoms, qkv, probs, mixed, token_in,
        in_b, out_b, up_b, down_b, inverse_counts, in_a, up_a,
    ) = front(
        single_trunk, noise_level, level_table, cond_w, jnp.transpose(cond_bias, (1, 0, 2)), pair,
        pair_weight.T,
        atoms_in, gain, qkv_w, atom_out, atom_agg, window_start, atom_token[None, :],
        attn_in, attn_out, mlp_up, mlp_down,
    )
    token_in = token_in.reshape(-1, width)
    inner, token_qkv, sig, heads_out, gated, token_probs, attn, middle = token_attention(
        token_in, cond_a, bias, in_a, in_b, attn_out, out_b
    )
    (
        result, other_result, token_grad, attn_grads, cond_bias_a, cond_bias_b, bias_grad, mlp_first,
        mlp_part,
    ) = (
        token_back(
            middle, cond_b, cotangent, low, up_a, up_b, mlp_down, down_b, token_in, cond_a, attn,
            inner, token_qkv, sig, heads_out, gated, token_probs, in_a, in_b, attn_out, out_b,
        )
    )
    (
        keep, got, attn_sum, cond_sum, cond_other, first, first_other, last, last_other, mlp_late,
    ) = atom_back(
        all_atoms, gain, qkv_w, atom_out, atom_agg, atom_token[None, :], inverse_counts,
        qkv, probs, mixed, token_grad.reshape(samples, tokens, width),
        low_pair, bias_grad, attn_grads, cond_bias_a, cond_bias_b, mlp_part, 3 * single,
    )

    outs = results(
        result.reshape(samples, tokens, width), other_result.reshape(samples, tokens, width),
        keep, got, first, first_other, last, last_other, cond_sum, cond_other, attn_sum,
        mlp_first, mlp_late, width, mlp_up.shape[2],
    )
    token_out, atoms_out, gain_out, qkv_out, out_out, agg_out, cond_out = outs[:7]
    cond_bias_out, pair_out, in_out, attn_out_grad, up_out, down_out = outs[7:]
    return (
        token_out.reshape(1, 1, batch, tokens, width),
        atoms_out.reshape(1, 1, batch, half_atoms, atom_width),
        gain_out[0],
        jnp.transpose(qkv_out, (1, 0, 2)),
        out_out,
        agg_out,
        jnp.transpose(cond_out, (1, 0, 2))[None],
        jnp.transpose(cond_bias_out, (1, 0, 2)),
        pair_out.T,
        in_out,
        attn_out_grad,
        up_out,
        down_out,
    )


def solution(mesh):
    in_specs = (
        P("dp", "mp", None),
        P(),
        P("mp"),
        P("dp"),
        P(),
        P(),
        P(),
        P(),
        P(),
        P(),
        P(),
        P(),
        P(),
        P(None, "mp"),
        P(None, None, "mp"),
        P("mp", None),
        P(None, None, "mp"),
        P("mp", None),
        P("dp", None, None),
    )
    out_specs = (
        P("dp", "section", None, None, None),
        P("dp", "section", None, "mp", None),
        P("section"),
        P("section", None, None),
        P("section", None),
        P("section", None),
        P("section", None, None, None),
        P("section", None, None),
        P("section", "mp"),
        P("section", None, "mp"),
        P("mp", "section"),
        P("section", None, "mp"),
        P("mp", "section"),
    )
    return jax.shard_map(local, mesh=mesh, in_specs=in_specs, out_specs=out_specs, check_vma=False)
```
